32 devices in a mesh: dp: 8 (over z, x), tensor: 4 (over y, core).
Axes of the slice: x: 2, y: 2, z: 4, core: 2. Of those that a mesh axis runs over, the one named last changes fastest.
Arguments:
- tokens: bfloat16 [1024, 2048], P('dp'), may hold values from -6 to 6
- segments: int32 [1024], replicated, may hold values from 0 to 2, as said below
- routes: int32 [1024, 8], P(('dp', 'tensor')), may hold values from 0 to 31, all different within a row; in each aligned block of 32 rows (0 to 31, 32 to 63, ...) at most 16 rows name the same one
- out_grad: bfloat16 [1024, 2048], P(('dp', 'tensor')), may hold values from -6 to 6
- norm_gain: bfloat16 [2048], replicated, may hold values from 0.5 to 1.5
- q_weight: bfloat16 [2048, 4096], P('dp', 'tensor'), may hold values from -0.125 to 0.125
- k_weight: bfloat16 [2048, 512], P('dp', 'tensor'), may hold values from -0.125 to 0.125
- v_weight: bfloat16 [2048, 512], P('dp', 'tensor'), may hold values from -0.125 to 0.125
- q_gain: bfloat16 [128], replicated, may hold values from 0.796875 to 1.59375
- k_gain: bfloat16 [128], replicated, may hold values from 0.796875 to 1.59375
- out_weight: bfloat16 [2048, 4096], P('dp', 'tensor'), may hold values from -0.75 to 0.75
- moe_gain: bfloat16 [2048], replicated, may hold values from 0.5 to 1.5
- router_weight: bfloat16 [2048, 32], replicated, may hold values from -0.0625 to 0.0625
- gate_weight: bfloat16 [32, 2048, 768], P(('dp', 'tensor')), may hold values from -0.125 to 0.125
- up_weight: bfloat16 [32, 2048, 768], P(('dp', 'tensor')), may hold values from -0.125 to 0.125
- down_weight: bfloat16 [32, 768, 2048], P(('dp', 'tensor')), may hold values from -0.875 to 0.875
Outputs:
- layer_out: bfloat16 [1024, 2048], P(('dp', 'tensor'))
- tokens_grad: float32 [1024, 2048], P(('dp', 'tensor'))
- norm_gain_grad: float32 [2048], replicated
- q_weight_grad: float32 [2048, 4096], P('dp', 'tensor')
- k_weight_grad: float32 [2048, 512], P('dp', 'tensor')
- v_weight_grad: float32 [2048, 512], P('dp', 'tensor')
- q_gain_grad: float32 [128], replicated
- k_gain_grad: float32 [128], replicated
- out_weight_grad: float32 [2048, 4096], P('dp', 'tensor')
- moe_gain_grad: float32 [2048], replicated
- router_weight_grad: float32 [2048, 32], replicated
- gate_weight_grad: float32 [32, 2048, 768], P(('dp', 'tensor'))
- up_weight_grad: float32 [32, 2048, 768], P(('dp', 'tensor'))
- down_weight_grad: float32 [32, 768, 2048], P(('dp', 'tensor'))
The draws below stay inside these ranges and needn't reach their ends.
Inputs may be any that keep to these rules, and one draw needn't show every extreme that they name: `routes`: each row names 8 different experts; in every aligned block of 32 rows no expert is named by more than 16 rows. `segments`: document numbers never fall along the tokens; document 1 begins within the first 128 tokens and ends within the last 128; documents 0 and 2 are not empty.
All inputs are finite; a program needn't handle non-finite values.
Results may differ from the reference program's by a relative error of at most 0.025.
Values may be sent and summed in bfloat16 or wider, within the bound.
A program may use at most 192 MiB of HBM per device.

```python
import math
import jax
import jax.numpy as jnp
import numpy as np
from jax import lax

D = 2048
HEADS = 32
KV_HEADS = 4
HEAD_DIM = 128
EXPERT_FF = 768
TOPK = 8
TOK_DEV = 128
EXPERTS = 32
TOKENS = 1024
TOK_Q = 32
CAP = 16


def draw_segments(key, part):
    key = jax.random.fold_in(key, 11)
    front_key, back_key = jax.random.split(key)
    opening = jax.random.randint(front_key, (), 1, TOK_DEV)
    closing = jax.random.randint(back_key, (), TOKENS - TOK_DEV + 1, TOKENS)
    places = jnp.arange(TOKENS)
    return (places >= opening).astype(jnp.int32) + (places >= closing).astype(jnp.int32)


def level_of(own_key, shape, cuts, smallest, largest):
    def one(position, parts):
        draws = jax.random.uniform(jax.random.fold_in(jax.random.fold_in(own_key, 6), position), (parts,), jnp.float32, smallest / len(cuts), largest / len(cuts))
        return jnp.repeat(jnp.exp(draws), shape[position] // parts).reshape((-1,) + (1,) * (len(shape) - position - 1))

    factor_of = one(*cuts[0])
    for cut in cuts[1:]:
        factor_of = factor_of * one(*cut)
    return factor_of


def assign_block(key, own, number, rows, count, top, most, lean):
    order = jax.random.permutation(key, count)
    heavy_load, usual = load_shares(count, rows * top, most, lean, True), load_shares(count, rows * top, most, lean, False)
    places = jnp.arange(count)

    def named(sizes, turn):
        used = int((sizes > 0).sum())
        fixed = max(1, used // 4)
        passed = fixed + (places - fixed + turn * (used - fixed)) % max(1, count - fixed)
        return jnp.zeros((count,), jnp.int32).at[order[jnp.where(places < fixed, places, passed)]].set(jnp.asarray(sizes, jnp.int32))

    sizes = jnp.where(number % 4 == 0, named(heavy_load, number // 4), named(usual, number - number // 4 - 1))
    mixed = jax.random.permutation(jax.random.fold_in(own, 3), count)
    giver, receiver = mixed[0:count // 2 * 2:2], mixed[1:count // 2 * 2:2]
    margin = jnp.minimum(sizes[giver] - 1, most - sizes[receiver]) // 2
    margin = jnp.where((giver == order[0]) | (receiver == order[0]) | (sizes[receiver] == 0), 0, jnp.maximum(margin, 0))
    passed = jax.random.randint(jax.random.fold_in(own, 4), (count // 2,), 0, 1 << 20) % (margin + 1)
    sizes = sizes.at[giver].add(-passed).at[receiver].add(passed)
    members = jnp.searchsorted(jnp.cumsum(sizes), jnp.arange(rows * top), side="right").astype(jnp.int32)
    listing = members.reshape(top, rows).T
    listing = listing[jax.random.permutation(jax.random.fold_in(own, 1), rows)]
    turn = jax.random.randint(jax.random.fold_in(own, 2), (rows, 1), 0, top)
    return jnp.take_along_axis(listing, (jnp.arange(top)[None, :] + turn) % top, axis=1)


def load_shares(count, total, limit, lean, full):
    loads = [(1 << 20) // math.isqrt(rank ** lean) + 1 for rank in range(1, count + 1)]
    largest = limit if full else min(limit, max(-(-total // count), total * loads[0] // sum(loads)))
    least = 1 if total - largest >= count - 1 else 0
    given, surplus = [largest] + [least] * (count - 1), total - largest - least * (count - 1)
    while surplus > 0:
        free = [i for i in range(1, count) if given[i] < largest] or [i for i in range(1, count) if given[i] < limit]
        whole, remaining = sum([loads[i] for i in free]), surplus
        for i in free:
            more = min(limit - given[i], max(1, remaining * loads[i] // whole), surplus)
            given[i] = given[i] + more
            surplus = surplus - more
    return np.array(given)


def centred(key, dims, deviation, most, pieces=(), kind=jnp.bfloat16):
    level = level_of(key, dims, pieces, -0.22, 0.18) if pieces else 1.0
    values = jax.random.normal(key, dims, jnp.float32) * deviation * level
    return jnp.minimum(jnp.maximum(values, -most), most).astype(kind)


def setup_inputs(seed: int = 0) -> dict:
    keys = jax.random.split(jax.random.key(seed), 17)
    tokens = centred(keys[0], (TOKENS, D), 1.0, 6.0, ((0, 8),))
    segments = draw_segments(jax.random.fold_in(keys[16], 71), 0)
    routes_keys = jax.random.split(jax.random.fold_in(keys[2], 1), TOKENS // TOK_Q)
    routes_turns = jax.random.permutation(jax.random.fold_in(keys[2], 3), TOKENS // TOK_Q)
    routes = jax.vmap(lambda own, number: assign_block(jax.random.fold_in(keys[2], 2), own, number, TOK_Q, EXPERTS, TOPK, CAP, 1))(routes_keys, routes_turns).reshape((TOKENS, TOPK))
    out_grad = centred(keys[3], (TOKENS, D), 1.0, 6.0, ((0, 32),))
    norm_gain = jnp.clip(1.0 + 0.1 * jax.random.normal(keys[4], (D,), jnp.float32), 0.5, 1.5).astype(jnp.bfloat16)
    q_weight = centred(keys[5], (D, HEADS * HEAD_DIM), D ** -0.5, 0.125, ((0, 8), (1, 4)))
    k_weight = centred(keys[6], (D, KV_HEADS * HEAD_DIM), D ** -0.5, 0.125, ((0, 8), (1, 4)))
    v_weight = centred(keys[7], (D, KV_HEADS * HEAD_DIM), D ** -0.5, 0.125, ((0, 8), (1, 4)))
    q_gain = jnp.clip(jax.random.uniform(keys[8], (HEAD_DIM,), jnp.float32, 0.796875, 1.59375), 0.796875, 1.59375).astype(jnp.bfloat16)
    k_gain = jnp.clip(jax.random.uniform(keys[9], (HEAD_DIM,), jnp.float32, 0.796875, 1.59375), 0.796875, 1.59375).astype(jnp.bfloat16)
    out_weight = centred(keys[10], (D, HEADS * HEAD_DIM), (HEADS * HEAD_DIM // 64) ** -0.5, 0.75, ((0, 8), (1, 4)))
    moe_gain = jnp.clip(1.0 + 0.1 * jax.random.normal(keys[11], (D,), jnp.float32), 0.5, 1.5).astype(jnp.bfloat16)
    router_weight = centred(keys[12], (D, EXPERTS), (4 * D) ** -0.5, 0.0625)
    gate_weight = centred(keys[13], (EXPERTS, D, EXPERT_FF), D ** -0.5, 0.125, ((0, 32),))
    up_weight = centred(keys[14], (EXPERTS, D, EXPERT_FF), D ** -0.5, 0.125, ((0, 32),))
    down_weight = centred(keys[15], (EXPERTS, EXPERT_FF, D), (EXPERT_FF // 16) ** -0.5, 0.875, ((0, 32),))
    return dict(tokens=tokens, segments=segments, routes=routes, out_grad=out_grad, norm_gain=norm_gain, q_weight=q_weight, k_weight=k_weight, v_weight=v_weight, q_gain=q_gain, k_gain=k_gain, out_weight=out_weight, moe_gain=moe_gain, router_weight=router_weight, gate_weight=gate_weight, up_weight=up_weight, down_weight=down_weight)


EPS = 1e-06
THETA = 1000000.0
HIGHEST = lax.Precision.HIGHEST

@jax.custom_vjp
def low(v):
    return lax.optimization_barrier(v.astype(jnp.bfloat16)).astype(jnp.float32)

@jax.custom_vjp
def low_back(v):
    return v

def low_keep(v):
    return (low(v), None)

def low_pass(kept, grad):
    return (grad,)

def back_keep(v):
    return (v, None)

def back_low(kept, grad):
    return (low(grad),)
low.defvjp(low_keep, low_pass)
low_back.defvjp(back_keep, back_low)

def norm_rows(values, gain):
    return values * lax.rsqrt(lax.optimization_barrier(jnp.mean(values * values, axis=-1, keepdims=True)) + EPS) * gain

def rotary(values, cosine, sine_part):
    half_dim = values.shape[-1] // 2
    front_half = values[..., :half_dim]
    back_half = values[..., half_dim:]
    return jnp.concatenate([front_half * cosine - back_half * sine_part, back_half * cosine + front_half * sine_part], axis=-1)

def angles(positions, head_dim):
    half_dim = head_dim // 2
    frequency = THETA ** (-(jnp.arange(half_dim).astype(jnp.float32) * 2.0) / head_dim)
    rotation = positions.astype(jnp.float32)[:, None] * frequency[None, :]
    return (jnp.cos(rotation), jnp.sin(rotation))

def doc_positions(segments):
    token_count = segments.shape[0]
    places = jnp.arange(token_count).astype(jnp.int32)
    begins = jnp.concatenate([jnp.ones((1,), dtype=bool), segments[1:] != segments[:-1]])
    heads_at = lax.cummax(jnp.where(begins, places, 0), axis=0)
    return places - heads_at

def attention(queries, keys_all, values_all, segments):
    token_count = queries.shape[0]
    query_block = min(512, token_count)
    group = HEADS // KV_HEADS
    places = jnp.arange(token_count).astype(jnp.int32)
    score_scale = HEAD_DIM ** (-0.5)

    def one_block(offset):
        query_rows = lax.dynamic_slice_in_dim(queries, offset, query_block, 0).reshape(query_block, KV_HEADS, group, HEAD_DIM)
        row_places = offset + jnp.arange(query_block).astype(jnp.int32)
        row_docs = lax.dynamic_slice_in_dim(segments, offset, query_block, 0)
        scores = low_back(jnp.einsum('bkgd,tkd->kgbt', query_rows, keys_all, precision=HIGHEST) * score_scale)
        allowed = (places[None, :] <= row_places[:, None]) & (segments[None, :] == row_docs[:, None])
        scores = jnp.where(allowed, scores, -1e+30)
        log_total = jax.nn.logsumexp(scores, axis=-1, keepdims=True)
        soft_weights = low(jnp.exp(scores - log_total))
        head_out = jnp.einsum('kgbt,tkd->bkgd', soft_weights, values_all, precision=HIGHEST)
        return low(low_back(head_out)).reshape(query_block, HEADS * HEAD_DIM)
    block_starts = (jnp.arange(token_count // query_block) * query_block).astype(jnp.int32)
    return lax.map(jax.checkpoint(one_block), block_starts).reshape(token_count, HEADS * HEAD_DIM)

def layer_forward(tokens, norm_gain, q_weight, k_weight, v_weight, q_gain, k_gain, out_weight, moe_gain, router_weight, gate_weight, up_weight, down_weight, segments, routes, cosine, sine_part):
    token_count = tokens.shape[0]
    hidden = low(norm_rows(tokens, norm_gain))
    projected_q = low_back(jnp.dot(hidden, q_weight, precision=HIGHEST)).reshape(token_count, HEADS, HEAD_DIM)
    projected_k = low_back(jnp.dot(hidden, k_weight, precision=HIGHEST)).reshape(token_count, KV_HEADS, HEAD_DIM)
    projected_v = low_back(jnp.dot(hidden, v_weight, precision=HIGHEST)).reshape(token_count, KV_HEADS, HEAD_DIM)
    queries = low(rotary(norm_rows(projected_q, q_gain), cosine[:, None, :], sine_part[:, None, :]))
    keys_all = low(rotary(norm_rows(projected_k, k_gain), cosine[:, None, :], sine_part[:, None, :]))
    values_all = low(projected_v)
    attended = attention(queries, keys_all, values_all, segments)
    branch = low_back(jnp.dot(attended, out_weight.T, precision=HIGHEST))
    middle = tokens + branch
    normed = low(norm_rows(middle, moe_gain))
    logits = low_back(jnp.dot(normed, router_weight, precision=HIGHEST))
    probabilities = jax.nn.softmax(logits, axis=-1)
    chosen = jnp.take_along_axis(probabilities, routes, axis=1)
    gate_values = chosen / lax.optimization_barrier(jnp.sum(chosen, axis=1, keepdims=True))
    combine = lax.optimization_barrier(jnp.sum(gate_values[:, :, None] * jax.nn.one_hot(routes, EXPERTS, dtype=jnp.float32), axis=1))

    def expert_step(running, packed):
        w_gate, w_up, w_down, column = packed
        inputs = low_back(normed)
        gate_act = low_back(jnp.dot(inputs, w_gate, precision=HIGHEST))
        up_act = low_back(jnp.dot(inputs, w_up, precision=HIGHEST))
        inner_act = low(jax.nn.silu(gate_act) * up_act)
        returned = low(low_back(jnp.dot(inner_act, w_down, precision=HIGHEST)))
        return (running + column[:, None] * returned, None)
    expert_sum, _ = lax.scan(jax.checkpoint(expert_step), jnp.zeros_like(middle), (gate_weight, up_weight, down_weight, combine.T))
    return middle + expert_sum

def reference(tokens, segments, routes, out_grad, norm_gain, q_weight, k_weight, v_weight, q_gain, k_gain, out_weight, moe_gain, router_weight, gate_weight, up_weight, down_weight):
    positions = doc_positions(segments)
    cosine, sine_part = angles(positions, HEAD_DIM)

    def forward(tokens_in, norm_in, query_in, key_in, value_in, qgain_in, kgain_in, output_in, moegain_in, router_in, gate_in, up_in, down_in):
        return layer_forward(tokens_in, norm_in, query_in, key_in, value_in, qgain_in, kgain_in, output_in, moegain_in, router_in, gate_in, up_in, down_in, segments, routes, cosine, sine_part)
    result, pullback = jax.vjp(forward, tokens.astype(jnp.float32), norm_gain.astype(jnp.float32), q_weight.astype(jnp.float32), k_weight.astype(jnp.float32), v_weight.astype(jnp.float32), q_gain.astype(jnp.float32), k_gain.astype(jnp.float32), out_weight.astype(jnp.float32), moe_gain.astype(jnp.float32), router_weight.astype(jnp.float32), gate_weight.astype(jnp.float32), up_weight.astype(jnp.float32), down_weight.astype(jnp.float32))
    grads = pullback(out_grad.astype(jnp.float32))
    return (result.astype(jnp.bfloat16), grads[0], grads[1], grads[2], grads[3], grads[4], grads[5], grads[6], grads[7], grads[8], grads[9], grads[10], grads[11], grads[12])
```

```python
import functools

import jax
import jax.numpy as jnp
from jax import lax
from jax.experimental import pallas as pl
from jax.experimental.pallas import tpu as pltpu
from jax.sharding import PartitionSpec as P

EPS = 1e-06
THETA = 1000000.0


def norm_rows(values, gain):
    return values * lax.rsqrt(jnp.mean(values * values, axis=-1, keepdims=True) + EPS) * gain


def rotary(values, cosine, sine_part):
    half_dim = values.shape[-1] // 2
    front_half = values[..., :half_dim]
    back_half = values[..., half_dim:]
    return jnp.concatenate(
        [front_half * cosine - back_half * sine_part, back_half * cosine + front_half * sine_part],
        axis=-1,
    )


def angles(positions, head_dim):
    half_dim = head_dim // 2
    frequency = THETA ** (-(jnp.arange(half_dim).astype(jnp.float32) * 2.0) / head_dim)
    rotation = positions.astype(jnp.float32)[:, None] * frequency[None, :]
    return (jnp.cos(rotation), jnp.sin(rotation))


def prepare(projected, q_gain, k_gain, cosine, sine_part, head_dim):
    tok_rows = projected.shape[0]
    query_width = projected.shape[1] - 2 * head_dim
    queries = projected[:, :query_width].reshape(tok_rows, query_width // head_dim, head_dim)
    keys_local = projected[:, query_width : query_width + head_dim]
    values_local = projected[:, query_width + head_dim :]
    queries = rotary(norm_rows(queries, q_gain), cosine[:, None, :], sine_part[:, None, :])
    keys_local = rotary(norm_rows(keys_local, k_gain), cosine, sine_part)
    return (queries, keys_local, values_local)


def swiglu(gate_in, up_in):
    return jax.nn.silu(gate_in) * up_in


def shards(
    tokens,
    segments,
    routes,
    out_grad,
    norm_gain,
    q_weight,
    k_weight,
    v_weight,
    q_gain,
    k_gain,
    out_weight,
    moe_gain,
    router_weight,
    gate_weight,
    up_weight,
    down_weight,
):
    head_dim = q_gain.shape[0]
    tok_rows = tokens.shape[0]
    model_width = tokens.shape[1]
    share_rows = out_grad.shape[0]
    all_tokens = segments.shape[0]
    expert_count = router_weight.shape[1]
    top_count = routes.shape[1]
    capacity = max(2, share_rows * top_count * 2 // expert_count)
    score_scale = head_dim ** (-0.5)
    first_row = lax.axis_index("dp") * tok_rows
    places = jnp.arange(all_tokens, dtype=jnp.int32)
    begins = jnp.concatenate([jnp.ones((1,), dtype=bool), segments[1:] != segments[:-1]])
    positions = places - lax.cummax(jnp.where(begins, places, 0), axis=0)
    local_positions = lax.dynamic_slice_in_dim(positions, first_row, tok_rows)
    local_docs = lax.dynamic_slice_in_dim(segments, first_row, tok_rows)
    query_places = first_row + jnp.arange(tok_rows, dtype=jnp.int32)
    cosine, sine_part = angles(local_positions, head_dim)
    weight_rows = (
        lax.all_gather(q_weight, "dp", axis=0, tiled=True),
        lax.all_gather(k_weight, "dp", axis=0, tiled=True),
        lax.all_gather(v_weight, "dp", axis=0, tiled=True),
        lax.all_gather(out_weight, "dp", axis=0, tiled=True),
    )
    input_weight = jnp.concatenate([weight_rows[0], weight_rows[1], weight_rows[2]], axis=1)
    output_weight = weight_rows[3]
    tokens_float = tokens.astype(jnp.float32)
    norm_gain_float = norm_gain.astype(jnp.float32)
    hidden = norm_rows(tokens_float, norm_gain_float).astype(jnp.bfloat16)
    projected = jnp.dot(hidden, input_weight, preferred_element_type=jnp.float32)

    def prepare_local(projected_in, qgain_in, kgain_in):
        return prepare(projected_in, qgain_in, kgain_in, cosine, sine_part, head_dim)

    prepared, prepare_back = jax.vjp(
        prepare_local, projected, q_gain.astype(jnp.float32), k_gain.astype(jnp.float32)
    )
    queries = prepared[0].astype(jnp.bfloat16)
    keys_local = prepared[1].astype(jnp.bfloat16)
    values_local = prepared[2].astype(jnp.bfloat16)
    local_heads = queries.shape[1]

    def visible(offset, length):
        key_places = offset + jnp.arange(length, dtype=jnp.int32)
        key_docs = lax.dynamic_slice_in_dim(segments, offset, length)
        return (key_places[None, :] <= query_places[:, None]) & (
            key_docs[None, :] == local_docs[:, None]
        )

    running_max = jnp.full((tok_rows, local_heads), -1e30, jnp.float32)
    key_piece = lax.all_gather(keys_local, "dp", axis=0, tiled=True)
    value_piece = lax.all_gather(values_local, "dp", axis=0, tiled=True)
    allowed = visible(jnp.int32(0), key_piece.shape[0])[:, None, :]
    scores = (
        jnp.einsum("thd,nd->thn", queries, key_piece, preferred_element_type=jnp.float32)
        * score_scale
    )
    scores = jnp.where(allowed, scores, -1e30)
    new_max = jnp.maximum(running_max, jnp.max(scores, axis=-1))
    soft_weights = jnp.where(allowed, jnp.exp(scores - new_max[:, :, None]), 0.0)
    softmax_mass = jnp.sum(soft_weights, axis=-1)
    weighted_sum = jnp.einsum(
        "thn,nd->thd",
        soft_weights.astype(jnp.bfloat16),
        value_piece,
        preferred_element_type=jnp.float32,
    )
    running_max, softmax_mass, weighted_sum = (new_max, softmax_mass, weighted_sum)
    head_out = weighted_sum / softmax_mass[:, :, None]
    log_total = running_max + jnp.log(softmax_mass)
    attended = head_out.astype(jnp.bfloat16).reshape(tok_rows, local_heads * head_dim)
    branch = lax.psum_scatter(
        jnp.einsum("tc,dc->td", attended, output_weight, preferred_element_type=jnp.float32).astype(
            jnp.bfloat16
        ),
        "tensor",
        scatter_dimension=0,
        tiled=True,
    ).astype(jnp.float32)
    tensor_lane = lax.axis_index("tensor")
    tokens_share = lax.dynamic_slice_in_dim(tokens_float, tensor_lane * share_rows, share_rows, 0)
    middle = tokens_share + branch
    normed_float, moe_norm_back = jax.vjp(norm_rows, middle, moe_gain.astype(jnp.float32))
    normed = normed_float.astype(jnp.bfloat16)
    logits = jnp.dot(normed, router_weight, preferred_element_type=jnp.float32)

    def gating(logit_rows):
        probabilities = jax.nn.softmax(logit_rows, axis=-1)
        chosen = jnp.take_along_axis(probabilities, routes, axis=1)
        return chosen / jnp.sum(chosen, axis=1, keepdims=True)

    gate_values, gating_back = jax.vjp(gating, logits)
    pair_routes = routes.reshape(-1)
    pair_count = pair_routes.shape[0]
    route_table = (
        pair_routes[:, None] == jnp.arange(expert_count, dtype=jnp.int32)[None, :]
    ).astype(jnp.int32)
    route_rank = jnp.sum(jnp.cumsum(route_table, axis=0) * route_table, axis=1) - 1
    slot_index = pair_routes * capacity + route_rank
    slot_owner = (
        jnp.full((expert_count * capacity,), pair_count, jnp.int32)
        .at[slot_index]
        .set(jnp.arange(pair_count, dtype=jnp.int32))
    )
    normed_padded = jnp.concatenate([normed, jnp.zeros((1, model_width), jnp.bfloat16)], axis=0)
    send_rows = normed_padded[slot_owner // top_count].reshape(expert_count, capacity, model_width)
    arrived = lax.all_to_all(send_rows, ("dp", "tensor"), split_axis=0, concat_axis=0, tiled=True)
    expert_inputs = arrived.reshape(-1, model_width)
    w_gate = gate_weight[0]
    w_up = up_weight[0]
    w_down = down_weight[0]
    gate_act = jnp.dot(expert_inputs, w_gate, preferred_element_type=jnp.float32)
    up_act = jnp.dot(expert_inputs, w_up, preferred_element_type=jnp.float32)
    inner_float, swiglu_back = jax.vjp(swiglu, gate_act, up_act)
    inner_act = inner_float.astype(jnp.bfloat16)
    produced = jnp.dot(inner_act, w_down, preferred_element_type=jnp.float32).astype(jnp.bfloat16)
    returned = lax.all_to_all(
        produced.reshape(expert_count, capacity, model_width),
        ("dp", "tensor"),
        split_axis=0,
        concat_axis=0,
        tiled=True,
    )
    picked = (
        returned.reshape(-1, model_width)[slot_index]
        .reshape(share_rows, top_count, model_width)
        .astype(jnp.float32)
    )
    layer_out = (middle + jnp.sum(gate_values[:, :, None] * picked, axis=1)).astype(jnp.bfloat16)
    grad_out = out_grad.astype(jnp.float32)
    grad_picked = (
        (gate_values[:, :, None] * grad_out[:, None, :])
        .astype(jnp.bfloat16)
        .reshape(pair_count, model_width)
    )
    grad_gates = jnp.sum(grad_out[:, None, :] * picked, axis=2)
    grad_padded = jnp.concatenate([grad_picked, jnp.zeros((1, model_width), jnp.bfloat16)], axis=0)
    grad_send = grad_padded[slot_owner].reshape(expert_count, capacity, model_width)
    grad_arrived = lax.all_to_all(
        grad_send, ("dp", "tensor"), split_axis=0, concat_axis=0, tiled=True
    ).reshape(-1, model_width)
    grad_inner = jnp.einsum("rd,fd->rf", grad_arrived, w_down, preferred_element_type=jnp.float32)
    grad_down = jnp.einsum("rf,rd->fd", inner_act, grad_arrived, preferred_element_type=jnp.float32)
    grad_gate_float, grad_up_float = swiglu_back(grad_inner)
    grad_gate_act = grad_gate_float.astype(jnp.bfloat16)
    grad_up_act = grad_up_float.astype(jnp.bfloat16)
    grad_gate_w = jnp.einsum(
        "rd,rf->df", expert_inputs, grad_gate_act, preferred_element_type=jnp.float32
    )
    grad_up_w = jnp.einsum(
        "rd,rf->df", expert_inputs, grad_up_act, preferred_element_type=jnp.float32
    )
    grad_inputs = jnp.einsum("rf,df->rd", grad_gate_act, w_gate, preferred_element_type=jnp.float32)
    grad_inputs = (
        grad_inputs + jnp.einsum("rf,df->rd", grad_up_act, w_up, preferred_element_type=jnp.float32)
    ).astype(jnp.bfloat16)
    grad_home = lax.all_to_all(
        grad_inputs.reshape(expert_count, capacity, model_width),
        ("dp", "tensor"),
        split_axis=0,
        concat_axis=0,
        tiled=True,
    )
    grad_normed = jnp.sum(
        grad_home.reshape(-1, model_width)[slot_index]
        .reshape(share_rows, top_count, model_width)
        .astype(jnp.float32),
        axis=1,
    )
    (grad_logit_float,) = gating_back(grad_gates)
    grad_logits = grad_logit_float.astype(jnp.bfloat16)
    grad_router = jnp.einsum("td,te->de", normed, grad_logits, preferred_element_type=jnp.float32)
    grad_normed = grad_normed + jnp.einsum(
        "te,de->td", grad_logits, router_weight, preferred_element_type=jnp.float32
    )
    grad_middle_part, grad_moe_gain = moe_norm_back(grad_normed)
    grad_middle = grad_out + grad_middle_part
    grad_branch = lax.all_gather(grad_middle.astype(jnp.bfloat16), "tensor", axis=0, tiled=True)
    again_rows = (
        lax.all_gather(q_weight, "dp", axis=0, tiled=True),
        lax.all_gather(k_weight, "dp", axis=0, tiled=True),
        lax.all_gather(v_weight, "dp", axis=0, tiled=True),
        lax.all_gather(out_weight, "dp", axis=0, tiled=True),
    )
    input_back = jnp.concatenate([again_rows[0], again_rows[1], again_rows[2]], axis=1)
    output_back = again_rows[3]
    grad_heads = (
        jnp.dot(grad_branch, output_back, preferred_element_type=jnp.float32)
        .astype(jnp.bfloat16)
        .reshape(tok_rows, local_heads, head_dim)
    )
    row_delta = jnp.sum(grad_heads.astype(jnp.float32) * head_out, axis=-1)
    key_rows, value_rows = (
        lax.all_gather(keys_local, "dp", axis=0, tiled=True),
        lax.all_gather(values_local, "dp", axis=0, tiled=True),
    )
    key_block = min(512, all_tokens)

    def key_step(grad_queries, block_number):
        offset = block_number * key_block
        key_piece = lax.dynamic_slice_in_dim(key_rows, offset, key_block, 0)
        value_piece = lax.dynamic_slice_in_dim(value_rows, offset, key_block, 0)
        allowed = visible(offset, key_block)[:, None, :]
        scores = (
            jnp.einsum("thd,nd->thn", queries, key_piece, preferred_element_type=jnp.float32)
            * score_scale
        )
        soft_weights = jnp.where(allowed, jnp.exp(scores - log_total[:, :, None]), 0.0)
        grad_weights = jnp.einsum(
            "thd,nd->thn", grad_heads, value_piece, preferred_element_type=jnp.float32
        )
        grad_scores = (soft_weights * (grad_weights - row_delta[:, :, None])).astype(jnp.bfloat16)
        grad_queries = (
            grad_queries
            + jnp.einsum("thn,nd->thd", grad_scores, key_piece, preferred_element_type=jnp.float32)
            * score_scale
        )
        grad_key_piece = (
            jnp.einsum("thn,thd->nd", grad_scores, queries, preferred_element_type=jnp.float32)
            * score_scale
        )
        grad_value_piece = jnp.einsum(
            "thn,thd->nd",
            soft_weights.astype(jnp.bfloat16),
            grad_heads,
            preferred_element_type=jnp.float32,
        )
        return (grad_queries, jnp.concatenate([grad_key_piece, grad_value_piece], axis=1))

    grad_queries, key_terms = lax.scan(
        key_step,
        jnp.zeros((tok_rows, local_heads, head_dim), jnp.float32),
        jnp.arange(all_tokens // key_block, dtype=jnp.int32),
    )
    key_grads = lax.psum_scatter(
        key_terms.reshape(all_tokens, 2 * head_dim).astype(jnp.bfloat16),
        "dp",
        scatter_dimension=0,
        tiled=True,
    ).astype(jnp.float32)
    grad_proj_float, grad_q_gain, grad_k_gain = prepare_back(
        (grad_queries, key_grads[:, :head_dim], key_grads[:, head_dim:])
    )
    grad_projected = grad_proj_float.astype(jnp.bfloat16)
    grad_hidden = jnp.einsum(
        "tc,dc->td", grad_projected, input_back, preferred_element_type=jnp.float32
    )
    grad_hidden_share = lax.psum_scatter(
        grad_hidden.astype(jnp.bfloat16), "tensor", scatter_dimension=0, tiled=True
    ).astype(jnp.float32)
    _, first_norm_back = jax.vjp(norm_rows, tokens_share, norm_gain_float)
    grad_tokens_part, grad_norm_gain = first_norm_back(grad_hidden_share)
    tokens_grad = grad_middle + grad_tokens_part
    input_part = jnp.einsum("td,tc->dc", hidden, grad_projected, preferred_element_type=jnp.float32)
    output_part = jnp.einsum("td,tc->dc", grad_branch, attended, preferred_element_type=jnp.float32)
    weight_share = lax.psum_scatter(
        jnp.concatenate([input_part, output_part], axis=1).astype(jnp.bfloat16),
        "dp",
        scatter_dimension=0,
        tiled=True,
    ).astype(jnp.float32)
    query_width = local_heads * head_dim
    grad_q_weight = weight_share[:, :query_width]
    grad_k_weight = weight_share[:, query_width : query_width + head_dim]
    grad_v_weight = weight_share[:, query_width + head_dim : query_width + 2 * head_dim]
    grad_out_weight = weight_share[:, query_width + 2 * head_dim :]
    small_sums = lax.psum(
        (grad_router, grad_norm_gain, grad_moe_gain, grad_q_gain, grad_k_gain), ("dp", "tensor")
    )
    return (
        layer_out,
        tokens_grad,
        small_sums[1],
        grad_q_weight,
        grad_k_weight,
        grad_v_weight,
        small_sums[3],
        small_sums[4],
        grad_out_weight,
        small_sums[2],
        small_sums[0],
        grad_gate_w[None],
        grad_up_w[None],
        grad_down[None],
    )


MESH = pl.DeviceIdType.MESH
HBM = pl.ANY


class Place:
    def __init__(self, depth):
        d = lax.axis_index("dp")
        t = lax.axis_index("tensor")
        self.depth = depth
        self.d, self.t = d, t
        self.z, self.x = d // 2, lax.rem(d, 2)
        self.y, self.c = t // 2, lax.rem(t, 2)
        self.next_to = {
            "x": (self.z * 2 + 1 - self.x, t),
            "y": (d, (1 - self.y) * 2 + self.c),
            "c": (d, self.y * 2 + 1 - self.c),
            "up": (d + 2, t),
            "down": (d - 2, t),
        }

    def block(self, z, fx=0, fy=0, fc=0):
        x = 1 - self.x if fx else self.x
        y = 1 - self.y if fy else self.y
        c = 1 - self.c if fc else self.c
        return (z * 2 + x) * 4 + y * 2 + c

    def at(self, dist, step):
        if dist == 0:
            step(self.z)
            return

        @pl.when(self.z >= dist)
        def _():
            step(self.z - dist)

        @pl.when(self.z + dist < self.depth)
        def _():
            step(self.z + dist)

    def greet(self):
        barrier = pltpu.get_barrier_semaphore()

        def signal(to):
            pl.semaphore_signal(barrier, inc=1, device_id=self.next_to[to], device_id_type=MESH)

        for to in ("x", "y", "c"):
            signal(to)

        @pl.when(self.z > 0)
        def _():
            signal("down")

        @pl.when(self.z < self.depth - 1)
        def _():
            signal("up")

        above = (self.z < self.depth - 1).astype(jnp.int32)
        below = (self.z > 0).astype(jnp.int32)
        pl.semaphore_wait(barrier, 3 + above + below)

    def copy(self, src, dst, send, recv, to):
        return pltpu.make_async_remote_copy(
            src_ref=src,
            dst_ref=dst,
            send_sem=send,
            recv_sem=recv,
            device_id=self.next_to[to],
            device_id_type=MESH,
        )


class Gather:
    SEND, RECV = 11, 10

    def __init__(self, pos, own, out, send, recv, halves):
        self.pos, self.own, self.out = pos, own, out
        self.send, self.recv = send, recv
        rows = out.shape[1]
        self.h0 = pl.ds(0, rows // 2 if halves else rows)
        self.h1 = pl.ds(rows // 2, rows // 2) if halves else None
        self.rounds = pos.depth + 2

    def link(self, src, dst, sends, recvs, zo, to):
        return self.pos.copy(src, dst, self.send.at[sends, zo], self.recv.at[recvs, zo], to)

    def col(self, zo):
        return self.out.at[self.pos.block(zo)]

    def src(self, zo, mine):
        return self.own if mine else self.col(zo)

    def up(self, zo, mine=False):
        return self.link(self.src(zo, mine), self.col(zo), 0, 0, zo, "up")

    def down(self, zo, mine=False):
        return self.link(self.src(zo, mine), self.col(zo), 1, 0, zo, "down")

    def to_x(self, zo, mine=False):
        return self.link(self.src(zo, mine), self.col(zo), 2, 1, zo, "x")

    def to_y(self, zo, mine=False):
        return self.link(self.src(zo, mine), self.col(zo), 3, 2, zo, "y")

    def to_c(self, zo, mine=False):
        return self.link(self.src(zo, mine), self.col(zo), 4, 5, zo, "c")

    def part(self, zo, fx, fy, rows):
        whole = self.out.at[self.pos.block(zo, fx, fy)]
        return whole if rows is None else whole.at[rows]

    def pass_on(self, zo, fx, fy, rows, sends, recvs, to):
        ref = self.part(zo, fx, fy, rows)
        return self.link(ref, ref, sends, recvs, zo, to)

    def x_to_y(self, zo):
        return self.pass_on(zo, 1, 0, self.h0, 5, 3, "y")

    def x_to_c(self, zo):
        return self.pass_on(zo, 1, 0, None, 6, 6, "c")

    def y_to_x(self, zo):
        return self.pass_on(zo, 0, 1, self.h1, 7, 4, "x")

    def y_to_c(self, zo):
        return self.pass_on(zo, 0, 1, None, 8, 7, "c")

    def far0_to_c(self, zo):
        return self.pass_on(zo, 1, 1, self.h0, 9, 8, "c")

    def far1_to_c(self, zo):
        return self.pass_on(zo, 1, 1, self.h1, 10, 9, "c")

    def along_z(self, zo, mine, what):
        z, depth = self.pos.z, self.pos.depth
        if mine:
            up, down = z < depth - 1, z > 0
        else:
            up, down = (zo < z) & (z < depth - 1), (zo > z) & (z > 0)

        @pl.when(up)
        def _():
            what(self.up(zo, mine))

        @pl.when(down)
        def _():
            what(self.down(zo, mine))

    def on_column(self, zo, mine=False):
        if not mine:
            self.up(zo).wait_recv()
        self.along_z(zo, mine, lambda c: c.start())
        self.to_x(zo, mine).start()
        self.to_y(zo, mine).start()
        self.to_c(zo, mine).start()

    def on_sides(self, zo):
        self.to_x(zo).wait_recv()
        self.x_to_y(zo).start()
        self.x_to_c(zo).start()
        self.to_y(zo).wait_recv()
        if self.h1 is not None:
            self.y_to_x(zo).start()
        self.y_to_c(zo).start()

    def on_far(self, zo):
        self.x_to_y(zo).wait_recv()
        self.far0_to_c(zo).start()
        if self.h1 is not None:
            self.y_to_x(zo).wait_recv()
            self.far1_to_c(zo).start()

    def start(self):
        self.on_column(self.pos.z, True)

    def round(self, r):
        if 1 <= r < self.pos.depth:
            self.pos.at(r, self.on_column)
        if 1 <= r <= self.pos.depth:
            self.pos.at(r - 1, self.on_sides)
        if 2 <= r <= self.pos.depth + 1:
            self.pos.at(r - 2, self.on_far)

    def end_one(self, zo, mine=False):
        split = self.h1 is not None
        arrivals = [self.to_c(zo, mine), self.x_to_c(zo), self.y_to_c(zo), self.far0_to_c(zo)]
        sends = [self.to_x(zo, mine), self.to_y(zo, mine), self.x_to_y(zo)] + arrivals
        if split:
            arrivals.append(self.far1_to_c(zo))
            sends += [self.y_to_x(zo), self.far1_to_c(zo)]
        for c in arrivals:
            c.wait_recv()
        self.along_z(zo, mine, lambda c: c.wait_send())
        for c in sends:
            c.wait_send()

    def end(self):
        self.end_one(self.pos.z, True)
        for r in range(1, self.pos.depth):
            self.pos.at(r, self.end_one)

    @staticmethod
    def sems(depth):
        return [pltpu.SemaphoreType.DMA((Gather.SEND, depth)), pltpu.SemaphoreType.DMA((Gather.RECV, depth))]


class Reduce:
    SEND, RECV = 4 + 4 + 2, 4 + 4 + 2

    def __init__(self, pos, part, core, far, side, column, send, recv):
        self.pos, self.part = pos, part
        self.core, self.far, self.side, self.column = core, far, side, column
        self.send, self.recv = send, recv
        rows = part.shape[1]
        self.half = (pl.ds(0, rows // 2), pl.ds(rows // 2, rows // 2))
        self.rounds = pos.depth + 2

    @staticmethod
    def scratch(depth, rows, width):
        b = jnp.bfloat16
        return [
            pltpu.VMEM((depth, 4, rows, width), b),
            pltpu.VMEM((depth, 2, rows // 2, width), b),
            pltpu.VMEM((depth, 2, rows, width), b),
            pltpu.VMEM((depth, 2, rows, width), b),
            pltpu.SemaphoreType.DMA((Reduce.SEND, depth)),
            pltpu.SemaphoreType.DMA((Reduce.RECV, depth)),
        ]

    def link(self, src, dst, k, zo, to):
        return self.pos.copy(src, dst, self.send.at[k, zo], self.recv.at[k, zo], to)

    def to_core(self, zo, fx, fy):
        k = fx * 2 + fy
        return self.link(self.part.at[self.pos.block(zo, fx, fy, 1)], self.core.at[zo, k], k, zo, "c")

    def far_to(self, zo, k):
        return self.link(self.core.at[zo, 3, self.half[k]], self.far.at[zo, k], 4 + k, zo, ("y", "x")[k])

    def side_to(self, zo, k):
        return self.link(self.core.at[zo, 2 - k], self.side.at[zo, k], 6 + k, zo, ("x", "y")[k])

    def down(self, zo):
        return self.link(self.core.at[zo, 0], self.column.at[zo, 0], 8, zo, "down")

    def up(self, zo):
        return self.link(self.core.at[zo, 0], self.column.at[zo, 1], 9, zo, "up")

    def start_one(self, zo):
        for fx, fy in ((1, 1), (1, 0), (0, 1), (0, 0)):
            self.to_core(zo, fx, fy).start()

    def start(self):
        for dist in reversed(range(self.pos.depth)):
            self.pos.at(dist, self.start_one)

    def total(self, *refs):
        f = refs[0][...].astype(jnp.float32)
        for r in refs[1:]:
            f = f + r[...].astype(jnp.float32)
        return f

    def on_core(self, zo):
        for fx, fy in ((1, 1), (1, 0), (0, 1), (0, 0)):
            k = fx * 2 + fy
            self.to_core(zo, fx, fy).wait_recv()
            mine = self.core.at[zo, k]
            mine[...] = self.total(mine, self.part.at[self.pos.block(zo, fx, fy)]).astype(mine.dtype)
            if k == 3:
                self.far_to(zo, 0).start()
                self.far_to(zo, 1).start()

    def on_far(self, zo):
        for k in range(2):
            self.far_to(zo, k).wait_recv()
            mine = self.core.at[zo, 2 - k, self.half[k]]
            mine[...] = self.total(mine, self.far.at[zo, k]).astype(mine.dtype)
            self.side_to(zo, k).start()

    def on_sides(self, zo, mine=False):
        z, depth = self.pos.z, self.pos.depth
        self.side_to(zo, 0).wait_recv()
        self.side_to(zo, 1).wait_recv()
        here = self.core.at[zo, 0]
        summed = self.total(here, self.side.at[zo, 0], self.side.at[zo, 1])
        if mine:
            self.out[...] = summed

            @pl.when(z < depth - 1)
            def _():
                self.down(zo).wait_recv()
                self.out[...] += self.column[zo, 0].astype(jnp.float32)

            @pl.when(z > 0)
            def _():
                self.up(zo).wait_recv()
                self.out[...] += self.column[zo, 1].astype(jnp.float32)

            return
        here[...] = summed.astype(here.dtype)

        @pl.when((zo < z) & (z < depth - 1))
        def _():
            self.down(zo).wait_recv()
            here[...] = self.total(here, self.column.at[zo, 0]).astype(here.dtype)

        @pl.when((zo > z) & (z > 0))
        def _():
            self.up(zo).wait_recv()
            here[...] = self.total(here, self.column.at[zo, 1]).astype(here.dtype)

        @pl.when(zo < z)
        def _():
            self.down(zo).start()

        @pl.when(zo > z)
        def _():
            self.up(zo).start()

    def round(self, r):
        depth = self.pos.depth
        for s in range(3):
            dist = depth - 1 - (r - s)
            if not 0 <= dist < depth:
                continue
            if s == 0:
                self.pos.at(dist, self.on_core)
            elif s == 1:
                self.pos.at(dist, self.on_far)
            elif dist:
                self.pos.at(dist, self.on_sides)
            else:
                self.on_sides(self.pos.z, True)

    def end_one(self, zo):
        for fx in range(2):
            for fy in range(2):
                self.to_core(zo, fx, fy).wait_send()
        for k in range(2):
            self.far_to(zo, k).wait_send()
            self.side_to(zo, k).wait_send()

        @pl.when(zo < self.pos.z)
        def _():
            self.down(zo).wait_send()

        @pl.when(zo > self.pos.z)
        def _():
            self.up(zo).wait_send()

    def end(self):
        for r in range(self.pos.depth):
            self.pos.at(r, self.end_one)


def drive(*parts):
    for p in parts:
        p.start()
    for r in range(max(p.rounds for p in parts)):
        for p in parts:
            p.round(r)
    for p in parts:
        p.end()


def params(number, vmem=None):
    return pltpu.CompilerParams(collective_id=number, has_side_effects=True, vmem_limit_bytes=vmem)


def all_gather(depth, number, name, *blocks):
    n = len(blocks)

    def body(*refs):
        own, out, sems, local = refs[:n], refs[n : 2 * n], refs[2 * n : 4 * n], refs[4 * n]
        pos = Place(depth)
        here = [pltpu.make_async_copy(own[i], out[i].at[pos.block(pos.z)], local.at[i]) for i in range(n)]
        for c in here:
            c.start()
        pos.greet()
        drive(*[Gather(pos, own[i], out[i], sems[2 * i], sems[2 * i + 1], own[i].shape[0] >= 32) for i in range(n)])
        for c in here:
            c.wait()

    scratch = []
    for _ in blocks:
        scratch += Gather.sems(depth)
    return pl.pallas_call(
        body,
        out_shape=[jax.ShapeDtypeStruct((depth * 8,) + b.shape, b.dtype) for b in blocks],
        in_specs=[pl.BlockSpec(memory_space=HBM)] * n,
        out_specs=[pl.BlockSpec(memory_space=HBM)] * n,
        scratch_shapes=scratch + [pltpu.SemaphoreType.DMA((n,))],
        compiler_params=params(number),
        name=name,
    )(*blocks)


def reduce_scatter(depth, number, name, part, *blocks):
    devices, rows, width = part.shape
    n = len(blocks)

    def body(part_ref, *refs):
        own, out_sum, out = refs[:n], refs[n], refs[n + 1 : 2 * n + 1]
        rest = refs[2 * n + 1 :]
        pos = Place(depth)
        here = [pltpu.make_async_copy(own[i], out[i].at[pos.block(pos.z)], rest[6].at[i]) for i in range(n)]
        for c in here:
            c.start()
        pos.greet()
        red = Reduce(pos, part_ref, *rest[:6])
        red.out = out_sum
        gathers = [
            Gather(pos, own[i], out[i], rest[7 + 2 * i], rest[8 + 2 * i], own[i].shape[0] >= 32) for i in range(n)
        ]
        drive(red, *gathers)
        for c in here:
            c.wait()

    scratch = Reduce.scratch(depth, rows, width) + [pltpu.SemaphoreType.DMA((max(n, 1),))]
    for _ in blocks:
        scratch += Gather.sems(depth)
    return pl.pallas_call(
        body,
        out_shape=[jax.ShapeDtypeStruct((rows, width), jnp.float32)]
        + [jax.ShapeDtypeStruct((devices,) + b.shape, b.dtype) for b in blocks],
        in_specs=[pl.BlockSpec(memory_space=pltpu.VMEM)] + [pl.BlockSpec(memory_space=HBM)] * n,
        out_specs=[pl.BlockSpec(memory_space=pltpu.VMEM)] + [pl.BlockSpec(memory_space=HBM)] * n,
        scratch_shapes=scratch,
        compiler_params=params(number, 40 * 2**20),
        name=name,
    )(part, *blocks)


def exchange(groups, number, name, arrays, out_shapes, src_of, dst_of):
    n = len(arrays)

    def body(*refs):
        src, out, send, recv, local = refs[:n], refs[n : 2 * n], refs[2 * n], refs[2 * n + 1], refs[2 * n + 2]
        d = lax.axis_index("dp")
        t = lax.axis_index("tensor")
        here = [pltpu.make_async_copy(src_of(i, src[i], d), dst_of(i, out[i], d), local.at[i]) for i in range(n)]
        for c in here:
            c.start()
        barrier = pltpu.get_barrier_semaphore()
        peers = [lax.rem(d + p, groups) for p in range(1, groups)]
        for p in peers:
            pl.semaphore_signal(barrier, inc=1, device_id=(p, t), device_id_type=MESH)
        pl.semaphore_wait(barrier, groups - 1)
        copies = []
        for k, p in enumerate(peers):
            for i in range(n):
                copies.append(
                    pltpu.make_async_remote_copy(
                        src_ref=src_of(i, src[i], p),
                        dst_ref=dst_of(i, out[i], d),
                        send_sem=send.at[i, k],
                        recv_sem=recv.at[i, k],
                        device_id=(p, t),
                        device_id_type=MESH,
                    )
                )
                copies[-1].start()
        for c in copies:
            c.wait()
        for c in here:
            c.wait()

    return pl.pallas_call(
        body,
        out_shape=out_shapes,
        in_specs=[pl.BlockSpec(memory_space=HBM)] * n,
        out_specs=[pl.BlockSpec(memory_space=HBM)] * n,
        scratch_shapes=[
            pltpu.SemaphoreType.DMA((n, groups - 1)),
            pltpu.SemaphoreType.DMA((n, groups - 1)),
            pltpu.SemaphoreType.DMA((n,)),
        ],
        compiler_params=params(number),
        name=name,
    )(*arrays)


def head_shards(
    tokens,
    segments,
    routes,
    out_grad,
    norm_gain,
    q_weight,
    k_weight,
    v_weight,
    q_gain,
    k_gain,
    out_weight,
    moe_gain,
    router_weight,
    gate_weight,
    up_weight,
    down_weight,
):
    f32, bf = jnp.float32, jnp.bfloat16
    head_dim = q_gain.shape[0]
    tok_rows, width = tokens.shape
    share_rows = out_grad.shape[0]
    all_tokens = segments.shape[0]
    expert_count = router_weight.shape[1]
    top_count = routes.shape[1]
    groups = all_tokens // tok_rows
    depth = groups // 2
    weight_rows = q_weight.shape[0]
    capacity = max(2, share_rows * top_count * 2 // expert_count)
    slots = capacity * expert_count
    score_scale = head_dim ** (-0.5)
    lane = lax.axis_index("tensor")
    expert = lax.axis_index("dp") * 4 + lane

    places = jnp.arange(all_tokens, dtype=jnp.int32)
    begins = jnp.concatenate([jnp.ones((1,), dtype=bool), segments[1:] != segments[:-1]])
    positions = places - lax.cummax(jnp.where(begins, places, 0), axis=0)
    cosine, sine_part = angles(positions, head_dim)
    allowed = (places[None, :] <= places[:, None]) & (segments[None, :] == segments[:, None])

    tokens_share = lax.dynamic_slice_in_dim(tokens, lane * share_rows, share_rows, 0)
    routes_block = jnp.zeros((8, 128), jnp.int32).at[: share_rows * top_count // 128].set(routes.reshape(-1, 128))
    all_tok, all_routes = all_gather(depth, 0, "gather_tokens", tokens_share, routes_block)
    all_tok = all_tok.reshape(all_tokens, width)
    all_routes = all_routes[:, : share_rows * top_count // 128].reshape(all_tokens, top_count)

    def rows_of(ref, p):
        return ref.at[pl.ds(p * weight_rows, weight_rows)]

    def cols_of(ref, p):
        return ref.at[:, pl.ds(pl.multiple_of(p * head_dim, head_dim), head_dim)]

    head_weight = jax.ShapeDtypeStruct((width, head_dim), bf)
    w_q, w_o, w_k, w_v = exchange(
        groups,
        1,
        "exchange_weights",
        [q_weight, out_weight, k_weight, v_weight],
        [head_weight] * 4,
        lambda i, ref, p: cols_of(ref, p) if i < 2 else ref,
        lambda i, ref, p: rows_of(ref, p),
    )
    (all_grad,) = all_gather(depth, 2, "gather_out_grad", out_grad)
    all_grad = all_grad.reshape(all_tokens, width)

    tok_float = all_tok.astype(f32)
    norm_gain_float = norm_gain.astype(f32)
    hidden = norm_rows(tok_float, norm_gain_float).astype(bf)
    w_in = jnp.concatenate([w_q, w_k, w_v], axis=1)
    projected = jnp.dot(hidden, w_in, preferred_element_type=f32)

    def prepare_local(projected_in, qgain_in, kgain_in):
        return prepare(projected_in, qgain_in, kgain_in, cosine, sine_part, head_dim)

    prepared, prepare_back = jax.vjp(prepare_local, projected, q_gain.astype(f32), k_gain.astype(f32))
    queries = prepared[0].astype(bf).reshape(all_tokens, head_dim)
    keys = prepared[1].astype(bf)
    values = prepared[2].astype(bf)
    scores = jnp.einsum("td,nd->tn", queries, keys, preferred_element_type=f32) * score_scale
    scores = jnp.where(allowed, scores, -1e30)
    top = jnp.max(scores, axis=-1, keepdims=True)
    weights = jnp.exp(scores - top)
    mass = jnp.sum(weights, axis=-1, keepdims=True)
    log_total = top + jnp.log(mass)
    head_out = jnp.dot(weights.astype(bf), values, preferred_element_type=f32) / mass
    attended = head_out.astype(bf)
    branch_part = jnp.einsum("tc,dc->td", attended, w_o, preferred_element_type=f32).astype(bf)
    (branch,) = reduce_scatter(
        depth, 3, "reduce_branch", branch_part.reshape(expert_count, share_rows, width)
    )

    middle = tokens_share.astype(f32) + branch
    normed_float, moe_norm_back = jax.vjp(norm_rows, middle, moe_gain.astype(f32))
    (normed,) = all_gather(depth, 4, "gather_normed", normed_float.astype(bf))
    normed = normed.reshape(all_tokens, width)
    logits = jnp.dot(normed, router_weight, preferred_element_type=f32)
    named = jnp.any(all_routes[:, :, None] == jnp.arange(expert_count, dtype=jnp.int32), axis=1)

    probabilities = jax.nn.softmax(logits, axis=-1)
    chosen = jnp.where(named, probabilities, 0.0)
    gate_all = chosen / jnp.sum(chosen, axis=1, keepdims=True)
    here = jnp.arange(expert_count, dtype=jnp.int32) == expert
    mine = jnp.any(named & here, axis=1)
    gate_mine = jnp.sum(jnp.where(here, gate_all, 0.0), axis=1)
    rank = jnp.cumsum(mine.astype(jnp.int32)) - 1
    select = ((rank[None, :] == jnp.arange(slots, dtype=jnp.int32)[:, None]) & mine[None, :]).astype(bf)
    inputs = jnp.dot(select, normed, preferred_element_type=f32).astype(bf)
    grads = jnp.dot(select, all_grad, preferred_element_type=f32)
    gate_rows = jnp.sum(jnp.where(select > 0, gate_mine[None, :], 0.0), axis=1)
    w_gate, w_up, w_down = gate_weight[0], up_weight[0], down_weight[0]
    gate_act = jnp.dot(inputs, w_gate, preferred_element_type=f32)
    up_act = jnp.dot(inputs, w_up, preferred_element_type=f32)
    inner_float, swiglu_back = jax.vjp(swiglu, gate_act, up_act)
    inner_act = inner_float.astype(bf)
    returned = jnp.dot(inner_act, w_down, preferred_element_type=f32).astype(bf)
    grad_returned = (gate_rows[:, None] * grads).astype(bf)
    grad_gate_rows = jnp.sum(grads * returned.astype(f32), axis=1)
    out_rows = (gate_rows[:, None] * returned.astype(f32)).astype(bf)
    out_part = jnp.einsum("rt,rd->td", select, out_rows, preferred_element_type=f32).astype(bf)
    (out_sum,) = reduce_scatter(
        depth, 5, "reduce_out", out_part.reshape(expert_count, share_rows, width)
    )
    layer_out = (middle + out_sum).astype(bf)
    grad_inner = jnp.einsum("rd,fd->rf", grad_returned, w_down, preferred_element_type=f32)
    grad_down = jnp.einsum("rf,rd->fd", inner_act, grad_returned, preferred_element_type=f32)
    grad_gate_float, grad_up_float = swiglu_back(grad_inner)
    grad_gate_act = grad_gate_float.astype(bf)
    grad_up_act = grad_up_float.astype(bf)
    grad_gate_w = jnp.einsum("rd,rf->df", inputs, grad_gate_act, preferred_element_type=f32)
    grad_up_w = jnp.einsum("rd,rf->df", inputs, grad_up_act, preferred_element_type=f32)
    grad_inputs = jnp.einsum("rf,df->rd", grad_gate_act, w_gate, preferred_element_type=f32)
    grad_inputs = (
        grad_inputs + jnp.einsum("rf,df->rd", grad_up_act, w_up, preferred_element_type=f32)
    ).astype(bf)
    grad_gate_mine = jnp.sum(jnp.where(select > 0, grad_gate_rows[:, None], 0.0), axis=0)
    own_grad = jnp.where(here, grad_gate_mine[:, None], 0.0)
    own_logit_grad = gate_all * (own_grad - jnp.sum(gate_all * own_grad, axis=1, keepdims=True))
    normed_part = jnp.einsum("rt,rd->td", select, grad_inputs, preferred_element_type=f32) + jnp.einsum(
        "te,de->td", own_logit_grad.astype(bf), router_weight, preferred_element_type=f32
    )
    (grad_normed,) = reduce_scatter(
        depth, 6, "reduce_normed", normed_part.astype(bf).reshape(expert_count, share_rows, width)
    )
    grad_middle_part, grad_moe_gain = moe_norm_back(grad_normed)
    grad_middle = out_grad.astype(f32) + grad_middle_part
    all_branch, all_gate_grads = all_gather(
        depth, 7, "gather_grad_branch", grad_middle.astype(bf), grad_gate_mine.reshape(8, -1)
    )
    grad_branch = all_branch.reshape(all_tokens, width)
    gate_grads = all_gate_grads.reshape(expert_count, all_tokens).T
    logit_grads = gate_all * (gate_grads - jnp.sum(gate_all * gate_grads, axis=1, keepdims=True))
    grad_router = jnp.einsum("td,te->de", normed, logit_grads.astype(bf), preferred_element_type=f32)

    grad_heads = jnp.dot(grad_branch, w_o, preferred_element_type=f32).astype(bf)
    out_weight_part = jnp.einsum("td,tc->dc", grad_branch, attended, preferred_element_type=f32).astype(bf)
    row_delta = jnp.sum(grad_heads.astype(f32) * head_out, axis=-1, keepdims=True)
    scores = jnp.einsum("td,nd->tn", queries, keys, preferred_element_type=f32) * score_scale
    soft = jnp.where(allowed, jnp.exp(scores - log_total), 0.0)
    grad_soft = jnp.einsum("td,nd->tn", grad_heads, values, preferred_element_type=f32)
    grad_scores = (soft * (grad_soft - row_delta)).astype(bf)
    grad_queries = jnp.dot(grad_scores, keys, preferred_element_type=f32) * score_scale
    grad_keys = jnp.einsum("tn,td->nd", grad_scores, queries, preferred_element_type=f32) * score_scale
    grad_values = jnp.einsum("tn,td->nd", soft.astype(bf), grad_heads, preferred_element_type=f32)
    grad_proj_float, grad_q_gain, grad_k_gain = prepare_back((grad_queries[:, None, :], grad_keys, grad_values))
    grad_projected = grad_proj_float.astype(bf)
    hidden_part = jnp.einsum("tc,dc->td", grad_projected, w_in, preferred_element_type=f32)
    _, first_norm_back = jax.vjp(norm_rows, tok_float, norm_gain_float)
    in_weight_part = jnp.einsum("td,tc->dc", hidden, grad_projected, preferred_element_type=f32).astype(bf)
    normalised = norm_rows(tok_float, 1.0)
    grad_norm_gain = jnp.sum(hidden_part * normalised, axis=0)
    small = jnp.concatenate([grad_norm_gain, grad_moe_gain, grad_q_gain, grad_k_gain])
    small_rows = -(-small.shape[0] // 1024) * 8
    small_block = jnp.pad(small, (0, small_rows * 128 - small.shape[0])).reshape(small_rows, 128)
    grad_hidden, all_small = reduce_scatter(
        depth, 8, "reduce_hidden", hidden_part.astype(bf).reshape(expert_count, share_rows, width), small_block
    )
    _, share_norm_back = jax.vjp(norm_rows, tokens_share.astype(f32), norm_gain_float)
    tokens_grad = grad_middle + share_norm_back(grad_hidden)[0]
    small_sums = jnp.sum(all_small, axis=0).reshape(-1)
    grad_q, grad_o, grad_kv = exchange(
        groups,
        9,
        "exchange_weight_grads",
        [in_weight_part[:, :head_dim], out_weight_part, in_weight_part[:, head_dim:]],
        [jax.ShapeDtypeStruct(q_weight.shape, bf)] * 2
        + [jax.ShapeDtypeStruct((groups, weight_rows, 2 * head_dim), bf)],
        lambda i, ref, p: rows_of(ref, p),
        lambda i, ref, p: cols_of(ref, p) if i < 2 else ref.at[p],
    )
    kv_sum = jnp.sum(grad_kv.astype(f32), axis=0)
    return (
        layer_out,
        tokens_grad,
        small_sums[:width],
        grad_q.astype(f32),
        kv_sum[:, :head_dim],
        kv_sum[:, head_dim:],
        small_sums[2 * width : 2 * width + head_dim],
        small_sums[2 * width + head_dim : 2 * width + 2 * head_dim],
        grad_o.astype(f32),
        small_sums[width : 2 * width],
        grad_router,
        grad_gate_w[None],
        grad_up_w[None],
        grad_down[None],
    )


def solution(mesh):
    per_device = shards if mesh.shape["dp"] != 8 or mesh.shape["tensor"] != 4 else head_shards
    placed = (
        P("dp", None),
        P(),
        P(("dp", "tensor"), None),
        P(("dp", "tensor"), None),
        P(),
        P("dp", "tensor"),
        P("dp", "tensor"),
        P("dp", "tensor"),
        P(),
        P(),
        P("dp", "tensor"),
        P(),
        P(),
        P(("dp", "tensor"), None, None),
        P(("dp", "tensor"), None, None),
        P(("dp", "tensor"), None, None),
    )
    return jax.shard_map(
        per_device,
        mesh=mesh,
        in_specs=placed,
        out_specs=(
            P(("dp", "tensor"), None),
            P(("dp", "tensor"), None),
            P(),
            P("dp", "tensor"),
            P("dp", "tensor"),
            P("dp", "tensor"),
            P(),
            P(),
            P("dp", "tensor"),
            P(),
            P(),
            P(("dp", "tensor"), None, None),
            P(("dp", "tensor"), None, None),
            P(("dp", "tensor"), None, None),
        ),
        check_vma=False,
    )
```

```python
import functools

import jax
import jax.numpy as jnp
from jax import lax
from jax.experimental import pallas as pl
from jax.experimental.pallas import tpu as pltpu
from jax.sharding import PartitionSpec as P

EPS = 1e-06
THETA = 1000000.0


def norm_rows(values, gain):
    return values * lax.rsqrt(jnp.mean(values * values, axis=-1, keepdims=True) + EPS) * gain


def rotary(values, cosine, sine_part):
    half_dim = values.shape[-1] // 2
    front_half = values[..., :half_dim]
    back_half = values[..., half_dim:]
    return jnp.concatenate(
        [front_half * cosine - back_half * sine_part, back_half * cosine + front_half * sine_part],
        axis=-1,
    )


def angles(positions, head_dim):
    half_dim = head_dim // 2
    frequency = THETA ** (-(jnp.arange(half_dim).astype(jnp.float32) * 2.0) / head_dim)
    rotation = positions.astype(jnp.float32)[:, None] * frequency[None, :]
    return (jnp.cos(rotation), jnp.sin(rotation))


def prepare(projected, q_gain, k_gain, cosine, sine_part, head_dim):
    tok_rows = projected.shape[0]
    query_width = projected.shape[1] - 2 * head_dim
    queries = projected[:, :query_width].reshape(tok_rows, query_width // head_dim, head_dim)
    keys_local = projected[:, query_width : query_width + head_dim]
    values_local = projected[:, query_width + head_dim :]
    queries = rotary(norm_rows(queries, q_gain), cosine[:, None, :], sine_part[:, None, :])
    keys_local = rotary(norm_rows(keys_local, k_gain), cosine, sine_part)
    return (queries, keys_local, values_local)


def swiglu(gate_in, up_in):
    return jax.nn.silu(gate_in) * up_in


def shards(
    tokens,
    segments,
    routes,
    out_grad,
    norm_gain,
    q_weight,
    k_weight,
    v_weight,
    q_gain,
    k_gain,
    out_weight,
    moe_gain,
    router_weight,
    gate_weight,
    up_weight,
    down_weight,
):
    head_dim = q_gain.shape[0]
    tok_rows = tokens.shape[0]
    model_width = tokens.shape[1]
    share_rows = out_grad.shape[0]
    all_tokens = segments.shape[0]
    expert_count = router_weight.shape[1]
    top_count = routes.shape[1]
    capacity = max(2, share_rows * top_count * 2 // expert_count)
    score_scale = head_dim ** (-0.5)
    first_row = lax.axis_index("dp") * tok_rows
    places = jnp.arange(all_tokens, dtype=jnp.int32)
    begins = jnp.concatenate([jnp.ones((1,), dtype=bool), segments[1:] != segments[:-1]])
    positions = places - lax.cummax(jnp.where(begins, places, 0), axis=0)
    local_positions = lax.dynamic_slice_in_dim(positions, first_row, tok_rows)
    local_docs = lax.dynamic_slice_in_dim(segments, first_row, tok_rows)
    query_places = first_row + jnp.arange(tok_rows, dtype=jnp.int32)
    cosine, sine_part = angles(local_positions, head_dim)
    weight_rows = (
        lax.all_gather(q_weight, "dp", axis=0, tiled=True),
        lax.all_gather(k_weight, "dp", axis=0, tiled=True),
        lax.all_gather(v_weight, "dp", axis=0, tiled=True),
        lax.all_gather(out_weight, "dp", axis=0, tiled=True),
    )
    input_weight = jnp.concatenate([weight_rows[0], weight_rows[1], weight_rows[2]], axis=1)
    output_weight = weight_rows[3]
    tokens_float = tokens.astype(jnp.float32)
    norm_gain_float = norm_gain.astype(jnp.float32)
    hidden = norm_rows(tokens_float, norm_gain_float).astype(jnp.bfloat16)
    projected = jnp.dot(hidden, input_weight, preferred_element_type=jnp.float32)

    def prepare_local(projected_in, qgain_in, kgain_in):
        return prepare(projected_in, qgain_in, kgain_in, cosine, sine_part, head_dim)

    prepared, prepare_back = jax.vjp(
        prepare_local, projected, q_gain.astype(jnp.float32), k_gain.astype(jnp.float32)
    )
    queries = prepared[0].astype(jnp.bfloat16)
    keys_local = prepared[1].astype(jnp.bfloat16)
    values_local = prepared[2].astype(jnp.bfloat16)
    local_heads = queries.shape[1]

    def visible(offset, length):
        key_places = offset + jnp.arange(length, dtype=jnp.int32)
        key_docs = lax.dynamic_slice_in_dim(segments, offset, length)
        return (key_places[None, :] <= query_places[:, None]) & (
            key_docs[None, :] == local_docs[:, None]
        )

    running_max = jnp.full((tok_rows, local_heads), -1e30, jnp.float32)
    key_piece = lax.all_gather(keys_local, "dp", axis=0, tiled=True)
    value_piece = lax.all_gather(values_local, "dp", axis=0, tiled=True)
    allowed = visible(jnp.int32(0), key_piece.shape[0])[:, None, :]
    scores = (
        jnp.einsum("thd,nd->thn", queries, key_piece, preferred_element_type=jnp.float32)
        * score_scale
    )
    scores = jnp.where(allowed, scores, -1e30)
    new_max = jnp.maximum(running_max, jnp.max(scores, axis=-1))
    soft_weights = jnp.where(allowed, jnp.exp(scores - new_max[:, :, None]), 0.0)
    softmax_mass = jnp.sum(soft_weights, axis=-1)
    weighted_sum = jnp.einsum(
        "thn,nd->thd",
        soft_weights.astype(jnp.bfloat16),
        value_piece,
        preferred_element_type=jnp.float32,
    )
    running_max, softmax_mass, weighted_sum = (new_max, softmax_mass, weighted_sum)
    head_out = weighted_sum / softmax_mass[:, :, None]
    log_total = running_max + jnp.log(softmax_mass)
    attended = head_out.astype(jnp.bfloat16).reshape(tok_rows, local_heads * head_dim)
    branch = lax.psum_scatter(
        jnp.einsum("tc,dc->td", attended, output_weight, preferred_element_type=jnp.float32).astype(
            jnp.bfloat16
        ),
        "tensor",
        scatter_dimension=0,
        tiled=True,
    ).astype(jnp.float32)
    tensor_lane = lax.axis_index("tensor")
    tokens_share = lax.dynamic_slice_in_dim(tokens_float, tensor_lane * share_rows, share_rows, 0)
    middle = tokens_share + branch
    normed_float, moe_norm_back = jax.vjp(norm_rows, middle, moe_gain.astype(jnp.float32))
    normed = normed_float.astype(jnp.bfloat16)
    logits = jnp.dot(normed, router_weight, preferred_element_type=jnp.float32)

    def gating(logit_rows):
        probabilities = jax.nn.softmax(logit_rows, axis=-1)
        chosen = jnp.take_along_axis(probabilities, routes, axis=1)
        return chosen / jnp.sum(chosen, axis=1, keepdims=True)

    gate_values, gating_back = jax.vjp(gating, logits)
    pair_routes = routes.reshape(-1)
    pair_count = pair_routes.shape[0]
    route_table = (
        pair_routes[:, None] == jnp.arange(expert_count, dtype=jnp.int32)[None, :]
    ).astype(jnp.int32)
    route_rank = jnp.sum(jnp.cumsum(route_table, axis=0) * route_table, axis=1) - 1
    slot_index = pair_routes * capacity + route_rank
    slot_owner = (
        jnp.full((expert_count * capacity,), pair_count, jnp.int32)
        .at[slot_index]
        .set(jnp.arange(pair_count, dtype=jnp.int32))
    )
    normed_padded = jnp.concatenate([normed, jnp.zeros((1, model_width), jnp.bfloat16)], axis=0)
    send_rows = normed_padded[slot_owner // top_count].reshape(expert_count, capacity, model_width)
    arrived = lax.all_to_all(send_rows, ("dp", "tensor"), split_axis=0, concat_axis=0, tiled=True)
    expert_inputs = arrived.reshape(-1, model_width)
    w_gate = gate_weight[0]
    w_up = up_weight[0]
    w_down = down_weight[0]
    gate_act = jnp.dot(expert_inputs, w_gate, preferred_element_type=jnp.float32)
    up_act = jnp.dot(expert_inputs, w_up, preferred_element_type=jnp.float32)
    inner_float, swiglu_back = jax.vjp(swiglu, gate_act, up_act)
    inner_act = inner_float.astype(jnp.bfloat16)
    produced = jnp.dot(inner_act, w_down, preferred_element_type=jnp.float32).astype(jnp.bfloat16)
    returned = lax.all_to_all(
        produced.reshape(expert_count, capacity, model_width),
        ("dp", "tensor"),
        split_axis=0,
        concat_axis=0,
        tiled=True,
    )
    picked = (
        returned.reshape(-1, model_width)[slot_index]
        .reshape(share_rows, top_count, model_width)
        .astype(jnp.float32)
    )
    layer_out = (middle + jnp.sum(gate_values[:, :, None] * picked, axis=1)).astype(jnp.bfloat16)
    grad_out = out_grad.astype(jnp.float32)
    grad_picked = (
        (gate_values[:, :, None] * grad_out[:, None, :])
        .astype(jnp.bfloat16)
        .reshape(pair_count, model_width)
    )
    grad_gates = jnp.sum(grad_out[:, None, :] * picked, axis=2)
    grad_padded = jnp.concatenate([grad_picked, jnp.zeros((1, model_width), jnp.bfloat16)], axis=0)
    grad_send = grad_padded[slot_owner].reshape(expert_count, capacity, model_width)
    grad_arrived = lax.all_to_all(
        grad_send, ("dp", "tensor"), split_axis=0, concat_axis=0, tiled=True
    ).reshape(-1, model_width)
    grad_inner = jnp.einsum("rd,fd->rf", grad_arrived, w_down, preferred_element_type=jnp.float32)
    grad_down = jnp.einsum("rf,rd->fd", inner_act, grad_arrived, preferred_element_type=jnp.float32)
    grad_gate_float, grad_up_float = swiglu_back(grad_inner)
    grad_gate_act = grad_gate_float.astype(jnp.bfloat16)
    grad_up_act = grad_up_float.astype(jnp.bfloat16)
    grad_gate_w = jnp.einsum(
        "rd,rf->df", expert_inputs, grad_gate_act, preferred_element_type=jnp.float32
    )
    grad_up_w = jnp.einsum(
        "rd,rf->df", expert_inputs, grad_up_act, preferred_element_type=jnp.float32
    )
    grad_inputs = jnp.einsum("rf,df->rd", grad_gate_act, w_gate, preferred_element_type=jnp.float32)
    grad_inputs = (
        grad_inputs + jnp.einsum("rf,df->rd", grad_up_act, w_up, preferred_element_type=jnp.float32)
    ).astype(jnp.bfloat16)
    grad_home = lax.all_to_all(
        grad_inputs.reshape(expert_count, capacity, model_width),
        ("dp", "tensor"),
        split_axis=0,
        concat_axis=0,
        tiled=True,
    )
    grad_normed = jnp.sum(
        grad_home.reshape(-1, model_width)[slot_index]
        .reshape(share_rows, top_count, model_width)
        .astype(jnp.float32),
        axis=1,
    )
    (grad_logit_float,) = gating_back(grad_gates)
    grad_logits = grad_logit_float.astype(jnp.bfloat16)
    grad_router = jnp.einsum("td,te->de", normed, grad_logits, preferred_element_type=jnp.float32)
    grad_normed = grad_normed + jnp.einsum(
        "te,de->td", grad_logits, router_weight, preferred_element_type=jnp.float32
    )
    grad_middle_part, grad_moe_gain = moe_norm_back(grad_normed)
    grad_middle = grad_out + grad_middle_part
    grad_branch = lax.all_gather(grad_middle.astype(jnp.bfloat16), "tensor", axis=0, tiled=True)
    again_rows = (
        lax.all_gather(q_weight, "dp", axis=0, tiled=True),
        lax.all_gather(k_weight, "dp", axis=0, tiled=True),
        lax.all_gather(v_weight, "dp", axis=0, tiled=True),
        lax.all_gather(out_weight, "dp", axis=0, tiled=True),
    )
    input_back = jnp.concatenate([again_rows[0], again_rows[1], again_rows[2]], axis=1)
    output_back = again_rows[3]
    grad_heads = (
        jnp.dot(grad_branch, output_back, preferred_element_type=jnp.float32)
        .astype(jnp.bfloat16)
        .reshape(tok_rows, local_heads, head_dim)
    )
    row_delta = jnp.sum(grad_heads.astype(jnp.float32) * head_out, axis=-1)
    key_rows, value_rows = (
        lax.all_gather(keys_local, "dp", axis=0, tiled=True),
        lax.all_gather(values_local, "dp", axis=0, tiled=True),
    )
    key_block = min(512, all_tokens)

    def key_step(grad_queries, block_number):
        offset = block_number * key_block
        key_piece = lax.dynamic_slice_in_dim(key_rows, offset, key_block, 0)
        value_piece = lax.dynamic_slice_in_dim(value_rows, offset, key_block, 0)
        allowed = visible(offset, key_block)[:, None, :]
        scores = (
            jnp.einsum("thd,nd->thn", queries, key_piece, preferred_element_type=jnp.float32)
            * score_scale
        )
        soft_weights = jnp.where(allowed, jnp.exp(scores - log_total[:, :, None]), 0.0)
        grad_weights = jnp.einsum(
            "thd,nd->thn", grad_heads, value_piece, preferred_element_type=jnp.float32
        )
        grad_scores = (soft_weights * (grad_weights - row_delta[:, :, None])).astype(jnp.bfloat16)
        grad_queries = (
            grad_queries
            + jnp.einsum("thn,nd->thd", grad_scores, key_piece, preferred_element_type=jnp.float32)
            * score_scale
        )
        grad_key_piece = (
            jnp.einsum("thn,thd->nd", grad_scores, queries, preferred_element_type=jnp.float32)
            * score_scale
        )
        grad_value_piece = jnp.einsum(
            "thn,thd->nd",
            soft_weights.astype(jnp.bfloat16),
            grad_heads,
            preferred_element_type=jnp.float32,
        )
        return (grad_queries, jnp.concatenate([grad_key_piece, grad_value_piece], axis=1))

    grad_queries, key_terms = lax.scan(
        key_step,
        jnp.zeros((tok_rows, local_heads, head_dim), jnp.float32),
        jnp.arange(all_tokens // key_block, dtype=jnp.int32),
    )
    key_grads = lax.psum_scatter(
        key_terms.reshape(all_tokens, 2 * head_dim).astype(jnp.bfloat16),
        "dp",
        scatter_dimension=0,
        tiled=True,
    ).astype(jnp.float32)
    grad_proj_float, grad_q_gain, grad_k_gain = prepare_back(
        (grad_queries, key_grads[:, :head_dim], key_grads[:, head_dim:])
    )
    grad_projected = grad_proj_float.astype(jnp.bfloat16)
    grad_hidden = jnp.einsum(
        "tc,dc->td", grad_projected, input_back, preferred_element_type=jnp.float32
    )
    grad_hidden_share = lax.psum_scatter(
        grad_hidden.astype(jnp.bfloat16), "tensor", scatter_dimension=0, tiled=True
    ).astype(jnp.float32)
    _, first_norm_back = jax.vjp(norm_rows, tokens_share, norm_gain_float)
    grad_tokens_part, grad_norm_gain = first_norm_back(grad_hidden_share)
    tokens_grad = grad_middle + grad_tokens_part
    input_part = jnp.einsum("td,tc->dc", hidden, grad_projected, preferred_element_type=jnp.float32)
    output_part = jnp.einsum("td,tc->dc", grad_branch, attended, preferred_element_type=jnp.float32)
    weight_share = lax.psum_scatter(
        jnp.concatenate([input_part, output_part], axis=1).astype(jnp.bfloat16),
        "dp",
        scatter_dimension=0,
        tiled=True,
    ).astype(jnp.float32)
    query_width = local_heads * head_dim
    grad_q_weight = weight_share[:, :query_width]
    grad_k_weight = weight_share[:, query_width : query_width + head_dim]
    grad_v_weight = weight_share[:, query_width + head_dim : query_width + 2 * head_dim]
    grad_out_weight = weight_share[:, query_width + 2 * head_dim :]
    small_sums = lax.psum(
        (grad_router, grad_norm_gain, grad_moe_gain, grad_q_gain, grad_k_gain), ("dp", "tensor")
    )
    return (
        layer_out,
        tokens_grad,
        small_sums[1],
        grad_q_weight,
        grad_k_weight,
        grad_v_weight,
        small_sums[3],
        small_sums[4],
        grad_out_weight,
        small_sums[2],
        small_sums[0],
        grad_gate_w[None],
        grad_up_w[None],
        grad_down[None],
    )


MESH = pl.DeviceIdType.MESH
HBM = pl.ANY


class Place:
    def __init__(self, depth):
        d = lax.axis_index("dp")
        t = lax.axis_index("tensor")
        self.depth = depth
        self.d, self.t = d, t
        self.z, self.x = d // 2, lax.rem(d, 2)
        self.y, self.c = t // 2, lax.rem(t, 2)
        self.next_to = {
            "x": (self.z * 2 + 1 - self.x, t),
            "y": (d, (1 - self.y) * 2 + self.c),
            "c": (d, self.y * 2 + 1 - self.c),
            "up": (d + 2, t),
            "down": (d - 2, t),
        }

    def block(self, z, fx=0, fy=0, fc=0):
        x = 1 - self.x if fx else self.x
        y = 1 - self.y if fy else self.y
        c = 1 - self.c if fc else self.c
        return (z * 2 + x) * 4 + y * 2 + c

    def at(self, dist, step):
        if dist == 0:
            step(self.z)
            return

        @pl.when(self.z >= dist)
        def _():
            step(self.z - dist)

        @pl.when(self.z + dist < self.depth)
        def _():
            step(self.z + dist)

    def greet(self, plane=False):
        barrier = pltpu.get_barrier_semaphore()

        def signal(to):
            pl.semaphore_signal(barrier, inc=1, device_id=self.next_to[to], device_id_type=MESH)

        if plane:
            groups = self.depth * 2
            for k in range(1, groups):
                to = (lax.rem(self.d + k, groups), self.t)
                pl.semaphore_signal(barrier, inc=1, device_id=to, device_id_type=MESH)
            signal("y")
            signal("c")
            pl.semaphore_wait(barrier, groups + 1)
            return
        for to in ("x", "y", "c"):
            signal(to)

        @pl.when(self.z > 0)
        def _():
            signal("down")

        @pl.when(self.z < self.depth - 1)
        def _():
            signal("up")

        above = (self.z < self.depth - 1).astype(jnp.int32)
        below = (self.z > 0).astype(jnp.int32)
        pl.semaphore_wait(barrier, 3 + above + below)

    def copy(self, src, dst, send, recv, to):
        return pltpu.make_async_remote_copy(
            src_ref=src,
            dst_ref=dst,
            send_sem=send,
            recv_sem=recv,
            device_id=self.next_to[to],
            device_id_type=MESH,
        )


class Gather:
    SEND, RECV = 11, 10

    def __init__(self, pos, own, out, send, recv, halves):
        self.pos, self.own, self.out = pos, own, out
        self.send, self.recv = send, recv
        rows = out.shape[1]
        self.h0 = pl.ds(0, rows // 2 if halves else rows)
        self.h1 = pl.ds(rows // 2, rows // 2) if halves else None
        self.rounds = pos.depth + 2

    def link(self, src, dst, sends, recvs, zo, to):
        return self.pos.copy(src, dst, self.send.at[sends, zo], self.recv.at[recvs, zo], to)

    def col(self, zo):
        return self.out.at[self.pos.block(zo)]

    def src(self, zo, mine):
        return self.own if mine else self.col(zo)

    def up(self, zo, mine=False):
        return self.link(self.src(zo, mine), self.col(zo), 0, 0, zo, "up")

    def down(self, zo, mine=False):
        return self.link(self.src(zo, mine), self.col(zo), 1, 0, zo, "down")

    def to_x(self, zo, mine=False):
        return self.link(self.src(zo, mine), self.col(zo), 2, 1, zo, "x")

    def to_y(self, zo, mine=False):
        return self.link(self.src(zo, mine), self.col(zo), 3, 2, zo, "y")

    def to_c(self, zo, mine=False):
        return self.link(self.src(zo, mine), self.col(zo), 4, 5, zo, "c")

    def part(self, zo, fx, fy, rows):
        whole = self.out.at[self.pos.block(zo, fx, fy)]
        return whole if rows is None else whole.at[rows]

    def pass_on(self, zo, fx, fy, rows, sends, recvs, to):
        ref = self.part(zo, fx, fy, rows)
        return self.link(ref, ref, sends, recvs, zo, to)

    def x_to_y(self, zo):
        return self.pass_on(zo, 1, 0, self.h0, 5, 3, "y")

    def x_to_c(self, zo):
        return self.pass_on(zo, 1, 0, None, 6, 6, "c")

    def y_to_x(self, zo):
        return self.pass_on(zo, 0, 1, self.h1, 7, 4, "x")

    def y_to_c(self, zo):
        return self.pass_on(zo, 0, 1, None, 8, 7, "c")

    def far0_to_c(self, zo):
        return self.pass_on(zo, 1, 1, self.h0, 9, 8, "c")

    def far1_to_c(self, zo):
        return self.pass_on(zo, 1, 1, self.h1, 10, 9, "c")

    def along_z(self, zo, mine, what):
        z, depth = self.pos.z, self.pos.depth
        if mine:
            up, down = z < depth - 1, z > 0
        else:
            up, down = (zo < z) & (z < depth - 1), (zo > z) & (z > 0)

        @pl.when(up)
        def _():
            what(self.up(zo, mine))

        @pl.when(down)
        def _():
            what(self.down(zo, mine))

    def on_column(self, zo, mine=False):
        if not mine:
            self.up(zo).wait_recv()
        self.along_z(zo, mine, lambda c: c.start())
        self.to_x(zo, mine).start()
        self.to_y(zo, mine).start()
        self.to_c(zo, mine).start()

    def on_sides(self, zo):
        self.to_x(zo).wait_recv()
        self.x_to_y(zo).start()
        self.x_to_c(zo).start()
        self.to_y(zo).wait_recv()
        if self.h1 is not None:
            self.y_to_x(zo).start()
        self.y_to_c(zo).start()

    def on_far(self, zo):
        self.x_to_y(zo).wait_recv()
        self.far0_to_c(zo).start()
        if self.h1 is not None:
            self.y_to_x(zo).wait_recv()
            self.far1_to_c(zo).start()

    def start(self):
        self.on_column(self.pos.z, True)

    def round(self, r):
        if 1 <= r < self.pos.depth:
            self.pos.at(r, self.on_column)
        if 1 <= r <= self.pos.depth:
            self.pos.at(r - 1, self.on_sides)
        if 2 <= r <= self.pos.depth + 1:
            self.pos.at(r - 2, self.on_far)

    def end_one(self, zo, mine=False):
        split = self.h1 is not None
        arrivals = [self.to_c(zo, mine), self.x_to_c(zo), self.y_to_c(zo), self.far0_to_c(zo)]
        sends = [self.to_x(zo, mine), self.to_y(zo, mine), self.x_to_y(zo)] + arrivals
        if split:
            arrivals.append(self.far1_to_c(zo))
            sends += [self.y_to_x(zo), self.far1_to_c(zo)]
        for c in arrivals:
            c.wait_recv()
        self.along_z(zo, mine, lambda c: c.wait_send())
        for c in sends:
            c.wait_send()

    def end(self):
        self.end_one(self.pos.z, True)
        for r in range(1, self.pos.depth):
            self.pos.at(r, self.end_one)

    @staticmethod
    def sems(depth):
        return [pltpu.SemaphoreType.DMA((Gather.SEND, depth)), pltpu.SemaphoreType.DMA((Gather.RECV, depth))]


class Reduce:
    SEND, RECV = 4 + 4 + 2, 4 + 4 + 2

    def __init__(self, pos, part, core, far, side, column, send, recv, halves=True):
        self.pos, self.part = pos, part
        self.core, self.far, self.side, self.column = core, far, side, column
        self.send, self.recv = send, recv
        rows = part.shape[1]
        self.half = (pl.ds(0, rows // 2), pl.ds(rows // 2, rows // 2)) if halves else (pl.ds(0, rows),)
        self.rounds = pos.depth + 2

    @staticmethod
    def scratch(depth, rows, width, halves=True):
        b = jnp.bfloat16
        return [
            pltpu.VMEM((depth, 4, rows, width), b),
            pltpu.VMEM((depth, 2, rows // 2, width) if halves else (depth, 1, rows, width), b),
            pltpu.VMEM((depth, 2, rows, width), b),
            pltpu.VMEM((depth, 2, rows, width), b),
            pltpu.SemaphoreType.DMA((Reduce.SEND, depth)),
            pltpu.SemaphoreType.DMA((Reduce.RECV, depth)),
        ]

    def link(self, src, dst, k, zo, to):
        return self.pos.copy(src, dst, self.send.at[k, zo], self.recv.at[k, zo], to)

    def to_core(self, zo, fx, fy):
        k = fx * 2 + fy
        return self.link(self.part.at[self.pos.block(zo, fx, fy, 1)], self.core.at[zo, k], k, zo, "c")

    def far_to(self, zo, k):
        return self.link(self.core.at[zo, 3, self.half[k]], self.far.at[zo, k], 4 + k, zo, ("y", "x")[k])

    def side_to(self, zo, k):
        return self.link(self.core.at[zo, 2 - k], self.side.at[zo, k], 6 + k, zo, ("x", "y")[k])

    def down(self, zo):
        return self.link(self.core.at[zo, 0], self.column.at[zo, 0], 8, zo, "down")

    def up(self, zo):
        return self.link(self.core.at[zo, 0], self.column.at[zo, 1], 9, zo, "up")

    def start_one(self, zo):
        for fx, fy in ((1, 1), (1, 0), (0, 1), (0, 0)):
            self.to_core(zo, fx, fy).start()

    def start(self):
        for dist in reversed(range(self.pos.depth)):
            self.pos.at(dist, self.start_one)

    def total(self, *refs):
        f = refs[0][...].astype(jnp.float32)
        for r in refs[1:]:
            f = f + r[...].astype(jnp.float32)
        return f

    def on_core(self, zo):
        for fx, fy in ((1, 1), (1, 0), (0, 1), (0, 0)):
            k = fx * 2 + fy
            self.to_core(zo, fx, fy).wait_recv()
            mine = self.core.at[zo, k]
            mine[...] = self.total(mine, self.part.at[self.pos.block(zo, fx, fy)]).astype(mine.dtype)
            if k == 3:
                for h in range(len(self.half)):
                    self.far_to(zo, h).start()

    def on_far(self, zo):
        for k in range(2):
            if k < len(self.half):
                self.far_to(zo, k).wait_recv()
                mine = self.core.at[zo, 2 - k, self.half[k]]
                mine[...] = self.total(mine, self.far.at[zo, k]).astype(mine.dtype)
            self.side_to(zo, k).start()

    def on_sides(self, zo, mine=False):
        z, depth = self.pos.z, self.pos.depth
        self.side_to(zo, 0).wait_recv()
        self.side_to(zo, 1).wait_recv()
        here = self.core.at[zo, 0]
        summed = self.total(here, self.side.at[zo, 0], self.side.at[zo, 1])
        if mine:
            self.out[...] = summed

            @pl.when(z < depth - 1)
            def _():
                self.down(zo).wait_recv()
                self.out[...] += self.column[zo, 0].astype(jnp.float32)

            @pl.when(z > 0)
            def _():
                self.up(zo).wait_recv()
                self.out[...] += self.column[zo, 1].astype(jnp.float32)

            return
        here[...] = summed.astype(here.dtype)

        @pl.when((zo < z) & (z < depth - 1))
        def _():
            self.down(zo).wait_recv()
            here[...] = self.total(here, self.column.at[zo, 0]).astype(here.dtype)

        @pl.when((zo > z) & (z > 0))
        def _():
            self.up(zo).wait_recv()
            here[...] = self.total(here, self.column.at[zo, 1]).astype(here.dtype)

        @pl.when(zo < z)
        def _():
            self.down(zo).start()

        @pl.when(zo > z)
        def _():
            self.up(zo).start()

    def round(self, r):
        depth = self.pos.depth
        for s in range(3):
            dist = depth - 1 - (r - s)
            if not 0 <= dist < depth:
                continue
            if s == 0:
                self.pos.at(dist, self.on_core)
            elif s == 1:
                self.pos.at(dist, self.on_far)
            elif dist:
                self.pos.at(dist, self.on_sides)
            else:
                self.on_sides(self.pos.z, True)

    def end_one(self, zo):
        for fx in range(2):
            for fy in range(2):
                self.to_core(zo, fx, fy).wait_send()
        for k in range(len(self.half)):
            self.far_to(zo, k).wait_send()
        for k in range(2):
            self.side_to(zo, k).wait_send()

        @pl.when(zo < self.pos.z)
        def _():
            self.down(zo).wait_send()

        @pl.when(zo > self.pos.z)
        def _():
            self.up(zo).wait_send()

    def end(self):
        for r in range(self.pos.depth):
            self.pos.at(r, self.end_one)


class PlaneGather:
    SEND, RECV = 3, 2

    def __init__(self, pos, own, dst, send, recv):
        self.pos, self.own, self.dst = pos, own, dst
        self.send, self.recv = send, recv
        self.rounds = pos.depth

    def link(self, zo, mine, sends, recvs, to):
        dst = self.dst(zo * 2 + self.pos.x)
        return self.pos.copy(self.own if mine else dst, dst, self.send.at[sends, zo], self.recv.at[recvs, zo], to)

    def along_z(self, zo, mine, what):
        z, depth = self.pos.z, self.pos.depth
        if mine:
            up, down = z < depth - 1, z > 0
        else:
            up, down = (zo < z) & (z < depth - 1), (zo > z) & (z > 0)

        @pl.when(up)
        def _():
            what(self.link(zo, mine, 0, 0, "up"))

        @pl.when(down)
        def _():
            what(self.link(zo, mine, 1, 0, "down"))

    def on_column(self, zo, mine=False):
        if not mine:
            self.link(zo, False, 0, 0, "up").wait_recv()
        self.along_z(zo, mine, lambda c: c.start())
        self.link(zo, mine, 2, 1, "x").start()

    def start(self):
        self.on_column(self.pos.z, True)

    def round(self, r):
        if 1 <= r < self.pos.depth:
            self.pos.at(r, self.on_column)

    def end_one(self, zo, mine=False):
        across = self.link(zo, mine, 2, 1, "x")
        across.wait_recv()
        self.along_z(zo, mine, lambda c: c.wait_send())
        across.wait_send()

    def end(self):
        self.end_one(self.pos.z, True)
        for r in range(1, self.pos.depth):
            self.pos.at(r, self.end_one)

    @staticmethod
    def sems(depth):
        return [pltpu.SemaphoreType.DMA((PlaneGather.SEND, depth)), pltpu.SemaphoreType.DMA((PlaneGather.RECV, depth))]


class PlaneReduce:
    def __init__(self, pos, part, out, across, column, send, recv):
        self.pos, self.part, self.out = pos, part, out
        self.across, self.column = across, column
        self.send, self.recv = send, recv
        self.rounds = pos.depth

    @staticmethod
    def scratch(depth, rows, width):
        b = jnp.bfloat16
        return [
            pltpu.VMEM((depth, rows, width), b),
            pltpu.VMEM((depth, 2, rows, width), b),
            pltpu.SemaphoreType.DMA((3, depth)),
            pltpu.SemaphoreType.DMA((3, depth)),
        ]

    def to_x(self, zo):
        src = self.part(zo * 2 + 1 - self.pos.x)
        return self.pos.copy(src, self.across.at[zo], self.send.at[0, zo], self.recv.at[0, zo], "x")

    def down(self, zo):
        return self.pos.copy(
            self.across.at[zo], self.column.at[zo, 0], self.send.at[1, zo], self.recv.at[1, zo], "down"
        )

    def up(self, zo):
        return self.pos.copy(
            self.across.at[zo], self.column.at[zo, 1], self.send.at[2, zo], self.recv.at[2, zo], "up"
        )

    def start(self):
        for dist in reversed(range(self.pos.depth)):
            self.pos.at(dist, lambda zo: self.to_x(zo).start())

    def on_column(self, zo):
        z, depth = self.pos.z, self.pos.depth
        f32 = jnp.float32
        here = self.across.at[zo]
        self.to_x(zo).wait_recv()
        here[...] = (here[...].astype(f32) + self.part(zo * 2 + self.pos.x)[...].astype(f32)).astype(here.dtype)

        @pl.when((zo < z) & (z < depth - 1))
        def _():
            self.down(zo).wait_recv()
            here[...] = (here[...].astype(f32) + self.column[zo, 0].astype(f32)).astype(here.dtype)

        @pl.when((zo > z) & (z > 0))
        def _():
            self.up(zo).wait_recv()
            here[...] = (here[...].astype(f32) + self.column[zo, 1].astype(f32)).astype(here.dtype)

        @pl.when(zo < z)
        def _():
            self.down(zo).start()

        @pl.when(zo > z)
        def _():
            self.up(zo).start()

    def on_own(self):
        z, depth = self.pos.z, self.pos.depth
        f32 = jnp.float32
        self.to_x(z).wait_recv()
        self.out[...] = self.across[z].astype(f32) + self.part(z * 2 + self.pos.x)[...].astype(f32)

        @pl.when(z < depth - 1)
        def _():
            self.down(z).wait_recv()
            self.out[...] += self.column[z, 0].astype(f32)

        @pl.when(z > 0)
        def _():
            self.up(z).wait_recv()
            self.out[...] += self.column[z, 1].astype(f32)

    def round(self, r):
        dist = self.pos.depth - 1 - r
        if dist > 0:
            self.pos.at(dist, self.on_column)
        elif dist == 0:
            self.on_own()

    def end_one(self, zo):
        self.to_x(zo).wait_send()

        @pl.when(zo < self.pos.z)
        def _():
            self.down(zo).wait_send()

        @pl.when(zo > self.pos.z)
        def _():
            self.up(zo).wait_send()

    def end(self):
        for r in range(self.pos.depth):
            self.pos.at(r, self.end_one)


class Exchange:
    def __init__(self, pos, piece, place, send, recv, local):
        self.pos, self.piece, self.place = pos, piece, place
        self.send, self.recv, self.local = send, recv, local
        self.groups = pos.depth * 2
        self.rounds = 0

    @staticmethod
    def sems(depth):
        n = depth * 2 - 1
        return [pltpu.SemaphoreType.DMA((n,)), pltpu.SemaphoreType.DMA((n,)), pltpu.SemaphoreType.DMA]

    def peer(self, k):
        return lax.rem(self.pos.d + k, self.groups)

    def copy(self, k):
        p = self.peer(k)
        return pltpu.make_async_remote_copy(
            src_ref=self.piece(p),
            dst_ref=self.place(self.pos.d),
            send_sem=self.send.at[k - 1],
            recv_sem=self.recv.at[k - 1],
            device_id=(p, self.pos.t),
            device_id_type=MESH,
        )

    def here(self):
        return pltpu.make_async_copy(self.piece(self.pos.d), self.place(self.pos.d), self.local)

    def start(self):
        self.here().start()
        for k in range(1, self.groups):
            self.copy(k).start()

    def round(self, r):
        pass

    def end(self):
        self.here().wait()
        for k in range(1, self.groups):
            self.copy(k).wait()


def drive(*parts):
    for p in parts:
        p.start()
    for r in range(max(p.rounds for p in parts)):
        for p in parts:
            p.round(r)
    for p in parts:
        p.end()


def params(number, vmem=None):
    return pltpu.CompilerParams(collective_id=number, has_side_effects=True, vmem_limit_bytes=vmem)


def all_gather(depth, number, name, *blocks):
    n = len(blocks)

    def body(*refs):
        own, out, sems, local = refs[:n], refs[n : 2 * n], refs[2 * n : 4 * n], refs[4 * n]
        pos = Place(depth)
        here = [pltpu.make_async_copy(own[i], out[i].at[pos.block(pos.z)], local.at[i]) for i in range(n)]
        for c in here:
            c.start()
        pos.greet()
        drive(*[Gather(pos, own[i], out[i], sems[2 * i], sems[2 * i + 1], own[i].shape[0] >= 32) for i in range(n)])
        for c in here:
            c.wait()

    scratch = []
    for _ in blocks:
        scratch += Gather.sems(depth)
    return pl.pallas_call(
        body,
        out_shape=[jax.ShapeDtypeStruct((depth * 8,) + b.shape, b.dtype) for b in blocks],
        in_specs=[pl.BlockSpec(memory_space=HBM)] * n,
        out_specs=[pl.BlockSpec(memory_space=HBM)] * n,
        scratch_shapes=scratch + [pltpu.SemaphoreType.DMA((n,))],
        compiler_params=params(number),
        name=name,
    )(*blocks)


def reduce_scatter(depth, number, name, part, *blocks):
    devices, rows, width = part.shape
    n = len(blocks)

    def body(part_ref, *refs):
        own, out_sum, out = refs[:n], refs[n], refs[n + 1 : 2 * n + 1]
        rest = refs[2 * n + 1 :]
        pos = Place(depth)
        here = [pltpu.make_async_copy(own[i], out[i].at[pos.block(pos.z)], rest[6].at[i]) for i in range(n)]
        for c in here:
            c.start()
        pos.greet()
        red = Reduce(pos, part_ref, *rest[:6])
        red.out = out_sum
        gathers = [
            Gather(pos, own[i], out[i], rest[7 + 2 * i], rest[8 + 2 * i], own[i].shape[0] >= 32) for i in range(n)
        ]
        drive(red, *gathers)
        for c in here:
            c.wait()

    scratch = Reduce.scratch(depth, rows, width) + [pltpu.SemaphoreType.DMA((max(n, 1),))]
    for _ in blocks:
        scratch += Gather.sems(depth)
    return pl.pallas_call(
        body,
        out_shape=[jax.ShapeDtypeStruct((rows, width), jnp.float32)]
        + [jax.ShapeDtypeStruct((devices,) + b.shape, b.dtype) for b in blocks],
        in_specs=[pl.BlockSpec(memory_space=pltpu.VMEM)] + [pl.BlockSpec(memory_space=HBM)] * n,
        out_specs=[pl.BlockSpec(memory_space=pltpu.VMEM)] + [pl.BlockSpec(memory_space=HBM)] * n,
        scratch_shapes=scratch,
        compiler_params=params(number, 40 * 2**20),
        name=name,
    )(part, *blocks)


def rows_of(ref, p, rows):
    return ref.at[pl.ds(p * rows, rows)]


def cols_of(ref, p, cols):
    return ref.at[:, pl.ds(pl.multiple_of(p * cols, cols), cols)]


def part_of(ref, p, rows, first, cols):
    return ref.at[pl.ds(p * rows, rows), pl.ds(first, cols)]


def gather_inputs(depth, number, tokens_share, q_weight, k_weight, v_weight):
    rows, width = tokens_share.shape
    w_rows, head = k_weight.shape

    def body(tok, wq, wk, wv, all_tok, w_in, *sems):
        pos = Place(depth)
        local = [
            pltpu.make_async_copy(tok, all_tok.at[pos.block(pos.z)], sems[9].at[0]),
            pltpu.make_async_copy(wk, part_of(w_in, pos.d, w_rows, head, head), sems[9].at[1]),
            pltpu.make_async_copy(wv, part_of(w_in, pos.d, w_rows, 2 * head, head), sems[9].at[2]),
        ]
        for c in local:
            c.start()
        pos.greet(plane=True)
        drive(
            PlaneGather(pos, wk, lambda p: part_of(w_in, p, w_rows, head, head), *sems[0:2]),
            PlaneGather(pos, wv, lambda p: part_of(w_in, p, w_rows, 2 * head, head), *sems[2:4]),
            Gather(pos, tok, all_tok, *sems[4:6], False),
            Exchange(pos, lambda p: cols_of(wq, p, head), lambda p: part_of(w_in, p, w_rows, 0, head), *sems[6:9]),
        )
        for c in local:
            c.wait()

    return pl.pallas_call(
        body,
        out_shape=[
            jax.ShapeDtypeStruct((depth * 8, rows, width), tokens_share.dtype),
            jax.ShapeDtypeStruct((width, 3 * head), q_weight.dtype),
        ],
        in_specs=[pl.BlockSpec(memory_space=HBM)] * 4,
        out_specs=[pl.BlockSpec(memory_space=HBM)] * 2,
        scratch_shapes=PlaneGather.sems(depth) * 2
        + Gather.sems(depth)
        + Exchange.sems(depth)
        + [pltpu.SemaphoreType.DMA((3,))],
        compiler_params=params(number),
        name="gather_inputs",
    )(tokens_share, q_weight, k_weight, v_weight)


def gather_heads(depth, number, routes, out_weight, head):
    w_rows, width = out_weight.shape[0], out_weight.shape[0] * depth * 2

    def body(route, wo, all_route, w_o, *sems):
        pos = Place(depth)
        local = pltpu.make_async_copy(route, all_route.at[pos.block(pos.z)], sems[5])
        local.start()
        pos.greet(plane=True)
        drive(
            Exchange(pos, lambda p: cols_of(wo, p, head), lambda p: rows_of(w_o, p, w_rows), *sems[2:5]),
            Gather(pos, route, all_route, *sems[0:2], False),
        )
        local.wait()

    return pl.pallas_call(
        body,
        out_shape=[
            jax.ShapeDtypeStruct((depth * 8,) + routes.shape, routes.dtype),
            jax.ShapeDtypeStruct((width, head), out_weight.dtype),
        ],
        in_specs=[pl.BlockSpec(memory_space=HBM)] * 2,
        out_specs=[pl.BlockSpec(memory_space=HBM)] * 2,
        scratch_shapes=Gather.sems(depth) + Exchange.sems(depth) + [pltpu.SemaphoreType.DMA],
        compiler_params=params(number),
        name="gather_heads",
    )(routes, out_weight)


def dot(a, b):
    return jnp.dot(a, b, preferred_element_type=jnp.float32)


def dot_nt(a, b):
    return lax.dot_general(a, b, (((1,), (1,)), ((), ())), preferred_element_type=jnp.float32)


def dot_tn(a, b):
    return lax.dot_general(a, b, (((0,), (0,)), ((), ())), preferred_element_type=jnp.float32)


def loop(count, step):
    lax.fori_loop(0, count, lambda i, _: (step(i), 0)[1], 0)


def experts(depth, number, normed, out_grad, select, select_t, named, router, w_gate, w_up, w_down):
    f32, bf = jnp.float32, jnp.bfloat16
    rows, width = normed.shape
    devices = depth * 8
    planes, picks, plane_rows = select.shape
    slots = planes * picks
    ff = w_gate.shape[1]
    lanes = router.shape[1]
    wide = width + lanes
    tile = 256

    def body(
        n_ref, g_ref, sel, sel_t, named_ref, router_ref, wg_hbm, wu_hbm, wd_hbm,
        out_sum, grad_sum, n_all, x_out, gret_out, inner_out, ggate_out, gup_out,
        wg, wu, wd, nb, gb, part, xin, gret, ret, inner, ggate, gup, act_a, act_u, gates,
        w_sem, own_sem, all_sem, keep_sem, *rest,
    ):
        pos = Place(depth)
        expert = pos.block(pos.z)
        loads = [
            pltpu.make_async_copy(src, dst, w_sem.at[i])
            for i, (src, dst) in enumerate(((wg_hbm, wg), (wu_hbm, wu), (wd_hbm, wd)))
        ]
        own = [
            pltpu.make_async_copy(n_ref, nb.at[expert], own_sem.at[0]),
            pltpu.make_async_copy(g_ref, gb.at[expert], own_sem.at[1]),
        ]
        for c in own + loads:
            c.start()
        pos.greet()
        g_normed = Gather(pos, n_ref, nb, *rest[0:2], True)
        g_grad = Gather(pos, g_ref, gb, *rest[2:4], True)
        r_out = Reduce(pos, nb, *rest[4:10])
        r_grad = Reduce(pos, part, *rest[10:16])
        r_out.out, r_grad.out = out_sum, grad_sum

        def plane(ref, z):
            return ref[pl.ds(z * 8, 8)].reshape(plane_rows, ref.shape[2])

        def picked(z):
            return pl.ds(pl.multiple_of(z * picks, picks), picks)

        def cols(i, size=tile):
            return pl.ds(pl.multiple_of(i * size, size), size)

        here = lax.broadcasted_iota(jnp.int32, (plane_rows, lanes), 1) == expert

        def choose(z):
            tok = plane(nb, z)
            logits = dot(tok, router_ref[...])
            chosen = named_ref[z] > 0
            top = jnp.max(jnp.where(chosen, logits, -1e30), axis=1, keepdims=True)
            raised = jnp.where(chosen, jnp.exp(jnp.minimum(logits - top, 0.0)), 0.0)
            gates[z] = raised / jnp.sum(raised, axis=1, keepdims=True)
            xin[picked(z), :] = dot(sel[z], tok).astype(bf)

        def forward(i):
            a = dot(xin[...], wg[:, cols(i)])
            u = dot(xin[...], wu[:, cols(i)])
            act_a[:, cols(i)] = a
            act_u[:, cols(i)] = u
            inner[:, cols(i)] = (a / (1.0 + jnp.exp(-a)) * u).astype(bf)

        def produce(i):
            ret[:, cols(i)] = dot(inner[...], wd[:, cols(i)]).astype(bf)

        def spread(z):
            gate = gates[z]
            mine = jnp.sum(jnp.where(here, gate, 0.0), axis=1, keepdims=True)
            summed = jnp.zeros((plane_rows, 1), f32)
            for i in range(width // 512):
                c = pl.ds(i * 512, 512)
                g = gb[pl.ds(z * 8, 8), :, c].reshape(plane_rows, 512).astype(f32)
                gret[picked(z), c] = dot(sel[z], (mine * g).astype(bf)).astype(bf)
                back = dot(sel_t[z], ret[picked(z), c])
                nb[pl.ds(z * 8, 8), :, c] = (mine * back).astype(bf).reshape(8, rows, 512)
                summed += jnp.sum(g * back, axis=1, keepdims=True)
            logit = gate * (jnp.where(here, 1.0, 0.0) - mine) * summed
            part[pl.ds(z * 8, 8), :, pl.ds(width, lanes)] = logit.astype(bf).reshape(8, rows, lanes)

        def backward(i):
            gi = dot_nt(gret[...], wd[cols(i), :])
            a = act_a[:, cols(i)]
            s = 1.0 / (1.0 + jnp.exp(-a))
            ggate[:, cols(i)] = (gi * act_u[:, cols(i)] * (s + a * s * (1.0 - s))).astype(bf)
            gup[:, cols(i)] = (gi * (a * s)).astype(bf)

        def inputs_back(i):
            ret[:, cols(i)] = (dot_nt(ggate[...], wg[cols(i), :]) + dot_nt(gup[...], wu[cols(i), :])).astype(bf)

        def scatter(z):
            for i in range(width // 512):
                c = pl.ds(i * 512, 512)
                part[pl.ds(z * 8, 8), :, c] = dot(sel_t[z], ret[picked(z), c]).astype(bf).reshape(8, rows, 512)
            r_grad.start_one(z)

        g_normed.start()
        for r in range(1, 4):
            g_normed.round(r)
        g_grad.start()
        for r in range(4, g_normed.rounds):
            g_normed.round(r)
        own[0].wait()
        g_normed.end()
        keep = pltpu.make_async_copy(nb, n_all, all_sem)
        keep.start()
        g_grad.round(1)
        loop(planes, choose)
        g_grad.round(2)
        loads[0].wait()
        loads[1].wait()
        loop(ff // tile, forward)
        g_grad.round(3)
        loads[2].wait()
        loop(width // tile, produce)
        for r in range(4, g_grad.rounds):
            g_grad.round(r)
        own[1].wait()
        g_grad.end()
        keep.wait()
        loop(planes, spread)
        r_out.start()
        loop(ff // tile, backward)
        r_out.round(0)
        loop(width // tile, inputs_back)
        r_out.round(1)
        for dist in reversed(range(depth)):
            pos.at(dist, scatter)
        kept = [
            pltpu.make_async_copy(src, dst, keep_sem.at[i])
            for i, (src, dst) in enumerate(
                ((xin, x_out), (gret, gret_out), (inner, inner_out), (ggate, ggate_out), (gup, gup_out))
            )
        ]
        for c in kept:
            c.start()
        for r in range(2, r_out.rounds):
            r_out.round(r)
            if r >= 3:
                r_grad.round(r - 3)
        for r in range(r_out.rounds - 3, r_grad.rounds):
            r_grad.round(r)
        for c in kept:
            c.wait()
        r_out.end()
        r_grad.end()

    vmem, hbm = pl.BlockSpec(memory_space=pltpu.VMEM), pl.BlockSpec(memory_space=HBM)
    dma = pltpu.SemaphoreType.DMA
    return pl.pallas_call(
        body,
        out_shape=[
            jax.ShapeDtypeStruct((rows, width), f32),
            jax.ShapeDtypeStruct((rows, wide), f32),
            jax.ShapeDtypeStruct((devices, rows, width), bf),
            jax.ShapeDtypeStruct((slots, width), bf),
            jax.ShapeDtypeStruct((slots, width), bf),
            jax.ShapeDtypeStruct((slots, ff), bf),
            jax.ShapeDtypeStruct((slots, ff), bf),
            jax.ShapeDtypeStruct((slots, ff), bf),
        ],
        in_specs=[hbm, hbm] + [vmem] * 4 + [hbm] * 3,
        out_specs=[vmem, vmem] + [hbm] * 6,
        scratch_shapes=[
            pltpu.VMEM((width, ff), bf),
            pltpu.VMEM((width, ff), bf),
            pltpu.VMEM((ff, width), bf),
            pltpu.VMEM((devices, rows, width), bf),
            pltpu.VMEM((devices, rows, width), bf),
            pltpu.VMEM((devices, rows, wide), bf),
            pltpu.VMEM((slots, width), bf),
            pltpu.VMEM((slots, width), bf),
            pltpu.VMEM((slots, width), bf),
            pltpu.VMEM((slots, ff), bf),
            pltpu.VMEM((slots, ff), bf),
            pltpu.VMEM((slots, ff), bf),
            pltpu.VMEM((slots, ff), f32),
            pltpu.VMEM((slots, ff), f32),
            pltpu.VMEM((planes, plane_rows, lanes), f32),
            dma((3,)),
            dma((2,)),
            dma,
            dma((5,)),
        ]
        + Gather.sems(depth) * 2
        + Reduce.scratch(depth, rows, width)
        + Reduce.scratch(depth, rows, wide),
        compiler_params=params(number, 60 * 2**20),
        name="experts",
    )(normed, out_grad, select, select_t, named, router, w_gate, w_up, w_down)


def expert_weight_grads(xin, gret, inner, ggate, gup):
    f32 = jnp.float32
    slots, width = xin.shape
    ff = inner.shape[1]
    steps = width // 256

    def body(x, g, i, gg, gu, wg, wu, wd):
        wg[...] = dot_tn(x[...], gg[...])
        wu[...] = dot_tn(x[...], gu[...])
        wd[...] = dot_tn(i[...], g[...])

    whole = pl.BlockSpec((slots, ff), lambda s: (0, 0))
    tall = pl.BlockSpec((slots, 256), lambda s: (0, s))
    return pl.pallas_call(
        body,
        grid=(steps,),
        out_shape=[jax.ShapeDtypeStruct((width, ff), f32)] * 2 + [jax.ShapeDtypeStruct((ff, width), f32)],
        in_specs=[tall, tall, whole, whole, whole],
        out_specs=[pl.BlockSpec((256, ff), lambda s: (s, 0))] * 2 + [pl.BlockSpec((ff, 256), lambda s: (0, s))],
        compiler_params=pltpu.CompilerParams(vmem_limit_bytes=40 * 2**20),
        name="expert_weight_grads",
    )(xin, gret, inner, ggate, gup)


def reduce_inputs(depth, number, part, w_part, o_part, small):
    devices, rows, width = part.shape
    w_rows, head = w_part.shape[0] // (depth * 2), o_part.shape[1]
    groups = depth * 2
    n_red, n_plane = 6, 4

    def body(part_ref, w_ref, o_ref, s_ref, sum_ref, kv_ref, q_ref, out_ref, s_all, *rest):
        red_scratch, rest = rest[:n_red], rest[n_red:]
        plane_scratch, rest = rest[:n_plane], rest[n_plane:]
        pos = Place(depth)
        local = pltpu.make_async_copy(s_ref, s_all.at[pos.block(pos.z)], rest[8])
        local.start()
        pos.greet(plane=True)
        red = Reduce(pos, part_ref, *red_scratch, halves=False)
        red.out = sum_ref
        drive(
            Exchange(
                pos, lambda p: part_of(w_ref, p, w_rows, 0, head), lambda p: cols_of(q_ref, p, head), *rest[0:3]
            ),
            Exchange(pos, lambda p: rows_of(o_ref, p, w_rows), lambda p: cols_of(out_ref, p, head), *rest[3:6]),
            red,
            PlaneReduce(pos, lambda p: part_of(w_ref, p, w_rows, head, 2 * head), kv_ref, *plane_scratch),
            Gather(pos, s_ref, s_all, *rest[6:8], False),
        )
        local.wait()

    vmem, hbm = pl.BlockSpec(memory_space=pltpu.VMEM), pl.BlockSpec(memory_space=HBM)
    return pl.pallas_call(
        body,
        out_shape=[
            jax.ShapeDtypeStruct((rows, width), jnp.float32),
            jax.ShapeDtypeStruct((w_rows, 2 * head), jnp.float32),
            jax.ShapeDtypeStruct((w_rows, groups * head), w_part.dtype),
            jax.ShapeDtypeStruct((w_rows, groups * head), w_part.dtype),
            jax.ShapeDtypeStruct((devices,) + small.shape, small.dtype),
        ],
        in_specs=[vmem, vmem, hbm, hbm],
        out_specs=[vmem, vmem, hbm, hbm, hbm],
        scratch_shapes=Reduce.scratch(depth, rows, width, False)
        + PlaneReduce.scratch(depth, w_rows, 2 * head)
        + Exchange.sems(depth) * 2
        + Gather.sems(depth)
        + [pltpu.SemaphoreType.DMA],
        compiler_params=params(number, 48 * 2**20),
        name="reduce_inputs",
    )(part, w_part, o_part, small)


def head_shards(
    tokens,
    segments,
    routes,
    out_grad,
    norm_gain,
    q_weight,
    k_weight,
    v_weight,
    q_gain,
    k_gain,
    out_weight,
    moe_gain,
    router_weight,
    gate_weight,
    up_weight,
    down_weight,
):
    f32, bf = jnp.float32, jnp.bfloat16
    head_dim = q_gain.shape[0]
    tok_rows, width = tokens.shape
    share_rows = out_grad.shape[0]
    all_tokens = segments.shape[0]
    expert_count = router_weight.shape[1]
    top_count = routes.shape[1]
    groups = all_tokens // tok_rows
    depth = groups // 2
    weight_rows = q_weight.shape[0]
    capacity = max(2, share_rows * top_count * 2 // expert_count)
    slots = capacity * expert_count
    score_scale = head_dim ** (-0.5)
    lane = lax.axis_index("tensor")
    expert = lax.axis_index("dp") * 4 + lane

    places = jnp.arange(all_tokens, dtype=jnp.int32)
    begins = jnp.concatenate([jnp.ones((1,), dtype=bool), segments[1:] != segments[:-1]])
    positions = places - lax.cummax(jnp.where(begins, places, 0), axis=0)
    cosine, sine_part = angles(positions, head_dim)
    allowed = (places[None, :] <= places[:, None]) & (segments[None, :] == segments[:, None])

    tokens_share = lax.dynamic_slice_in_dim(tokens, lane * share_rows, share_rows, 0)
    routes_block = jnp.zeros((8, 128), jnp.int32).at[: share_rows * top_count // 128].set(routes.reshape(-1, 128))
    all_tok, w_in = gather_inputs(depth, 0, tokens_share, q_weight, k_weight, v_weight)
    all_tok = all_tok.reshape(all_tokens, width)
    all_routes, w_o = gather_heads(depth, 1, routes_block, out_weight, head_dim)
    all_routes = all_routes[:, : share_rows * top_count // 128].reshape(all_tokens, top_count)

    tok_float = all_tok.astype(f32)
    norm_gain_float = norm_gain.astype(f32)
    hidden = norm_rows(tok_float, norm_gain_float).astype(bf)
    projected = jnp.dot(hidden, w_in, preferred_element_type=f32)

    def prepare_local(projected_in, qgain_in, kgain_in):
        return prepare(projected_in, qgain_in, kgain_in, cosine, sine_part, head_dim)

    prepared, prepare_back = jax.vjp(prepare_local, projected, q_gain.astype(f32), k_gain.astype(f32))
    queries = prepared[0].astype(bf).reshape(all_tokens, head_dim)
    keys = prepared[1].astype(bf)
    values = prepared[2].astype(bf)
    scores = jnp.einsum("td,nd->tn", queries, keys, preferred_element_type=f32) * score_scale
    scores = jnp.where(allowed, scores, -1e30)
    top = jnp.max(scores, axis=-1, keepdims=True)
    weights = jnp.exp(scores - top)
    mass = jnp.sum(weights, axis=-1, keepdims=True)
    log_total = top + jnp.log(mass)
    head_out = jnp.dot(weights.astype(bf), values, preferred_element_type=f32) / mass
    attended = head_out.astype(bf)
    branch_part = jnp.einsum("tc,dc->td", attended, w_o, preferred_element_type=f32).astype(bf)
    (branch,) = reduce_scatter(
        depth, 3, "reduce_branch", branch_part.reshape(expert_count, share_rows, width)
    )

    middle = tokens_share.astype(f32) + branch
    normed_float, moe_norm_back = jax.vjp(norm_rows, middle, moe_gain.astype(f32))
    plane_rows = all_tokens // depth
    picks = slots // depth
    lanes = 128
    mine = jnp.any(all_routes == expert, axis=1).reshape(depth, plane_rows)
    rank = jnp.cumsum(mine.astype(jnp.int32), axis=1) - 1
    pick = jnp.arange(picks, dtype=jnp.int32)
    select = ((rank[:, None, :] == pick[None, :, None]) & mine[:, None, :]).astype(bf)
    select_t = ((rank[:, :, None] == pick[None, None, :]) & mine[:, :, None]).astype(bf)
    named = jnp.any(all_routes[:, :, None] == jnp.arange(lanes, dtype=jnp.int32), axis=1).astype(f32)
    router = jnp.pad(router_weight, ((0, 0), (0, lanes - expert_count)))
    out_sum, grad_sum, all_normed, *kept = experts(
        depth,
        4,
        normed_float.astype(bf),
        out_grad,
        select,
        select_t,
        named.reshape(depth, plane_rows, lanes),
        router,
        gate_weight[0],
        up_weight[0],
        down_weight[0],
    )
    grad_gate_w, grad_up_w, grad_down = expert_weight_grads(*kept)
    layer_out = (middle + out_sum).astype(bf)
    logit_grad = grad_sum[:, width:].astype(bf)
    grad_normed = grad_sum[:, :width] + jnp.einsum("te,de->td", logit_grad, router, preferred_element_type=f32)
    grad_middle_part, grad_moe_gain = moe_norm_back(grad_normed)
    grad_middle = out_grad.astype(f32) + grad_middle_part
    (all_branch,) = all_gather(
        depth, 7, "gather_grad_branch", jnp.concatenate([grad_middle.astype(bf), logit_grad], axis=1)
    )
    all_branch = all_branch.reshape(all_tokens, width + lanes)
    grad_branch = all_branch[:, :width]
    grad_router = jnp.einsum(
        "td,te->de", all_normed.reshape(all_tokens, width), all_branch[:, width : width + expert_count],
        preferred_element_type=f32,
    )

    grad_heads = jnp.dot(grad_branch, w_o, preferred_element_type=f32).astype(bf)
    out_weight_part = jnp.einsum("td,tc->dc", grad_branch, attended, preferred_element_type=f32).astype(bf)
    row_delta = jnp.sum(grad_heads.astype(f32) * head_out, axis=-1, keepdims=True)
    scores = jnp.einsum("td,nd->tn", queries, keys, preferred_element_type=f32) * score_scale
    soft = jnp.where(allowed, jnp.exp(scores - log_total), 0.0)
    grad_soft = jnp.einsum("td,nd->tn", grad_heads, values, preferred_element_type=f32)
    grad_scores = (soft * (grad_soft - row_delta)).astype(bf)
    grad_queries = jnp.dot(grad_scores, keys, preferred_element_type=f32) * score_scale
    grad_keys = jnp.einsum("tn,td->nd", grad_scores, queries, preferred_element_type=f32) * score_scale
    grad_values = jnp.einsum("tn,td->nd", soft.astype(bf), grad_heads, preferred_element_type=f32)
    grad_proj_float, grad_q_gain, grad_k_gain = prepare_back((grad_queries[:, None, :], grad_keys, grad_values))
    grad_projected = grad_proj_float.astype(bf)
    hidden_part = jnp.einsum("tc,dc->td", grad_projected, w_in, preferred_element_type=f32)
    _, first_norm_back = jax.vjp(norm_rows, tok_float, norm_gain_float)
    in_weight_part = jnp.einsum("td,tc->dc", hidden, grad_projected, preferred_element_type=f32).astype(bf)
    normalised = norm_rows(tok_float, 1.0)
    grad_norm_gain = jnp.sum(hidden_part * normalised, axis=0)
    small = jnp.concatenate([grad_norm_gain, grad_moe_gain, grad_q_gain, grad_k_gain])
    small_rows = -(-small.shape[0] // 1024) * 8
    small_block = jnp.pad(small, (0, small_rows * 128 - small.shape[0])).reshape(small_rows, 128)
    grad_hidden, kv_sum, grad_q, grad_o, all_small = reduce_inputs(
        depth, 8, hidden_part.astype(bf).reshape(expert_count, share_rows, width), in_weight_part, out_weight_part, small_block
    )
    _, share_norm_back = jax.vjp(norm_rows, tokens_share.astype(f32), norm_gain_float)
    tokens_grad = grad_middle + share_norm_back(grad_hidden)[0]
    small_sums = jnp.sum(all_small, axis=0).reshape(-1)
    return (
        layer_out,
        tokens_grad,
        small_sums[:width],
        grad_q.astype(f32),
        kv_sum[:, :head_dim],
        kv_sum[:, head_dim:],
        small_sums[2 * width : 2 * width + head_dim],
        small_sums[2 * width + head_dim : 2 * width + 2 * head_dim],
        grad_o.astype(f32),
        small_sums[width : 2 * width],
        grad_router,
        grad_gate_w[None],
        grad_up_w[None],
        grad_down[None],
    )


def solution(mesh):
    per_device = shards if mesh.shape["dp"] != 8 or mesh.shape["tensor"] != 4 else head_shards
    placed = (
        P("dp", None),
        P(),
        P(("dp", "tensor"), None),
        P(("dp", "tensor"), None),
        P(),
        P("dp", "tensor"),
        P("dp", "tensor"),
        P("dp", "tensor"),
        P(),
        P(),
        P("dp", "tensor"),
        P(),
        P(),
        P(("dp", "tensor"), None, None),
        P(("dp", "tensor"), None, None),
        P(("dp", "tensor"), None, None),
    )
    return jax.shard_map(
        per_device,
        mesh=mesh,
        in_specs=placed,
        out_specs=(
            P(("dp", "tensor"), None),
            P(("dp", "tensor"), None),
            P(),
            P("dp", "tensor"),
            P("dp", "tensor"),
            P("dp", "tensor"),
            P(),
            P(),
            P("dp", "tensor"),
            P(),
            P(),
            P(("dp", "tensor"), None, None),
            P(("dp", "tensor"), None, None),
            P(("dp", "tensor"), None, None),
        ),
        check_vma=False,
    )
```

```python
import functools

import jax
import jax.numpy as jnp
from jax import lax
from jax.experimental import pallas as pl
from jax.experimental.pallas import tpu as pltpu
from jax.sharding import PartitionSpec as P

EPS = 1e-06
THETA = 1000000.0


def norm_rows(values, gain):
    return values * lax.rsqrt(jnp.mean(values * values, axis=-1, keepdims=True) + EPS) * gain


def rotary(values, cosine, sine_part):
    half_dim = values.shape[-1] // 2
    front_half = values[..., :half_dim]
    back_half = values[..., half_dim:]
    return jnp.concatenate(
        [front_half * cosine - back_half * sine_part, back_half * cosine + front_half * sine_part],
        axis=-1,
    )


def angles(positions, head_dim):
    half_dim = head_dim // 2
    frequency = THETA ** (-(jnp.arange(half_dim).astype(jnp.float32) * 2.0) / head_dim)
    rotation = positions.astype(jnp.float32)[:, None] * frequency[None, :]
    return (jnp.cos(rotation), jnp.sin(rotation))


def prepare(projected, q_gain, k_gain, cosine, sine_part, head_dim):
    tok_rows = projected.shape[0]
    query_width = projected.shape[1] - 2 * head_dim
    queries = projected[:, :query_width].reshape(tok_rows, query_width // head_dim, head_dim)
    keys_local = projected[:, query_width : query_width + head_dim]
    values_local = projected[:, query_width + head_dim :]
    queries = rotary(norm_rows(queries, q_gain), cosine[:, None, :], sine_part[:, None, :])
    keys_local = rotary(norm_rows(keys_local, k_gain), cosine, sine_part)
    return (queries, keys_local, values_local)


def swiglu(gate_in, up_in):
    return jax.nn.silu(gate_in) * up_in


def shards(
    tokens,
    segments,
    routes,
    out_grad,
    norm_gain,
    q_weight,
    k_weight,
    v_weight,
    q_gain,
    k_gain,
    out_weight,
    moe_gain,
    router_weight,
    gate_weight,
    up_weight,
    down_weight,
):
    head_dim = q_gain.shape[0]
    tok_rows = tokens.shape[0]
    model_width = tokens.shape[1]
    share_rows = out_grad.shape[0]
    all_tokens = segments.shape[0]
    expert_count = router_weight.shape[1]
    top_count = routes.shape[1]
    capacity = max(2, share_rows * top_count * 2 // expert_count)
    score_scale = head_dim ** (-0.5)
    first_row = lax.axis_index("dp") * tok_rows
    places = jnp.arange(all_tokens, dtype=jnp.int32)
    begins = jnp.concatenate([jnp.ones((1,), dtype=bool), segments[1:] != segments[:-1]])
    positions = places - lax.cummax(jnp.where(begins, places, 0), axis=0)
    local_positions = lax.dynamic_slice_in_dim(positions, first_row, tok_rows)
    local_docs = lax.dynamic_slice_in_dim(segments, first_row, tok_rows)
    query_places = first_row + jnp.arange(tok_rows, dtype=jnp.int32)
    cosine, sine_part = angles(local_positions, head_dim)
    weight_rows = (
        lax.all_gather(q_weight, "dp", axis=0, tiled=True),
        lax.all_gather(k_weight, "dp", axis=0, tiled=True),
        lax.all_gather(v_weight, "dp", axis=0, tiled=True),
        lax.all_gather(out_weight, "dp", axis=0, tiled=True),
    )
    input_weight = jnp.concatenate([weight_rows[0], weight_rows[1], weight_rows[2]], axis=1)
    output_weight = weight_rows[3]
    tokens_float = tokens.astype(jnp.float32)
    norm_gain_float = norm_gain.astype(jnp.float32)
    hidden = norm_rows(tokens_float, norm_gain_float).astype(jnp.bfloat16)
    projected = jnp.dot(hidden, input_weight, preferred_element_type=jnp.float32)

    def prepare_local(projected_in, qgain_in, kgain_in):
        return prepare(projected_in, qgain_in, kgain_in, cosine, sine_part, head_dim)

    prepared, prepare_back = jax.vjp(
        prepare_local, projected, q_gain.astype(jnp.float32), k_gain.astype(jnp.float32)
    )
    queries = prepared[0].astype(jnp.bfloat16)
    keys_local = prepared[1].astype(jnp.bfloat16)
    values_local = prepared[2].astype(jnp.bfloat16)
    local_heads = queries.shape[1]

    def visible(offset, length):
        key_places = offset + jnp.arange(length, dtype=jnp.int32)
        key_docs = lax.dynamic_slice_in_dim(segments, offset, length)
        return (key_places[None, :] <= query_places[:, None]) & (
            key_docs[None, :] == local_docs[:, None]
        )

    running_max = jnp.full((tok_rows, local_heads), -1e30, jnp.float32)
    key_piece = lax.all_gather(keys_local, "dp", axis=0, tiled=True)
    value_piece = lax.all_gather(values_local, "dp", axis=0, tiled=True)
    allowed = visible(jnp.int32(0), key_piece.shape[0])[:, None, :]
    scores = (
        jnp.einsum("thd,nd->thn", queries, key_piece, preferred_element_type=jnp.float32)
        * score_scale
    )
    scores = jnp.where(allowed, scores, -1e30)
    new_max = jnp.maximum(running_max, jnp.max(scores, axis=-1))
    soft_weights = jnp.where(allowed, jnp.exp(scores - new_max[:, :, None]), 0.0)
    softmax_mass = jnp.sum(soft_weights, axis=-1)
    weighted_sum = jnp.einsum(
        "thn,nd->thd",
        soft_weights.astype(jnp.bfloat16),
        value_piece,
        preferred_element_type=jnp.float32,
    )
    running_max, softmax_mass, weighted_sum = (new_max, softmax_mass, weighted_sum)
    head_out = weighted_sum / softmax_mass[:, :, None]
    log_total = running_max + jnp.log(softmax_mass)
    attended = head_out.astype(jnp.bfloat16).reshape(tok_rows, local_heads * head_dim)
    branch = lax.psum_scatter(
        jnp.einsum("tc,dc->td", attended, output_weight, preferred_element_type=jnp.float32).astype(
            jnp.bfloat16
        ),
        "tensor",
        scatter_dimension=0,
        tiled=True,
    ).astype(jnp.float32)
    tensor_lane = lax.axis_index("tensor")
    tokens_share = lax.dynamic_slice_in_dim(tokens_float, tensor_lane * share_rows, share_rows, 0)
    middle = tokens_share + branch
    normed_float, moe_norm_back = jax.vjp(norm_rows, middle, moe_gain.astype(jnp.float32))
    normed = normed_float.astype(jnp.bfloat16)
    logits = jnp.dot(normed, router_weight, preferred_element_type=jnp.float32)

    def gating(logit_rows):
        probabilities = jax.nn.softmax(logit_rows, axis=-1)
        chosen = jnp.take_along_axis(probabilities, routes, axis=1)
        return chosen / jnp.sum(chosen, axis=1, keepdims=True)

    gate_values, gating_back = jax.vjp(gating, logits)
    pair_routes = routes.reshape(-1)
    pair_count = pair_routes.shape[0]
    route_table = (
        pair_routes[:, None] == jnp.arange(expert_count, dtype=jnp.int32)[None, :]
    ).astype(jnp.int32)
    route_rank = jnp.sum(jnp.cumsum(route_table, axis=0) * route_table, axis=1) - 1
    slot_index = pair_routes * capacity + route_rank
    slot_owner = (
        jnp.full((expert_count * capacity,), pair_count, jnp.int32)
        .at[slot_index]
        .set(jnp.arange(pair_count, dtype=jnp.int32))
    )
    normed_padded = jnp.concatenate([normed, jnp.zeros((1, model_width), jnp.bfloat16)], axis=0)
    send_rows = normed_padded[slot_owner // top_count].reshape(expert_count, capacity, model_width)
    arrived = lax.all_to_all(send_rows, ("dp", "tensor"), split_axis=0, concat_axis=0, tiled=True)
    expert_inputs = arrived.reshape(-1, model_width)
    w_gate = gate_weight[0]
    w_up = up_weight[0]
    w_down = down_weight[0]
    gate_act = jnp.dot(expert_inputs, w_gate, preferred_element_type=jnp.float32)
    up_act = jnp.dot(expert_inputs, w_up, preferred_element_type=jnp.float32)
    inner_float, swiglu_back = jax.vjp(swiglu, gate_act, up_act)
    inner_act = inner_float.astype(jnp.bfloat16)
    produced = jnp.dot(inner_act, w_down, preferred_element_type=jnp.float32).astype(jnp.bfloat16)
    returned = lax.all_to_all(
        produced.reshape(expert_count, capacity, model_width),
        ("dp", "tensor"),
        split_axis=0,
        concat_axis=0,
        tiled=True,
    )
    picked = (
        returned.reshape(-1, model_width)[slot_index]
        .reshape(share_rows, top_count, model_width)
        .astype(jnp.float32)
    )
    layer_out = (middle + jnp.sum(gate_values[:, :, None] * picked, axis=1)).astype(jnp.bfloat16)
    grad_out = out_grad.astype(jnp.float32)
    grad_picked = (
        (gate_values[:, :, None] * grad_out[:, None, :])
        .astype(jnp.bfloat16)
        .reshape(pair_count, model_width)
    )
    grad_gates = jnp.sum(grad_out[:, None, :] * picked, axis=2)
    grad_padded = jnp.concatenate([grad_picked, jnp.zeros((1, model_width), jnp.bfloat16)], axis=0)
    grad_send = grad_padded[slot_owner].reshape(expert_count, capacity, model_width)
    grad_arrived = lax.all_to_all(
        grad_send, ("dp", "tensor"), split_axis=0, concat_axis=0, tiled=True
    ).reshape(-1, model_width)
    grad_inner = jnp.einsum("rd,fd->rf", grad_arrived, w_down, preferred_element_type=jnp.float32)
    grad_down = jnp.einsum("rf,rd->fd", inner_act, grad_arrived, preferred_element_type=jnp.float32)
    grad_gate_float, grad_up_float = swiglu_back(grad_inner)
    grad_gate_act = grad_gate_float.astype(jnp.bfloat16)
    grad_up_act = grad_up_float.astype(jnp.bfloat16)
    grad_gate_w = jnp.einsum(
        "rd,rf->df", expert_inputs, grad_gate_act, preferred_element_type=jnp.float32
    )
    grad_up_w = jnp.einsum(
        "rd,rf->df", expert_inputs, grad_up_act, preferred_element_type=jnp.float32
    )
    grad_inputs = jnp.einsum("rf,df->rd", grad_gate_act, w_gate, preferred_element_type=jnp.float32)
    grad_inputs = (
        grad_inputs + jnp.einsum("rf,df->rd", grad_up_act, w_up, preferred_element_type=jnp.float32)
    ).astype(jnp.bfloat16)
    grad_home = lax.all_to_all(
        grad_inputs.reshape(expert_count, capacity, model_width),
        ("dp", "tensor"),
        split_axis=0,
        concat_axis=0,
        tiled=True,
    )
    grad_normed = jnp.sum(
        grad_home.reshape(-1, model_width)[slot_index]
        .reshape(share_rows, top_count, model_width)
        .astype(jnp.float32),
        axis=1,
    )
    (grad_logit_float,) = gating_back(grad_gates)
    grad_logits = grad_logit_float.astype(jnp.bfloat16)
    grad_router = jnp.einsum("td,te->de", normed, grad_logits, preferred_element_type=jnp.float32)
    grad_normed = grad_normed + jnp.einsum(
        "te,de->td", grad_logits, router_weight, preferred_element_type=jnp.float32
    )
    grad_middle_part, grad_moe_gain = moe_norm_back(grad_normed)
    grad_middle = grad_out + grad_middle_part
    grad_branch = lax.all_gather(grad_middle.astype(jnp.bfloat16), "tensor", axis=0, tiled=True)
    again_rows = (
        lax.all_gather(q_weight, "dp", axis=0, tiled=True),
        lax.all_gather(k_weight, "dp", axis=0, tiled=True),
        lax.all_gather(v_weight, "dp", axis=0, tiled=True),
        lax.all_gather(out_weight, "dp", axis=0, tiled=True),
    )
    input_back = jnp.concatenate([again_rows[0], again_rows[1], again_rows[2]], axis=1)
    output_back = again_rows[3]
    grad_heads = (
        jnp.dot(grad_branch, output_back, preferred_element_type=jnp.float32)
        .astype(jnp.bfloat16)
        .reshape(tok_rows, local_heads, head_dim)
    )
    row_delta = jnp.sum(grad_heads.astype(jnp.float32) * head_out, axis=-1)
    key_rows, value_rows = (
        lax.all_gather(keys_local, "dp", axis=0, tiled=True),
        lax.all_gather(values_local, "dp", axis=0, tiled=True),
    )
    key_block = min(512, all_tokens)

    def key_step(grad_queries, block_number):
        offset = block_number * key_block
        key_piece = lax.dynamic_slice_in_dim(key_rows, offset, key_block, 0)
        value_piece = lax.dynamic_slice_in_dim(value_rows, offset, key_block, 0)
        allowed = visible(offset, key_block)[:, None, :]
        scores = (
            jnp.einsum("thd,nd->thn", queries, key_piece, preferred_element_type=jnp.float32)
            * score_scale
        )
        soft_weights = jnp.where(allowed, jnp.exp(scores - log_total[:, :, None]), 0.0)
        grad_weights = jnp.einsum(
            "thd,nd->thn", grad_heads, value_piece, preferred_element_type=jnp.float32
        )
        grad_scores = (soft_weights * (grad_weights - row_delta[:, :, None])).astype(jnp.bfloat16)
        grad_queries = (
            grad_queries
            + jnp.einsum("thn,nd->thd", grad_scores, key_piece, preferred_element_type=jnp.float32)
            * score_scale
        )
        grad_key_piece = (
            jnp.einsum("thn,thd->nd", grad_scores, queries, preferred_element_type=jnp.float32)
            * score_scale
        )
        grad_value_piece = jnp.einsum(
            "thn,thd->nd",
            soft_weights.astype(jnp.bfloat16),
            grad_heads,
            preferred_element_type=jnp.float32,
        )
        return (grad_queries, jnp.concatenate([grad_key_piece, grad_value_piece], axis=1))

    grad_queries, key_terms = lax.scan(
        key_step,
        jnp.zeros((tok_rows, local_heads, head_dim), jnp.float32),
        jnp.arange(all_tokens // key_block, dtype=jnp.int32),
    )
    key_grads = lax.psum_scatter(
        key_terms.reshape(all_tokens, 2 * head_dim).astype(jnp.bfloat16),
        "dp",
        scatter_dimension=0,
        tiled=True,
    ).astype(jnp.float32)
    grad_proj_float, grad_q_gain, grad_k_gain = prepare_back(
        (grad_queries, key_grads[:, :head_dim], key_grads[:, head_dim:])
    )
    grad_projected = grad_proj_float.astype(jnp.bfloat16)
    grad_hidden = jnp.einsum(
        "tc,dc->td", grad_projected, input_back, preferred_element_type=jnp.float32
    )
    grad_hidden_share = lax.psum_scatter(
        grad_hidden.astype(jnp.bfloat16), "tensor", scatter_dimension=0, tiled=True
    ).astype(jnp.float32)
    _, first_norm_back = jax.vjp(norm_rows, tokens_share, norm_gain_float)
    grad_tokens_part, grad_norm_gain = first_norm_back(grad_hidden_share)
    tokens_grad = grad_middle + grad_tokens_part
    input_part = jnp.einsum("td,tc->dc", hidden, grad_projected, preferred_element_type=jnp.float32)
    output_part = jnp.einsum("td,tc->dc", grad_branch, attended, preferred_element_type=jnp.float32)
    weight_share = lax.psum_scatter(
        jnp.concatenate([input_part, output_part], axis=1).astype(jnp.bfloat16),
        "dp",
        scatter_dimension=0,
        tiled=True,
    ).astype(jnp.float32)
    query_width = local_heads * head_dim
    grad_q_weight = weight_share[:, :query_width]
    grad_k_weight = weight_share[:, query_width : query_width + head_dim]
    grad_v_weight = weight_share[:, query_width + head_dim : query_width + 2 * head_dim]
    grad_out_weight = weight_share[:, query_width + 2 * head_dim :]
    small_sums = lax.psum(
        (grad_router, grad_norm_gain, grad_moe_gain, grad_q_gain, grad_k_gain), ("dp", "tensor")
    )
    return (
        layer_out,
        tokens_grad,
        small_sums[1],
        grad_q_weight,
        grad_k_weight,
        grad_v_weight,
        small_sums[3],
        small_sums[4],
        grad_out_weight,
        small_sums[2],
        small_sums[0],
        grad_gate_w[None],
        grad_up_w[None],
        grad_down[None],
    )


MESH = pl.DeviceIdType.MESH
HBM = pl.ANY


class Place:
    def __init__(self, depth):
        d = lax.axis_index("dp")
        t = lax.axis_index("tensor")
        self.depth = depth
        self.d, self.t = d, t
        self.z, self.x = d // 2, lax.rem(d, 2)
        self.y, self.c = t // 2, lax.rem(t, 2)
        self.next_to = {
            "x": (self.z * 2 + 1 - self.x, t),
            "y": (d, (1 - self.y) * 2 + self.c),
            "c": (d, self.y * 2 + 1 - self.c),
            "up": (d + 2, t),
            "down": (d - 2, t),
        }

    def block(self, z, fx=0, fy=0, fc=0):
        x = 1 - self.x if fx else self.x
        y = 1 - self.y if fy else self.y
        c = 1 - self.c if fc else self.c
        return (z * 2 + x) * 4 + y * 2 + c

    def at(self, dist, step):
        if dist == 0:
            step(self.z)
            return

        @pl.when(self.z >= dist)
        def _():
            step(self.z - dist)

        @pl.when(self.z + dist < self.depth)
        def _():
            step(self.z + dist)

    def greet(self, plane=False):
        barrier = pltpu.get_barrier_semaphore()

        def signal(to):
            pl.semaphore_signal(barrier, inc=1, device_id=self.next_to[to], device_id_type=MESH)

        if plane:
            groups = self.depth * 2
            for k in range(1, groups):
                to = (lax.rem(self.d + k, groups), self.t)
                pl.semaphore_signal(barrier, inc=1, device_id=to, device_id_type=MESH)
            signal("y")
            signal("c")
            pl.semaphore_wait(barrier, groups + 1)
            return
        for to in ("x", "y", "c"):
            signal(to)

        @pl.when(self.z > 0)
        def _():
            signal("down")

        @pl.when(self.z < self.depth - 1)
        def _():
            signal("up")

        above = (self.z < self.depth - 1).astype(jnp.int32)
        below = (self.z > 0).astype(jnp.int32)
        pl.semaphore_wait(barrier, 3 + above + below)

    def copy(self, src, dst, send, recv, to):
        return pltpu.make_async_remote_copy(
            src_ref=src,
            dst_ref=dst,
            send_sem=send,
            recv_sem=recv,
            device_id=self.next_to[to],
            device_id_type=MESH,
        )


class Gather:
    SEND, RECV = 11, 10

    def __init__(self, pos, own, out, send, recv, halves):
        self.pos, self.own, self.out = pos, own, out
        self.send, self.recv = send, recv
        rows = out.shape[1]
        self.h0 = pl.ds(0, rows // 2 if halves else rows)
        self.h1 = pl.ds(rows // 2, rows // 2) if halves else None
        self.rounds = pos.depth + 2

    def link(self, src, dst, sends, recvs, zo, to):
        return self.pos.copy(src, dst, self.send.at[sends, zo], self.recv.at[recvs, zo], to)

    def col(self, zo):
        return self.out.at[self.pos.block(zo)]

    def src(self, zo, mine):
        return self.own if mine else self.col(zo)

    def up(self, zo, mine=False):
        return self.link(self.src(zo, mine), self.col(zo), 0, 0, zo, "up")

    def down(self, zo, mine=False):
        return self.link(self.src(zo, mine), self.col(zo), 1, 0, zo, "down")

    def to_x(self, zo, mine=False):
        return self.link(self.src(zo, mine), self.col(zo), 2, 1, zo, "x")

    def to_y(self, zo, mine=False):
        return self.link(self.src(zo, mine), self.col(zo), 3, 2, zo, "y")

    def to_c(self, zo, mine=False):
        return self.link(self.src(zo, mine), self.col(zo), 4, 5, zo, "c")

    def part(self, zo, fx, fy, rows):
        whole = self.out.at[self.pos.block(zo, fx, fy)]
        return whole if rows is None else whole.at[rows]

    def pass_on(self, zo, fx, fy, rows, sends, recvs, to):
        ref = self.part(zo, fx, fy, rows)
        return self.link(ref, ref, sends, recvs, zo, to)

    def x_to_y(self, zo):
        return self.pass_on(zo, 1, 0, self.h0, 5, 3, "y")

    def x_to_c(self, zo):
        return self.pass_on(zo, 1, 0, None, 6, 6, "c")

    def y_to_x(self, zo):
        return self.pass_on(zo, 0, 1, self.h1, 7, 4, "x")

    def y_to_c(self, zo):
        return self.pass_on(zo, 0, 1, None, 8, 7, "c")

    def far0_to_c(self, zo):
        return self.pass_on(zo, 1, 1, self.h0, 9, 8, "c")

    def far1_to_c(self, zo):
        return self.pass_on(zo, 1, 1, self.h1, 10, 9, "c")

    def along_z(self, zo, mine, what):
        z, depth = self.pos.z, self.pos.depth
        if mine:
            up, down = z < depth - 1, z > 0
        else:
            up, down = (zo < z) & (z < depth - 1), (zo > z) & (z > 0)

        @pl.when(up)
        def _():
            what(self.up(zo, mine))

        @pl.when(down)
        def _():
            what(self.down(zo, mine))

    def on_column(self, zo, mine=False):
        if not mine:
            self.up(zo).wait_recv()
        self.along_z(zo, mine, lambda c: c.start())
        self.to_x(zo, mine).start()
        self.to_y(zo, mine).start()
        self.to_c(zo, mine).start()

    def on_sides(self, zo):
        self.to_x(zo).wait_recv()
        self.x_to_y(zo).start()
        self.x_to_c(zo).start()
        self.to_y(zo).wait_recv()
        if self.h1 is not None:
            self.y_to_x(zo).start()
        self.y_to_c(zo).start()

    def on_far(self, zo):
        self.x_to_y(zo).wait_recv()
        self.far0_to_c(zo).start()
        if self.h1 is not None:
            self.y_to_x(zo).wait_recv()
            self.far1_to_c(zo).start()

    def start(self):
        self.on_column(self.pos.z, True)

    def round(self, r):
        if 1 <= r < self.pos.depth:
            self.pos.at(r, self.on_column)
        if 1 <= r <= self.pos.depth:
            self.pos.at(r - 1, self.on_sides)
        if 2 <= r <= self.pos.depth + 1:
            self.pos.at(r - 2, self.on_far)

    def end_one(self, zo, mine=False):
        split = self.h1 is not None
        arrivals = [self.to_c(zo, mine), self.x_to_c(zo), self.y_to_c(zo), self.far0_to_c(zo)]
        sends = [self.to_x(zo, mine), self.to_y(zo, mine), self.x_to_y(zo)] + arrivals
        if split:
            arrivals.append(self.far1_to_c(zo))
            sends += [self.y_to_x(zo), self.far1_to_c(zo)]
        for c in arrivals:
            c.wait_recv()
        self.along_z(zo, mine, lambda c: c.wait_send())
        for c in sends:
            c.wait_send()

    def end(self):
        self.end_one(self.pos.z, True)
        for r in range(1, self.pos.depth):
            self.pos.at(r, self.end_one)

    @staticmethod
    def sems(depth):
        return [pltpu.SemaphoreType.DMA((Gather.SEND, depth)), pltpu.SemaphoreType.DMA((Gather.RECV, depth))]


class Reduce:
    SEND, RECV = 4 + 4 + 2, 4 + 4 + 2

    def __init__(self, pos, part, core, far, side, column, send, recv, halves=True):
        self.pos, self.part = pos, part
        self.core, self.far, self.side, self.column = core, far, side, column
        self.send, self.recv = send, recv
        rows = part.shape[1]
        self.half = (pl.ds(0, rows // 2), pl.ds(rows // 2, rows // 2)) if halves else (pl.ds(0, rows),)
        self.rounds = pos.depth + 2

    @staticmethod
    def scratch(depth, rows, width, halves=True):
        b = jnp.bfloat16
        return [
            pltpu.VMEM((depth, 4, rows, width), b),
            pltpu.VMEM((depth, 2, rows // 2, width) if halves else (depth, 1, rows, width), b),
            pltpu.VMEM((depth, 2, rows, width), b),
            pltpu.VMEM((depth, 2, rows, width), b),
            pltpu.SemaphoreType.DMA((Reduce.SEND, depth)),
            pltpu.SemaphoreType.DMA((Reduce.RECV, depth)),
        ]

    def link(self, src, dst, k, zo, to):
        return self.pos.copy(src, dst, self.send.at[k, zo], self.recv.at[k, zo], to)

    def to_core(self, zo, fx, fy):
        k = fx * 2 + fy
        return self.link(self.part.at[self.pos.block(zo, fx, fy, 1)], self.core.at[zo, k], k, zo, "c")

    def far_to(self, zo, k):
        return self.link(self.core.at[zo, 3, self.half[k]], self.far.at[zo, k], 4 + k, zo, ("y", "x")[k])

    def side_to(self, zo, k):
        return self.link(self.core.at[zo, 2 - k], self.side.at[zo, k], 6 + k, zo, ("x", "y")[k])

    def down(self, zo):
        return self.link(self.core.at[zo, 0], self.column.at[zo, 0], 8, zo, "down")

    def up(self, zo):
        return self.link(self.core.at[zo, 0], self.column.at[zo, 1], 9, zo, "up")

    def start_one(self, zo):
        for fx, fy in ((1, 1), (1, 0), (0, 1), (0, 0)):
            self.to_core(zo, fx, fy).start()

    def start(self):
        for dist in reversed(range(self.pos.depth)):
            self.pos.at(dist, self.start_one)

    def total(self, *refs):
        f = refs[0][...].astype(jnp.float32)
        for r in refs[1:]:
            f = f + r[...].astype(jnp.float32)
        return f

    def on_core(self, zo):
        for fx, fy in ((1, 1), (1, 0), (0, 1), (0, 0)):
            k = fx * 2 + fy
            self.to_core(zo, fx, fy).wait_recv()
            mine = self.core.at[zo, k]
            mine[...] = self.total(mine, self.part.at[self.pos.block(zo, fx, fy)]).astype(mine.dtype)
            if k == 3:
                for h in range(len(self.half)):
                    self.far_to(zo, h).start()

    def on_far(self, zo):
        for k in range(2):
            if k < len(self.half):
                self.far_to(zo, k).wait_recv()
                mine = self.core.at[zo, 2 - k, self.half[k]]
                mine[...] = self.total(mine, self.far.at[zo, k]).astype(mine.dtype)
            self.side_to(zo, k).start()

    def on_sides(self, zo, mine=False):
        z, depth = self.pos.z, self.pos.depth
        self.side_to(zo, 0).wait_recv()
        self.side_to(zo, 1).wait_recv()
        here = self.core.at[zo, 0]
        summed = self.total(here, self.side.at[zo, 0], self.side.at[zo, 1])
        if mine:
            self.out[...] = summed

            @pl.when(z < depth - 1)
            def _():
                self.down(zo).wait_recv()
                self.out[...] += self.column[zo, 0].astype(jnp.float32)

            @pl.when(z > 0)
            def _():
                self.up(zo).wait_recv()
                self.out[...] += self.column[zo, 1].astype(jnp.float32)

            return
        here[...] = summed.astype(here.dtype)

        @pl.when((zo < z) & (z < depth - 1))
        def _():
            self.down(zo).wait_recv()
            here[...] = self.total(here, self.column.at[zo, 0]).astype(here.dtype)

        @pl.when((zo > z) & (z > 0))
        def _():
            self.up(zo).wait_recv()
            here[...] = self.total(here, self.column.at[zo, 1]).astype(here.dtype)

        @pl.when(zo < z)
        def _():
            self.down(zo).start()

        @pl.when(zo > z)
        def _():
            self.up(zo).start()

    def round(self, r):
        depth = self.pos.depth
        for s in range(3):
            dist = depth - 1 - (r - s)
            if not 0 <= dist < depth:
                continue
            if s == 0:
                self.pos.at(dist, self.on_core)
            elif s == 1:
                self.pos.at(dist, self.on_far)
            elif dist:
                self.pos.at(dist, self.on_sides)
            else:
                self.on_sides(self.pos.z, True)

    def end_one(self, zo):
        for fx in range(2):
            for fy in range(2):
                self.to_core(zo, fx, fy).wait_send()
        for k in range(len(self.half)):
            self.far_to(zo, k).wait_send()
        for k in range(2):
            self.side_to(zo, k).wait_send()

        @pl.when(zo < self.pos.z)
        def _():
            self.down(zo).wait_send()

        @pl.when(zo > self.pos.z)
        def _():
            self.up(zo).wait_send()

    def end(self):
        for r in range(self.pos.depth):
            self.pos.at(r, self.end_one)


class PlaneGather:
    SEND, RECV = 3, 2

    def __init__(self, pos, own, dst, send, recv):
        self.pos, self.own, self.dst = pos, own, dst
        self.send, self.recv = send, recv
        self.rounds = pos.depth

    def link(self, zo, mine, sends, recvs, to):
        dst = self.dst(zo * 2 + self.pos.x)
        return self.pos.copy(self.own if mine else dst, dst, self.send.at[sends, zo], self.recv.at[recvs, zo], to)

    def along_z(self, zo, mine, what):
        z, depth = self.pos.z, self.pos.depth
        if mine:
            up, down = z < depth - 1, z > 0
        else:
            up, down = (zo < z) & (z < depth - 1), (zo > z) & (z > 0)

        @pl.when(up)
        def _():
            what(self.link(zo, mine, 0, 0, "up"))

        @pl.when(down)
        def _():
            what(self.link(zo, mine, 1, 0, "down"))

    def on_column(self, zo, mine=False):
        if not mine:
            self.link(zo, False, 0, 0, "up").wait_recv()
        self.along_z(zo, mine, lambda c: c.start())
        self.link(zo, mine, 2, 1, "x").start()

    def start(self):
        self.on_column(self.pos.z, True)

    def round(self, r):
        if 1 <= r < self.pos.depth:
            self.pos.at(r, self.on_column)

    def end_one(self, zo, mine=False):
        across = self.link(zo, mine, 2, 1, "x")
        across.wait_recv()
        self.along_z(zo, mine, lambda c: c.wait_send())
        across.wait_send()

    def end(self):
        self.end_one(self.pos.z, True)
        for r in range(1, self.pos.depth):
            self.pos.at(r, self.end_one)

    @staticmethod
    def sems(depth):
        return [pltpu.SemaphoreType.DMA((PlaneGather.SEND, depth)), pltpu.SemaphoreType.DMA((PlaneGather.RECV, depth))]


class PlaneReduce:
    def __init__(self, pos, part, out, across, column, send, recv):
        self.pos, self.part, self.out = pos, part, out
        self.across, self.column = across, column
        self.send, self.recv = send, recv
        self.rounds = pos.depth

    @staticmethod
    def scratch(depth, rows, width):
        b = jnp.bfloat16
        return [
            pltpu.VMEM((depth, rows, width), b),
            pltpu.VMEM((depth, 2, rows, width), b),
            pltpu.SemaphoreType.DMA((3, depth)),
            pltpu.SemaphoreType.DMA((3, depth)),
        ]

    def to_x(self, zo):
        src = self.part(zo * 2 + 1 - self.pos.x)
        return self.pos.copy(src, self.across.at[zo], self.send.at[0, zo], self.recv.at[0, zo], "x")

    def down(self, zo):
        return self.pos.copy(
            self.across.at[zo], self.column.at[zo, 0], self.send.at[1, zo], self.recv.at[1, zo], "down"
        )

    def up(self, zo):
        return self.pos.copy(
            self.across.at[zo], self.column.at[zo, 1], self.send.at[2, zo], self.recv.at[2, zo], "up"
        )

    def start(self):
        for dist in reversed(range(self.pos.depth)):
            self.pos.at(dist, lambda zo: self.to_x(zo).start())

    def on_column(self, zo):
        z, depth = self.pos.z, self.pos.depth
        f32 = jnp.float32
        here = self.across.at[zo]
        self.to_x(zo).wait_recv()
        here[...] = (here[...].astype(f32) + self.part(zo * 2 + self.pos.x)[...].astype(f32)).astype(here.dtype)

        @pl.when((zo < z) & (z < depth - 1))
        def _():
            self.down(zo).wait_recv()
            here[...] = (here[...].astype(f32) + self.column[zo, 0].astype(f32)).astype(here.dtype)

        @pl.when((zo > z) & (z > 0))
        def _():
            self.up(zo).wait_recv()
            here[...] = (here[...].astype(f32) + self.column[zo, 1].astype(f32)).astype(here.dtype)

        @pl.when(zo < z)
        def _():
            self.down(zo).start()

        @pl.when(zo > z)
        def _():
            self.up(zo).start()

    def on_own(self):
        z, depth = self.pos.z, self.pos.depth
        f32 = jnp.float32
        self.to_x(z).wait_recv()
        self.out[...] = self.across[z].astype(f32) + self.part(z * 2 + self.pos.x)[...].astype(f32)

        @pl.when(z < depth - 1)
        def _():
            self.down(z).wait_recv()
            self.out[...] += self.column[z, 0].astype(f32)

        @pl.when(z > 0)
        def _():
            self.up(z).wait_recv()
            self.out[...] += self.column[z, 1].astype(f32)

    def round(self, r):
        dist = self.pos.depth - 1 - r
        if dist > 0:
            self.pos.at(dist, self.on_column)
        elif dist == 0:
            self.on_own()

    def end_one(self, zo):
        self.to_x(zo).wait_send()

        @pl.when(zo < self.pos.z)
        def _():
            self.down(zo).wait_send()

        @pl.when(zo > self.pos.z)
        def _():
            self.up(zo).wait_send()

    def end(self):
        for r in range(self.pos.depth):
            self.pos.at(r, self.end_one)


class Exchange:
    def __init__(self, pos, piece, place, send, recv, local):
        self.pos, self.piece, self.place = pos, piece, place
        self.send, self.recv, self.local = send, recv, local
        self.groups = pos.depth * 2
        self.rounds = 0

    @staticmethod
    def sems(depth):
        n = depth * 2 - 1
        return [pltpu.SemaphoreType.DMA((n,)), pltpu.SemaphoreType.DMA((n,)), pltpu.SemaphoreType.DMA]

    def peer(self, k):
        return lax.rem(self.pos.d + k, self.groups)

    def copy(self, k):
        p = self.peer(k)
        return pltpu.make_async_remote_copy(
            src_ref=self.piece(p),
            dst_ref=self.place(self.pos.d),
            send_sem=self.send.at[k - 1],
            recv_sem=self.recv.at[k - 1],
            device_id=(p, self.pos.t),
            device_id_type=MESH,
        )

    def here(self):
        return pltpu.make_async_copy(self.piece(self.pos.d), self.place(self.pos.d), self.local)

    def start(self):
        self.here().start()
        for k in range(1, self.groups):
            self.copy(k).start()

    def round(self, r):
        pass

    def end(self):
        self.here().wait()
        for k in range(1, self.groups):
            self.copy(k).wait()


def drive(*parts):
    for p in parts:
        p.start()
    for r in range(max(p.rounds for p in parts)):
        for p in parts:
            p.round(r)
    for p in parts:
        p.end()


def params(number, vmem=None):
    return pltpu.CompilerParams(collective_id=number, has_side_effects=True, vmem_limit_bytes=vmem)


def rows_of(ref, p, rows):
    return ref.at[pl.ds(p * rows, rows)]


def cols_of(ref, p, cols):
    return ref.at[:, pl.ds(pl.multiple_of(p * cols, cols), cols)]


def part_of(ref, p, rows, first, cols):
    return ref.at[pl.ds(p * rows, rows), pl.ds(first, cols)]


def dot(a, b):
    return jnp.dot(a, b, preferred_element_type=jnp.float32)


def dot_nt(a, b):
    return lax.dot_general(a, b, (((1,), (1,)), ((), ())), preferred_element_type=jnp.float32)


def dot_tn(a, b):
    return lax.dot_general(a, b, (((0,), (0,)), ((), ())), preferred_element_type=jnp.float32)


def loop(count, step):
    lax.fori_loop(0, count, lambda i, _: (step(i), 0)[1], 0)


def norm_back(values, gain, grad):
    r = lax.rsqrt(jnp.mean(values * values, axis=-1, keepdims=True) + EPS)
    unit = values * r
    scaled = grad * gain
    return r * (scaled - unit * jnp.mean(scaled * unit, axis=-1, keepdims=True)), grad * unit


def experts(depth, number, normed, out_grad, all_named, middle, moe_gain, router, w_gate, w_up, w_down):
    f32, bf = jnp.float32, jnp.bfloat16
    rows, width = normed.shape
    devices = depth * 8
    plane_rows = rows * 8
    picks = plane_rows // 2
    slots = depth * picks
    ff = w_gate.shape[1]
    lanes = all_named.shape[2]
    count = router.shape[1]
    wide = width + lanes
    tile = 256

    def body(
        n_ref, g_ref, named_hbm, mid_ref, gain_ref, router_ref, wg_hbm, wu_hbm, wd_hbm,
        layer_out, grad_middle, grad_block, gain_grad, n_all, x_out, gret_out, inner_out, ggate_out, gup_out,
        wg, wu, wd, nb, gb, part, xin, gret, ret, inner, ggate, gup, act_a, act_u, gates, out_sum, grad_sum,
        named, select_t, router_wide,
        w_sem, own_sem, all_sem, keep_sem, *rest,
    ):
        pos = Place(depth)
        expert = pos.block(pos.z)
        loads = [
            pltpu.make_async_copy(src, dst, w_sem.at[i])
            for i, (src, dst) in enumerate(((wg_hbm, wg), (wu_hbm, wu), (wd_hbm, wd), (named_hbm, named)))
        ]
        own = [
            pltpu.make_async_copy(n_ref, nb.at[expert], own_sem.at[0]),
            pltpu.make_async_copy(g_ref, gb.at[expert], own_sem.at[1]),
        ]
        for c in own + loads:
            c.start()
        pos.greet()
        g_normed = Gather(pos, n_ref, nb, *rest[0:2], True)
        g_grad = Gather(pos, g_ref, gb, *rest[2:4], True)
        r_out = Reduce(pos, nb, *rest[4:10])
        r_grad = Reduce(pos, part, *rest[10:16])
        r_out.out, r_grad.out = out_sum, grad_sum

        def plane(ref, z):
            return ref[pl.ds(z * 8, 8)].reshape(plane_rows, ref.shape[2])

        def picked(z):
            return pl.ds(pl.multiple_of(z * picks, picks), picks)

        def cols(i, size=tile):
            return pl.ds(pl.multiple_of(i * size, size), size)

        here = lax.broadcasted_iota(jnp.int32, (plane_rows, lanes), 1) == expert

        def choose(z):
            names = plane(named, z)
            ones = names.astype(f32)
            above = lax.broadcasted_iota(jnp.int32, (plane_rows, plane_rows), 0)
            upto = lax.broadcasted_iota(jnp.int32, (plane_rows, plane_rows), 1) <= above
            counts = dot(upto.astype(f32).astype(bf), names)
            place = jnp.sum(jnp.where(here, counts * ones, 0.0), axis=1, keepdims=True) - 1.0
            pick = lax.broadcasted_iota(jnp.int32, (plane_rows, picks), 1).astype(f32)
            select_t[z] = jnp.where(place == pick, 1.0, 0.0).astype(bf)

        def take(z):
            tok = plane(nb, z)
            logits = dot(tok, router_wide[...])
            chosen = plane(named, z).astype(f32) > 0
            top = jnp.max(jnp.where(chosen, logits, -1e30), axis=1, keepdims=True)
            raised = jnp.where(chosen, jnp.exp(jnp.minimum(logits - top, 0.0)), 0.0)
            gates[z] = raised / jnp.sum(raised, axis=1, keepdims=True)
            xin[picked(z), :] = dot_tn(select_t[z], tok).astype(bf)

        def forward(i):
            a = dot(xin[...], wg[:, cols(i)])
            u = dot(xin[...], wu[:, cols(i)])
            act_a[:, cols(i)] = a
            act_u[:, cols(i)] = u
            inner[:, cols(i)] = (a / (1.0 + jnp.exp(-a)) * u).astype(bf)

        def produce(i):
            ret[:, cols(i)] = dot(inner[...], wd[:, cols(i)]).astype(bf)

        def spread(z):
            gate = gates[z]
            mine = jnp.sum(jnp.where(here, gate, 0.0), axis=1, keepdims=True)
            summed = jnp.zeros((plane_rows, 1), f32)
            for i in range(width // 512):
                c = pl.ds(i * 512, 512)
                g = gb[pl.ds(z * 8, 8), :, c].reshape(plane_rows, 512).astype(f32)
                gret[picked(z), c] = dot_tn(select_t[z], (mine * g).astype(bf)).astype(bf)
                back = dot(select_t[z], ret[picked(z), c])
                nb[pl.ds(z * 8, 8), :, c] = (mine * back).astype(bf).reshape(8, rows, 512)
                summed += jnp.sum(g * back, axis=1, keepdims=True)
            logit = gate * (jnp.where(here, 1.0, 0.0) - mine) * summed
            part[pl.ds(z * 8, 8), :, pl.ds(width, lanes)] = logit.astype(bf).reshape(8, rows, lanes)

        def backward(i):
            gi = dot_nt(gret[...], wd[cols(i), :])
            a = act_a[:, cols(i)]
            s = 1.0 / (1.0 + jnp.exp(-a))
            ggate[:, cols(i)] = (gi * act_u[:, cols(i)] * (s + a * s * (1.0 - s))).astype(bf)
            gup[:, cols(i)] = (gi * (a * s)).astype(bf)

        def inputs_back(i):
            ret[:, cols(i)] = (dot_nt(ggate[...], wg[cols(i), :]) + dot_nt(gup[...], wu[cols(i), :])).astype(bf)

        def scatter(z):
            for i in range(width // 512):
                c = pl.ds(i * 512, 512)
                part[pl.ds(z * 8, 8), :, c] = dot(select_t[z], ret[picked(z), c]).astype(bf).reshape(8, rows, 512)
            r_grad.start_one(z)

        g_normed.start()
        router_wide[...] = jnp.zeros(router_wide.shape, bf)
        router_wide[:, pl.ds(0, count)] = router_ref[...]
        loads[3].wait()
        loop(depth, choose)
        for r in range(1, 4):
            g_normed.round(r)
        g_grad.start()
        for r in range(4, g_normed.rounds):
            g_normed.round(r)
        own[0].wait()
        g_normed.end()
        keep = pltpu.make_async_copy(nb, n_all, all_sem)
        keep.start()
        g_grad.round(1)
        loop(depth, take)
        g_grad.round(2)
        loads[0].wait()
        loads[1].wait()
        loop(ff // tile, forward)
        g_grad.round(3)
        loads[2].wait()
        loop(width // tile, produce)
        for r in range(4, g_grad.rounds):
            g_grad.round(r)
        own[1].wait()
        g_grad.end()
        keep.wait()
        loop(depth, spread)
        r_out.start()
        loop(ff // tile, backward)
        r_out.round(0)
        loop(width // tile, inputs_back)
        r_out.round(1)
        for dist in reversed(range(depth)):
            pos.at(dist, scatter)
        kept = [
            pltpu.make_async_copy(src, dst, keep_sem.at[i])
            for i, (src, dst) in enumerate(
                ((xin, x_out), (gret, gret_out), (inner, inner_out), (ggate, ggate_out), (gup, gup_out))
            )
        ]
        for c in kept:
            c.start()
        for r in range(2, r_out.rounds):
            r_out.round(r)
            if r >= 3:
                r_grad.round(r - 3)
        for r in range(r_out.rounds - 3, r_grad.rounds):
            r_grad.round(r)
        mid = mid_ref[...]
        layer_out[...] = (mid + out_sum[...]).astype(bf)
        logit = grad_sum[:, pl.ds(width, lanes)].astype(bf)
        change, by_gain = norm_back(mid, gain_ref[...], grad_sum[:, pl.ds(0, width)] + dot_nt(logit, router_wide[...]))
        gain_grad[...] = jnp.sum(by_gain, axis=0, keepdims=True)
        change = gb[expert].astype(f32) + change
        grad_middle[...] = change
        grad_block[:, pl.ds(0, width)] = change.astype(bf)
        grad_block[:, pl.ds(width, lanes)] = logit
        for c in kept:
            c.wait()
        r_out.end()
        r_grad.end()

    vmem, hbm = pl.BlockSpec(memory_space=pltpu.VMEM), pl.BlockSpec(memory_space=HBM)
    dma = pltpu.SemaphoreType.DMA
    shape = jax.ShapeDtypeStruct
    return pl.pallas_call(
        body,
        out_shape=[
            shape((rows, width), bf),
            shape((rows, width), f32),
            shape((rows, wide), bf),
            shape((1, width), f32),
            shape((devices, rows, width), bf),
            shape((slots, width), bf),
            shape((slots, width), bf),
            shape((slots, ff), bf),
            shape((slots, ff), bf),
            shape((slots, ff), bf),
        ],
        in_specs=[hbm] * 3 + [vmem] * 3 + [hbm] * 3,
        out_specs=[vmem] * 4 + [hbm] * 6,
        scratch_shapes=[
            pltpu.VMEM((width, ff), bf),
            pltpu.VMEM((width, ff), bf),
            pltpu.VMEM((ff, width), bf),
            pltpu.VMEM((devices, rows, width), bf),
            pltpu.VMEM((devices, rows, width), bf),
            pltpu.VMEM((devices, rows, wide), bf),
            pltpu.VMEM((slots, width), bf),
            pltpu.VMEM((slots, width), bf),
            pltpu.VMEM((slots, width), bf),
            pltpu.VMEM((slots, ff), bf),
            pltpu.VMEM((slots, ff), bf),
            pltpu.VMEM((slots, ff), bf),
            pltpu.VMEM((slots, ff), f32),
            pltpu.VMEM((slots, ff), f32),
            pltpu.VMEM((depth, plane_rows, lanes), f32),
            pltpu.VMEM((rows, width), f32),
            pltpu.VMEM((rows, wide), f32),
            pltpu.VMEM((devices, rows, lanes), bf),
            pltpu.VMEM((depth, plane_rows, picks), bf),
            pltpu.VMEM((width, lanes), bf),
            dma((4,)),
            dma((2,)),
            dma,
            dma((5,)),
        ]
        + Gather.sems(depth) * 2
        + Reduce.scratch(depth, rows, width)
        + Reduce.scratch(depth, rows, wide),
        compiler_params=params(number, 60 * 2**20),
        name="experts",
    )(normed, out_grad, all_named, middle, moe_gain, router, w_gate, w_up, w_down)


def local_weight_grads(xin, gret, inner, ggate, gup, normed, logit_grad):
    f32 = jnp.float32
    slots, width = xin.shape
    ff = inner.shape[1]
    total, lanes = logit_grad.shape
    steps = width // 256

    def body(x, g, i, gg, gu, n, lg, wg, wu, wd, wr):
        wg[...] = dot_tn(x[...], gg[...])
        wu[...] = dot_tn(x[...], gu[...])
        wd[...] = dot_tn(i[...], g[...])
        wr[...] = dot_tn(n[...], lg[...])

    whole = pl.BlockSpec((slots, ff), lambda s: (0, 0))
    tall = pl.BlockSpec((slots, 256), lambda s: (0, s))
    return pl.pallas_call(
        body,
        grid=(steps,),
        out_shape=[jax.ShapeDtypeStruct((width, ff), f32)] * 2
        + [jax.ShapeDtypeStruct((ff, width), f32), jax.ShapeDtypeStruct((width, lanes), f32)],
        in_specs=[tall, tall, whole, whole, whole]
        + [pl.BlockSpec((total, 256), lambda s: (0, s)), pl.BlockSpec((total, lanes), lambda s: (0, 0))],
        out_specs=[pl.BlockSpec((256, ff), lambda s: (s, 0))] * 2
        + [pl.BlockSpec((ff, 256), lambda s: (0, s)), pl.BlockSpec((256, lanes), lambda s: (s, 0))],
        compiler_params=pltpu.CompilerParams(vmem_limit_bytes=40 * 2**20),
        name="local_weight_grads",
    )(xin, gret, inner, ggate, gup, normed, logit_grad)


def turn(u, cosine, sine):
    return u * cosine + pltpu.roll(u, u.shape[1] // 2, 1) * sine


def attend(depth, number, tokens, named, q_weight, k_weight, v_weight, out_weight, gains, frequency, docs):
    f32, bf = jnp.float32, jnp.bfloat16
    norm_gain, q_gain, k_gain, moe_gain = gains
    devices = depth * 8
    rows, width = tokens.shape[0] // 4, tokens.shape[1]
    w_rows, head = k_weight.shape
    total = devices * rows
    plane_rows = total // depth
    scale = head ** (-0.5)

    def body(
        tok, names, wq, wk, wv, wo, ng, qg, kg, mg, freq, drow,
        middle, normed, all_named, all_tok, hidden_out, wi_out, wo_out, projected, queries, keys, values, heads, totals,
        cosines, sines,
        tb, w_in, w_o, part, branch, doc, home, own_sem, keep_sem, *rest,
    ):
        pos = Place(depth)
        device = pos.block(pos.z)
        share = tok.at[pl.ds(pl.multiple_of(pos.t * rows, rows), rows)]
        own = [
            pltpu.make_async_copy(src, dst, own_sem.at[i])
            for i, (src, dst) in enumerate(
                (
                    (share, tb.at[device]),
                    (wk, part_of(w_in, pos.d, w_rows, head, head)),
                    (wv, part_of(w_in, pos.d, w_rows, 2 * head, head)),
                    (names, all_named.at[device]),
                    (share, home),
                )
            )
        ]
        for c in own:
            c.start()
        pos.greet(plane=True)
        g_k = PlaneGather(pos, wk, lambda p: part_of(w_in, p, w_rows, head, head), *rest[0:2])
        g_v = PlaneGather(pos, wv, lambda p: part_of(w_in, p, w_rows, 2 * head, head), *rest[2:4])
        g_tok = Gather(pos, share, tb, *rest[4:6], False)
        g_names = Gather(pos, names, all_named, *rest[6:8], False)
        x_q = Exchange(pos, lambda p: cols_of(wq, p, head), lambda p: part_of(w_in, p, w_rows, 0, head), *rest[8:11])
        x_o = Exchange(pos, lambda p: cols_of(wo, p, head), lambda p: rows_of(w_o, p, w_rows), *rest[11:14])
        red = Reduce(pos, part, *rest[14:20], halves=False)
        red.out = branch

        def span(z):
            return pl.ds(pl.multiple_of(z * plane_rows, plane_rows), plane_rows)

        def angle(z):
            place = lax.broadcasted_iota(jnp.int32, (plane_rows, total), 0) + z * plane_rows
            other = lax.broadcasted_iota(jnp.int32, (plane_rows, total), 1)
            all_docs = drow[...].astype(f32)
            docs_here = jnp.sum(jnp.where(other == place, all_docs, 0.0), axis=1, keepdims=True)
            doc[span(z), :] = jnp.broadcast_to(docs_here, (plane_rows, head))
            before = jnp.where((other < place) & (all_docs == docs_here), 1.0, 0.0)
            turned = jnp.sum(before, axis=1, keepdims=True) * freq[...]
            cosines[span(z), :] = jnp.cos(turned)
            sign = jnp.where(lax.broadcasted_iota(jnp.int32, (plane_rows, head), 1) < head // 2, -1.0, 1.0)
            sines[span(z), :] = jnp.sin(turned) * sign

        def project(z):
            t = tb[pl.ds(z * 8, 8)].reshape(plane_rows, width).astype(f32)
            r = lax.rsqrt(jnp.mean(t * t, axis=1, keepdims=True) + EPS)
            h = (t * r * ng[...]).astype(bf)
            tb[pl.ds(z * 8, 8)] = h.reshape(8, rows, width)
            p = dot(h, w_in[...])
            projected[span(z), :] = p
            for ref, first, gain in ((queries, 0, qg), (keys, head, kg)):
                u = p[:, first : first + head]
                u = u * lax.rsqrt(jnp.mean(u * u, axis=1, keepdims=True) + EPS) * gain[...]
                ref[span(z), :] = turn(u, cosines[span(z), :], sines[span(z), :]).astype(bf)
            values[span(z), :] = p[:, 2 * head :].astype(bf)

        def attention(z):
            place = lax.broadcasted_iota(jnp.int32, (plane_rows, total), 0) + z * plane_rows
            allowed = (lax.broadcasted_iota(jnp.int32, (plane_rows, total), 1) <= place) & (
                doc[span(z), pl.ds(0, 1)] == drow[...].astype(f32)
            )
            s = jnp.where(allowed, dot_nt(queries[span(z), :], keys[...]) * scale, -1e30)
            top = jnp.max(s, axis=1, keepdims=True)
            w = jnp.exp(s - top)
            mass = jnp.sum(w, axis=1, keepdims=True)
            out = dot(w.astype(bf), values[...]) / mass
            heads[span(z), :] = out
            totals[span(z), :] = jnp.broadcast_to(top + jnp.log(mass), (plane_rows, head))

        def spread(z):
            a = heads[span(z), :].astype(bf)
            for i in range(width // 512):
                c = pl.ds(i * 512, 512)
                part[pl.ds(z * 8, 8), :, c] = dot_nt(a, w_o[c, :]).astype(bf).reshape(8, rows, 512)
            red.start_one(z)

        g_tok.start()
        g_k.start()
        g_v.start()
        loop(depth, angle)
        for r in range(1, g_tok.rounds):
            g_tok.round(r)
            g_k.round(r)
            g_v.round(r)
            if r == 2:
                x_q.start()
            if r == 4:
                x_o.start()
        for c in own:
            c.wait()
        g_tok.end()
        g_names.start()
        keep = [pltpu.make_async_copy(tb, all_tok, keep_sem.at[0])]
        keep[0].start()
        g_k.end()
        g_v.end()
        x_q.end()
        keep.append(pltpu.make_async_copy(w_in, wi_out, keep_sem.at[1]))
        keep[1].start()
        keep[0].wait()
        loop(depth, project)
        keep[0] = pltpu.make_async_copy(tb, hidden_out, keep_sem.at[0])
        keep[0].start()
        loop(depth, attention)
        x_o.end()
        keep.append(pltpu.make_async_copy(w_o, wo_out, keep_sem.at[2]))
        keep[2].start()
        for dist in reversed(range(depth)):
            pos.at(dist, spread)
        for r in range(red.rounds):
            red.round(r)
            g_names.round(r)
        mid = home[...].astype(f32) + branch[...]
        middle[...] = mid
        normed[...] = (mid * lax.rsqrt(jnp.mean(mid * mid, axis=1, keepdims=True) + EPS) * mg[...]).astype(bf)
        g_names.end()
        for c in keep:
            c.wait()
        red.end()

    vmem, hbm = pl.BlockSpec(memory_space=pltpu.VMEM), pl.BlockSpec(memory_space=HBM)
    dma = pltpu.SemaphoreType.DMA
    shape = jax.ShapeDtypeStruct
    return pl.pallas_call(
        body,
        out_shape=[
            shape((rows, width), f32),
            shape((rows, width), bf),
            shape((devices,) + named.shape, named.dtype),
            shape((devices, rows, width), bf),
            shape((devices, rows, width), bf),
            shape((width, 3 * head), bf),
            shape((width, head), bf),
            shape((total, 3 * head), f32),
            shape((total, head), bf),
            shape((total, head), bf),
            shape((total, head), bf),
            shape((total, head), f32),
            shape((total, head), f32),
            shape((total, head), f32),
            shape((total, head), f32),
        ],
        in_specs=[hbm] * 6 + [vmem] * 6,
        out_specs=[vmem] * 2 + [hbm] * 5 + [vmem] * 8,
        scratch_shapes=[
            pltpu.VMEM((devices, rows, width), bf),
            pltpu.VMEM((width, 3 * head), bf),
            pltpu.VMEM((width, head), bf),
            pltpu.VMEM((devices, rows, width), bf),
            pltpu.VMEM((rows, width), f32),
            pltpu.VMEM((total, head), f32),
            pltpu.VMEM((rows, width), bf),
            dma((5,)),
            dma((3,)),
        ]
        + PlaneGather.sems(depth) * 2
        + Gather.sems(depth) * 2
        + Exchange.sems(depth) * 2
        + Reduce.scratch(depth, rows, width, False),
        compiler_params=params(number, 60 * 2**20),
        name="attend",
    )(tokens, named, q_weight, k_weight, v_weight, out_weight, norm_gain, q_gain, k_gain, moe_gain, frequency, docs)


def attend_back(depth, number, block, moe_gain_grad, grad_middle, kept, gains, docs):
    f32, bf = jnp.float32, jnp.bfloat16
    all_tok, hidden, w_in, w_o, projected, queries, keys, values, heads, totals, cosines, sines = kept
    norm_gain, q_gain, k_gain = gains
    devices, rows, width = all_tok.shape
    wide = block.shape[1]
    lanes = wide - width
    total, head = queries.shape
    groups = depth * 2
    w_rows = width // groups
    plane_rows = total // depth
    scale = head ** (-0.5)
    gain_rows = width // 128
    small_rows = 2 * gain_rows + 8

    def body(
        blk, moe, gm, tok_h, hid_h, wi_h, wo_h, proj_h, q_h, k_h, v_h, head_h, tot_h, cos_h, sin_h, ng, qg, kg, drow,
        tokens_grad, q_grad, k_grad, v_grad, o_grad, small_sum, all_logit,
        gb, tb, hb, w_in, w_o, proj, qs, ks, vs, hs, ts, cos, sin, part, gh, dq, dk, dv, gproj, wpart, opart,
        q_got, o_got, kv_sum, hidden_sum, small, small_all, by_norm, by_q, by_k, doc, load_sem, own_sem, keep_sem, *rest,
    ):
        pos = Place(depth)
        device = pos.block(pos.z)
        loads = [
            pltpu.make_async_copy(src, dst, load_sem.at[i])
            for i, (src, dst) in enumerate(
                (
                    (wo_h, w_o), (head_h, hs), (tok_h, tb), (hid_h, hb), (wi_h, w_in), (proj_h, proj), (q_h, qs),
                    (k_h, ks), (v_h, vs), (tot_h, ts), (cos_h, cos), (sin_h, sin),
                )
            )
        ]
        own = pltpu.make_async_copy(blk, gb.at[device], own_sem)
        own.start()
        for c in loads:
            c.start()
        pos.greet(plane=True)
        g_branch = Gather(pos, blk, gb, *rest[0:2], True)
        g_small = Gather(pos, small, small_all, *rest[2:4], False)
        x_q = Exchange(
            pos, lambda p: part_of(wpart, p, w_rows, 0, head), lambda p: cols_of(q_got, p, head), *rest[4:7]
        )
        x_o = Exchange(pos, lambda p: rows_of(opart, p, w_rows), lambda p: cols_of(o_got, p, head), *rest[7:10])
        red = Reduce(pos, part, *rest[10:16], halves=False)
        red.out = hidden_sum
        r_kv = PlaneReduce(pos, lambda p: part_of(wpart, p, w_rows, head, 2 * head), kv_sum, *rest[16:20])

        def span(z):
            return pl.ds(pl.multiple_of(z * plane_rows, plane_rows), plane_rows)

        def column(z):
            place = lax.broadcasted_iota(jnp.int32, (plane_rows, total), 0) + z * plane_rows
            other = lax.broadcasted_iota(jnp.int32, (plane_rows, total), 1)
            docs_here = jnp.sum(jnp.where(other == place, drow[...].astype(f32), 0.0), axis=1, keepdims=True)
            doc[span(z), :] = jnp.broadcast_to(docs_here, (plane_rows, head))

        def heads_back(z):
            g = gb[pl.ds(z * 8, 8), :, pl.ds(0, width)].reshape(plane_rows, width)
            gh[span(z), :] = dot(g, w_o[...]).astype(bf)

        def out_weight_back(i):
            c = pl.ds(pl.multiple_of(i * w_rows, w_rows), w_rows)
            g = gb[:, :, c].reshape(total, w_rows)
            opart[c, :] = dot_tn(g, hs[...].astype(bf)).astype(bf)

        def attention_back(z):
            place = lax.broadcasted_iota(jnp.int32, (plane_rows, total), 0) + z * plane_rows
            allowed = (lax.broadcasted_iota(jnp.int32, (plane_rows, total), 1) <= place) & (
                doc[span(z), pl.ds(0, 1)] == drow[...].astype(f32)
            )
            q = qs[span(z), :]
            g = gh[span(z), :]
            delta = jnp.sum(g.astype(f32) * hs[span(z), :], axis=1, keepdims=True)
            s = dot_nt(q, ks[...]) * scale
            p = jnp.where(allowed, jnp.exp(jnp.minimum(s - ts[span(z), pl.ds(0, 1)], 0.0)), 0.0)
            ds = (p * (dot_nt(g, vs[...]) - delta)).astype(bf)
            dq[span(z), :] = dot(ds, ks[...]) * scale
            dk[...] += dot_tn(ds, q) * scale
            dv[...] += dot_tn(p.astype(bf), g)

        def project_back(z):
            for first, grad, gain, total_ref in ((0, dq, qg, by_q), (head, dk, kg, by_k)):
                g = turn(grad[span(z), :], cos[span(z), :], -sin[span(z), :])
                change, by_gain = norm_back(proj[span(z), pl.ds(first, head)], gain[...], g)
                gproj[span(z), pl.ds(first, head)] = change.astype(bf)
                total_ref[...] += jnp.sum(by_gain, axis=0, keepdims=True)
            gproj[span(z), pl.ds(2 * head, head)] = dv[span(z), :].astype(bf)

        def spread(z):
            g = gproj[span(z), :]
            t = tb[pl.ds(z * 8, 8)].reshape(plane_rows, width).astype(f32)
            r = lax.rsqrt(jnp.mean(t * t, axis=1, keepdims=True) + EPS)
            for i in range(width // 512):
                c = pl.ds(i * 512, 512)
                back = dot_nt(g, w_in[c, :])
                part[pl.ds(z * 8, 8), :, c] = back.astype(bf).reshape(8, rows, 512)
                unit = tb[pl.ds(z * 8, 8), :, c].reshape(plane_rows, 512).astype(f32) * r
                by_norm[:, c] += jnp.sum(back * unit, axis=0, keepdims=True)
            red.start_one(z)

        def in_weight_back(i):
            c = pl.ds(pl.multiple_of(i * w_rows, w_rows), w_rows)
            h = hb[:, :, c].reshape(total, w_rows)
            wpart[c, :] = dot_tn(h, gproj[...]).astype(bf)

        g_branch.start()
        loop(depth, column)
        dk[...] = jnp.zeros(dk.shape, f32)
        dv[...] = jnp.zeros(dv.shape, f32)
        by_norm[...] = jnp.zeros(by_norm.shape, f32)
        by_q[...] = jnp.zeros(by_q.shape, f32)
        by_k[...] = jnp.zeros(by_k.shape, f32)
        small[...] = jnp.zeros(small.shape, f32)
        for r in range(1, g_branch.rounds):
            g_branch.round(r)
        own.wait()
        g_branch.end()
        keep = pltpu.make_async_copy(gb.at[:, :, pl.ds(width, lanes)], all_logit, keep_sem)
        keep.start()
        for c in loads:
            c.wait()
        loop(depth, heads_back)
        loop(groups, out_weight_back)
        x_o.start()
        loop(depth, attention_back)
        loop(depth, project_back)
        for dist in reversed(range(depth)):
            pos.at(dist, spread)
        loop(groups, in_weight_back)
        r_kv.start()
        x_q.start()
        for i in range(gain_rows):
            small[pl.ds(i, 1), :] = by_norm[:, pl.ds(i * 128, 128)]
            small[pl.ds(gain_rows + i, 1), :] = moe[:, pl.ds(i * 128, 128)]
        small[pl.ds(2 * gain_rows, 1), :] = by_q[...]
        small[pl.ds(2 * gain_rows + 1, 1), :] = by_k[...]
        small_all[device] = small[...]
        g_small.start()
        for r in range(red.rounds):
            red.round(r)
            r_kv.round(r)
            g_small.round(r)
        change, _ = norm_back(tb[device].astype(f32), ng[...], hidden_sum[...])
        tokens_grad[...] = gm[...] + change
        k_grad[...] = kv_sum[:, pl.ds(0, head)]
        v_grad[...] = kv_sum[:, pl.ds(head, head)]
        g_small.end()
        small_sum[...] = jnp.sum(small_all[...], axis=0)
        x_o.end()
        o_grad[...] = o_got[...].astype(f32)
        x_q.end()
        q_grad[...] = q_got[...].astype(f32)
        keep.wait()
        red.end()
        r_kv.end()

    vmem, hbm = pl.BlockSpec(memory_space=pltpu.VMEM), pl.BlockSpec(memory_space=HBM)
    dma = pltpu.SemaphoreType.DMA
    shape = jax.ShapeDtypeStruct
    V = pltpu.VMEM
    return pl.pallas_call(
        body,
        out_shape=[
            shape((rows, width), f32),
            shape((w_rows, groups * head), f32),
            shape((w_rows, head), f32),
            shape((w_rows, head), f32),
            shape((w_rows, groups * head), f32),
            shape((small_rows, 128), f32),
            shape((devices, rows, lanes), bf),
        ],
        in_specs=[hbm, vmem, vmem] + [hbm] * 12 + [vmem] * 4,
        out_specs=[vmem] * 6 + [hbm],
        scratch_shapes=[
            V((devices, rows, wide), bf),
            V((devices, rows, width), bf),
            V((devices, rows, width), bf),
            V((width, 3 * head), bf),
            V((width, head), bf),
            V((total, 3 * head), f32),
            V((total, head), bf),
            V((total, head), bf),
            V((total, head), bf),
            V((total, head), f32),
            V((total, head), f32),
            V((total, head), f32),
            V((total, head), f32),
            V((devices, rows, width), bf),
            V((total, head), bf),
            V((total, head), f32),
            V((total, head), f32),
            V((total, head), f32),
            V((total, 3 * head), bf),
            V((width, 3 * head), bf),
            V((width, head), bf),
            V((w_rows, groups * head), bf),
            V((w_rows, groups * head), bf),
            V((w_rows, 2 * head), f32),
            V((rows, width), f32),
            V((small_rows, 128), f32),
            V((devices, small_rows, 128), f32),
            V((1, width), f32),
            V((1, head), f32),
            V((1, head), f32),
            V((total, head), f32),
            dma((12,)),
            dma,
            dma,
        ]
        + Gather.sems(depth) * 2
        + Exchange.sems(depth) * 2
        + Reduce.scratch(depth, rows, width, False)
        + PlaneReduce.scratch(depth, w_rows, 2 * head),
        compiler_params=params(number, 60 * 2**20),
        name="attend_back",
    )(block, moe_gain_grad, grad_middle, *kept, norm_gain, q_gain, k_gain, docs)


def head_shards(
    tokens,
    segments,
    routes,
    out_grad,
    norm_gain,
    q_weight,
    k_weight,
    v_weight,
    q_gain,
    k_gain,
    out_weight,
    moe_gain,
    router_weight,
    gate_weight,
    up_weight,
    down_weight,
):
    f32, bf = jnp.float32, jnp.bfloat16
    f32, bf = jnp.float32, jnp.bfloat16
    head_dim = q_gain.shape[0]
    tok_rows, width = tokens.shape
    all_tokens = segments.shape[0]
    expert_count = router_weight.shape[1]
    depth = all_tokens // tok_rows // 2
    lanes = 128
    norm_gain, q_gain, k_gain, moe_gain = (g.astype(f32)[None] for g in (norm_gain, q_gain, k_gain, moe_gain))
    docs = segments[None]
    frequency = THETA ** (-(jnp.arange(head_dim // 2).astype(f32) * 2.0) / head_dim)
    named = jnp.any(routes[:, :, None] == jnp.arange(lanes, dtype=jnp.int32), axis=1).astype(bf)
    middle, normed, all_named, *kept = attend(
        depth,
        0,
        tokens,
        named,
        q_weight,
        k_weight,
        v_weight,
        out_weight,
        (norm_gain, q_gain, k_gain, moe_gain),
        jnp.concatenate([frequency, frequency])[None],
        docs,
    )
    layer_out, grad_middle, grad_block, moe_gain_grad, all_normed, *pairs = experts(
        depth,
        1,
        normed,
        out_grad,
        all_named,
        middle,
        moe_gain,
        router_weight,
        gate_weight[0],
        up_weight[0],
        down_weight[0],
    )
    tokens_grad, grad_q, grad_k, grad_v, grad_o, small, all_logit = attend_back(
        depth, 2, grad_block, moe_gain_grad, grad_middle, kept, (norm_gain, q_gain, k_gain), docs
    )
    grad_gate_w, grad_up_w, grad_down, grad_router = local_weight_grads(
        *pairs, all_normed.reshape(all_tokens, width), all_logit.reshape(all_tokens, lanes)
    )
    gain_rows = width // 128
    return (
        layer_out,
        tokens_grad,
        small[:gain_rows].reshape(-1),
        grad_q,
        grad_k,
        grad_v,
        small[2 * gain_rows],
        small[2 * gain_rows + 1],
        grad_o,
        small[gain_rows : 2 * gain_rows].reshape(-1),
        grad_router[:, :expert_count],
        grad_gate_w[None],
        grad_up_w[None],
        grad_down[None],
    )


def solution(mesh):
    per_device = shards if mesh.shape["dp"] != 8 or mesh.shape["tensor"] != 4 else head_shards
    placed = (
        P("dp", None),
        P(),
        P(("dp", "tensor"), None),
        P(("dp", "tensor"), None),
        P(),
        P("dp", "tensor"),
        P("dp", "tensor"),
        P("dp", "tensor"),
        P(),
        P(),
        P("dp", "tensor"),
        P(),
        P(),
        P(("dp", "tensor"), None, None),
        P(("dp", "tensor"), None, None),
        P(("dp", "tensor"), None, None),
    )
    return jax.shard_map(
        per_device,
        mesh=mesh,
        in_specs=placed,
        out_specs=(
            P(("dp", "tensor"), None),
            P(("dp", "tensor"), None),
            P(),
            P("dp", "tensor"),
            P("dp", "tensor"),
            P("dp", "tensor"),
            P(),
            P(),
            P("dp", "tensor"),
            P(),
            P(),
            P(("dp", "tensor"), None, None),
            P(("dp", "tensor"), None, None),
            P(("dp", "tensor"), None, None),
        ),
        check_vma=False,
    )
```

```python
import functools

import jax
import jax.numpy as jnp
import numpy as np
from jax import lax
from jax.experimental import pallas as pl
from jax.experimental.pallas import tpu as pltpu
from jax.sharding import PartitionSpec as P

EPS = 1e-06
THETA = 1000000.0


def norm_rows(values, gain):
    return values * lax.rsqrt(jnp.mean(values * values, axis=-1, keepdims=True) + EPS) * gain


def rotary(values, cosine, sine_part):
    half_dim = values.shape[-1] // 2
    front_half = values[..., :half_dim]
    back_half = values[..., half_dim:]
    return jnp.concatenate(
        [front_half * cosine - back_half * sine_part, back_half * cosine + front_half * sine_part],
        axis=-1,
    )


def angles(positions, head_dim):
    half_dim = head_dim // 2
    frequency = THETA ** (-(jnp.arange(half_dim).astype(jnp.float32) * 2.0) / head_dim)
    rotation = positions.astype(jnp.float32)[:, None] * frequency[None, :]
    return (jnp.cos(rotation), jnp.sin(rotation))


def prepare(projected, q_gain, k_gain, cosine, sine_part, head_dim):
    tok_rows = projected.shape[0]
    query_width = projected.shape[1] - 2 * head_dim
    queries = projected[:, :query_width].reshape(tok_rows, query_width // head_dim, head_dim)
    keys_local = projected[:, query_width : query_width + head_dim]
    values_local = projected[:, query_width + head_dim :]
    queries = rotary(norm_rows(queries, q_gain), cosine[:, None, :], sine_part[:, None, :])
    keys_local = rotary(norm_rows(keys_local, k_gain), cosine, sine_part)
    return (queries, keys_local, values_local)


def swiglu(gate_in, up_in):
    return jax.nn.silu(gate_in) * up_in


def shards(
    tokens,
    segments,
    routes,
    out_grad,
    norm_gain,
    q_weight,
    k_weight,
    v_weight,
    q_gain,
    k_gain,
    out_weight,
    moe_gain,
    router_weight,
    gate_weight,
    up_weight,
    down_weight,
):
    head_dim = q_gain.shape[0]
    tok_rows = tokens.shape[0]
    model_width = tokens.shape[1]
    share_rows = out_grad.shape[0]
    all_tokens = segments.shape[0]
    expert_count = router_weight.shape[1]
    top_count = routes.shape[1]
    capacity = max(2, share_rows * top_count * 2 // expert_count)
    score_scale = head_dim ** (-0.5)
    first_row = lax.axis_index("dp") * tok_rows
    places = jnp.arange(all_tokens, dtype=jnp.int32)
    begins = jnp.concatenate([jnp.ones((1,), dtype=bool), segments[1:] != segments[:-1]])
    positions = places - lax.cummax(jnp.where(begins, places, 0), axis=0)
    local_positions = lax.dynamic_slice_in_dim(positions, first_row, tok_rows)
    local_docs = lax.dynamic_slice_in_dim(segments, first_row, tok_rows)
    query_places = first_row + jnp.arange(tok_rows, dtype=jnp.int32)
    cosine, sine_part = angles(local_positions, head_dim)
    weight_rows = (
        lax.all_gather(q_weight, "dp", axis=0, tiled=True),
        lax.all_gather(k_weight, "dp", axis=0, tiled=True),
        lax.all_gather(v_weight, "dp", axis=0, tiled=True),
        lax.all_gather(out_weight, "dp", axis=0, tiled=True),
    )
    input_weight = jnp.concatenate([weight_rows[0], weight_rows[1], weight_rows[2]], axis=1)
    output_weight = weight_rows[3]
    tokens_float = tokens.astype(jnp.float32)
    norm_gain_float = norm_gain.astype(jnp.float32)
    hidden = norm_rows(tokens_float, norm_gain_float).astype(jnp.bfloat16)
    projected = jnp.dot(hidden, input_weight, preferred_element_type=jnp.float32)

    def prepare_local(projected_in, qgain_in, kgain_in):
        return prepare(projected_in, qgain_in, kgain_in, cosine, sine_part, head_dim)

    prepared, prepare_back = jax.vjp(
        prepare_local, projected, q_gain.astype(jnp.float32), k_gain.astype(jnp.float32)
    )
    queries = prepared[0].astype(jnp.bfloat16)
    keys_local = prepared[1].astype(jnp.bfloat16)
    values_local = prepared[2].astype(jnp.bfloat16)
    local_heads = queries.shape[1]

    def visible(offset, length):
        key_places = offset + jnp.arange(length, dtype=jnp.int32)
        key_docs = lax.dynamic_slice_in_dim(segments, offset, length)
        return (key_places[None, :] <= query_places[:, None]) & (
            key_docs[None, :] == local_docs[:, None]
        )

    running_max = jnp.full((tok_rows, local_heads), -1e30, jnp.float32)
    key_piece = lax.all_gather(keys_local, "dp", axis=0, tiled=True)
    value_piece = lax.all_gather(values_local, "dp", axis=0, tiled=True)
    allowed = visible(jnp.int32(0), key_piece.shape[0])[:, None, :]
    scores = (
        jnp.einsum("thd,nd->thn", queries, key_piece, preferred_element_type=jnp.float32)
        * score_scale
    )
    scores = jnp.where(allowed, scores, -1e30)
    new_max = jnp.maximum(running_max, jnp.max(scores, axis=-1))
    soft_weights = jnp.where(allowed, jnp.exp(scores - new_max[:, :, None]), 0.0)
    softmax_mass = jnp.sum(soft_weights, axis=-1)
    weighted_sum = jnp.einsum(
        "thn,nd->thd",
        soft_weights.astype(jnp.bfloat16),
        value_piece,
        preferred_element_type=jnp.float32,
    )
    running_max, softmax_mass, weighted_sum = (new_max, softmax_mass, weighted_sum)
    head_out = weighted_sum / softmax_mass[:, :, None]
    log_total = running_max + jnp.log(softmax_mass)
    attended = head_out.astype(jnp.bfloat16).reshape(tok_rows, local_heads * head_dim)
    branch = lax.psum_scatter(
        jnp.einsum("tc,dc->td", attended, output_weight, preferred_element_type=jnp.float32).astype(
            jnp.bfloat16
        ),
        "tensor",
        scatter_dimension=0,
        tiled=True,
    ).astype(jnp.float32)
    tensor_lane = lax.axis_index("tensor")
    tokens_share = lax.dynamic_slice_in_dim(tokens_float, tensor_lane * share_rows, share_rows, 0)
    middle = tokens_share + branch
    normed_float, moe_norm_back = jax.vjp(norm_rows, middle, moe_gain.astype(jnp.float32))
    normed = normed_float.astype(jnp.bfloat16)
    logits = jnp.dot(normed, router_weight, preferred_element_type=jnp.float32)

    def gating(logit_rows):
        probabilities = jax.nn.softmax(logit_rows, axis=-1)
        chosen = jnp.take_along_axis(probabilities, routes, axis=1)
        return chosen / jnp.sum(chosen, axis=1, keepdims=True)

    gate_values, gating_back = jax.vjp(gating, logits)
    pair_routes = routes.reshape(-1)
    pair_count = pair_routes.shape[0]
    route_table = (
        pair_routes[:, None] == jnp.arange(expert_count, dtype=jnp.int32)[None, :]
    ).astype(jnp.int32)
    route_rank = jnp.sum(jnp.cumsum(route_table, axis=0) * route_table, axis=1) - 1
    slot_index = pair_routes * capacity + route_rank
    slot_owner = (
        jnp.full((expert_count * capacity,), pair_count, jnp.int32)
        .at[slot_index]
        .set(jnp.arange(pair_count, dtype=jnp.int32))
    )
    normed_padded = jnp.concatenate([normed, jnp.zeros((1, model_width), jnp.bfloat16)], axis=0)
    send_rows = normed_padded[slot_owner // top_count].reshape(expert_count, capacity, model_width)
    arrived = lax.all_to_all(send_rows, ("dp", "tensor"), split_axis=0, concat_axis=0, tiled=True)
    expert_inputs = arrived.reshape(-1, model_width)
    w_gate = gate_weight[0]
    w_up = up_weight[0]
    w_down = down_weight[0]
    gate_act = jnp.dot(expert_inputs, w_gate, preferred_element_type=jnp.float32)
    up_act = jnp.dot(expert_inputs, w_up, preferred_element_type=jnp.float32)
    inner_float, swiglu_back = jax.vjp(swiglu, gate_act, up_act)
    inner_act = inner_float.astype(jnp.bfloat16)
    produced = jnp.dot(inner_act, w_down, preferred_element_type=jnp.float32).astype(jnp.bfloat16)
    returned = lax.all_to_all(
        produced.reshape(expert_count, capacity, model_width),
        ("dp", "tensor"),
        split_axis=0,
        concat_axis=0,
        tiled=True,
    )
    picked = (
        returned.reshape(-1, model_width)[slot_index]
        .reshape(share_rows, top_count, model_width)
        .astype(jnp.float32)
    )
    layer_out = (middle + jnp.sum(gate_values[:, :, None] * picked, axis=1)).astype(jnp.bfloat16)
    grad_out = out_grad.astype(jnp.float32)
    grad_picked = (
        (gate_values[:, :, None] * grad_out[:, None, :])
        .astype(jnp.bfloat16)
        .reshape(pair_count, model_width)
    )
    grad_gates = jnp.sum(grad_out[:, None, :] * picked, axis=2)
    grad_padded = jnp.concatenate([grad_picked, jnp.zeros((1, model_width), jnp.bfloat16)], axis=0)
    grad_send = grad_padded[slot_owner].reshape(expert_count, capacity, model_width)
    grad_arrived = lax.all_to_all(
        grad_send, ("dp", "tensor"), split_axis=0, concat_axis=0, tiled=True
    ).reshape(-1, model_width)
    grad_inner = jnp.einsum("rd,fd->rf", grad_arrived, w_down, preferred_element_type=jnp.float32)
    grad_down = jnp.einsum("rf,rd->fd", inner_act, grad_arrived, preferred_element_type=jnp.float32)
    grad_gate_float, grad_up_float = swiglu_back(grad_inner)
    grad_gate_act = grad_gate_float.astype(jnp.bfloat16)
    grad_up_act = grad_up_float.astype(jnp.bfloat16)
    grad_gate_w = jnp.einsum(
        "rd,rf->df", expert_inputs, grad_gate_act, preferred_element_type=jnp.float32
    )
    grad_up_w = jnp.einsum(
        "rd,rf->df", expert_inputs, grad_up_act, preferred_element_type=jnp.float32
    )
    grad_inputs = jnp.einsum("rf,df->rd", grad_gate_act, w_gate, preferred_element_type=jnp.float32)
    grad_inputs = (
        grad_inputs + jnp.einsum("rf,df->rd", grad_up_act, w_up, preferred_element_type=jnp.float32)
    ).astype(jnp.bfloat16)
    grad_home = lax.all_to_all(
        grad_inputs.reshape(expert_count, capacity, model_width),
        ("dp", "tensor"),
        split_axis=0,
        concat_axis=0,
        tiled=True,
    )
    grad_normed = jnp.sum(
        grad_home.reshape(-1, model_width)[slot_index]
        .reshape(share_rows, top_count, model_width)
        .astype(jnp.float32),
        axis=1,
    )
    (grad_logit_float,) = gating_back(grad_gates)
    grad_logits = grad_logit_float.astype(jnp.bfloat16)
    grad_router = jnp.einsum("td,te->de", normed, grad_logits, preferred_element_type=jnp.float32)
    grad_normed = grad_normed + jnp.einsum(
        "te,de->td", grad_logits, router_weight, preferred_element_type=jnp.float32
    )
    grad_middle_part, grad_moe_gain = moe_norm_back(grad_normed)
    grad_middle = grad_out + grad_middle_part
    grad_branch = lax.all_gather(grad_middle.astype(jnp.bfloat16), "tensor", axis=0, tiled=True)
    again_rows = (
        lax.all_gather(q_weight, "dp", axis=0, tiled=True),
        lax.all_gather(k_weight, "dp", axis=0, tiled=True),
        lax.all_gather(v_weight, "dp", axis=0, tiled=True),
        lax.all_gather(out_weight, "dp", axis=0, tiled=True),
    )
    input_back = jnp.concatenate([again_rows[0], again_rows[1], again_rows[2]], axis=1)
    output_back = again_rows[3]
    grad_heads = (
        jnp.dot(grad_branch, output_back, preferred_element_type=jnp.float32)
        .astype(jnp.bfloat16)
        .reshape(tok_rows, local_heads, head_dim)
    )
    row_delta = jnp.sum(grad_heads.astype(jnp.float32) * head_out, axis=-1)
    key_rows, value_rows = (
        lax.all_gather(keys_local, "dp", axis=0, tiled=True),
        lax.all_gather(values_local, "dp", axis=0, tiled=True),
    )
    key_block = min(512, all_tokens)

    def key_step(grad_queries, block_number):
        offset = block_number * key_block
        key_piece = lax.dynamic_slice_in_dim(key_rows, offset, key_block, 0)
        value_piece = lax.dynamic_slice_in_dim(value_rows, offset, key_block, 0)
        allowed = visible(offset, key_block)[:, None, :]
        scores = (
            jnp.einsum("thd,nd->thn", queries, key_piece, preferred_element_type=jnp.float32)
            * score_scale
        )
        soft_weights = jnp.where(allowed, jnp.exp(scores - log_total[:, :, None]), 0.0)
        grad_weights = jnp.einsum(
            "thd,nd->thn", grad_heads, value_piece, preferred_element_type=jnp.float32
        )
        grad_scores = (soft_weights * (grad_weights - row_delta[:, :, None])).astype(jnp.bfloat16)
        grad_queries = (
            grad_queries
            + jnp.einsum("thn,nd->thd", grad_scores, key_piece, preferred_element_type=jnp.float32)
            * score_scale
        )
        grad_key_piece = (
            jnp.einsum("thn,thd->nd", grad_scores, queries, preferred_element_type=jnp.float32)
            * score_scale
        )
        grad_value_piece = jnp.einsum(
            "thn,thd->nd",
            soft_weights.astype(jnp.bfloat16),
            grad_heads,
            preferred_element_type=jnp.float32,
        )
        return (grad_queries, jnp.concatenate([grad_key_piece, grad_value_piece], axis=1))

    grad_queries, key_terms = lax.scan(
        key_step,
        jnp.zeros((tok_rows, local_heads, head_dim), jnp.float32),
        jnp.arange(all_tokens // key_block, dtype=jnp.int32),
    )
    key_grads = lax.psum_scatter(
        key_terms.reshape(all_tokens, 2 * head_dim).astype(jnp.bfloat16),
        "dp",
        scatter_dimension=0,
        tiled=True,
    ).astype(jnp.float32)
    grad_proj_float, grad_q_gain, grad_k_gain = prepare_back(
        (grad_queries, key_grads[:, :head_dim], key_grads[:, head_dim:])
    )
    grad_projected = grad_proj_float.astype(jnp.bfloat16)
    grad_hidden = jnp.einsum(
        "tc,dc->td", grad_projected, input_back, preferred_element_type=jnp.float32
    )
    grad_hidden_share = lax.psum_scatter(
        grad_hidden.astype(jnp.bfloat16), "tensor", scatter_dimension=0, tiled=True
    ).astype(jnp.float32)
    _, first_norm_back = jax.vjp(norm_rows, tokens_share, norm_gain_float)
    grad_tokens_part, grad_norm_gain = first_norm_back(grad_hidden_share)
    tokens_grad = grad_middle + grad_tokens_part
    input_part = jnp.einsum("td,tc->dc", hidden, grad_projected, preferred_element_type=jnp.float32)
    output_part = jnp.einsum("td,tc->dc", grad_branch, attended, preferred_element_type=jnp.float32)
    weight_share = lax.psum_scatter(
        jnp.concatenate([input_part, output_part], axis=1).astype(jnp.bfloat16),
        "dp",
        scatter_dimension=0,
        tiled=True,
    ).astype(jnp.float32)
    query_width = local_heads * head_dim
    grad_q_weight = weight_share[:, :query_width]
    grad_k_weight = weight_share[:, query_width : query_width + head_dim]
    grad_v_weight = weight_share[:, query_width + head_dim : query_width + 2 * head_dim]
    grad_out_weight = weight_share[:, query_width + 2 * head_dim :]
    small_sums = lax.psum(
        (grad_router, grad_norm_gain, grad_moe_gain, grad_q_gain, grad_k_gain), ("dp", "tensor")
    )
    return (
        layer_out,
        tokens_grad,
        small_sums[1],
        grad_q_weight,
        grad_k_weight,
        grad_v_weight,
        small_sums[3],
        small_sums[4],
        grad_out_weight,
        small_sums[2],
        small_sums[0],
        grad_gate_w[None],
        grad_up_w[None],
        grad_down[None],
    )


MESH = pl.DeviceIdType.MESH
HBM = pl.ANY


class Place:
    def __init__(self, depth):
        d = lax.axis_index("dp")
        t = lax.axis_index("tensor")
        self.depth = depth
        self.d, self.t = d, t
        self.z, self.x = d // 2, lax.rem(d, 2)
        self.y, self.c = t // 2, lax.rem(t, 2)
        self.next_to = {
            "x": (self.z * 2 + 1 - self.x, t),
            "y": (d, (1 - self.y) * 2 + self.c),
            "c": (d, self.y * 2 + 1 - self.c),
            "up": (d + 2, t),
            "down": (d - 2, t),
        }

    def block(self, z, fx=0, fy=0, fc=0):
        x = 1 - self.x if fx else self.x
        y = 1 - self.y if fy else self.y
        c = 1 - self.c if fc else self.c
        return (z * 2 + x) * 4 + y * 2 + c

    def at(self, dist, step):
        if dist == 0:
            step(self.z)
            return

        @pl.when(self.z >= dist)
        def _():
            step(self.z - dist)

        @pl.when(self.z + dist < self.depth)
        def _():
            step(self.z + dist)

    def greet(self, plane=False):
        barrier = pltpu.get_barrier_semaphore()

        def signal(to):
            pl.semaphore_signal(barrier, inc=1, device_id=self.next_to[to], device_id_type=MESH)

        if plane:
            groups = self.depth * 2
            for k in range(1, groups):
                to = (lax.rem(self.d + k, groups), self.t)
                pl.semaphore_signal(barrier, inc=1, device_id=to, device_id_type=MESH)
            signal("y")
            signal("c")
            pl.semaphore_wait(barrier, groups + 1)
            return
        for to in ("x", "y", "c"):
            signal(to)

        @pl.when(self.z > 0)
        def _():
            signal("down")

        @pl.when(self.z < self.depth - 1)
        def _():
            signal("up")

        above = (self.z < self.depth - 1).astype(jnp.int32)
        below = (self.z > 0).astype(jnp.int32)
        pl.semaphore_wait(barrier, 3 + above + below)

    def copy(self, src, dst, send, recv, to):
        return pltpu.make_async_remote_copy(
            src_ref=src,
            dst_ref=dst,
            send_sem=send,
            recv_sem=recv,
            device_id=self.next_to[to],
            device_id_type=MESH,
        )


class Gather:
    SEND, RECV = 11, 10

    def __init__(self, pos, own, out, send, recv, halves, cols=None):
        self.pos, self.own, self.out = pos, own, out
        self.send, self.recv = send, recv
        if cols is not None:
            self.own, self.out = own.at[:, cols], out.at[:, :, cols]
        rows = out.shape[1]
        self.h0 = pl.ds(0, rows // 2 if halves else rows)
        self.h1 = pl.ds(rows // 2, rows // 2) if halves else None
        self.rounds = pos.depth + 2
        self.seen = set()

    def link(self, src, dst, sends, recvs, zo, to):
        return self.pos.copy(src, dst, self.send.at[sends, zo], self.recv.at[recvs, zo], to)

    def col(self, zo):
        return self.out.at[self.pos.block(zo)]

    def src(self, zo, mine):
        return self.own if mine else self.col(zo)

    def up(self, zo, mine=False):
        return self.link(self.src(zo, mine), self.col(zo), 0, 0, zo, "up")

    def down(self, zo, mine=False):
        return self.link(self.src(zo, mine), self.col(zo), 1, 0, zo, "down")

    def to_x(self, zo, mine=False):
        return self.link(self.src(zo, mine), self.col(zo), 2, 1, zo, "x")

    def to_y(self, zo, mine=False):
        return self.link(self.src(zo, mine), self.col(zo), 3, 2, zo, "y")

    def to_c(self, zo, mine=False):
        return self.link(self.src(zo, mine), self.col(zo), 4, 5, zo, "c")

    def part(self, zo, fx, fy, rows):
        whole = self.out.at[self.pos.block(zo, fx, fy)]
        return whole if rows is None else whole.at[rows]

    def pass_on(self, zo, fx, fy, rows, sends, recvs, to):
        ref = self.part(zo, fx, fy, rows)
        return self.link(ref, ref, sends, recvs, zo, to)

    def x_to_y(self, zo):
        return self.pass_on(zo, 1, 0, self.h0, 5, 3, "y")

    def x_to_c(self, zo):
        return self.pass_on(zo, 1, 0, None, 6, 6, "c")

    def y_to_x(self, zo):
        return self.pass_on(zo, 0, 1, self.h1, 7, 4, "x")

    def y_to_c(self, zo):
        return self.pass_on(zo, 0, 1, None, 8, 7, "c")

    def far0_to_c(self, zo):
        return self.pass_on(zo, 1, 1, self.h0, 9, 8, "c")

    def far1_to_c(self, zo):
        return self.pass_on(zo, 1, 1, self.h1, 10, 9, "c")

    def along_z(self, zo, mine, what):
        z, depth = self.pos.z, self.pos.depth
        if mine:
            up, down = z < depth - 1, z > 0
        else:
            up, down = (zo < z) & (z < depth - 1), (zo > z) & (z > 0)

        @pl.when(up)
        def _():
            what(self.up(zo, mine))

        @pl.when(down)
        def _():
            what(self.down(zo, mine))

    def on_column(self, zo, mine=False):
        if not mine:
            self.up(zo).wait_recv()
        self.along_z(zo, mine, lambda c: c.start())
        self.to_x(zo, mine).start()
        self.to_y(zo, mine).start()
        self.to_c(zo, mine).start()

    def on_sides(self, zo):
        self.to_x(zo).wait_recv()
        self.x_to_y(zo).start()
        self.x_to_c(zo).start()
        self.to_y(zo).wait_recv()
        if self.h1 is not None:
            self.y_to_x(zo).start()
        self.y_to_c(zo).start()

    def on_far(self, zo):
        self.x_to_y(zo).wait_recv()
        self.far0_to_c(zo).start()
        if self.h1 is not None:
            self.y_to_x(zo).wait_recv()
            self.far1_to_c(zo).start()

    def start(self):
        self.on_column(self.pos.z, True)

    def round(self, r):
        if 1 <= r < self.pos.depth:
            self.pos.at(r, self.on_column)
        if 1 <= r <= self.pos.depth:
            self.pos.at(r - 1, self.on_sides)
        if 2 <= r <= self.pos.depth + 1:
            self.pos.at(r - 2, self.on_far)

    def from_core(self, zo, mine=False):
        copies = [self.to_c(zo, mine), self.x_to_c(zo), self.y_to_c(zo), self.far0_to_c(zo)]
        return copies if self.h1 is None else copies + [self.far1_to_c(zo)]

    def arrived(self, dist):
        self.seen.add(dist)
        self.pos.at(dist, lambda zo: [c.wait_recv() for c in self.from_core(zo)])

    def end_one(self, zo, mine=False, seen=False):
        arrivals = self.from_core(zo, mine)
        sends = [self.to_x(zo, mine), self.to_y(zo, mine), self.x_to_y(zo)] + arrivals
        if self.h1 is not None:
            sends.append(self.y_to_x(zo))
        if not seen:
            for c in arrivals:
                c.wait_recv()
        self.along_z(zo, mine, lambda c: c.wait_send())
        for c in sends:
            c.wait_send()

    def end(self):
        self.end_one(self.pos.z, True, 0 in self.seen)
        for r in range(1, self.pos.depth):
            self.pos.at(r, lambda zo: self.end_one(zo, False, r in self.seen))

    @staticmethod
    def sems(depth):
        return [pltpu.SemaphoreType.DMA((Gather.SEND, depth)), pltpu.SemaphoreType.DMA((Gather.RECV, depth))]


class SideGather:
    def __init__(self, pos, own, out, send, recv, side_send, side_recv, cols):
        self.pos, self.own, self.out = pos, own.at[:, cols], out.at[:, :, cols]
        self.send, self.recv = send, recv
        self.side_send, self.side_recv = side_send, side_recv
        rows = out.shape[1]
        self.half = (pl.ds(0, rows // 2), pl.ds(rows // 2, rows // 2))
        self.rounds = pos.depth + 2

    @staticmethod
    def sems(depth):
        dma = pltpu.SemaphoreType.DMA
        return [dma((4, depth, 3)), dma((4, depth, 2)), dma((4,)), dma((4,))]

    def place(self, zo, k):
        return self.out.at[self.pos.block(zo, k // 2, k % 2)]

    def src(self, zo, k, mine):
        return self.own if mine and k == 0 else self.place(zo, k)

    def along(self, zo, k, way, mine=False):
        return self.pos.copy(
            self.src(zo, k, mine), self.place(zo, k), self.send.at[k, zo, way], self.recv.at[k, zo, 0], ("up", "down")[way]
        )

    def to_core(self, zo, k, mine=False):
        return self.pos.copy(self.src(zo, k, mine), self.place(zo, k), self.send.at[k, zo, 2], self.recv.at[k, zo, 1], "c")

    def across(self, k, to):
        z = self.pos.z
        if k < 2:
            src, dst = self.own, self.place(z, 0)
        else:
            src = dst = self.place(z, k - 1).at[self.half[k - 2]]
        return self.pos.copy(src, dst, self.side_send.at[k], self.side_recv.at[k], to)

    def on(self, zo, k, mine=False):
        self.along_z(zo, k, mine, lambda c: c.start())
        self.to_core(zo, k, mine).start()

    def along_z(self, zo, k, mine, what):
        z, depth = self.pos.z, self.pos.depth
        if mine:
            up, down = z < depth - 1, z > 0
        else:
            up, down = (zo < z) & (z < depth - 1), (zo > z) & (z > 0)

        @pl.when(up)
        def _():
            what(self.along(zo, k, 0, mine))

        @pl.when(down)
        def _():
            what(self.along(zo, k, 1, mine))

    def start(self):
        self.across(0, "x").start()
        self.across(1, "y").start()
        self.on(self.pos.z, 0, True)

    def on_far_height(self, zo):
        for k in range(4):
            self.along(zo, k, 0).wait_recv()
            self.on(zo, k)

    def round(self, r):
        z = self.pos.z
        if r == 1:
            self.across(0, "x").wait_recv()
            self.across(3, "y").start()
            self.on(z, 2, True)
            self.across(1, "y").wait_recv()
            self.across(2, "x").start()
            self.on(z, 1, True)
        if r == 2:
            self.across(2, "x").wait_recv()
            self.across(3, "y").wait_recv()
            self.on(z, 3, True)
        if 3 <= r <= self.pos.depth + 1:
            self.pos.at(r - 2, self.on_far_height)

    def end_one(self, zo, mine=False):
        for k in range(4):
            self.to_core(zo, k, mine).wait_recv()
            self.to_core(zo, k, mine).wait_send()
            self.along_z(zo, k, mine, lambda c: c.wait_send())

    def end(self):
        for k in range(4):
            self.across(k, "xyxy"[k]).wait_send()
        self.end_one(self.pos.z, True)
        for r in range(1, self.pos.depth):
            self.pos.at(r, self.end_one)


class Reduce:
    SEND, RECV = 4 + 4 + 2, 4 + 4 + 2

    def __init__(self, pos, part, core, far, side, column, send, recv, halves=True):
        self.pos, self.part = pos, part
        self.core, self.far, self.side, self.column = core, far, side, column
        self.send, self.recv = send, recv
        rows = part.shape[1]
        self.half = (pl.ds(0, rows // 2), pl.ds(rows // 2, rows // 2)) if halves else (pl.ds(0, rows),)
        self.rounds = pos.depth + 2

    @staticmethod
    def scratch(depth, rows, width, halves=True):
        b = jnp.bfloat16
        return [
            pltpu.VMEM((depth, 4, rows, width), b),
            pltpu.VMEM((depth, 2, rows // 2, width) if halves else (depth, 1, rows, width), b),
            pltpu.VMEM((depth, 2, rows, width), b),
            pltpu.VMEM((depth, 2, rows, width), b),
            pltpu.SemaphoreType.DMA((Reduce.SEND, depth)),
            pltpu.SemaphoreType.DMA((Reduce.RECV, depth)),
        ]

    def link(self, src, dst, k, zo, to):
        return self.pos.copy(src, dst, self.send.at[k, zo], self.recv.at[k, zo], to)

    def to_core(self, zo, fx, fy):
        k = fx * 2 + fy
        return self.link(self.part.at[self.pos.block(zo, fx, fy, 1)], self.core.at[zo, k], k, zo, "c")

    def far_to(self, zo, k):
        return self.link(self.core.at[zo, 3, self.half[k]], self.far.at[zo, k], 4 + k, zo, ("y", "x")[k])

    def side_to(self, zo, k):
        return self.link(self.core.at[zo, 2 - k], self.side.at[zo, k], 6 + k, zo, ("x", "y")[k])

    def down(self, zo):
        return self.link(self.core.at[zo, 0], self.column.at[zo, 0], 8, zo, "down")

    def up(self, zo):
        return self.link(self.core.at[zo, 0], self.column.at[zo, 1], 9, zo, "up")

    def start_one(self, zo):
        for fx, fy in ((1, 1), (1, 0), (0, 1), (0, 0)):
            self.to_core(zo, fx, fy).start()

    def start(self):
        for dist in reversed(range(self.pos.depth)):
            self.pos.at(dist, self.start_one)

    def total(self, *refs):
        f = refs[0][...].astype(jnp.float32)
        for r in refs[1:]:
            f = f + r[...].astype(jnp.float32)
        return f

    def on_core(self, zo):
        for fx, fy in ((1, 1), (1, 0), (0, 1), (0, 0)):
            k = fx * 2 + fy
            self.to_core(zo, fx, fy).wait_recv()
            mine = self.core.at[zo, k]
            mine[...] = self.total(mine, self.part.at[self.pos.block(zo, fx, fy)]).astype(mine.dtype)
            if k == 3:
                for h in range(len(self.half)):
                    self.far_to(zo, h).start()

    def on_far(self, zo):
        for k in range(2):
            if k < len(self.half):
                self.far_to(zo, k).wait_recv()
                mine = self.core.at[zo, 2 - k, self.half[k]]
                mine[...] = self.total(mine, self.far.at[zo, k]).astype(mine.dtype)
            self.side_to(zo, k).start()

    def on_sides(self, zo, mine=False):
        z, depth = self.pos.z, self.pos.depth
        self.side_to(zo, 0).wait_recv()
        self.side_to(zo, 1).wait_recv()
        here = self.core.at[zo, 0]
        summed = self.total(here, self.side.at[zo, 0], self.side.at[zo, 1])
        if mine:
            self.out[...] = summed

            @pl.when(z < depth - 1)
            def _():
                self.down(zo).wait_recv()
                self.out[...] += self.column[zo, 0].astype(jnp.float32)

            @pl.when(z > 0)
            def _():
                self.up(zo).wait_recv()
                self.out[...] += self.column[zo, 1].astype(jnp.float32)

            return
        here[...] = summed.astype(here.dtype)

        @pl.when((zo < z) & (z < depth - 1))
        def _():
            self.down(zo).wait_recv()
            here[...] = self.total(here, self.column.at[zo, 0]).astype(here.dtype)

        @pl.when((zo > z) & (z > 0))
        def _():
            self.up(zo).wait_recv()
            here[...] = self.total(here, self.column.at[zo, 1]).astype(here.dtype)

        @pl.when(zo < z)
        def _():
            self.down(zo).start()

        @pl.when(zo > z)
        def _():
            self.up(zo).start()

    def round(self, r):
        depth = self.pos.depth
        for s in range(3):
            dist = depth - 1 - (r - s)
            if not 0 <= dist < depth:
                continue
            if s == 0:
                self.pos.at(dist, self.on_core)
            elif s == 1:
                self.pos.at(dist, self.on_far)
            elif dist:
                self.pos.at(dist, self.on_sides)
            else:
                self.on_sides(self.pos.z, True)

    def end_one(self, zo):
        for fx in range(2):
            for fy in range(2):
                self.to_core(zo, fx, fy).wait_send()
        for k in range(len(self.half)):
            self.far_to(zo, k).wait_send()
        for k in range(2):
            self.side_to(zo, k).wait_send()

        @pl.when(zo < self.pos.z)
        def _():
            self.down(zo).wait_send()

        @pl.when(zo > self.pos.z)
        def _():
            self.up(zo).wait_send()

    def end(self):
        for r in range(self.pos.depth):
            self.pos.at(r, self.end_one)


class PlaneGather:
    SEND, RECV = 3, 2

    def __init__(self, pos, own, dst, send, recv):
        self.pos, self.own, self.dst = pos, own, dst
        self.send, self.recv = send, recv
        self.rounds = pos.depth

    def link(self, zo, mine, sends, recvs, to):
        dst = self.dst(zo * 2 + self.pos.x)
        return self.pos.copy(self.own if mine else dst, dst, self.send.at[sends, zo], self.recv.at[recvs, zo], to)

    def along_z(self, zo, mine, what):
        z, depth = self.pos.z, self.pos.depth
        if mine:
            up, down = z < depth - 1, z > 0
        else:
            up, down = (zo < z) & (z < depth - 1), (zo > z) & (z > 0)

        @pl.when(up)
        def _():
            what(self.link(zo, mine, 0, 0, "up"))

        @pl.when(down)
        def _():
            what(self.link(zo, mine, 1, 0, "down"))

    def on_column(self, zo, mine=False):
        if not mine:
            self.link(zo, False, 0, 0, "up").wait_recv()
        self.along_z(zo, mine, lambda c: c.start())
        self.link(zo, mine, 2, 1, "x").start()

    def start(self):
        self.on_column(self.pos.z, True)

    def round(self, r):
        if 1 <= r < self.pos.depth:
            self.pos.at(r, self.on_column)

    def end_one(self, zo, mine=False):
        across = self.link(zo, mine, 2, 1, "x")
        across.wait_recv()
        self.along_z(zo, mine, lambda c: c.wait_send())
        across.wait_send()

    def end(self):
        self.end_one(self.pos.z, True)
        for r in range(1, self.pos.depth):
            self.pos.at(r, self.end_one)

    @staticmethod
    def sems(depth):
        return [pltpu.SemaphoreType.DMA((PlaneGather.SEND, depth)), pltpu.SemaphoreType.DMA((PlaneGather.RECV, depth))]


class PlaneReduce:
    def __init__(self, pos, part, out, across, column, send, recv):
        self.pos, self.part, self.out = pos, part, out
        self.across, self.column = across, column
        self.send, self.recv = send, recv
        self.rounds = pos.depth

    @staticmethod
    def scratch(depth, rows, width):
        b = jnp.bfloat16
        return [
            pltpu.VMEM((depth, rows, width), b),
            pltpu.VMEM((depth, 2, rows, width), b),
            pltpu.SemaphoreType.DMA((3, depth)),
            pltpu.SemaphoreType.DMA((3, depth)),
        ]

    def to_x(self, zo):
        src = self.part(zo * 2 + 1 - self.pos.x)
        return self.pos.copy(src, self.across.at[zo], self.send.at[0, zo], self.recv.at[0, zo], "x")

    def down(self, zo):
        return self.pos.copy(
            self.across.at[zo], self.column.at[zo, 0], self.send.at[1, zo], self.recv.at[1, zo], "down"
        )

    def up(self, zo):
        return self.pos.copy(
            self.across.at[zo], self.column.at[zo, 1], self.send.at[2, zo], self.recv.at[2, zo], "up"
        )

    def start(self):
        for dist in reversed(range(self.pos.depth)):
            self.pos.at(dist, lambda zo: self.to_x(zo).start())

    def on_column(self, zo):
        z, depth = self.pos.z, self.pos.depth
        f32 = jnp.float32
        here = self.across.at[zo]
        self.to_x(zo).wait_recv()
        here[...] = (here[...].astype(f32) + self.part(zo * 2 + self.pos.x)[...].astype(f32)).astype(here.dtype)

        @pl.when((zo < z) & (z < depth - 1))
        def _():
            self.down(zo).wait_recv()
            here[...] = (here[...].astype(f32) + self.column[zo, 0].astype(f32)).astype(here.dtype)

        @pl.when((zo > z) & (z > 0))
        def _():
            self.up(zo).wait_recv()
            here[...] = (here[...].astype(f32) + self.column[zo, 1].astype(f32)).astype(here.dtype)

        @pl.when(zo < z)
        def _():
            self.down(zo).start()

        @pl.when(zo > z)
        def _():
            self.up(zo).start()

    def on_own(self):
        z, depth = self.pos.z, self.pos.depth
        f32 = jnp.float32
        self.to_x(z).wait_recv()
        self.out[...] = self.across[z].astype(f32) + self.part(z * 2 + self.pos.x)[...].astype(f32)

        @pl.when(z < depth - 1)
        def _():
            self.down(z).wait_recv()
            self.out[...] += self.column[z, 0].astype(f32)

        @pl.when(z > 0)
        def _():
            self.up(z).wait_recv()
            self.out[...] += self.column[z, 1].astype(f32)

    def round(self, r):
        dist = self.pos.depth - 1 - r
        if dist > 0:
            self.pos.at(dist, self.on_column)
        elif dist == 0:
            self.on_own()

    def end_one(self, zo):
        self.to_x(zo).wait_send()

        @pl.when(zo < self.pos.z)
        def _():
            self.down(zo).wait_send()

        @pl.when(zo > self.pos.z)
        def _():
            self.up(zo).wait_send()

    def end(self):
        for r in range(self.pos.depth):
            self.pos.at(r, self.end_one)


class Exchange:
    def __init__(self, pos, piece, place, send, recv, local):
        self.pos, self.piece, self.place = pos, piece, place
        self.send, self.recv, self.local = send, recv, local
        self.groups = pos.depth * 2
        self.rounds = 0

    @staticmethod
    def sems(depth):
        n = depth * 2 - 1
        return [pltpu.SemaphoreType.DMA((n,)), pltpu.SemaphoreType.DMA((n,)), pltpu.SemaphoreType.DMA]

    def peer(self, k):
        return lax.rem(self.pos.d + k, self.groups)

    def copy(self, k):
        p = self.peer(k)
        return pltpu.make_async_remote_copy(
            src_ref=self.piece(p),
            dst_ref=self.place(self.pos.d),
            send_sem=self.send.at[k - 1],
            recv_sem=self.recv.at[k - 1],
            device_id=(p, self.pos.t),
            device_id_type=MESH,
        )

    def here(self):
        return pltpu.make_async_copy(self.piece(self.pos.d), self.place(self.pos.d), self.local)

    def start(self):
        self.here().start()
        for k in range(1, self.groups):
            self.copy(k).start()

    def round(self, r):
        pass

    def end(self):
        self.here().wait()
        for k in range(1, self.groups):
            self.copy(k).wait()


def drive(*parts):
    for p in parts:
        p.start()
    for r in range(max(p.rounds for p in parts)):
        for p in parts:
            p.round(r)
    for p in parts:
        p.end()


def params(number, vmem=None):
    return pltpu.CompilerParams(collective_id=number, has_side_effects=True, vmem_limit_bytes=vmem)


def rows_of(ref, p, rows):
    return ref.at[pl.ds(p * rows, rows)]


def cols_of(ref, p, cols):
    return ref.at[:, pl.ds(pl.multiple_of(p * cols, cols), cols)]


def part_of(ref, p, rows, first, cols):
    return ref.at[pl.ds(p * rows, rows), pl.ds(first, cols)]


def dot(a, b):
    return jnp.dot(a, b, preferred_element_type=jnp.float32)


def dot_nt(a, b):
    return lax.dot_general(a, b, (((1,), (1,)), ((), ())), preferred_element_type=jnp.float32)


def dot_tn(a, b):
    return lax.dot_general(a, b, (((0,), (0,)), ((), ())), preferred_element_type=jnp.float32)


def loop(count, step):
    lax.fori_loop(0, count, lambda i, _: (step(i), 0)[1], 0)


def norm_back(values, gain, grad):
    r = lax.rsqrt(jnp.mean(values * values, axis=-1, keepdims=True) + EPS)
    unit = values * r
    scaled = grad * gain
    return r * (scaled - unit * jnp.mean(scaled * unit, axis=-1, keepdims=True)), grad * unit


def experts(depth, number, normed, all_grad, all_named, middle, moe_gain, router_t, w_gate, w_up, w_down):
    f32, bf = jnp.float32, jnp.bfloat16
    rows, width = normed.shape
    devices = depth * 8
    plane_rows = rows * 8
    picks = plane_rows // 2
    slots = depth * picks
    ff = w_gate.shape[1]
    lanes = all_named.shape[2]
    count = router_t.shape[0]
    wide = width + lanes

    def body(
        n_ref, g_ref, named_hbm, mid_ref, gain_ref, router_ref, wg_hbm, wu_hbm, wd_hbm,
        layer_out, grad_middle, grad_block, gain_grad, n_all, x_out, gret_out, inner_out, gboth_out,
        wg, wu, wd, nb, gb, ob, part, xin, gret, ret, inner, gboth, act_a, act_u, gates, out_sum, grad_sum,
        named, select_t, router_wide, gain_row,
        w_sem, own_sem, all_sem, keep_sem, *rest,
    ):
        pos = Place(depth)
        expert = pos.block(pos.z)
        loads = [
            pltpu.make_async_copy(src, dst, w_sem.at[i])
            for i, (src, dst) in enumerate(((wg_hbm, wg), (wu_hbm, wu), (wd_hbm, wd), (named_hbm, named)))
        ]
        own = [
            pltpu.make_async_copy(n_ref, nb.at[expert], own_sem.at[0]),
            pltpu.make_async_copy(g_ref, gb, own_sem.at[1]),
        ]
        for c in own + loads:
            c.start()
        pos.greet()
        g_normed = Gather(pos, n_ref, nb, *rest[0:2], True)
        r_out = Reduce(pos, ob, *rest[2:8])
        r_grad = Reduce(pos, part, *rest[8:14])
        r_out.out, r_grad.out = out_sum, grad_sum

        def plane(ref, z):
            return ref[pl.ds(z * 8, 8)].reshape(plane_rows, ref.shape[2])

        def picked(z):
            return pl.ds(pl.multiple_of(z * picks, picks), picks)

        here = lax.broadcasted_iota(jnp.int32, (plane_rows, lanes), 1) == expert

        def choose(z):
            names = plane(named, z)
            ones = names.astype(f32)
            above = lax.broadcasted_iota(jnp.int32, (plane_rows, plane_rows), 0)
            upto = lax.broadcasted_iota(jnp.int32, (plane_rows, plane_rows), 1) <= above
            counts = dot(upto.astype(f32).astype(bf), names)
            place = jnp.sum(jnp.where(here, counts * ones, 0.0), axis=1, keepdims=True) - 1.0
            pick = lax.broadcasted_iota(jnp.int32, (plane_rows, picks), 1).astype(f32)
            select_t[z] = jnp.where(place == pick, 1.0, 0.0).astype(bf)

        def take(z):
            tok = plane(nb, z)
            logits = dot_nt(tok, router_wide[...])
            chosen = plane(named, z).astype(f32) > 0
            top = jnp.max(jnp.where(chosen, logits, -1e30), axis=1, keepdims=True)
            raised = jnp.where(chosen, jnp.exp(jnp.minimum(logits - top, 0.0)), 0.0)
            gates[z] = raised / jnp.sum(raised, axis=1, keepdims=True)
            xin[picked(z), :] = dot_tn(select_t[z], tok).astype(bf)

        near = pos.z // 2
        apart = 1 - near

        def in_pair(h):
            return pl.ds(pl.multiple_of(h * 2 * picks, 2 * picks), 2 * picks)

        def both(h, step):
            loop(2, lambda j: step(2 * h + j))

        def forward(h):
            x = xin[in_pair(h), :]
            a = dot(x, wg[...])
            u = dot(x, wu[...])
            act_a[in_pair(h), :] = a
            act_u[in_pair(h), :] = u
            inner[in_pair(h), :] = (a / (1.0 + jnp.exp(-a)) * u).astype(bf)

        def produce(h):
            ret[in_pair(h), :] = dot(inner[in_pair(h), :], wd[...]).astype(bf)

        def spread(z):
            gate = gates[z]
            mine = jnp.sum(jnp.where(here, gate, 0.0), axis=1, keepdims=True)
            g = plane(gb, z).astype(f32)
            gret[picked(z), :] = dot_tn(select_t[z], (mine * g).astype(bf)).astype(bf)
            back = dot(select_t[z], ret[picked(z), :])
            ob[pl.ds(z * 8, 8)] = (mine * back).astype(bf).reshape(8, rows, width)
            summed = jnp.sum(g * back, axis=1, keepdims=True)
            logit = gate * (jnp.where(here, 1.0, 0.0) - mine) * summed
            part[pl.ds(z * 8, 8), :, pl.ds(width, lanes)] = logit.astype(bf).reshape(8, rows, lanes)

        def backward(h):
            gi = dot_nt(gret[in_pair(h), :], wd[...])
            a = act_a[in_pair(h), :]
            s = 1.0 / (1.0 + jnp.exp(-a))
            gboth[in_pair(h), pl.ds(0, ff)] = (gi * act_u[in_pair(h), :] * (s + a * s * (1.0 - s))).astype(bf)
            gboth[in_pair(h), pl.ds(ff, ff)] = (gi * (a * s)).astype(bf)

        def inputs_back(h):
            by_gate, by_up = gboth[in_pair(h), pl.ds(0, ff)], gboth[in_pair(h), pl.ds(ff, ff)]
            ret[in_pair(h), :] = (dot_nt(by_gate, wg[...]) + dot_nt(by_up, wu[...])).astype(bf)

        def scatter(z):
            back = dot(select_t[z], ret[picked(z), :]).astype(bf)
            part[pl.ds(z * 8, 8), :, pl.ds(0, width)] = back.reshape(8, rows, width)
            r_grad.start_one(z)

        g_normed.start()
        as_row(gain_ref, gain_row)
        router_wide[...] = jnp.zeros(router_wide.shape, bf)
        router_wide[pl.ds(0, count), :] = router_ref[...]
        loads[3].wait()
        loop(depth, choose)
        for r in range(1, 4):
            g_normed.round(r)
        own[0].wait()
        g_normed.arrived(0)
        g_normed.arrived(1)
        both(near, take)
        g_normed.round(4)
        loads[0].wait()
        loads[1].wait()
        forward(near)
        g_normed.round(5)
        loads[2].wait()
        produce(near)
        own[1].wait()
        both(near, spread)
        for dist in range(2, depth):
            g_normed.arrived(dist)
        both(apart, take)
        g_normed.end()
        keep = pltpu.make_async_copy(nb, n_all, all_sem)
        keep.start()
        forward(apart)
        produce(apart)
        both(apart, spread)
        r_out.start()
        backward(apart)
        r_out.round(0)
        inputs_back(apart)
        for dist in reversed(range(2, depth)):
            pos.at(dist, scatter)
        r_out.round(1)
        r_grad.round(0)
        backward(near)
        r_out.round(2)
        r_grad.round(1)
        inputs_back(near)
        for dist in reversed(range(2)):
            pos.at(dist, scatter)
        kept = [
            pltpu.make_async_copy(src, dst, keep_sem.at[i])
            for i, (src, dst) in enumerate(((xin, x_out), (gret, gret_out), (inner, inner_out), (gboth, gboth_out)))
        ]
        for c in kept:
            c.start()
        for r in range(3, r_out.rounds):
            r_out.round(r)
            r_grad.round(r - 1)
        r_grad.round(r_out.rounds - 1)
        keep.wait()
        mid = mid_ref[...]
        layer_out[...] = (mid + out_sum[...]).astype(bf)
        logit = grad_sum[:, pl.ds(width, lanes)].astype(bf)
        change, by_gain = norm_back(mid, gain_row[...], grad_sum[:, pl.ds(0, width)] + dot(logit, router_wide[...]))
        gain_grad[...] = jnp.sum(by_gain, axis=0, keepdims=True)
        change = gb[expert].astype(f32) + change
        grad_middle[...] = change
        grad_block[:, pl.ds(0, width)] = change.astype(bf)
        grad_block[:, pl.ds(width, lanes)] = logit
        for c in kept:
            c.wait()
        r_out.end()
        r_grad.end()

    vmem, hbm = pl.BlockSpec(memory_space=pltpu.VMEM), pl.BlockSpec(memory_space=HBM)
    dma = pltpu.SemaphoreType.DMA
    shape = jax.ShapeDtypeStruct
    return pl.pallas_call(
        body,
        out_shape=[
            shape((rows, width), bf),
            shape((rows, width), f32),
            shape((rows, wide), bf),
            shape((1, width), f32),
            shape((devices, rows, width), bf),
            shape((slots, width), bf),
            shape((slots, width), bf),
            shape((slots, ff), bf),
            shape((slots, 2 * ff), bf),
        ],
        in_specs=[hbm] * 3 + [vmem] * 3 + [hbm] * 3,
        out_specs=[vmem] * 4 + [hbm] * 5,
        scratch_shapes=[
            pltpu.VMEM((width, ff), bf),
            pltpu.VMEM((width, ff), bf),
            pltpu.VMEM((ff, width), bf),
            pltpu.VMEM((devices, rows, width), bf),
            pltpu.VMEM((devices, rows, width), bf),
            pltpu.VMEM((devices, rows, width), bf),
            pltpu.VMEM((devices, rows, wide), bf),
            pltpu.VMEM((slots, width), bf),
            pltpu.VMEM((slots, width), bf),
            pltpu.VMEM((slots, width), bf),
            pltpu.VMEM((slots, ff), bf),
            pltpu.VMEM((slots, 2 * ff), bf),
            pltpu.VMEM((slots, ff), f32),
            pltpu.VMEM((slots, ff), f32),
            pltpu.VMEM((depth, plane_rows, lanes), f32),
            pltpu.VMEM((rows, width), f32),
            pltpu.VMEM((rows, wide), f32),
            pltpu.VMEM((devices, rows, lanes), bf),
            pltpu.VMEM((depth, plane_rows, picks), bf),
            pltpu.VMEM((lanes, width), bf),
            pltpu.VMEM((1, width), f32),
            dma((4,)),
            dma((2,)),
            dma,
            dma((5,)),
        ]
        + Gather.sems(depth)
        + Reduce.scratch(depth, rows, width)
        + Reduce.scratch(depth, rows, wide),
        compiler_params=params(number, 60 * 2**20),
        name="experts",
    )(normed, all_grad, all_named, middle, moe_gain, router_t, w_gate, w_up, w_down)


def finish(pairs, grad_q, grad_o, as_they_are):
    f32 = jnp.float32
    xin, gret, inner, gboth = pairs
    slots, width = xin.shape
    ff = inner.shape[1]
    steps = width // 512
    w_rows, w_cols = grad_q.shape
    n = len(as_they_are)

    def body(x, g, i, gg, q, o, *refs):
        given, (wg, wu, wd, wq, wo), same, turned = refs[:n], refs[n : n + 5], refs[n + 5 : 2 * n + 5], refs[2 * n + 5]

        @pl.when(pl.program_id(0) == 0)
        def _():
            turned[...] = i[...].T

        both = dot_tn(x[...], gg[...])
        wg[...] = both[:, :ff]
        wu[...] = both[:, ff:]
        wd[...] = dot(turned[...], g[...])
        wq[...] = q[...].astype(f32)
        wo[...] = o[...].astype(f32)

        @pl.when(pl.program_id(0) == 0)
        def _():
            for src, dst in zip(given, same):
                dst[...] = src[...]

    whole = pl.BlockSpec((slots, ff), lambda s: (0, 0))
    tall = pl.BlockSpec((slots, 512), lambda s: (0, s))
    part = pl.BlockSpec((w_rows, w_cols // steps), lambda s: (0, s))
    same = [pl.BlockSpec(a.shape, lambda s: (0, 0)) for a in as_they_are]
    shape = jax.ShapeDtypeStruct
    return pl.pallas_call(
        body,
        grid=(steps,),
        out_shape=[shape((width, ff), f32)] * 2
        + [shape((ff, width), f32)]
        + [shape((w_rows, w_cols), f32)] * 2
        + [shape(a.shape, a.dtype) for a in as_they_are],
        in_specs=[tall, tall, whole, pl.BlockSpec((slots, 2 * ff), lambda s: (0, 0)), part, part] + same,
        out_specs=[pl.BlockSpec((512, ff), lambda s: (s, 0))] * 2
        + [pl.BlockSpec((ff, 512), lambda s: (0, s)), part, part]
        + same,
        scratch_shapes=[pltpu.VMEM((ff, slots), xin.dtype)],
        compiler_params=pltpu.CompilerParams(vmem_limit_bytes=62 * 2**20),
        name="finish",
    )(*pairs, grad_q, grad_o, *as_they_are)


def as_row(ref, row):
    for i in range(ref.shape[0]):
        row[:, pl.ds(i * 128, 128)] = ref[pl.ds(i, 1), :].astype(jnp.float32)


def turn(u, cosine, sine):
    return u * cosine + pltpu.roll(u, u.shape[1] // 2, 1) * sine


def attend(depth, number, tokens, routes_t, out_grad, q_weight, k_weight, v_weight, out_weight, gains, frequency, docs):
    f32, bf = jnp.float32, jnp.bfloat16
    norm_gain, q_gain, k_gain, moe_gain = gains
    devices = depth * 8
    rows, width = tokens.shape[0] // 4, tokens.shape[1]
    w_rows, head = k_weight.shape
    total = devices * rows
    plane_rows = total // depth
    scale = head ** (-0.5)

    def body(
        tok, route, grad, wq, wk, wv, wo, ng, qg, kg, mg, freq, drow,
        middle, normed, all_named, all_grad, all_tok, hidden_out, wi_out, wo_out, proj_out, q_out, k_out, v_out, head_out,
        total_out, cos_out, sin_out,
        projected, queries, keys, values, heads, totals, cosines, sines, tb, hb, w_in, w_o, part, branch, doc, home, norm_row, moe_row, route_wide, names, own_sem, keep_sem, *rest,
    ):
        pos = Place(depth)
        device = pos.block(pos.z)
        share = tok.at[pl.ds(pl.multiple_of(pos.t * rows, rows), rows)]
        route_wide[...] = jnp.full(route_wide.shape, -1, jnp.int32)
        route_wide[pl.ds(0, route.shape[0]), pl.ds(0, rows)] = route[...]
        one = lax.broadcasted_iota(jnp.int32, (128, 128), 0)
        hits = jnp.zeros((128, 128), f32)
        for k in range(route.shape[0]):
            hits += jnp.where(route_wide[pl.ds(k, 1), :] == one, 1.0, 0.0)
        names[...] = hits.T[:rows].astype(bf)
        own = [
            pltpu.make_async_copy(src, dst, own_sem.at[i])
            for i, (src, dst) in enumerate(
                (
                    (names, all_named.at[device]),
                    (share, tb.at[device]),
                    (wk, part_of(w_in, pos.d, w_rows, head, head)),
                    (wv, part_of(w_in, pos.d, w_rows, 2 * head, head)),
                    (share, home),
                    (grad, all_grad.at[device]),
                )
            )
        ]
        for c in own:
            c.start()
        pos.greet(plane=True)
        g_k = PlaneGather(pos, wk, lambda p: part_of(w_in, p, w_rows, head, head), *rest[0:2])
        g_v = PlaneGather(pos, wv, lambda p: part_of(w_in, p, w_rows, 2 * head, head), *rest[2:4])
        g_tok = Gather(pos, share, tb, *rest[4:6], False)
        g_names = Gather(pos, names, all_named, *rest[6:8], False)
        x_q = Exchange(pos, lambda p: cols_of(wq, p, head), lambda p: part_of(w_in, p, w_rows, 0, head), *rest[8:11])
        x_o = Exchange(pos, lambda p: cols_of(wo, p, head), lambda p: rows_of(w_o, p, w_rows), *rest[11:14])
        red = Reduce(pos, part, *rest[14:20], halves=False)
        red.out = branch
        g_grad = Gather(pos, grad, all_grad, *rest[20:22], True)

        def span(z):
            return pl.ds(pl.multiple_of(z * plane_rows, plane_rows), plane_rows)

        def angle(z):
            place = lax.broadcasted_iota(jnp.int32, (plane_rows, total), 0) + z * plane_rows
            other = lax.broadcasted_iota(jnp.int32, (plane_rows, total), 1)
            all_docs = drow[...].astype(f32)
            docs_here = jnp.sum(jnp.where(other == place, all_docs, 0.0), axis=1, keepdims=True)
            doc[span(z), :] = jnp.broadcast_to(docs_here, (plane_rows, head))
            before = jnp.where((other < place) & (all_docs == docs_here), 1.0, 0.0)
            turned = jnp.sum(before, axis=1, keepdims=True) * freq[...]
            cosines[span(z), :] = jnp.cos(turned)
            sign = jnp.where(lax.broadcasted_iota(jnp.int32, (plane_rows, head), 1) < head // 2, -1.0, 1.0)
            sines[span(z), :] = jnp.sin(turned) * sign

        def normalise(z):
            t = tb[pl.ds(z * 8, 8)].reshape(plane_rows, width).astype(f32)
            r = lax.rsqrt(jnp.mean(t * t, axis=1, keepdims=True) + EPS)
            hb[pl.ds(z * 8, 8)] = (t * r * norm_row[...]).astype(bf).reshape(8, rows, width)

        def project(z):
            p = dot(hb[pl.ds(z * 8, 8)].reshape(plane_rows, width), w_in[...])
            projected[span(z), :] = p
            for ref, first, gain in ((queries, 0, qg), (keys, head, kg)):
                u = p[:, first : first + head]
                u = u * lax.rsqrt(jnp.mean(u * u, axis=1, keepdims=True) + EPS) * gain[...].astype(f32)
                ref[span(z), :] = turn(u, cosines[span(z), :], sines[span(z), :]).astype(bf)
            values[span(z), :] = p[:, 2 * head :].astype(bf)

        def attention(z):
            place = lax.broadcasted_iota(jnp.int32, (plane_rows, total), 0) + z * plane_rows
            allowed = (lax.broadcasted_iota(jnp.int32, (plane_rows, total), 1) <= place) & (
                doc[span(z), pl.ds(0, 1)] == drow[...].astype(f32)
            )
            s = jnp.where(allowed, dot_nt(queries[span(z), :], keys[...]) * scale, -1e30)
            top = jnp.max(s, axis=1, keepdims=True)
            w = jnp.exp(s - top)
            mass = jnp.sum(w, axis=1, keepdims=True)
            out = dot(w.astype(bf), values[...]) / mass
            heads[span(z), :] = out
            totals[span(z), :] = jnp.broadcast_to(top + jnp.log(mass), (plane_rows, head))

        def spread(z):
            a = heads[span(z), :].astype(bf)
            part[pl.ds(z * 8, 8)] = dot_nt(a, w_o[...]).astype(bf).reshape(8, rows, width)
            red.start_one(z)

        kept = []

        def keep(src, dst):
            kept.append(pltpu.make_async_copy(src, dst, keep_sem.at[len(kept)]))
            kept[-1].start()

        g_tok.start()
        as_row(ng, norm_row)
        as_row(mg, moe_row)
        loop(depth, angle)
        keep(cosines, cos_out)
        keep(sines, sin_out)
        for c in own:
            c.wait()
        for r in range(1, g_tok.rounds):
            g_tok.round(r)
            if r == 1:
                g_k.start()
                g_v.start()
            else:
                g_k.round(r - 1)
                g_v.round(r - 1)
            if r == 3:
                x_q.start()
            if r == 5:
                x_o.start()
            if r >= 3:
                g_tok.arrived(r - 3)
                pos.at(r - 3, normalise)
        g_names.start()
        g_grad.start()
        g_tok.arrived(depth - 1)
        pos.at(depth - 1, normalise)
        g_tok.end()
        keep(tb, all_tok)
        keep(hb, hidden_out)
        g_k.end()
        g_v.end()
        x_q.end()
        keep(w_in, wi_out)
        loop(depth, project)
        for src, dst in ((projected, proj_out), (queries, q_out), (keys, k_out), (values, v_out)):
            keep(src, dst)
        g_grad.round(1)
        pos.at(depth - 1, attention)
        x_o.end()
        keep(w_o, wo_out)
        pos.at(depth - 1, spread)
        for dist in reversed(range(depth - 1)):
            pos.at(dist, attention)
            pos.at(dist, spread)
        keep(heads, head_out)
        keep(totals, total_out)
        for r in range(red.rounds):
            red.round(r)
            g_names.round(r)
            if r >= 2:
                g_grad.round(r)
        mid = home[...].astype(f32) + branch[...]
        middle[...] = mid
        normed[...] = (mid * lax.rsqrt(jnp.mean(mid * mid, axis=1, keepdims=True) + EPS) * moe_row[...]).astype(bf)
        g_names.end()
        g_grad.end()
        for c in kept:
            c.wait()
        red.end()

    vmem, hbm = pl.BlockSpec(memory_space=pltpu.VMEM), pl.BlockSpec(memory_space=HBM)
    dma = pltpu.SemaphoreType.DMA
    shape = jax.ShapeDtypeStruct
    return pl.pallas_call(
        body,
        out_shape=[
            shape((rows, width), f32),
            shape((rows, width), bf),
            shape((devices, rows, 128), bf),
            shape((devices, rows, width), bf),
            shape((devices, rows, width), bf),
            shape((devices, rows, width), bf),
            shape((width, 3 * head), bf),
            shape((width, head), bf),
            shape((total, 3 * head), f32),
            shape((total, head), bf),
            shape((total, head), bf),
            shape((total, head), bf),
            shape((total, head), f32),
            shape((total, head), f32),
            shape((total, head), f32),
            shape((total, head), f32),
        ],
        in_specs=[hbm, vmem] + [hbm] * 5 + [vmem] * 6,
        out_specs=[vmem] * 2 + [hbm] * 14,
        scratch_shapes=[
            pltpu.VMEM((total, 3 * head), f32),
            pltpu.VMEM((total, head), bf),
            pltpu.VMEM((total, head), bf),
            pltpu.VMEM((total, head), bf),
            pltpu.VMEM((total, head), f32),
            pltpu.VMEM((total, head), f32),
            pltpu.VMEM((total, head), f32),
            pltpu.VMEM((total, head), f32),
            pltpu.VMEM((devices, rows, width), bf),
            pltpu.VMEM((devices, rows, width), bf),
            pltpu.VMEM((width, 3 * head), bf),
            pltpu.VMEM((width, head), bf),
            pltpu.VMEM((devices, rows, width), bf),
            pltpu.VMEM((rows, width), f32),
            pltpu.VMEM((total, head), f32),
            pltpu.VMEM((rows, width), bf),
            pltpu.VMEM((1, width), f32),
            pltpu.VMEM((1, width), f32),
            pltpu.VMEM((8, 128), jnp.int32),
            pltpu.VMEM((rows, 128), bf),
            dma((6,)),
            dma((12,)),
        ]
        + PlaneGather.sems(depth) * 2
        + Gather.sems(depth) * 2
        + Exchange.sems(depth) * 2
        + Reduce.scratch(depth, rows, width, False)
        + Gather.sems(depth),
        compiler_params=params(number, 60 * 2**20),
        name="attend",
    )(tokens, routes_t, out_grad, q_weight, k_weight, v_weight, out_weight, norm_gain, q_gain, k_gain, moe_gain, frequency, docs)


def attend_back(depth, number, block, moe_gain_grad, grad_middle, all_normed, experts_in_all, kept, gains, docs):
    f32, bf = jnp.float32, jnp.bfloat16
    all_tok, hidden, w_in, w_o, projected, queries, keys, values, heads, totals, cosines, sines = kept
    norm_gain, q_gain, k_gain = gains
    devices, rows, width = all_tok.shape
    wide = block.shape[1]
    lanes = wide - width
    total, head = queries.shape
    groups = depth * 2
    w_rows = width // groups
    plane_rows = total // depth
    scale = head ** (-0.5)
    gain_rows = width // 128
    small_rows = 2 * gain_rows + 8

    def body(
        blk, moe, gm, n_h, tok_h, hid_h, wi_h, wo_h, proj_h, q_h, k_h, v_h, head_h, tot_h, cos_h, sin_h, ng, qg, kg, drow,
        tokens_grad, q_grad, k_grad, v_grad, o_grad, norm_sum, moe_sum, q_sum, k_sum, router_grad,
        gb, nb, tb, hb, w_in, w_o, proj, qs, ks, vs, hs, ts, cos, sin, part, gh, dq, dk, dv, gproj, wpart, opart,
        kv_sum, hidden_sum, small, small_all, by_norm, by_q, by_k, doc, turned, norm_row, load_sem, own_sem, *rest,
    ):
        pos = Place(depth)
        device = pos.block(pos.z)
        loads = [
            pltpu.make_async_copy(src, dst, load_sem.at[i])
            for i, (src, dst) in enumerate(
                (
                    (wo_h, w_o), (head_h, hs), (tok_h, tb), (hid_h, hb), (wi_h, w_in), (proj_h, proj), (q_h, qs),
                    (k_h, ks), (v_h, vs), (tot_h, ts), (cos_h, cos), (sin_h, sin), (n_h, nb),
                )
            )
        ]
        own = pltpu.make_async_copy(blk, gb.at[device], own_sem)
        own.start()
        for c in loads:
            c.start()
        pos.greet(plane=True)
        g_branch = Gather(pos, blk, gb, *rest[0:2], True)
        g_small = Gather(pos, small, small_all, *rest[2:4], False)
        x_q = Exchange(
            pos, lambda p: part_of(wpart, p, w_rows, 0, head), lambda p: cols_of(q_grad, p, head), *rest[4:7]
        )
        x_o = Exchange(pos, lambda p: rows_of(opart, p, w_rows), lambda p: cols_of(o_grad, p, head), *rest[7:10])
        red = Reduce(pos, part, *rest[10:16], halves=False)
        red.out = hidden_sum
        r_kv = PlaneReduce(pos, lambda p: part_of(wpart, p, w_rows, head, 2 * head), kv_sum, *rest[16:20])

        def span(z):
            return pl.ds(pl.multiple_of(z * plane_rows, plane_rows), plane_rows)

        def column(z):
            place = lax.broadcasted_iota(jnp.int32, (plane_rows, total), 0) + z * plane_rows
            other = lax.broadcasted_iota(jnp.int32, (plane_rows, total), 1)
            docs_here = jnp.sum(jnp.where(other == place, drow[...].astype(f32), 0.0), axis=1, keepdims=True)
            doc[span(z), :] = jnp.broadcast_to(docs_here, (plane_rows, head))

        def heads_back(z):
            g = gb[pl.ds(z * 8, 8), :, pl.ds(0, width)].reshape(plane_rows, width)
            gh[span(z), :] = dot(g, w_o[...]).astype(bf)

        def out_weight_back():
            g = gb[:, :, pl.ds(0, width)].reshape(total, width)
            opart[...] = dot(turned[pl.ds(0, head), :], g).T.astype(bf)

        def attention_back(z):
            place = lax.broadcasted_iota(jnp.int32, (plane_rows, total), 0) + z * plane_rows
            allowed = (lax.broadcasted_iota(jnp.int32, (plane_rows, total), 1) <= place) & (
                doc[span(z), pl.ds(0, 1)] == drow[...].astype(f32)
            )
            q = qs[span(z), :]
            g = gh[span(z), :]
            delta = jnp.sum(g.astype(f32) * hs[span(z), :], axis=1, keepdims=True)
            s = dot_nt(q, ks[...]) * scale
            p = jnp.where(allowed, jnp.exp(jnp.minimum(s - ts[span(z), pl.ds(0, 1)], 0.0)), 0.0)
            ds = (p * (dot_nt(g, vs[...]) - delta)).astype(bf)
            dq[span(z), :] = dot(ds, ks[...]) * scale
            dk[...] += dot_tn(ds, q) * scale
            dv[...] += dot_tn(p.astype(bf), g)

        def project_back(z):
            for first, grad, gain, total_ref in ((0, dq, qg, by_q), (head, dk, kg, by_k)):
                g = turn(grad[span(z), :], cos[span(z), :], -sin[span(z), :])
                change, by_gain = norm_back(proj[span(z), pl.ds(first, head)], gain[...].astype(f32), g)
                gproj[span(z), pl.ds(first, head)] = change.astype(bf)
                total_ref[...] += jnp.sum(by_gain, axis=0, keepdims=True)
            gproj[span(z), pl.ds(2 * head, head)] = dv[span(z), :].astype(bf)

        def spread(z):
            g = gproj[span(z), :]
            t = tb[pl.ds(z * 8, 8)].reshape(plane_rows, width).astype(f32)
            r = lax.rsqrt(jnp.mean(t * t, axis=1, keepdims=True) + EPS)
            back = dot_nt(g, w_in[...])
            part[pl.ds(z * 8, 8)] = back.astype(bf).reshape(8, rows, width)
            by_norm[...] += jnp.sum(back * (t * r), axis=0, keepdims=True)
            red.start_one(z)

        def router_back():
            router_grad[...] = dot(turned[pl.ds(0, experts_in_all), :], nb[...].reshape(total, width))

        def in_weight_back():
            wpart[...] = dot(turned[...], hb[...].reshape(total, width)).T.astype(bf)

        g_branch.start()
        as_row(ng, norm_row)
        loop(depth, column)
        dk[...] = jnp.zeros(dk.shape, f32)
        dv[...] = jnp.zeros(dv.shape, f32)
        by_norm[...] = jnp.zeros(by_norm.shape, f32)
        by_q[...] = jnp.zeros(by_q.shape, f32)
        by_k[...] = jnp.zeros(by_k.shape, f32)
        small[...] = jnp.zeros(small.shape, f32)
        for c in loads:
            c.wait()
        own.wait()

        def plane_back(z):
            heads_back(z)
            attention_back(z)

        for r in range(1, g_branch.rounds):
            g_branch.round(r)
            if r >= 3:
                g_branch.arrived(r - 3)
                pos.at(r - 3, plane_back)
        turned[pl.ds(0, head), :] = hs[...].T.astype(bf)
        g_branch.arrived(depth - 1)
        g_branch.end()
        out_weight_back()
        x_o.start()
        pos.at(depth - 1, plane_back)
        loop(depth, project_back)
        turned[...] = gproj[...].T
        in_weight_back()
        x_q.start()
        r_kv.start()
        for dist in reversed(range(depth)):
            pos.at(dist, spread)
        for i in range(gain_rows):
            small[pl.ds(i, 1), :] = by_norm[:, pl.ds(i * 128, 128)]
            small[pl.ds(gain_rows + i, 1), :] = moe[:, pl.ds(i * 128, 128)]
        small[pl.ds(2 * gain_rows, 1), :] = by_q[...]
        small[pl.ds(2 * gain_rows + 1, 1), :] = by_k[...]
        small_all[device] = small[...]
        g_small.start()
        for r in range(red.rounds):
            red.round(r)
            r_kv.round(r)
            g_small.round(r)
            if r == 2:
                turned[pl.ds(0, lanes), :] = gb[:, :, pl.ds(width, lanes)].reshape(total, lanes).T
                router_back()
        change, _ = norm_back(tb[device].astype(f32), norm_row[...], hidden_sum[...])
        tokens_grad[...] = gm[...] + change
        k_grad[...] = kv_sum[:, pl.ds(0, head)]
        v_grad[...] = kv_sum[:, pl.ds(head, head)]
        g_small.end()
        summed = jnp.sum(small_all[...], axis=0)
        norm_sum[...] = summed[:gain_rows]
        moe_sum[...] = summed[gain_rows : 2 * gain_rows]
        q_sum[...] = summed[2 * gain_rows : 2 * gain_rows + 1]
        k_sum[...] = summed[2 * gain_rows + 1 : 2 * gain_rows + 2]
        x_o.end()
        x_q.end()
        red.end()
        r_kv.end()

    vmem, hbm = pl.BlockSpec(memory_space=pltpu.VMEM), pl.BlockSpec(memory_space=HBM)
    dma = pltpu.SemaphoreType.DMA
    shape = jax.ShapeDtypeStruct
    V = pltpu.VMEM
    return pl.pallas_call(
        body,
        out_shape=[
            shape((rows, width), f32),
            shape((w_rows, groups * head), bf),
            shape((w_rows, head), f32),
            shape((w_rows, head), f32),
            shape((w_rows, groups * head), bf),
            shape((gain_rows, 128), f32),
            shape((gain_rows, 128), f32),
            shape((1, 128), f32),
            shape((1, 128), f32),
            shape((experts_in_all, width), f32),
        ],
        in_specs=[hbm, vmem, vmem] + [hbm] * 13 + [vmem] * 4,
        out_specs=[vmem, hbm, vmem, vmem, hbm] + [vmem] * 5,
        scratch_shapes=[
            V((devices, rows, wide), bf),
            V((devices, rows, width), bf),
            V((devices, rows, width), bf),
            V((devices, rows, width), bf),
            V((width, 3 * head), bf),
            V((width, head), bf),
            V((total, 3 * head), f32),
            V((total, head), bf),
            V((total, head), bf),
            V((total, head), bf),
            V((total, head), f32),
            V((total, head), f32),
            V((total, head), f32),
            V((total, head), f32),
            V((devices, rows, width), bf),
            V((total, head), bf),
            V((total, head), f32),
            V((total, head), f32),
            V((total, head), f32),
            V((total, 3 * head), bf),
            V((width, 3 * head), bf),
            V((width, head), bf),
            V((w_rows, 2 * head), f32),
            V((rows, width), f32),
            V((small_rows, 128), f32),
            V((devices, small_rows, 128), f32),
            V((1, width), f32),
            V((1, head), f32),
            V((1, head), f32),
            V((total, head), f32),
            V((3 * head, total), bf),
            V((1, width), f32),
            dma((13,)),
            dma,
        ]
        + Gather.sems(depth) * 2
        + Exchange.sems(depth) * 2
        + Reduce.scratch(depth, rows, width, False)
        + PlaneReduce.scratch(depth, w_rows, 2 * head),
        compiler_params=params(number, 60 * 2**20),
        name="attend_back",
    )(block, moe_gain_grad, grad_middle, all_normed, *kept, norm_gain, q_gain, k_gain, docs)


def head_shards(
    tokens,
    segments,
    routes,
    out_grad,
    norm_gain,
    q_weight,
    k_weight,
    v_weight,
    q_gain,
    k_gain,
    out_weight,
    moe_gain,
    router_weight,
    gate_weight,
    up_weight,
    down_weight,
):
    f32, bf = jnp.float32, jnp.bfloat16
    f32, bf = jnp.float32, jnp.bfloat16
    head_dim = q_gain.shape[0]
    tok_rows, width = tokens.shape
    all_tokens = segments.shape[0]
    expert_count = router_weight.shape[1]
    depth = all_tokens // tok_rows // 2
    norm_gain, q_gain, k_gain, moe_gain = (g.reshape(-1, 128) for g in (norm_gain, q_gain, k_gain, moe_gain))
    docs = segments[None]
    frequency = (THETA ** (np.arange(head_dim // 2) * -2.0 / head_dim)).astype(np.float32)
    middle, normed, all_named, all_grad, *kept = attend(
        depth,
        0,
        tokens,
        routes.T,
        out_grad,
        q_weight,
        k_weight,
        v_weight,
        out_weight,
        (norm_gain, q_gain, k_gain, moe_gain),
        np.concatenate([frequency, frequency])[None],
        docs,
    )
    layer_out, grad_middle, grad_block, moe_gain_grad, all_normed, *pairs = experts(
        depth,
        1,
        normed,
        all_grad,
        all_named,
        middle,
        moe_gain,
        router_weight.T,
        gate_weight[0],
        up_weight[0],
        down_weight[0],
    )
    tokens_grad, grad_q, grad_k, grad_v, grad_o, norm_sum, moe_sum, q_sum, k_sum, grad_router = attend_back(
        depth,
        2,
        grad_block,
        moe_gain_grad,
        grad_middle,
        all_normed,
        expert_count,
        kept,
        (norm_gain, q_gain, k_gain),
        docs,
    )
    grad_gate_w, grad_up_w, grad_down, grad_q, grad_o, *rest = finish(
        pairs,
        grad_q,
        grad_o,
        (layer_out, tokens_grad, grad_k, grad_v, norm_sum, moe_sum, q_sum, k_sum, grad_router),
    )
    layer_out, tokens_grad, grad_k, grad_v, norm_sum, moe_sum, q_sum, k_sum, grad_router = rest
    return (
        layer_out,
        tokens_grad,
        norm_sum.reshape(-1),
        grad_q,
        grad_k,
        grad_v,
        q_sum.reshape(-1),
        k_sum.reshape(-1),
        grad_o,
        moe_sum.reshape(-1),
        grad_router.T,
        grad_gate_w[None],
        grad_up_w[None],
        grad_down[None],
    )


def solution(mesh):
    per_device = shards if mesh.shape["dp"] != 8 or mesh.shape["tensor"] != 4 else head_shards
    placed = (
        P("dp", None),
        P(),
        P(("dp", "tensor"), None),
        P(("dp", "tensor"), None),
        P(),
        P("dp", "tensor"),
        P("dp", "tensor"),
        P("dp", "tensor"),
        P(),
        P(),
        P("dp", "tensor"),
        P(),
        P(),
        P(("dp", "tensor"), None, None),
        P(("dp", "tensor"), None, None),
        P(("dp", "tensor"), None, None),
    )
    return jax.shard_map(
        per_device,
        mesh=mesh,
        in_specs=placed,
        out_specs=(
            P(("dp", "tensor"), None),
            P(("dp", "tensor"), None),
            P(),
            P("dp", "tensor"),
            P("dp", "tensor"),
            P("dp", "tensor"),
            P(),
            P(),
            P("dp", "tensor"),
            P(),
            P(),
            P(("dp", "tensor"), None, None),
            P(("dp", "tensor"), None, None),
            P(("dp", "tensor"), None, None),
        ),
        check_vma=False,
    )
```

```python
import functools

import jax
import jax.numpy as jnp
import numpy as np
from jax import lax
from jax.experimental import pallas as pl
from jax.experimental.pallas import tpu as pltpu
from jax.sharding import PartitionSpec as P

EPS = 1e-06
THETA = 1000000.0


def norm_rows(values, gain):
    return values * lax.rsqrt(jnp.mean(values * values, axis=-1, keepdims=True) + EPS) * gain


def rotary(values, cosine, sine_part):
    half_dim = values.shape[-1] // 2
    front_half = values[..., :half_dim]
    back_half = values[..., half_dim:]
    return jnp.concatenate(
        [front_half * cosine - back_half * sine_part, back_half * cosine + front_half * sine_part],
        axis=-1,
    )


def angles(positions, head_dim):
    half_dim = head_dim // 2
    frequency = THETA ** (-(jnp.arange(half_dim).astype(jnp.float32) * 2.0) / head_dim)
    rotation = positions.astype(jnp.float32)[:, None] * frequency[None, :]
    return (jnp.cos(rotation), jnp.sin(rotation))


def prepare(projected, q_gain, k_gain, cosine, sine_part, head_dim):
    tok_rows = projected.shape[0]
    query_width = projected.shape[1] - 2 * head_dim
    queries = projected[:, :query_width].reshape(tok_rows, query_width // head_dim, head_dim)
    keys_local = projected[:, query_width : query_width + head_dim]
    values_local = projected[:, query_width + head_dim :]
    queries = rotary(norm_rows(queries, q_gain), cosine[:, None, :], sine_part[:, None, :])
    keys_local = rotary(norm_rows(keys_local, k_gain), cosine, sine_part)
    return (queries, keys_local, values_local)


def swiglu(gate_in, up_in):
    return jax.nn.silu(gate_in) * up_in


def shards(
    tokens,
    segments,
    routes,
    out_grad,
    norm_gain,
    q_weight,
    k_weight,
    v_weight,
    q_gain,
    k_gain,
    out_weight,
    moe_gain,
    router_weight,
    gate_weight,
    up_weight,
    down_weight,
):
    head_dim = q_gain.shape[0]
    tok_rows = tokens.shape[0]
    model_width = tokens.shape[1]
    share_rows = out_grad.shape[0]
    all_tokens = segments.shape[0]
    expert_count = router_weight.shape[1]
    top_count = routes.shape[1]
    capacity = max(2, share_rows * top_count * 2 // expert_count)
    score_scale = head_dim ** (-0.5)
    first_row = lax.axis_index("dp") * tok_rows
    places = jnp.arange(all_tokens, dtype=jnp.int32)
    begins = jnp.concatenate([jnp.ones((1,), dtype=bool), segments[1:] != segments[:-1]])
    positions = places - lax.cummax(jnp.where(begins, places, 0), axis=0)
    local_positions = lax.dynamic_slice_in_dim(positions, first_row, tok_rows)
    local_docs = lax.dynamic_slice_in_dim(segments, first_row, tok_rows)
    query_places = first_row + jnp.arange(tok_rows, dtype=jnp.int32)
    cosine, sine_part = angles(local_positions, head_dim)
    weight_rows = (
        lax.all_gather(q_weight, "dp", axis=0, tiled=True),
        lax.all_gather(k_weight, "dp", axis=0, tiled=True),
        lax.all_gather(v_weight, "dp", axis=0, tiled=True),
        lax.all_gather(out_weight, "dp", axis=0, tiled=True),
    )
    input_weight = jnp.concatenate([weight_rows[0], weight_rows[1], weight_rows[2]], axis=1)
    output_weight = weight_rows[3]
    tokens_float = tokens.astype(jnp.float32)
    norm_gain_float = norm_gain.astype(jnp.float32)
    hidden = norm_rows(tokens_float, norm_gain_float).astype(jnp.bfloat16)
    projected = jnp.dot(hidden, input_weight, preferred_element_type=jnp.float32)

    def prepare_local(projected_in, qgain_in, kgain_in):
        return prepare(projected_in, qgain_in, kgain_in, cosine, sine_part, head_dim)

    prepared, prepare_back = jax.vjp(
        prepare_local, projected, q_gain.astype(jnp.float32), k_gain.astype(jnp.float32)
    )
    queries = prepared[0].astype(jnp.bfloat16)
    keys_local = prepared[1].astype(jnp.bfloat16)
    values_local = prepared[2].astype(jnp.bfloat16)
    local_heads = queries.shape[1]

    def visible(offset, length):
        key_places = offset + jnp.arange(length, dtype=jnp.int32)
        key_docs = lax.dynamic_slice_in_dim(segments, offset, length)
        return (key_places[None, :] <= query_places[:, None]) & (
            key_docs[None, :] == local_docs[:, None]
        )

    running_max = jnp.full((tok_rows, local_heads), -1e30, jnp.float32)
    key_piece = lax.all_gather(keys_local, "dp", axis=0, tiled=True)
    value_piece = lax.all_gather(values_local, "dp", axis=0, tiled=True)
    allowed = visible(jnp.int32(0), key_piece.shape[0])[:, None, :]
    scores = (
        jnp.einsum("thd,nd->thn", queries, key_piece, preferred_element_type=jnp.float32)
        * score_scale
    )
    scores = jnp.where(allowed, scores, -1e30)
    new_max = jnp.maximum(running_max, jnp.max(scores, axis=-1))
    soft_weights = jnp.where(allowed, jnp.exp(scores - new_max[:, :, None]), 0.0)
    softmax_mass = jnp.sum(soft_weights, axis=-1)
    weighted_sum = jnp.einsum(
        "thn,nd->thd",
        soft_weights.astype(jnp.bfloat16),
        value_piece,
        preferred_element_type=jnp.float32,
    )
    running_max, softmax_mass, weighted_sum = (new_max, softmax_mass, weighted_sum)
    head_out = weighted_sum / softmax_mass[:, :, None]
    log_total = running_max + jnp.log(softmax_mass)
    attended = head_out.astype(jnp.bfloat16).reshape(tok_rows, local_heads * head_dim)
    branch = lax.psum_scatter(
        jnp.einsum("tc,dc->td", attended, output_weight, preferred_element_type=jnp.float32).astype(
            jnp.bfloat16
        ),
        "tensor",
        scatter_dimension=0,
        tiled=True,
    ).astype(jnp.float32)
    tensor_lane = lax.axis_index("tensor")
    tokens_share = lax.dynamic_slice_in_dim(tokens_float, tensor_lane * share_rows, share_rows, 0)
    middle = tokens_share + branch
    normed_float, moe_norm_back = jax.vjp(norm_rows, middle, moe_gain.astype(jnp.float32))
    normed = normed_float.astype(jnp.bfloat16)
    logits = jnp.dot(normed, router_weight, preferred_element_type=jnp.float32)

    def gating(logit_rows):
        probabilities = jax.nn.softmax(logit_rows, axis=-1)
        chosen = jnp.take_along_axis(probabilities, routes, axis=1)
        return chosen / jnp.sum(chosen, axis=1, keepdims=True)

    gate_values, gating_back = jax.vjp(gating, logits)
    pair_routes = routes.reshape(-1)
    pair_count = pair_routes.shape[0]
    route_table = (
        pair_routes[:, None] == jnp.arange(expert_count, dtype=jnp.int32)[None, :]
    ).astype(jnp.int32)
    route_rank = jnp.sum(jnp.cumsum(route_table, axis=0) * route_table, axis=1) - 1
    slot_index = pair_routes * capacity + route_rank
    slot_owner = (
        jnp.full((expert_count * capacity,), pair_count, jnp.int32)
        .at[slot_index]
        .set(jnp.arange(pair_count, dtype=jnp.int32))
    )
    normed_padded = jnp.concatenate([normed, jnp.zeros((1, model_width), jnp.bfloat16)], axis=0)
    send_rows = normed_padded[slot_owner // top_count].reshape(expert_count, capacity, model_width)
    arrived = lax.all_to_all(send_rows, ("dp", "tensor"), split_axis=0, concat_axis=0, tiled=True)
    expert_inputs = arrived.reshape(-1, model_width)
    w_gate = gate_weight[0]
    w_up = up_weight[0]
    w_down = down_weight[0]
    gate_act = jnp.dot(expert_inputs, w_gate, preferred_element_type=jnp.float32)
    up_act = jnp.dot(expert_inputs, w_up, preferred_element_type=jnp.float32)
    inner_float, swiglu_back = jax.vjp(swiglu, gate_act, up_act)
    inner_act = inner_float.astype(jnp.bfloat16)
    produced = jnp.dot(inner_act, w_down, preferred_element_type=jnp.float32).astype(jnp.bfloat16)
    returned = lax.all_to_all(
        produced.reshape(expert_count, capacity, model_width),
        ("dp", "tensor"),
        split_axis=0,
        concat_axis=0,
        tiled=True,
    )
    picked = (
        returned.reshape(-1, model_width)[slot_index]
        .reshape(share_rows, top_count, model_width)
        .astype(jnp.float32)
    )
    layer_out = (middle + jnp.sum(gate_values[:, :, None] * picked, axis=1)).astype(jnp.bfloat16)
    grad_out = out_grad.astype(jnp.float32)
    grad_picked = (
        (gate_values[:, :, None] * grad_out[:, None, :])
        .astype(jnp.bfloat16)
        .reshape(pair_count, model_width)
    )
    grad_gates = jnp.sum(grad_out[:, None, :] * picked, axis=2)
    grad_padded = jnp.concatenate([grad_picked, jnp.zeros((1, model_width), jnp.bfloat16)], axis=0)
    grad_send = grad_padded[slot_owner].reshape(expert_count, capacity, model_width)
    grad_arrived = lax.all_to_all(
        grad_send, ("dp", "tensor"), split_axis=0, concat_axis=0, tiled=True
    ).reshape(-1, model_width)
    grad_inner = jnp.einsum("rd,fd->rf", grad_arrived, w_down, preferred_element_type=jnp.float32)
    grad_down = jnp.einsum("rf,rd->fd", inner_act, grad_arrived, preferred_element_type=jnp.float32)
    grad_gate_float, grad_up_float = swiglu_back(grad_inner)
    grad_gate_act = grad_gate_float.astype(jnp.bfloat16)
    grad_up_act = grad_up_float.astype(jnp.bfloat16)
    grad_gate_w = jnp.einsum(
        "rd,rf->df", expert_inputs, grad_gate_act, preferred_element_type=jnp.float32
    )
    grad_up_w = jnp.einsum(
        "rd,rf->df", expert_inputs, grad_up_act, preferred_element_type=jnp.float32
    )
    grad_inputs = jnp.einsum("rf,df->rd", grad_gate_act, w_gate, preferred_element_type=jnp.float32)
    grad_inputs = (
        grad_inputs + jnp.einsum("rf,df->rd", grad_up_act, w_up, preferred_element_type=jnp.float32)
    ).astype(jnp.bfloat16)
    grad_home = lax.all_to_all(
        grad_inputs.reshape(expert_count, capacity, model_width),
        ("dp", "tensor"),
        split_axis=0,
        concat_axis=0,
        tiled=True,
    )
    grad_normed = jnp.sum(
        grad_home.reshape(-1, model_width)[slot_index]
        .reshape(share_rows, top_count, model_width)
        .astype(jnp.float32),
        axis=1,
    )
    (grad_logit_float,) = gating_back(grad_gates)
    grad_logits = grad_logit_float.astype(jnp.bfloat16)
    grad_router = jnp.einsum("td,te->de", normed, grad_logits, preferred_element_type=jnp.float32)
    grad_normed = grad_normed + jnp.einsum(
        "te,de->td", grad_logits, router_weight, preferred_element_type=jnp.float32
    )
    grad_middle_part, grad_moe_gain = moe_norm_back(grad_normed)
    grad_middle = grad_out + grad_middle_part
    grad_branch = lax.all_gather(grad_middle.astype(jnp.bfloat16), "tensor", axis=0, tiled=True)
    again_rows = (
        lax.all_gather(q_weight, "dp", axis=0, tiled=True),
        lax.all_gather(k_weight, "dp", axis=0, tiled=True),
        lax.all_gather(v_weight, "dp", axis=0, tiled=True),
        lax.all_gather(out_weight, "dp", axis=0, tiled=True),
    )
    input_back = jnp.concatenate([again_rows[0], again_rows[1], again_rows[2]], axis=1)
    output_back = again_rows[3]
    grad_heads = (
        jnp.dot(grad_branch, output_back, preferred_element_type=jnp.float32)
        .astype(jnp.bfloat16)
        .reshape(tok_rows, local_heads, head_dim)
    )
    row_delta = jnp.sum(grad_heads.astype(jnp.float32) * head_out, axis=-1)
    key_rows, value_rows = (
        lax.all_gather(keys_local, "dp", axis=0, tiled=True),
        lax.all_gather(values_local, "dp", axis=0, tiled=True),
    )
    key_block = min(512, all_tokens)

    def key_step(grad_queries, block_number):
        offset = block_number * key_block
        key_piece = lax.dynamic_slice_in_dim(key_rows, offset, key_block, 0)
        value_piece = lax.dynamic_slice_in_dim(value_rows, offset, key_block, 0)
        allowed = visible(offset, key_block)[:, None, :]
        scores = (
            jnp.einsum("thd,nd->thn", queries, key_piece, preferred_element_type=jnp.float32)
            * score_scale
        )
        soft_weights = jnp.where(allowed, jnp.exp(scores - log_total[:, :, None]), 0.0)
        grad_weights = jnp.einsum(
            "thd,nd->thn", grad_heads, value_piece, preferred_element_type=jnp.float32
        )
        grad_scores = (soft_weights * (grad_weights - row_delta[:, :, None])).astype(jnp.bfloat16)
        grad_queries = (
            grad_queries
            + jnp.einsum("thn,nd->thd", grad_scores, key_piece, preferred_element_type=jnp.float32)
            * score_scale
        )
        grad_key_piece = (
            jnp.einsum("thn,thd->nd", grad_scores, queries, preferred_element_type=jnp.float32)
            * score_scale
        )
        grad_value_piece = jnp.einsum(
            "thn,thd->nd",
            soft_weights.astype(jnp.bfloat16),
            grad_heads,
            preferred_element_type=jnp.float32,
        )
        return (grad_queries, jnp.concatenate([grad_key_piece, grad_value_piece], axis=1))

    grad_queries, key_terms = lax.scan(
        key_step,
        jnp.zeros((tok_rows, local_heads, head_dim), jnp.float32),
        jnp.arange(all_tokens // key_block, dtype=jnp.int32),
    )
    key_grads = lax.psum_scatter(
        key_terms.reshape(all_tokens, 2 * head_dim).astype(jnp.bfloat16),
        "dp",
        scatter_dimension=0,
        tiled=True,
    ).astype(jnp.float32)
    grad_proj_float, grad_q_gain, grad_k_gain = prepare_back(
        (grad_queries, key_grads[:, :head_dim], key_grads[:, head_dim:])
    )
    grad_projected = grad_proj_float.astype(jnp.bfloat16)
    grad_hidden = jnp.einsum(
        "tc,dc->td", grad_projected, input_back, preferred_element_type=jnp.float32
    )
    grad_hidden_share = lax.psum_scatter(
        grad_hidden.astype(jnp.bfloat16), "tensor", scatter_dimension=0, tiled=True
    ).astype(jnp.float32)
    _, first_norm_back = jax.vjp(norm_rows, tokens_share, norm_gain_float)
    grad_tokens_part, grad_norm_gain = first_norm_back(grad_hidden_share)
    tokens_grad = grad_middle + grad_tokens_part
    input_part = jnp.einsum("td,tc->dc", hidden, grad_projected, preferred_element_type=jnp.float32)
    output_part = jnp.einsum("td,tc->dc", grad_branch, attended, preferred_element_type=jnp.float32)
    weight_share = lax.psum_scatter(
        jnp.concatenate([input_part, output_part], axis=1).astype(jnp.bfloat16),
        "dp",
        scatter_dimension=0,
        tiled=True,
    ).astype(jnp.float32)
    query_width = local_heads * head_dim
    grad_q_weight = weight_share[:, :query_width]
    grad_k_weight = weight_share[:, query_width : query_width + head_dim]
    grad_v_weight = weight_share[:, query_width + head_dim : query_width + 2 * head_dim]
    grad_out_weight = weight_share[:, query_width + 2 * head_dim :]
    small_sums = lax.psum(
        (grad_router, grad_norm_gain, grad_moe_gain, grad_q_gain, grad_k_gain), ("dp", "tensor")
    )
    return (
        layer_out,
        tokens_grad,
        small_sums[1],
        grad_q_weight,
        grad_k_weight,
        grad_v_weight,
        small_sums[3],
        small_sums[4],
        grad_out_weight,
        small_sums[2],
        small_sums[0],
        grad_gate_w[None],
        grad_up_w[None],
        grad_down[None],
    )


MESH = pl.DeviceIdType.MESH
HBM = pl.ANY
GATHER_FLANK = 384
REDUCE_FLANK = 256
ATTEND_FLANK = 256
OUT_GRAD_FLANK = 384
ATTEND_HALVES = True
BACK_HALVES = True


class Place:
    def __init__(self, depth):
        d = lax.axis_index("dp")
        t = lax.axis_index("tensor")
        self.depth = depth
        self.d, self.t = d, t
        self.z, self.x = d // 2, lax.rem(d, 2)
        self.y, self.c = t // 2, lax.rem(t, 2)
        self.next_to = {
            "x": (self.z * 2 + 1 - self.x, t),
            "y": (d, (1 - self.y) * 2 + self.c),
            "c": (d, self.y * 2 + 1 - self.c),
            "up": (d + 2, t),
            "down": (d - 2, t),
        }

    def block(self, z, fx=0, fy=0, fc=0):
        x = 1 - self.x if fx else self.x
        y = 1 - self.y if fy else self.y
        c = 1 - self.c if fc else self.c
        return (z * 2 + x) * 4 + y * 2 + c

    def at(self, dist, step):
        if dist == 0:
            step(self.z)
            return

        @pl.when(self.z >= dist)
        def _():
            step(self.z - dist)

        @pl.when(self.z + dist < self.depth)
        def _():
            step(self.z + dist)

    def greet(self, plane=False):
        barrier = pltpu.get_barrier_semaphore()

        def signal(to):
            pl.semaphore_signal(barrier, inc=1, device_id=self.next_to[to], device_id_type=MESH)

        if plane:
            groups = self.depth * 2
            for k in range(1, groups):
                to = (lax.rem(self.d + k, groups), self.t)
                pl.semaphore_signal(barrier, inc=1, device_id=to, device_id_type=MESH)
            signal("y")
            signal("c")
            pl.semaphore_wait(barrier, groups + 1)
            return
        for to in ("x", "y", "c"):
            signal(to)

        @pl.when(self.z > 0)
        def _():
            signal("down")

        @pl.when(self.z < self.depth - 1)
        def _():
            signal("up")

        above = (self.z < self.depth - 1).astype(jnp.int32)
        below = (self.z > 0).astype(jnp.int32)
        pl.semaphore_wait(barrier, 3 + above + below)

    def copy(self, src, dst, send, recv, to):
        return pltpu.make_async_remote_copy(
            src_ref=src,
            dst_ref=dst,
            send_sem=send,
            recv_sem=recv,
            device_id=self.next_to[to],
            device_id_type=MESH,
        )


class Gather:
    SEND, RECV = 11, 10

    def __init__(self, pos, own, out, send, recv, halves, cols=None):
        self.pos, self.own, self.out = pos, own, out
        self.send, self.recv = send, recv
        if cols is not None:
            self.own, self.out = own.at[:, cols], out.at[:, :, cols]
        rows = out.shape[1]
        self.h0 = pl.ds(0, rows // 2 if halves else rows)
        self.h1 = pl.ds(rows // 2, rows // 2) if halves else None
        self.rounds = pos.depth + 2
        self.seen = set()

    def link(self, src, dst, sends, recvs, zo, to):
        return self.pos.copy(src, dst, self.send.at[sends, zo], self.recv.at[recvs, zo], to)

    def col(self, zo):
        return self.out.at[self.pos.block(zo)]

    def src(self, zo, mine):
        return self.own if mine else self.col(zo)

    def up(self, zo, mine=False):
        return self.link(self.src(zo, mine), self.col(zo), 0, 0, zo, "up")

    def down(self, zo, mine=False):
        return self.link(self.src(zo, mine), self.col(zo), 1, 0, zo, "down")

    def to_x(self, zo, mine=False):
        return self.link(self.src(zo, mine), self.col(zo), 2, 1, zo, "x")

    def to_y(self, zo, mine=False):
        return self.link(self.src(zo, mine), self.col(zo), 3, 2, zo, "y")

    def to_c(self, zo, mine=False):
        return self.link(self.src(zo, mine), self.col(zo), 4, 5, zo, "c")

    def part(self, zo, fx, fy, rows):
        whole = self.out.at[self.pos.block(zo, fx, fy)]
        return whole if rows is None else whole.at[rows]

    def pass_on(self, zo, fx, fy, rows, sends, recvs, to):
        ref = self.part(zo, fx, fy, rows)
        return self.link(ref, ref, sends, recvs, zo, to)

    def x_to_y(self, zo):
        return self.pass_on(zo, 1, 0, self.h0, 5, 3, "y")

    def x_to_c(self, zo):
        return self.pass_on(zo, 1, 0, None, 6, 6, "c")

    def y_to_x(self, zo):
        return self.pass_on(zo, 0, 1, self.h1, 7, 4, "x")

    def y_to_c(self, zo):
        return self.pass_on(zo, 0, 1, None, 8, 7, "c")

    def far0_to_c(self, zo):
        return self.pass_on(zo, 1, 1, self.h0, 9, 8, "c")

    def far1_to_c(self, zo):
        return self.pass_on(zo, 1, 1, self.h1, 10, 9, "c")

    def along_z(self, zo, mine, what):
        z, depth = self.pos.z, self.pos.depth
        if mine:
            up, down = z < depth - 1, z > 0
        else:
            up, down = (zo < z) & (z < depth - 1), (zo > z) & (z > 0)

        @pl.when(up)
        def _():
            what(self.up(zo, mine))

        @pl.when(down)
        def _():
            what(self.down(zo, mine))

    def on_column(self, zo, mine=False):
        if not mine:
            self.up(zo).wait_recv()
        self.along_z(zo, mine, lambda c: c.start())
        self.to_x(zo, mine).start()
        self.to_y(zo, mine).start()
        self.to_c(zo, mine).start()

    def on_sides(self, zo):
        self.to_x(zo).wait_recv()
        self.x_to_y(zo).start()
        self.x_to_c(zo).start()
        self.to_y(zo).wait_recv()
        if self.h1 is not None:
            self.y_to_x(zo).start()
        self.y_to_c(zo).start()

    def on_far(self, zo):
        self.x_to_y(zo).wait_recv()
        self.far0_to_c(zo).start()
        if self.h1 is not None:
            self.y_to_x(zo).wait_recv()
            self.far1_to_c(zo).start()

    def start(self):
        self.on_column(self.pos.z, True)

    def round(self, r):
        if 1 <= r < self.pos.depth:
            self.pos.at(r, self.on_column)
        if 1 <= r <= self.pos.depth:
            self.pos.at(r - 1, self.on_sides)
        if 2 <= r <= self.pos.depth + 1:
            self.pos.at(r - 2, self.on_far)

    def from_core(self, zo, mine=False):
        copies = [self.to_c(zo, mine), self.x_to_c(zo), self.y_to_c(zo), self.far0_to_c(zo)]
        return copies if self.h1 is None else copies + [self.far1_to_c(zo)]

    def arrived(self, dist):
        self.seen.add(dist)
        self.pos.at(dist, lambda zo: [c.wait_recv() for c in self.from_core(zo)])

    def end_one(self, zo, mine=False, seen=False):
        arrivals = self.from_core(zo, mine)
        sends = [self.to_x(zo, mine), self.to_y(zo, mine), self.x_to_y(zo)] + arrivals
        if self.h1 is not None:
            sends.append(self.y_to_x(zo))
        if not seen:
            for c in arrivals:
                c.wait_recv()
        self.along_z(zo, mine, lambda c: c.wait_send())
        for c in sends:
            c.wait_send()

    def end(self):
        self.end_one(self.pos.z, True, 0 in self.seen)
        for r in range(1, self.pos.depth):
            self.pos.at(r, lambda zo: self.end_one(zo, False, r in self.seen))

    @staticmethod
    def sems(depth):
        return [pltpu.SemaphoreType.DMA((Gather.SEND, depth)), pltpu.SemaphoreType.DMA((Gather.RECV, depth))]


class SideGather:
    def __init__(self, pos, own, out, send, recv, side_send, side_recv, cols):
        self.pos, self.own, self.out = pos, own.at[:, cols], out.at[:, :, cols]
        self.send, self.recv = send, recv
        self.side_send, self.side_recv = side_send, side_recv
        rows = out.shape[1]
        self.half = (pl.ds(0, rows // 2), pl.ds(rows // 2, rows // 2))
        self.rounds = pos.depth + 2
        self.seen = set()

    @staticmethod
    def sems(depth):
        dma = pltpu.SemaphoreType.DMA
        return [dma((4, depth, 3)), dma((4, depth, 2)), dma((4,)), dma((4,))]

    def place(self, zo, k):
        return self.out.at[self.pos.block(zo, k // 2, k % 2)]

    def src(self, zo, k, mine):
        return self.own if mine and k == 0 else self.place(zo, k)

    def along(self, zo, k, way, mine=False):
        return self.pos.copy(
            self.src(zo, k, mine), self.place(zo, k), self.send.at[k, zo, way], self.recv.at[k, zo, 0], ("up", "down")[way]
        )

    def to_core(self, zo, k, mine=False):
        return self.pos.copy(self.src(zo, k, mine), self.place(zo, k), self.send.at[k, zo, 2], self.recv.at[k, zo, 1], "c")

    def across(self, k, to):
        z = self.pos.z
        if k < 2:
            src, dst = self.own, self.place(z, 0)
        else:
            src = dst = self.place(z, k - 1).at[self.half[k - 2]]
        return self.pos.copy(src, dst, self.side_send.at[k], self.side_recv.at[k], to)

    def on(self, zo, k, mine=False):
        self.along_z(zo, k, mine, lambda c: c.start())
        self.to_core(zo, k, mine).start()

    def along_z(self, zo, k, mine, what):
        z, depth = self.pos.z, self.pos.depth
        if mine:
            up, down = z < depth - 1, z > 0
        else:
            up, down = (zo < z) & (z < depth - 1), (zo > z) & (z > 0)

        @pl.when(up)
        def _():
            what(self.along(zo, k, 0, mine))

        @pl.when(down)
        def _():
            what(self.along(zo, k, 1, mine))

    def start(self):
        self.across(0, "x").start()
        self.across(1, "y").start()
        self.on(self.pos.z, 0, True)

    def on_far_height(self, zo):
        for k in range(4):
            self.along(zo, k, 0).wait_recv()
            self.on(zo, k)

    def round(self, r):
        z = self.pos.z
        if r == 1:
            self.across(0, "x").wait_recv()
            self.across(3, "y").start()
            self.on(z, 2, True)
            self.across(1, "y").wait_recv()
            self.across(2, "x").start()
            self.on(z, 1, True)
        if r == 2:
            self.across(2, "x").wait_recv()
            self.across(3, "y").wait_recv()
            self.on(z, 3, True)
        if 3 <= r <= self.pos.depth + 1:
            self.pos.at(r - 2, self.on_far_height)

    def arrived(self, dist):
        self.seen.add(dist)
        self.pos.at(dist, lambda zo: [self.to_core(zo, k).wait_recv() for k in range(4)])

    def end_one(self, zo, mine=False, seen=False):
        for k in range(4):
            if not seen:
                self.to_core(zo, k, mine).wait_recv()
            self.to_core(zo, k, mine).wait_send()
            self.along_z(zo, k, mine, lambda c: c.wait_send())

    def end(self):
        for k in range(4):
            self.across(k, "xyxy"[k]).wait_send()
        self.end_one(self.pos.z, True, 0 in self.seen)
        for r in range(1, self.pos.depth):
            self.pos.at(r, lambda zo: self.end_one(zo, False, r in self.seen))


class Reduce:
    SENDS = 16

    def __init__(self, pos, part, core, far, side, column, flank_z, flank_far, flank_side, send, recv, halves=True):
        self.pos, self.part = pos, part
        self.core, self.far, self.side, self.column = core, far, side, column
        self.flank_z, self.flank_far, self.flank_side = flank_z, flank_far, flank_side
        self.send, self.recv = send, recv
        rows, width = part.shape[1:]
        flank = flank_z.shape[-1] if len(flank_z.shape) == 5 else 0
        self.main, self.flank = pl.ds(0, width - flank), pl.ds(width - flank, flank)
        self.flanked = flank > 0
        self.half = (pl.ds(0, rows // 2), pl.ds(rows // 2, rows // 2)) if halves else (pl.ds(0, rows),)
        self.rounds = pos.depth + 2

    @staticmethod
    def scratch(depth, rows, width, halves=True, flank=0):
        b = jnp.bfloat16
        main = width - flank
        refs = [
            pltpu.VMEM((depth, 4, rows, width), b),
            pltpu.VMEM((depth, 2, rows // 2, main) if halves else (depth, 1, rows, main), b),
            pltpu.VMEM((depth, 2, rows, main), b),
            pltpu.VMEM((depth, 2, rows, main), b),
        ]
        refs += [
            pltpu.VMEM((depth, 2, 4, rows, flank) if flank else (8, 128), b),
            pltpu.VMEM((2, rows // 2, flank) if flank else (8, 128), b),
            pltpu.VMEM((2, rows, flank) if flank else (8, 128), b),
        ]
        dma = pltpu.SemaphoreType.DMA
        return refs + [dma((Reduce.SENDS, depth)), dma((Reduce.SENDS, depth))]

    SCRATCH = 9

    def link(self, src, dst, k, zo, to):
        return self.pos.copy(src, dst, self.send.at[k, zo], self.recv.at[k, zo], to)

    def to_core(self, zo, fx, fy):
        k = fx * 2 + fy
        return self.link(self.part.at[self.pos.block(zo, fx, fy, 1)], self.core.at[zo, k], k, zo, "c")

    def far_to(self, zo, k):
        src = self.core.at[zo, 3, self.half[k], self.main]
        return self.link(src, self.far.at[zo, k], 4 + k, zo, ("y", "x")[k])

    def side_to(self, zo, k):
        return self.link(self.core.at[zo, 2 - k, :, self.main], self.side.at[zo, k], 6 + k, zo, ("x", "y")[k])

    def down(self, zo):
        return self.link(self.core.at[zo, 0, :, self.main], self.column.at[zo, 0], 8, zo, "down")

    def up(self, zo):
        return self.link(self.core.at[zo, 0, :, self.main], self.column.at[zo, 1], 9, zo, "up")

    def flank_down(self, zo):
        return self.link(self.core.at[zo, :, :, self.flank], self.flank_z.at[zo, 0], 10, zo, "down")

    def flank_up(self, zo):
        return self.link(self.core.at[zo, :, :, self.flank], self.flank_z.at[zo, 1], 11, zo, "up")

    def flank_far_to(self, k):
        z = self.pos.z
        rows = self.core.shape[2] // 2
        src = self.core.at[z, 3, pl.ds(k * rows, rows), self.flank]
        return self.link(src, self.flank_far.at[k], 12 + k, z, ("y", "x")[k])

    def flank_side_to(self, k):
        z = self.pos.z
        return self.link(self.core.at[z, 2 - k, :, self.flank], self.flank_side.at[k], 14 + k, z, ("x", "y")[k])

    def start_one(self, zo):
        for fx, fy in ((1, 1), (1, 0), (0, 1), (0, 0)):
            self.to_core(zo, fx, fy).start()

    def start(self):
        for dist in reversed(range(self.pos.depth)):
            self.pos.at(dist, self.start_one)

    def total(self, *refs):
        f = refs[0][...].astype(jnp.float32)
        for r in refs[1:]:
            f = f + r[...].astype(jnp.float32)
        return f

    def add(self, here, *refs):
        here[...] = self.total(here, *refs).astype(here.dtype)

    def on_core(self, zo):
        for fx, fy in ((1, 1), (1, 0), (0, 1), (0, 0)):
            k = fx * 2 + fy
            self.to_core(zo, fx, fy).wait_recv()
            self.add(self.core.at[zo, k], self.part.at[self.pos.block(zo, fx, fy)])
            if k == 3:
                for h in range(len(self.half)):
                    self.far_to(zo, h).start()

    def from_farther(self, zo, down, up, take):
        z, depth = self.pos.z, self.pos.depth

        @pl.when((zo <= z) & (z < depth - 1))
        def _():
            down(zo).wait_recv()
            take(0)

        @pl.when((zo >= z) & (z > 0))
        def _():
            up(zo).wait_recv()
            take(1)

    def to_nearer(self, zo, down, up, what):
        @pl.when(zo < self.pos.z)
        def _():
            what(down(zo))

        @pl.when(zo > self.pos.z)
        def _():
            what(up(zo))

    def flank_along_z(self, zo):
        here = self.core.at[zo, :, :, self.flank]
        self.from_farther(zo, self.flank_down, self.flank_up, lambda k: self.add(here, self.flank_z.at[zo, k]))
        self.to_nearer(zo, self.flank_down, self.flank_up, lambda c: c.start())

    def flank_far_start(self):
        for k in range(2):
            self.flank_far_to(k).start()

    def flank_on_far(self):
        z, rows = self.pos.z, self.core.shape[2] // 2
        for k in range(2):
            self.flank_far_to(k).wait_recv()
            self.add(self.core.at[z, 2 - k, pl.ds(k * rows, rows), self.flank], self.flank_far.at[k])
            self.flank_side_to(k).start()

    def flank_on_sides(self):
        self.flank_side_to(0).wait_recv()
        self.flank_side_to(1).wait_recv()
        here = self.core.at[self.pos.z, 0, :, self.flank]
        self.out[:, self.flank] = self.total(here, self.flank_side.at[0], self.flank_side.at[1])

    def on_far(self, zo):
        for k in range(2):
            if k < len(self.half):
                self.far_to(zo, k).wait_recv()
                self.add(self.core.at[zo, 2 - k, self.half[k], self.main], self.far.at[zo, k])
            self.side_to(zo, k).start()

    def on_sides(self, zo, mine=False):
        self.side_to(zo, 0).wait_recv()
        self.side_to(zo, 1).wait_recv()
        here = self.core.at[zo, 0, :, self.main]
        summed = self.total(here, self.side.at[zo, 0], self.side.at[zo, 1])
        if mine:
            self.out[:, self.main] = summed

            def take(k):
                self.out[:, self.main] += self.column[zo, k].astype(jnp.float32)

            self.from_farther(zo, self.down, self.up, take)
            return
        here[...] = summed.astype(here.dtype)
        self.from_farther(zo, self.down, self.up, lambda k: self.add(here, self.column.at[zo, k]))
        self.to_nearer(zo, self.down, self.up, lambda c: c.start())

    def round(self, r):
        depth = self.pos.depth
        for s in range(3):
            dist = depth - 1 - (r - s)
            if not 0 <= dist < depth:
                continue
            if s == 0:
                self.pos.at(dist, self.on_core)
                if self.flanked:
                    self.pos.at(dist, self.flank_along_z)
            elif s == 1:
                self.pos.at(dist, self.on_far)
            elif dist:
                self.pos.at(dist, self.on_sides)
            else:
                self.on_sides(self.pos.z, True)
        if self.flanked and r == depth - 1:
            self.flank_far_start()
        if self.flanked and r == depth:
            self.flank_on_far()
        if self.flanked and r == depth + 1:
            self.flank_on_sides()

    def end_one(self, zo):
        for fx in range(2):
            for fy in range(2):
                self.to_core(zo, fx, fy).wait_send()
        for k in range(len(self.half)):
            self.far_to(zo, k).wait_send()
        for k in range(2):
            self.side_to(zo, k).wait_send()
        self.to_nearer(zo, self.down, self.up, lambda c: c.wait_send())
        if self.flanked:
            self.to_nearer(zo, self.flank_down, self.flank_up, lambda c: c.wait_send())

    def end(self):
        for r in range(self.pos.depth):
            self.pos.at(r, self.end_one)
        if self.flanked:
            for k in range(2):
                self.flank_far_to(k).wait_send()
                self.flank_side_to(k).wait_send()


class WideGather:
    def __init__(self, pos, own, out, flank, refs):
        main = out.shape[2] - flank
        self.parts = (
            SideGather(pos, own, out, *refs[2:6], pl.ds(main, flank)),
            Gather(pos, own, out, *refs[0:2], True, pl.ds(0, main)),
        )
        self.rounds = self.parts[0].rounds

    REFS = 6

    @staticmethod
    def sems(depth):
        return Gather.sems(depth) + SideGather.sems(depth)

    def start(self):
        for p in self.parts:
            p.start()

    def round(self, r):
        for p in self.parts:
            p.round(r)

    def arrived(self, dist):
        for p in self.parts:
            p.arrived(dist)

    def end(self):
        for p in self.parts:
            p.end()


class PlaneGather:
    SEND, RECV = 3, 2

    def __init__(self, pos, own, dst, send, recv):
        self.pos, self.own, self.dst = pos, own, dst
        self.send, self.recv = send, recv
        self.rounds = pos.depth

    def link(self, zo, mine, sends, recvs, to):
        dst = self.dst(zo * 2 + self.pos.x)
        return self.pos.copy(self.own if mine else dst, dst, self.send.at[sends, zo], self.recv.at[recvs, zo], to)

    def along_z(self, zo, mine, what):
        z, depth = self.pos.z, self.pos.depth
        if mine:
            up, down = z < depth - 1, z > 0
        else:
            up, down = (zo < z) & (z < depth - 1), (zo > z) & (z > 0)

        @pl.when(up)
        def _():
            what(self.link(zo, mine, 0, 0, "up"))

        @pl.when(down)
        def _():
            what(self.link(zo, mine, 1, 0, "down"))

    def on_column(self, zo, mine=False):
        if not mine:
            self.link(zo, False, 0, 0, "up").wait_recv()
        self.along_z(zo, mine, lambda c: c.start())
        self.link(zo, mine, 2, 1, "x").start()

    def start(self):
        self.on_column(self.pos.z, True)

    def round(self, r):
        if 1 <= r < self.pos.depth:
            self.pos.at(r, self.on_column)

    def end_one(self, zo, mine=False):
        across = self.link(zo, mine, 2, 1, "x")
        across.wait_recv()
        self.along_z(zo, mine, lambda c: c.wait_send())
        across.wait_send()

    def end(self):
        self.end_one(self.pos.z, True)
        for r in range(1, self.pos.depth):
            self.pos.at(r, self.end_one)

    @staticmethod
    def sems(depth):
        return [pltpu.SemaphoreType.DMA((PlaneGather.SEND, depth)), pltpu.SemaphoreType.DMA((PlaneGather.RECV, depth))]


class PlaneReduce:
    def __init__(self, pos, part, out, across, column, send, recv):
        self.pos, self.part, self.out = pos, part, out
        self.across, self.column = across, column
        self.send, self.recv = send, recv
        self.rounds = pos.depth

    @staticmethod
    def scratch(depth, rows, width):
        b = jnp.bfloat16
        return [
            pltpu.VMEM((depth, rows, width), b),
            pltpu.VMEM((depth, 2, rows, width), b),
            pltpu.SemaphoreType.DMA((3, depth)),
            pltpu.SemaphoreType.DMA((3, depth)),
        ]

    def to_x(self, zo):
        src = self.part(zo * 2 + 1 - self.pos.x)
        return self.pos.copy(src, self.across.at[zo], self.send.at[0, zo], self.recv.at[0, zo], "x")

    def down(self, zo):
        return self.pos.copy(
            self.across.at[zo], self.column.at[zo, 0], self.send.at[1, zo], self.recv.at[1, zo], "down"
        )

    def up(self, zo):
        return self.pos.copy(
            self.across.at[zo], self.column.at[zo, 1], self.send.at[2, zo], self.recv.at[2, zo], "up"
        )

    def start(self):
        for dist in reversed(range(self.pos.depth)):
            self.pos.at(dist, lambda zo: self.to_x(zo).start())

    def on_column(self, zo):
        z, depth = self.pos.z, self.pos.depth
        f32 = jnp.float32
        here = self.across.at[zo]
        self.to_x(zo).wait_recv()
        here[...] = (here[...].astype(f32) + self.part(zo * 2 + self.pos.x)[...].astype(f32)).astype(here.dtype)

        @pl.when((zo < z) & (z < depth - 1))
        def _():
            self.down(zo).wait_recv()
            here[...] = (here[...].astype(f32) + self.column[zo, 0].astype(f32)).astype(here.dtype)

        @pl.when((zo > z) & (z > 0))
        def _():
            self.up(zo).wait_recv()
            here[...] = (here[...].astype(f32) + self.column[zo, 1].astype(f32)).astype(here.dtype)

        @pl.when(zo < z)
        def _():
            self.down(zo).start()

        @pl.when(zo > z)
        def _():
            self.up(zo).start()

    def on_own(self):
        z, depth = self.pos.z, self.pos.depth
        f32 = jnp.float32
        self.to_x(z).wait_recv()
        self.out[...] = self.across[z].astype(f32) + self.part(z * 2 + self.pos.x)[...].astype(f32)

        @pl.when(z < depth - 1)
        def _():
            self.down(z).wait_recv()
            self.out[...] += self.column[z, 0].astype(f32)

        @pl.when(z > 0)
        def _():
            self.up(z).wait_recv()
            self.out[...] += self.column[z, 1].astype(f32)

    def round(self, r):
        dist = self.pos.depth - 1 - r
        if dist > 0:
            self.pos.at(dist, self.on_column)
        elif dist == 0:
            self.on_own()

    def end_one(self, zo):
        self.to_x(zo).wait_send()

        @pl.when(zo < self.pos.z)
        def _():
            self.down(zo).wait_send()

        @pl.when(zo > self.pos.z)
        def _():
            self.up(zo).wait_send()

    def end(self):
        for r in range(self.pos.depth):
            self.pos.at(r, self.end_one)


class Exchange:
    def __init__(self, pos, piece, place, send, recv, local):
        self.pos, self.piece, self.place = pos, piece, place
        self.send, self.recv, self.local = send, recv, local
        self.groups = pos.depth * 2
        self.rounds = 0

    @staticmethod
    def sems(depth):
        n = depth * 2 - 1
        return [pltpu.SemaphoreType.DMA((n,)), pltpu.SemaphoreType.DMA((n,)), pltpu.SemaphoreType.DMA]

    def peer(self, k):
        return lax.rem(self.pos.d + k, self.groups)

    def copy(self, k):
        p = self.peer(k)
        return pltpu.make_async_remote_copy(
            src_ref=self.piece(p),
            dst_ref=self.place(self.pos.d),
            send_sem=self.send.at[k - 1],
            recv_sem=self.recv.at[k - 1],
            device_id=(p, self.pos.t),
            device_id_type=MESH,
        )

    def here(self):
        return pltpu.make_async_copy(self.piece(self.pos.d), self.place(self.pos.d), self.local)

    def start(self):
        self.here().start()
        for k in range(1, self.groups):
            self.copy(k).start()

    def round(self, r):
        pass

    def end(self):
        self.here().wait()
        for k in range(1, self.groups):
            self.copy(k).wait()


def drive(*parts):
    for p in parts:
        p.start()
    for r in range(max(p.rounds for p in parts)):
        for p in parts:
            p.round(r)
    for p in parts:
        p.end()


def params(number, vmem=None):
    return pltpu.CompilerParams(collective_id=number, has_side_effects=True, vmem_limit_bytes=vmem)


def rows_of(ref, p, rows):
    return ref.at[pl.ds(p * rows, rows)]


def cols_of(ref, p, cols):
    return ref.at[:, pl.ds(pl.multiple_of(p * cols, cols), cols)]


def part_of(ref, p, rows, first, cols):
    return ref.at[pl.ds(p * rows, rows), pl.ds(first, cols)]


def dot(a, b):
    return jnp.dot(a, b, preferred_element_type=jnp.float32)


def dot_nt(a, b):
    return lax.dot_general(a, b, (((1,), (1,)), ((), ())), preferred_element_type=jnp.float32)


def dot_tn(a, b):
    return lax.dot_general(a, b, (((0,), (0,)), ((), ())), preferred_element_type=jnp.float32)


def loop(count, step):
    lax.fori_loop(0, count, lambda i, _: (step(i), 0)[1], 0)


def norm_back(values, gain, grad):
    r = lax.rsqrt(jnp.mean(values * values, axis=-1, keepdims=True) + EPS)
    unit = values * r
    scaled = grad * gain
    return r * (scaled - unit * jnp.mean(scaled * unit, axis=-1, keepdims=True)), grad * unit


def experts(depth, number, normed, all_grad, all_named, middle, moe_gain, router_t, w_gate, w_up, w_down):
    f32, bf = jnp.float32, jnp.bfloat16
    rows, width = normed.shape
    devices = depth * 8
    plane_rows = rows * 8
    picks = plane_rows // 2
    slots = depth * picks
    ff = w_gate.shape[1]
    lanes = all_named.shape[2]
    count = router_t.shape[0]
    wide = width + lanes

    def body(
        n_ref, g_ref, named_hbm, mid_ref, gain_ref, router_ref, wg_hbm, wu_hbm, wd_hbm,
        layer_out, grad_middle, grad_block, gain_grad, n_all, x_out, gret_out, inner_out, gboth_out,
        wg, wu, wd, nb, gb, ob, part, xin, gret, ret, inner, gboth, act_a, act_u, gates, out_sum, grad_sum,
        named, select_t, router_wide, gain_row,
        w_sem, own_sem, all_sem, keep_sem, *rest,
    ):
        pos = Place(depth)
        expert = pos.block(pos.z)
        loads = [
            pltpu.make_async_copy(src, dst, w_sem.at[i])
            for i, (src, dst) in enumerate(((wg_hbm, wg), (wu_hbm, wu), (wd_hbm, wd), (named_hbm, named)))
        ]
        own = [
            pltpu.make_async_copy(n_ref, nb.at[expert], own_sem.at[0]),
            pltpu.make_async_copy(g_ref, gb, own_sem.at[1]),
        ]
        for c in own + loads:
            c.start()
        pos.greet()
        g_normed = WideGather(pos, n_ref, nb, GATHER_FLANK, rest[0:6])
        r_out = Reduce(pos, ob, *rest[6:15])
        r_grad = Reduce(pos, part, *rest[15:24])
        r_out.out, r_grad.out = out_sum, grad_sum

        def plane(ref, z):
            return ref[pl.ds(z * 8, 8)].reshape(plane_rows, ref.shape[2])

        def picked(z):
            return pl.ds(pl.multiple_of(z * picks, picks), picks)

        here = lax.broadcasted_iota(jnp.int32, (plane_rows, lanes), 1) == expert

        def choose(z):
            names = plane(named, z)
            ones = names.astype(f32)
            above = lax.broadcasted_iota(jnp.int32, (plane_rows, plane_rows), 0)
            upto = lax.broadcasted_iota(jnp.int32, (plane_rows, plane_rows), 1) <= above
            counts = dot(upto.astype(f32).astype(bf), names)
            place = jnp.sum(jnp.where(here, counts * ones, 0.0), axis=1, keepdims=True) - 1.0
            pick = lax.broadcasted_iota(jnp.int32, (plane_rows, picks), 1).astype(f32)
            select_t[z] = jnp.where(place == pick, 1.0, 0.0).astype(bf)

        def take(z):
            tok = plane(nb, z)
            logits = dot_nt(tok, router_wide[...])
            chosen = plane(named, z).astype(f32) > 0
            top = jnp.max(jnp.where(chosen, logits, -1e30), axis=1, keepdims=True)
            raised = jnp.where(chosen, jnp.exp(jnp.minimum(logits - top, 0.0)), 0.0)
            gates[z] = raised / jnp.sum(raised, axis=1, keepdims=True)
            xin[picked(z), :] = dot_tn(select_t[z], tok).astype(bf)

        near = pos.z // 2
        apart = 1 - near

        def in_pair(h):
            return pl.ds(pl.multiple_of(h * 2 * picks, 2 * picks), 2 * picks)

        def both(h, step):
            loop(2, lambda j: step(2 * h + j))

        def forward(h):
            x = xin[in_pair(h), :]
            a = dot(x, wg[...])
            u = dot(x, wu[...])
            act_a[in_pair(h), :] = a
            act_u[in_pair(h), :] = u
            inner[in_pair(h), :] = (a / (1.0 + jnp.exp(-a)) * u).astype(bf)

        def produce(h):
            ret[in_pair(h), :] = dot(inner[in_pair(h), :], wd[...]).astype(bf)

        def spread(z):
            gate = gates[z]
            mine = jnp.sum(jnp.where(here, gate, 0.0), axis=1, keepdims=True)
            g = plane(gb, z).astype(f32)
            gret[picked(z), :] = dot_tn(select_t[z], (mine * g).astype(bf)).astype(bf)
            back = dot(select_t[z], ret[picked(z), :])
            ob[pl.ds(z * 8, 8)] = (mine * back).astype(bf).reshape(8, rows, width)
            summed = jnp.sum(g * back, axis=1, keepdims=True)
            logit = gate * (jnp.where(here, 1.0, 0.0) - mine) * summed
            part[pl.ds(z * 8, 8), :, pl.ds(width, lanes)] = logit.astype(bf).reshape(8, rows, lanes)

        def backward(h):
            gi = dot_nt(gret[in_pair(h), :], wd[...])
            a = act_a[in_pair(h), :]
            s = 1.0 / (1.0 + jnp.exp(-a))
            gboth[in_pair(h), pl.ds(0, ff)] = (gi * act_u[in_pair(h), :] * (s + a * s * (1.0 - s))).astype(bf)
            gboth[in_pair(h), pl.ds(ff, ff)] = (gi * (a * s)).astype(bf)

        def inputs_back(h):
            by_gate, by_up = gboth[in_pair(h), pl.ds(0, ff)], gboth[in_pair(h), pl.ds(ff, ff)]
            ret[in_pair(h), :] = (dot_nt(by_gate, wg[...]) + dot_nt(by_up, wu[...])).astype(bf)

        def scatter(z):
            back = dot(select_t[z], ret[picked(z), :]).astype(bf)
            part[pl.ds(z * 8, 8), :, pl.ds(0, width)] = back.reshape(8, rows, width)
            r_grad.start_one(z)

        g_normed.start()
        as_row(gain_ref, gain_row)
        router_wide[...] = jnp.zeros(router_wide.shape, bf)
        router_wide[pl.ds(0, count), :] = router_ref[...]
        loads[3].wait()
        loop(depth, choose)
        for r in range(1, 4):
            g_normed.round(r)
        own[0].wait()
        g_normed.arrived(0)
        g_normed.arrived(1)
        both(near, take)
        g_normed.round(4)
        loads[0].wait()
        loads[1].wait()
        forward(near)
        g_normed.round(5)
        loads[2].wait()
        produce(near)
        own[1].wait()
        both(near, spread)
        for dist in range(2, depth):
            g_normed.arrived(dist)
        both(apart, take)
        g_normed.end()
        keep = pltpu.make_async_copy(nb, n_all, all_sem)
        keep.start()
        forward(apart)
        produce(apart)
        both(apart, spread)
        r_out.start()
        backward(apart)
        r_out.round(0)
        inputs_back(apart)
        for dist in reversed(range(2, depth)):
            pos.at(dist, scatter)
        r_grad.round(0)
        r_out.round(1)
        backward(near)
        r_grad.round(1)
        r_out.round(2)
        inputs_back(near)
        for dist in reversed(range(2)):
            pos.at(dist, scatter)
        kept = [
            pltpu.make_async_copy(src, dst, keep_sem.at[i])
            for i, (src, dst) in enumerate(((xin, x_out), (gret, gret_out), (inner, inner_out), (gboth, gboth_out)))
        ]
        for c in kept:
            c.start()
        for r in range(3, r_out.rounds):
            r_grad.round(r - 1)
            r_out.round(r)
        r_grad.round(r_out.rounds - 1)
        keep.wait()
        mid = mid_ref[...]
        layer_out[...] = (mid + out_sum[...]).astype(bf)
        logit = grad_sum[:, pl.ds(width, lanes)].astype(bf)
        change, by_gain = norm_back(mid, gain_row[...], grad_sum[:, pl.ds(0, width)] + dot(logit, router_wide[...]))
        gain_grad[...] = jnp.sum(by_gain, axis=0, keepdims=True)
        change = gb[expert].astype(f32) + change
        grad_middle[...] = change
        grad_block[:, pl.ds(0, width)] = change.astype(bf)
        grad_block[:, pl.ds(width, lanes)] = logit
        for c in kept:
            c.wait()
        r_out.end()
        r_grad.end()

    vmem, hbm = pl.BlockSpec(memory_space=pltpu.VMEM), pl.BlockSpec(memory_space=HBM)
    dma = pltpu.SemaphoreType.DMA
    shape = jax.ShapeDtypeStruct
    return pl.pallas_call(
        body,
        out_shape=[
            shape((rows, width), bf),
            shape((rows, width), f32),
            shape((rows, wide), bf),
            shape((1, width), f32),
            shape((devices, rows, width), bf),
            shape((slots, width), bf),
            shape((slots, width), bf),
            shape((slots, ff), bf),
            shape((slots, 2 * ff), bf),
        ],
        in_specs=[hbm] * 3 + [vmem] * 3 + [hbm] * 3,
        out_specs=[vmem] * 4 + [hbm] * 5,
        scratch_shapes=[
            pltpu.VMEM((width, ff), bf),
            pltpu.VMEM((width, ff), bf),
            pltpu.VMEM((ff, width), bf),
            pltpu.VMEM((devices, rows, width), bf),
            pltpu.VMEM((devices, rows, width), bf),
            pltpu.VMEM((devices, rows, width), bf),
            pltpu.VMEM((devices, rows, wide), bf),
            pltpu.VMEM((slots, width), bf),
            pltpu.VMEM((slots, width), bf),
            pltpu.VMEM((slots, width), bf),
            pltpu.VMEM((slots, ff), bf),
            pltpu.VMEM((slots, 2 * ff), bf),
            pltpu.VMEM((slots, ff), f32),
            pltpu.VMEM((slots, ff), f32),
            pltpu.VMEM((depth, plane_rows, lanes), f32),
            pltpu.VMEM((rows, width), f32),
            pltpu.VMEM((rows, wide), f32),
            pltpu.VMEM((devices, rows, lanes), bf),
            pltpu.VMEM((depth, plane_rows, picks), bf),
            pltpu.VMEM((lanes, width), bf),
            pltpu.VMEM((1, width), f32),
            dma((4,)),
            dma((2,)),
            dma,
            dma((5,)),
        ]
        + WideGather.sems(depth)
        + Reduce.scratch(depth, rows, width, flank=REDUCE_FLANK)
        + Reduce.scratch(depth, rows, wide, flank=REDUCE_FLANK),
        compiler_params=params(number, 60 * 2**20),
        name="experts",
    )(normed, all_grad, all_named, middle, moe_gain, router_t, w_gate, w_up, w_down)


def finish(pairs, grad_q, grad_o, as_they_are):
    f32 = jnp.float32
    xin, gret, inner, gboth = pairs
    slots, width = xin.shape
    ff = inner.shape[1]
    steps = width // 512
    w_rows, w_cols = grad_q.shape
    n = len(as_they_are)

    def body(x, g, i, gg, q, o, *refs):
        given, (wg, wu, wd, wq, wo), same, turned = refs[:n], refs[n : n + 5], refs[n + 5 : 2 * n + 5], refs[2 * n + 5]

        @pl.when(pl.program_id(0) == 0)
        def _():
            turned[...] = i[...].T

        both = dot_tn(x[...], gg[...])
        wg[...] = both[:, :ff]
        wu[...] = both[:, ff:]
        wd[...] = dot(turned[...], g[...])
        wq[...] = q[...].astype(f32)
        wo[...] = o[...].astype(f32)

        @pl.when(pl.program_id(0) == 0)
        def _():
            for src, dst in zip(given, same):
                dst[...] = src[...]

    whole = pl.BlockSpec((slots, ff), lambda s: (0, 0))
    tall = pl.BlockSpec((slots, 512), lambda s: (0, s))
    part = pl.BlockSpec((w_rows, w_cols // steps), lambda s: (0, s))
    same = [pl.BlockSpec(a.shape, lambda s: (0, 0)) for a in as_they_are]
    shape = jax.ShapeDtypeStruct
    return pl.pallas_call(
        body,
        grid=(steps,),
        out_shape=[shape((width, ff), f32)] * 2
        + [shape((ff, width), f32)]
        + [shape((w_rows, w_cols), f32)] * 2
        + [shape(a.shape, a.dtype) for a in as_they_are],
        in_specs=[tall, tall, whole, pl.BlockSpec((slots, 2 * ff), lambda s: (0, 0)), part, part] + same,
        out_specs=[pl.BlockSpec((512, ff), lambda s: (s, 0))] * 2
        + [pl.BlockSpec((ff, 512), lambda s: (0, s)), part, part]
        + same,
        scratch_shapes=[pltpu.VMEM((ff, slots), xin.dtype)],
        compiler_params=pltpu.CompilerParams(vmem_limit_bytes=62 * 2**20),
        name="finish",
    )(*pairs, grad_q, grad_o, *as_they_are)


def as_row(ref, row):
    for i in range(ref.shape[0]):
        row[:, pl.ds(i * 128, 128)] = ref[pl.ds(i, 1), :].astype(jnp.float32)


def turn(u, cosine, sine):
    return u * cosine + pltpu.roll(u, u.shape[1] // 2, 1) * sine


def attend(depth, number, tokens, routes_t, out_grad, q_weight, k_weight, v_weight, out_weight, gains, frequency, docs):
    f32, bf = jnp.float32, jnp.bfloat16
    norm_gain, q_gain, k_gain, moe_gain = gains
    devices = depth * 8
    rows, width = tokens.shape[0] // 4, tokens.shape[1]
    w_rows, head = k_weight.shape
    total = devices * rows
    plane_rows = total // depth
    scale = head ** (-0.5)

    def body(
        tok, route, grad, wq, wk, wv, wo, ng, qg, kg, mg, freq, drow,
        middle, normed, all_named, all_grad, all_tok, hidden_out, wi_out, wo_out, proj_out, q_out, k_out, v_out, head_out,
        total_out, cos_out, sin_out,
        projected, queries, keys, values, heads, totals, cosines, sines, tb, hb, w_in, w_o, part, branch, doc, home, norm_row, moe_row, route_wide, names, own_sem, keep_sem, *rest,
    ):
        pos = Place(depth)
        device = pos.block(pos.z)
        share = tok.at[pl.ds(pl.multiple_of(pos.t * rows, rows), rows)]
        route_wide[...] = jnp.full(route_wide.shape, -1, jnp.int32)
        route_wide[pl.ds(0, route.shape[0]), pl.ds(0, rows)] = route[...]
        one = lax.broadcasted_iota(jnp.int32, (128, 128), 0)
        hits = jnp.zeros((128, 128), f32)
        for k in range(route.shape[0]):
            hits += jnp.where(route_wide[pl.ds(k, 1), :] == one, 1.0, 0.0)
        names[...] = hits.T[:rows].astype(bf)
        own = [
            pltpu.make_async_copy(src, dst, own_sem.at[i])
            for i, (src, dst) in enumerate(
                (
                    (names, all_named.at[device]),
                    (share, tb.at[device]),
                    (wk, part_of(w_in, pos.d, w_rows, head, head)),
                    (wv, part_of(w_in, pos.d, w_rows, 2 * head, head)),
                    (share, home),
                    (grad, all_grad.at[device]),
                )
            )
        ]
        for c in own:
            c.start()
        pos.greet(plane=True)
        g_k = PlaneGather(pos, wk, lambda p: part_of(w_in, p, w_rows, head, head), *rest[0:2])
        g_v = PlaneGather(pos, wv, lambda p: part_of(w_in, p, w_rows, 2 * head, head), *rest[2:4])
        g_tok = Gather(pos, share, tb, *rest[4:6], False)
        g_names = Gather(pos, names, all_named, *rest[6:8], False)
        x_q = Exchange(pos, lambda p: cols_of(wq, p, head), lambda p: part_of(w_in, p, w_rows, 0, head), *rest[8:11])
        x_o = Exchange(pos, lambda p: cols_of(wo, p, head), lambda p: rows_of(w_o, p, w_rows), *rest[11:14])
        red = Reduce(pos, part, *rest[14:23], halves=ATTEND_HALVES)
        red.out = branch
        g_grad = WideGather(pos, grad, all_grad, OUT_GRAD_FLANK, rest[23:29])

        def span(z):
            return pl.ds(pl.multiple_of(z * plane_rows, plane_rows), plane_rows)

        def angle(z):
            place = lax.broadcasted_iota(jnp.int32, (plane_rows, total), 0) + z * plane_rows
            other = lax.broadcasted_iota(jnp.int32, (plane_rows, total), 1)
            all_docs = drow[...].astype(f32)
            docs_here = jnp.sum(jnp.where(other == place, all_docs, 0.0), axis=1, keepdims=True)
            doc[span(z), :] = jnp.broadcast_to(docs_here, (plane_rows, head))
            before = jnp.where((other < place) & (all_docs == docs_here), 1.0, 0.0)
            turned = jnp.sum(before, axis=1, keepdims=True) * freq[...]
            cosines[span(z), :] = jnp.cos(turned)
            sign = jnp.where(lax.broadcasted_iota(jnp.int32, (plane_rows, head), 1) < head // 2, -1.0, 1.0)
            sines[span(z), :] = jnp.sin(turned) * sign

        def normalise(z):
            t = tb[pl.ds(z * 8, 8)].reshape(plane_rows, width).astype(f32)
            r = lax.rsqrt(jnp.mean(t * t, axis=1, keepdims=True) + EPS)
            hb[pl.ds(z * 8, 8)] = (t * r * norm_row[...]).astype(bf).reshape(8, rows, width)

        def project(z):
            p = dot(hb[pl.ds(z * 8, 8)].reshape(plane_rows, width), w_in[...])
            projected[span(z), :] = p
            for ref, first, gain in ((queries, 0, qg), (keys, head, kg)):
                u = p[:, first : first + head]
                u = u * lax.rsqrt(jnp.mean(u * u, axis=1, keepdims=True) + EPS) * gain[...].astype(f32)
                ref[span(z), :] = turn(u, cosines[span(z), :], sines[span(z), :]).astype(bf)
            values[span(z), :] = p[:, 2 * head :].astype(bf)

        def attention(z):
            place = lax.broadcasted_iota(jnp.int32, (plane_rows, total), 0) + z * plane_rows
            allowed = (lax.broadcasted_iota(jnp.int32, (plane_rows, total), 1) <= place) & (
                doc[span(z), pl.ds(0, 1)] == drow[...].astype(f32)
            )
            s = jnp.where(allowed, dot_nt(queries[span(z), :], keys[...]) * scale, -1e30)
            top = jnp.max(s, axis=1, keepdims=True)
            w = jnp.exp(s - top)
            mass = jnp.sum(w, axis=1, keepdims=True)
            out = dot(w.astype(bf), values[...]) / mass
            heads[span(z), :] = out
            totals[span(z), :] = jnp.broadcast_to(top + jnp.log(mass), (plane_rows, head))

        def spread(z):
            a = heads[span(z), :].astype(bf)
            part[pl.ds(z * 8, 8)] = dot_nt(a, w_o[...]).astype(bf).reshape(8, rows, width)
            red.start_one(z)

        kept = []

        def keep(src, dst):
            kept.append(pltpu.make_async_copy(src, dst, keep_sem.at[len(kept)]))
            kept[-1].start()

        g_tok.start()
        as_row(ng, norm_row)
        as_row(mg, moe_row)
        loop(depth, angle)
        keep(cosines, cos_out)
        keep(sines, sin_out)
        for c in own:
            c.wait()
        for r in range(1, g_tok.rounds):
            g_tok.round(r)
            if r == 1:
                g_k.start()
                g_v.start()
            else:
                g_k.round(r - 1)
                g_v.round(r - 1)
            if r == 3:
                x_q.start()
            if r == 5:
                x_o.start()
            if r >= 3:
                g_tok.arrived(r - 3)
                pos.at(r - 3, normalise)
        g_names.start()
        g_grad.start()
        g_tok.arrived(depth - 1)
        pos.at(depth - 1, normalise)
        g_tok.end()
        keep(tb, all_tok)
        keep(hb, hidden_out)
        g_k.end()
        g_v.end()
        x_q.end()
        keep(w_in, wi_out)
        loop(depth, project)
        for src, dst in ((projected, proj_out), (queries, q_out), (keys, k_out), (values, v_out)):
            keep(src, dst)
        g_grad.round(1)
        pos.at(depth - 1, attention)
        x_o.end()
        keep(w_o, wo_out)
        pos.at(depth - 1, spread)
        for dist in reversed(range(depth - 1)):
            pos.at(dist, attention)
            pos.at(dist, spread)
        keep(heads, head_out)
        keep(totals, total_out)
        for r in range(red.rounds):
            red.round(r)
            g_names.round(r)
            if r >= 2:
                g_grad.round(r)
        mid = home[...].astype(f32) + branch[...]
        middle[...] = mid
        normed[...] = (mid * lax.rsqrt(jnp.mean(mid * mid, axis=1, keepdims=True) + EPS) * moe_row[...]).astype(bf)
        g_names.end()
        g_grad.end()
        for c in kept:
            c.wait()
        red.end()

    vmem, hbm = pl.BlockSpec(memory_space=pltpu.VMEM), pl.BlockSpec(memory_space=HBM)
    dma = pltpu.SemaphoreType.DMA
    shape = jax.ShapeDtypeStruct
    return pl.pallas_call(
        body,
        out_shape=[
            shape((rows, width), f32),
            shape((rows, width), bf),
            shape((devices, rows, 128), bf),
            shape((devices, rows, width), bf),
            shape((devices, rows, width), bf),
            shape((devices, rows, width), bf),
            shape((width, 3 * head), bf),
            shape((width, head), bf),
            shape((total, 3 * head), f32),
            shape((total, head), bf),
            shape((total, head), bf),
            shape((total, head), bf),
            shape((total, head), f32),
            shape((total, head), f32),
            shape((total, head), f32),
            shape((total, head), f32),
        ],
        in_specs=[hbm, vmem] + [hbm] * 5 + [vmem] * 6,
        out_specs=[vmem] * 2 + [hbm] * 14,
        scratch_shapes=[
            pltpu.VMEM((total, 3 * head), f32),
            pltpu.VMEM((total, head), bf),
            pltpu.VMEM((total, head), bf),
            pltpu.VMEM((total, head), bf),
            pltpu.VMEM((total, head), f32),
            pltpu.VMEM((total, head), f32),
            pltpu.VMEM((total, head), f32),
            pltpu.VMEM((total, head), f32),
            pltpu.VMEM((devices, rows, width), bf),
            pltpu.VMEM((devices, rows, width), bf),
            pltpu.VMEM((width, 3 * head), bf),
            pltpu.VMEM((width, head), bf),
            pltpu.VMEM((devices, rows, width), bf),
            pltpu.VMEM((rows, width), f32),
            pltpu.VMEM((total, head), f32),
            pltpu.VMEM((rows, width), bf),
            pltpu.VMEM((1, width), f32),
            pltpu.VMEM((1, width), f32),
            pltpu.VMEM((8, 128), jnp.int32),
            pltpu.VMEM((rows, 128), bf),
            dma((6,)),
            dma((12,)),
        ]
        + PlaneGather.sems(depth) * 2
        + Gather.sems(depth) * 2
        + Exchange.sems(depth) * 2
        + Reduce.scratch(depth, rows, width, ATTEND_HALVES, ATTEND_FLANK)
        + WideGather.sems(depth),
        compiler_params=params(number, 60 * 2**20),
        name="attend",
    )(tokens, routes_t, out_grad, q_weight, k_weight, v_weight, out_weight, norm_gain, q_gain, k_gain, moe_gain, frequency, docs)


def attend_back(depth, number, block, moe_gain_grad, grad_middle, all_normed, experts_in_all, kept, gains, docs):
    f32, bf = jnp.float32, jnp.bfloat16
    all_tok, hidden, w_in, w_o, projected, queries, keys, values, heads, totals, cosines, sines = kept
    norm_gain, q_gain, k_gain = gains
    devices, rows, width = all_tok.shape
    wide = block.shape[1]
    lanes = wide - width
    total, head = queries.shape
    groups = depth * 2
    w_rows = width // groups
    plane_rows = total // depth
    scale = head ** (-0.5)
    gain_rows = width // 128
    small_rows = 2 * gain_rows + 8

    def body(
        blk, moe, gm, n_h, tok_h, hid_h, wi_h, wo_h, proj_h, q_h, k_h, v_h, head_h, tot_h, cos_h, sin_h, ng, qg, kg, drow,
        tokens_grad, q_grad, k_grad, v_grad, o_grad, norm_sum, moe_sum, q_sum, k_sum, router_grad,
        gb, nb, tb, hb, w_in, w_o, proj, qs, ks, vs, hs, ts, cos, sin, part, gh, dq, dk, dv, gproj, wpart, opart,
        kv_sum, hidden_sum, small, small_all, by_norm, by_q, by_k, doc, turned, norm_row, load_sem, own_sem, *rest,
    ):
        pos = Place(depth)
        device = pos.block(pos.z)
        loads = [
            pltpu.make_async_copy(src, dst, load_sem.at[i])
            for i, (src, dst) in enumerate(
                (
                    (wo_h, w_o), (head_h, hs), (tok_h, tb), (hid_h, hb), (wi_h, w_in), (proj_h, proj), (q_h, qs),
                    (k_h, ks), (v_h, vs), (tot_h, ts), (cos_h, cos), (sin_h, sin), (n_h, nb),
                )
            )
        ]
        own = pltpu.make_async_copy(blk, gb.at[device], own_sem)
        own.start()
        for c in loads:
            c.start()
        pos.greet(plane=True)
        g_branch = WideGather(pos, blk, gb, GATHER_FLANK, rest[0:6])
        g_small = Gather(pos, small, small_all, *rest[6:8], False)
        x_q = Exchange(
            pos, lambda p: part_of(wpart, p, w_rows, 0, head), lambda p: cols_of(q_grad, p, head), *rest[8:11]
        )
        x_o = Exchange(pos, lambda p: rows_of(opart, p, w_rows), lambda p: cols_of(o_grad, p, head), *rest[11:14])
        red = Reduce(pos, part, *rest[14:23], halves=BACK_HALVES)
        red.out = hidden_sum
        r_kv = PlaneReduce(pos, lambda p: part_of(wpart, p, w_rows, head, 2 * head), kv_sum, *rest[23:27])

        def span(z):
            return pl.ds(pl.multiple_of(z * plane_rows, plane_rows), plane_rows)

        def column(z):
            place = lax.broadcasted_iota(jnp.int32, (plane_rows, total), 0) + z * plane_rows
            other = lax.broadcasted_iota(jnp.int32, (plane_rows, total), 1)
            docs_here = jnp.sum(jnp.where(other == place, drow[...].astype(f32), 0.0), axis=1, keepdims=True)
            doc[span(z), :] = jnp.broadcast_to(docs_here, (plane_rows, head))

        def heads_back(z):
            g = gb[pl.ds(z * 8, 8), :, pl.ds(0, width)].reshape(plane_rows, width)
            gh[span(z), :] = dot(g, w_o[...]).astype(bf)

        def out_weight_back():
            g = gb[:, :, pl.ds(0, width)].reshape(total, width)
            opart[...] = dot(turned[pl.ds(0, head), :], g).T.astype(bf)

        def attention_back(z):
            place = lax.broadcasted_iota(jnp.int32, (plane_rows, total), 0) + z * plane_rows
            allowed = (lax.broadcasted_iota(jnp.int32, (plane_rows, total), 1) <= place) & (
                doc[span(z), pl.ds(0, 1)] == drow[...].astype(f32)
            )
            q = qs[span(z), :]
            g = gh[span(z), :]
            delta = jnp.sum(g.astype(f32) * hs[span(z), :], axis=1, keepdims=True)
            s = dot_nt(q, ks[...]) * scale
            p = jnp.where(allowed, jnp.exp(jnp.minimum(s - ts[span(z), pl.ds(0, 1)], 0.0)), 0.0)
            ds = (p * (dot_nt(g, vs[...]) - delta)).astype(bf)
            dq[span(z), :] = dot(ds, ks[...]) * scale
            dk[...] += dot_tn(ds, q) * scale
            dv[...] += dot_tn(p.astype(bf), g)

        def project_back(z):
            for first, grad, gain, total_ref in ((0, dq, qg, by_q), (head, dk, kg, by_k)):
                g = turn(grad[span(z), :], cos[span(z), :], -sin[span(z), :])
                change, by_gain = norm_back(proj[span(z), pl.ds(first, head)], gain[...].astype(f32), g)
                gproj[span(z), pl.ds(first, head)] = change.astype(bf)
                total_ref[...] += jnp.sum(by_gain, axis=0, keepdims=True)
            gproj[span(z), pl.ds(2 * head, head)] = dv[span(z), :].astype(bf)

        def spread(z):
            g = gproj[span(z), :]
            t = tb[pl.ds(z * 8, 8)].reshape(plane_rows, width).astype(f32)
            r = lax.rsqrt(jnp.mean(t * t, axis=1, keepdims=True) + EPS)
            back = dot_nt(g, w_in[...])
            part[pl.ds(z * 8, 8)] = back.astype(bf).reshape(8, rows, width)
            by_norm[...] += jnp.sum(back * (t * r), axis=0, keepdims=True)
            red.start_one(z)

        def router_back():
            router_grad[...] = dot(turned[pl.ds(0, experts_in_all), :], nb[...].reshape(total, width))

        def in_weight_back():
            wpart[...] = dot(turned[...], hb[...].reshape(total, width)).T.astype(bf)

        g_branch.start()
        as_row(ng, norm_row)
        loop(depth, column)
        dk[...] = jnp.zeros(dk.shape, f32)
        dv[...] = jnp.zeros(dv.shape, f32)
        by_norm[...] = jnp.zeros(by_norm.shape, f32)
        by_q[...] = jnp.zeros(by_q.shape, f32)
        by_k[...] = jnp.zeros(by_k.shape, f32)
        small[...] = jnp.zeros(small.shape, f32)
        for c in loads:
            c.wait()
        own.wait()

        def plane_back(z):
            heads_back(z)
            attention_back(z)

        for r in range(1, g_branch.rounds):
            g_branch.round(r)
            if r >= 3:
                g_branch.arrived(r - 3)
                pos.at(r - 3, plane_back)
        turned[pl.ds(0, head), :] = hs[...].T.astype(bf)
        g_branch.arrived(depth - 1)
        g_branch.end()
        out_weight_back()
        x_o.start()
        pos.at(depth - 1, plane_back)
        loop(depth, project_back)
        turned[...] = gproj[...].T
        in_weight_back()
        x_q.start()
        r_kv.start()
        for dist in reversed(range(depth)):
            pos.at(dist, spread)
        for i in range(gain_rows):
            small[pl.ds(i, 1), :] = by_norm[:, pl.ds(i * 128, 128)]
            small[pl.ds(gain_rows + i, 1), :] = moe[:, pl.ds(i * 128, 128)]
        small[pl.ds(2 * gain_rows, 1), :] = by_q[...]
        small[pl.ds(2 * gain_rows + 1, 1), :] = by_k[...]
        small_all[device] = small[...]
        g_small.start()
        for r in range(red.rounds):
            red.round(r)
            r_kv.round(r)
            g_small.round(r)
            if r == 2:
                turned[pl.ds(0, lanes), :] = gb[:, :, pl.ds(width, lanes)].reshape(total, lanes).T
                router_back()
        change, _ = norm_back(tb[device].astype(f32), norm_row[...], hidden_sum[...])
        tokens_grad[...] = gm[...] + change
        k_grad[...] = kv_sum[:, pl.ds(0, head)]
        v_grad[...] = kv_sum[:, pl.ds(head, head)]
        g_small.end()
        summed = jnp.sum(small_all[...], axis=0)
        norm_sum[...] = summed[:gain_rows]
        moe_sum[...] = summed[gain_rows : 2 * gain_rows]
        q_sum[...] = summed[2 * gain_rows : 2 * gain_rows + 1]
        k_sum[...] = summed[2 * gain_rows + 1 : 2 * gain_rows + 2]
        x_o.end()
        x_q.end()
        red.end()
        r_kv.end()

    vmem, hbm = pl.BlockSpec(memory_space=pltpu.VMEM), pl.BlockSpec(memory_space=HBM)
    dma = pltpu.SemaphoreType.DMA
    shape = jax.ShapeDtypeStruct
    V = pltpu.VMEM
    return pl.pallas_call(
        body,
        out_shape=[
            shape((rows, width), f32),
            shape((w_rows, groups * head), bf),
            shape((w_rows, head), f32),
            shape((w_rows, head), f32),
            shape((w_rows, groups * head), bf),
            shape((gain_rows, 128), f32),
            shape((gain_rows, 128), f32),
            shape((1, 128), f32),
            shape((1, 128), f32),
            shape((experts_in_all, width), f32),
        ],
        in_specs=[hbm, vmem, vmem] + [hbm] * 13 + [vmem] * 4,
        out_specs=[vmem, hbm, vmem, vmem, hbm] + [vmem] * 5,
        scratch_shapes=[
            V((devices, rows, wide), bf),
            V((devices, rows, width), bf),
            V((devices, rows, width), bf),
            V((devices, rows, width), bf),
            V((width, 3 * head), bf),
            V((width, head), bf),
            V((total, 3 * head), f32),
            V((total, head), bf),
            V((total, head), bf),
            V((total, head), bf),
            V((total, head), f32),
            V((total, head), f32),
            V((total, head), f32),
            V((total, head), f32),
            V((devices, rows, width), bf),
            V((total, head), bf),
            V((total, head), f32),
            V((total, head), f32),
            V((total, head), f32),
            V((total, 3 * head), bf),
            V((width, 3 * head), bf),
            V((width, head), bf),
            V((w_rows, 2 * head), f32),
            V((rows, width), f32),
            V((small_rows, 128), f32),
            V((devices, small_rows, 128), f32),
            V((1, width), f32),
            V((1, head), f32),
            V((1, head), f32),
            V((total, head), f32),
            V((3 * head, total), bf),
            V((1, width), f32),
            dma((13,)),
            dma,
        ]
        + WideGather.sems(depth)
        + Gather.sems(depth)
        + Exchange.sems(depth) * 2
        + Reduce.scratch(depth, rows, width, BACK_HALVES)
        + PlaneReduce.scratch(depth, w_rows, 2 * head),
        compiler_params=params(number, 60 * 2**20),
        name="attend_back",
    )(block, moe_gain_grad, grad_middle, all_normed, *kept, norm_gain, q_gain, k_gain, docs)


def head_shards(
    tokens,
    segments,
    routes,
    out_grad,
    norm_gain,
    q_weight,
    k_weight,
    v_weight,
    q_gain,
    k_gain,
    out_weight,
    moe_gain,
    router_weight,
    gate_weight,
    up_weight,
    down_weight,
):
    f32, bf = jnp.float32, jnp.bfloat16
    f32, bf = jnp.float32, jnp.bfloat16
    head_dim = q_gain.shape[0]
    tok_rows, width = tokens.shape
    all_tokens = segments.shape[0]
    expert_count = router_weight.shape[1]
    depth = all_tokens // tok_rows // 2
    norm_gain, q_gain, k_gain, moe_gain = (g.reshape(-1, 128) for g in (norm_gain, q_gain, k_gain, moe_gain))
    docs = segments[None]
    frequency = (THETA ** (np.arange(head_dim // 2) * -2.0 / head_dim)).astype(np.float32)
    middle, normed, all_named, all_grad, *kept = attend(
        depth,
        0,
        tokens,
        routes.T,
        out_grad,
        q_weight,
        k_weight,
        v_weight,
        out_weight,
        (norm_gain, q_gain, k_gain, moe_gain),
        np.concatenate([frequency, frequency])[None],
        docs,
    )
    layer_out, grad_middle, grad_block, moe_gain_grad, all_normed, *pairs = experts(
        depth,
        1,
        normed,
        all_grad,
        all_named,
        middle,
        moe_gain,
        router_weight.T,
        gate_weight[0],
        up_weight[0],
        down_weight[0],
    )
    tokens_grad, grad_q, grad_k, grad_v, grad_o, norm_sum, moe_sum, q_sum, k_sum, grad_router = attend_back(
        depth,
        2,
        grad_block,
        moe_gain_grad,
        grad_middle,
        all_normed,
        expert_count,
        kept,
        (norm_gain, q_gain, k_gain),
        docs,
    )
    grad_gate_w, grad_up_w, grad_down, grad_q, grad_o, *rest = finish(
        pairs,
        grad_q,
        grad_o,
        (layer_out, tokens_grad, grad_k, grad_v, norm_sum, moe_sum, q_sum, k_sum, grad_router),
    )
    layer_out, tokens_grad, grad_k, grad_v, norm_sum, moe_sum, q_sum, k_sum, grad_router = rest
    return (
        layer_out,
        tokens_grad,
        norm_sum.reshape(-1),
        grad_q,
        grad_k,
        grad_v,
        q_sum.reshape(-1),
        k_sum.reshape(-1),
        grad_o,
        moe_sum.reshape(-1),
        grad_router.T,
        grad_gate_w[None],
        grad_up_w[None],
        grad_down[None],
    )


def solution(mesh):
    per_device = shards if mesh.shape["dp"] != 8 or mesh.shape["tensor"] != 4 else head_shards
    placed = (
        P("dp", None),
        P(),
        P(("dp", "tensor"), None),
        P(("dp", "tensor"), None),
        P(),
        P("dp", "tensor"),
        P("dp", "tensor"),
        P("dp", "tensor"),
        P(),
        P(),
        P("dp", "tensor"),
        P(),
        P(),
        P(("dp", "tensor"), None, None),
        P(("dp", "tensor"), None, None),
        P(("dp", "tensor"), None, None),
    )
    return jax.shard_map(
        per_device,
        mesh=mesh,
        in_specs=placed,
        out_specs=(
            P(("dp", "tensor"), None),
            P(("dp", "tensor"), None),
            P(),
            P("dp", "tensor"),
            P("dp", "tensor"),
            P("dp", "tensor"),
            P(),
            P(),
            P("dp", "tensor"),
            P(),
            P(),
            P(("dp", "tensor"), None, None),
            P(("dp", "tensor"), None, None),
            P(("dp", "tensor"), None, None),
        ),
        check_vma=False,
    )
```

```python
import functools

import jax
import jax.numpy as jnp
import numpy as np
from jax import lax
from jax.experimental import pallas as pl
from jax.experimental.pallas import tpu as pltpu
from jax.sharding import PartitionSpec as P

EPS = 1e-06
THETA = 1000000.0


def norm_rows(values, gain):
    return values * lax.rsqrt(jnp.mean(values * values, axis=-1, keepdims=True) + EPS) * gain


def rotary(values, cosine, sine_part):
    half_dim = values.shape[-1] // 2
    front_half = values[..., :half_dim]
    back_half = values[..., half_dim:]
    return jnp.concatenate(
        [front_half * cosine - back_half * sine_part, back_half * cosine + front_half * sine_part],
        axis=-1,
    )


def angles(positions, head_dim):
    half_dim = head_dim // 2
    frequency = THETA ** (-(jnp.arange(half_dim).astype(jnp.float32) * 2.0) / head_dim)
    rotation = positions.astype(jnp.float32)[:, None] * frequency[None, :]
    return (jnp.cos(rotation), jnp.sin(rotation))


def prepare(projected, q_gain, k_gain, cosine, sine_part, head_dim):
    tok_rows = projected.shape[0]
    query_width = projected.shape[1] - 2 * head_dim
    queries = projected[:, :query_width].reshape(tok_rows, query_width // head_dim, head_dim)
    keys_local = projected[:, query_width : query_width + head_dim]
    values_local = projected[:, query_width + head_dim :]
    queries = rotary(norm_rows(queries, q_gain), cosine[:, None, :], sine_part[:, None, :])
    keys_local = rotary(norm_rows(keys_local, k_gain), cosine, sine_part)
    return (queries, keys_local, values_local)


def swiglu(gate_in, up_in):
    return jax.nn.silu(gate_in) * up_in


def shards(
    tokens,
    segments,
    routes,
    out_grad,
    norm_gain,
    q_weight,
    k_weight,
    v_weight,
    q_gain,
    k_gain,
    out_weight,
    moe_gain,
    router_weight,
    gate_weight,
    up_weight,
    down_weight,
):
    head_dim = q_gain.shape[0]
    tok_rows = tokens.shape[0]
    model_width = tokens.shape[1]
    share_rows = out_grad.shape[0]
    all_tokens = segments.shape[0]
    expert_count = router_weight.shape[1]
    top_count = routes.shape[1]
    capacity = max(2, share_rows * top_count * 2 // expert_count)
    score_scale = head_dim ** (-0.5)
    first_row = lax.axis_index("dp") * tok_rows
    places = jnp.arange(all_tokens, dtype=jnp.int32)
    begins = jnp.concatenate([jnp.ones((1,), dtype=bool), segments[1:] != segments[:-1]])
    positions = places - lax.cummax(jnp.where(begins, places, 0), axis=0)
    local_positions = lax.dynamic_slice_in_dim(positions, first_row, tok_rows)
    local_docs = lax.dynamic_slice_in_dim(segments, first_row, tok_rows)
    query_places = first_row + jnp.arange(tok_rows, dtype=jnp.int32)
    cosine, sine_part = angles(local_positions, head_dim)
    weight_rows = (
        lax.all_gather(q_weight, "dp", axis=0, tiled=True),
        lax.all_gather(k_weight, "dp", axis=0, tiled=True),
        lax.all_gather(v_weight, "dp", axis=0, tiled=True),
        lax.all_gather(out_weight, "dp", axis=0, tiled=True),
    )
    input_weight = jnp.concatenate([weight_rows[0], weight_rows[1], weight_rows[2]], axis=1)
    output_weight = weight_rows[3]
    tokens_float = tokens.astype(jnp.float32)
    norm_gain_float = norm_gain.astype(jnp.float32)
    hidden = norm_rows(tokens_float, norm_gain_float).astype(jnp.bfloat16)
    projected = jnp.dot(hidden, input_weight, preferred_element_type=jnp.float32)

    def prepare_local(projected_in, qgain_in, kgain_in):
        return prepare(projected_in, qgain_in, kgain_in, cosine, sine_part, head_dim)

    prepared, prepare_back = jax.vjp(
        prepare_local, projected, q_gain.astype(jnp.float32), k_gain.astype(jnp.float32)
    )
    queries = prepared[0].astype(jnp.bfloat16)
    keys_local = prepared[1].astype(jnp.bfloat16)
    values_local = prepared[2].astype(jnp.bfloat16)
    local_heads = queries.shape[1]

    def visible(offset, length):
        key_places = offset + jnp.arange(length, dtype=jnp.int32)
        key_docs = lax.dynamic_slice_in_dim(segments, offset, length)
        return (key_places[None, :] <= query_places[:, None]) & (
            key_docs[None, :] == local_docs[:, None]
        )

    running_max = jnp.full((tok_rows, local_heads), -1e30, jnp.float32)
    key_piece = lax.all_gather(keys_local, "dp", axis=0, tiled=True)
    value_piece = lax.all_gather(values_local, "dp", axis=0, tiled=True)
    allowed = visible(jnp.int32(0), key_piece.shape[0])[:, None, :]
    scores = (
        jnp.einsum("thd,nd->thn", queries, key_piece, preferred_element_type=jnp.float32)
        * score_scale
    )
    scores = jnp.where(allowed, scores, -1e30)
    new_max = jnp.maximum(running_max, jnp.max(scores, axis=-1))
    soft_weights = jnp.where(allowed, jnp.exp(scores - new_max[:, :, None]), 0.0)
    softmax_mass = jnp.sum(soft_weights, axis=-1)
    weighted_sum = jnp.einsum(
        "thn,nd->thd",
        soft_weights.astype(jnp.bfloat16),
        value_piece,
        preferred_element_type=jnp.float32,
    )
    running_max, softmax_mass, weighted_sum = (new_max, softmax_mass, weighted_sum)
    head_out = weighted_sum / softmax_mass[:, :, None]
    log_total = running_max + jnp.log(softmax_mass)
    attended = head_out.astype(jnp.bfloat16).reshape(tok_rows, local_heads * head_dim)
    branch = lax.psum_scatter(
        jnp.einsum("tc,dc->td", attended, output_weight, preferred_element_type=jnp.float32).astype(
            jnp.bfloat16
        ),
        "tensor",
        scatter_dimension=0,
        tiled=True,
    ).astype(jnp.float32)
    tensor_lane = lax.axis_index("tensor")
    tokens_share = lax.dynamic_slice_in_dim(tokens_float, tensor_lane * share_rows, share_rows, 0)
    middle = tokens_share + branch
    normed_float, moe_norm_back = jax.vjp(norm_rows, middle, moe_gain.astype(jnp.float32))
    normed = normed_float.astype(jnp.bfloat16)
    logits = jnp.dot(normed, router_weight, preferred_element_type=jnp.float32)

    def gating(logit_rows):
        probabilities = jax.nn.softmax(logit_rows, axis=-1)
        chosen = jnp.take_along_axis(probabilities, routes, axis=1)
        return chosen / jnp.sum(chosen, axis=1, keepdims=True)

    gate_values, gating_back = jax.vjp(gating, logits)
    pair_routes = routes.reshape(-1)
    pair_count = pair_routes.shape[0]
    route_table = (
        pair_routes[:, None] == jnp.arange(expert_count, dtype=jnp.int32)[None, :]
    ).astype(jnp.int32)
    route_rank = jnp.sum(jnp.cumsum(route_table, axis=0) * route_table, axis=1) - 1
    slot_index = pair_routes * capacity + route_rank
    slot_owner = (
        jnp.full((expert_count * capacity,), pair_count, jnp.int32)
        .at[slot_index]
        .set(jnp.arange(pair_count, dtype=jnp.int32))
    )
    normed_padded = jnp.concatenate([normed, jnp.zeros((1, model_width), jnp.bfloat16)], axis=0)
    send_rows = normed_padded[slot_owner // top_count].reshape(expert_count, capacity, model_width)
    arrived = lax.all_to_all(send_rows, ("dp", "tensor"), split_axis=0, concat_axis=0, tiled=True)
    expert_inputs = arrived.reshape(-1, model_width)
    w_gate = gate_weight[0]
    w_up = up_weight[0]
    w_down = down_weight[0]
    gate_act = jnp.dot(expert_inputs, w_gate, preferred_element_type=jnp.float32)
    up_act = jnp.dot(expert_inputs, w_up, preferred_element_type=jnp.float32)
    inner_float, swiglu_back = jax.vjp(swiglu, gate_act, up_act)
    inner_act = inner_float.astype(jnp.bfloat16)
    produced = jnp.dot(inner_act, w_down, preferred_element_type=jnp.float32).astype(jnp.bfloat16)
    returned = lax.all_to_all(
        produced.reshape(expert_count, capacity, model_width),
        ("dp", "tensor"),
        split_axis=0,
        concat_axis=0,
        tiled=True,
    )
    picked = (
        returned.reshape(-1, model_width)[slot_index]
        .reshape(share_rows, top_count, model_width)
        .astype(jnp.float32)
    )
    layer_out = (middle + jnp.sum(gate_values[:, :, None] * picked, axis=1)).astype(jnp.bfloat16)
    grad_out = out_grad.astype(jnp.float32)
    grad_picked = (
        (gate_values[:, :, None] * grad_out[:, None, :])
        .astype(jnp.bfloat16)
        .reshape(pair_count, model_width)
    )
    grad_gates = jnp.sum(grad_out[:, None, :] * picked, axis=2)
    grad_padded = jnp.concatenate([grad_picked, jnp.zeros((1, model_width), jnp.bfloat16)], axis=0)
    grad_send = grad_padded[slot_owner].reshape(expert_count, capacity, model_width)
    grad_arrived = lax.all_to_all(
        grad_send, ("dp", "tensor"), split_axis=0, concat_axis=0, tiled=True
    ).reshape(-1, model_width)
    grad_inner = jnp.einsum("rd,fd->rf", grad_arrived, w_down, preferred_element_type=jnp.float32)
    grad_down = jnp.einsum("rf,rd->fd", inner_act, grad_arrived, preferred_element_type=jnp.float32)
    grad_gate_float, grad_up_float = swiglu_back(grad_inner)
    grad_gate_act = grad_gate_float.astype(jnp.bfloat16)
    grad_up_act = grad_up_float.astype(jnp.bfloat16)
    grad_gate_w = jnp.einsum(
        "rd,rf->df", expert_inputs, grad_gate_act, preferred_element_type=jnp.float32
    )
    grad_up_w = jnp.einsum(
        "rd,rf->df", expert_inputs, grad_up_act, preferred_element_type=jnp.float32
    )
    grad_inputs = jnp.einsum("rf,df->rd", grad_gate_act, w_gate, preferred_element_type=jnp.float32)
    grad_inputs = (
        grad_inputs + jnp.einsum("rf,df->rd", grad_up_act, w_up, preferred_element_type=jnp.float32)
    ).astype(jnp.bfloat16)
    grad_home = lax.all_to_all(
        grad_inputs.reshape(expert_count, capacity, model_width),
        ("dp", "tensor"),
        split_axis=0,
        concat_axis=0,
        tiled=True,
    )
    grad_normed = jnp.sum(
        grad_home.reshape(-1, model_width)[slot_index]
        .reshape(share_rows, top_count, model_width)
        .astype(jnp.float32),
        axis=1,
    )
    (grad_logit_float,) = gating_back(grad_gates)
    grad_logits = grad_logit_float.astype(jnp.bfloat16)
    grad_router = jnp.einsum("td,te->de", normed, grad_logits, preferred_element_type=jnp.float32)
    grad_normed = grad_normed + jnp.einsum(
        "te,de->td", grad_logits, router_weight, preferred_element_type=jnp.float32
    )
    grad_middle_part, grad_moe_gain = moe_norm_back(grad_normed)
    grad_middle = grad_out + grad_middle_part
    grad_branch = lax.all_gather(grad_middle.astype(jnp.bfloat16), "tensor", axis=0, tiled=True)
    again_rows = (
        lax.all_gather(q_weight, "dp", axis=0, tiled=True),
        lax.all_gather(k_weight, "dp", axis=0, tiled=True),
        lax.all_gather(v_weight, "dp", axis=0, tiled=True),
        lax.all_gather(out_weight, "dp", axis=0, tiled=True),
    )
    input_back = jnp.concatenate([again_rows[0], again_rows[1], again_rows[2]], axis=1)
    output_back = again_rows[3]
    grad_heads = (
        jnp.dot(grad_branch, output_back, preferred_element_type=jnp.float32)
        .astype(jnp.bfloat16)
        .reshape(tok_rows, local_heads, head_dim)
    )
    row_delta = jnp.sum(grad_heads.astype(jnp.float32) * head_out, axis=-1)
    key_rows, value_rows = (
        lax.all_gather(keys_local, "dp", axis=0, tiled=True),
        lax.all_gather(values_local, "dp", axis=0, tiled=True),
    )
    key_block = min(512, all_tokens)

    def key_step(grad_queries, block_number):
        offset = block_number * key_block
        key_piece = lax.dynamic_slice_in_dim(key_rows, offset, key_block, 0)
        value_piece = lax.dynamic_slice_in_dim(value_rows, offset, key_block, 0)
        allowed = visible(offset, key_block)[:, None, :]
        scores = (
            jnp.einsum("thd,nd->thn", queries, key_piece, preferred_element_type=jnp.float32)
            * score_scale
        )
        soft_weights = jnp.where(allowed, jnp.exp(scores - log_total[:, :, None]), 0.0)
        grad_weights = jnp.einsum(
            "thd,nd->thn", grad_heads, value_piece, preferred_element_type=jnp.float32
        )
        grad_scores = (soft_weights * (grad_weights - row_delta[:, :, None])).astype(jnp.bfloat16)
        grad_queries = (
            grad_queries
            + jnp.einsum("thn,nd->thd", grad_scores, key_piece, preferred_element_type=jnp.float32)
            * score_scale
        )
        grad_key_piece = (
            jnp.einsum("thn,thd->nd", grad_scores, queries, preferred_element_type=jnp.float32)
            * score_scale
        )
        grad_value_piece = jnp.einsum(
            "thn,thd->nd",
            soft_weights.astype(jnp.bfloat16),
            grad_heads,
            preferred_element_type=jnp.float32,
        )
        return (grad_queries, jnp.concatenate([grad_key_piece, grad_value_piece], axis=1))

    grad_queries, key_terms = lax.scan(
        key_step,
        jnp.zeros((tok_rows, local_heads, head_dim), jnp.float32),
        jnp.arange(all_tokens // key_block, dtype=jnp.int32),
    )
    key_grads = lax.psum_scatter(
        key_terms.reshape(all_tokens, 2 * head_dim).astype(jnp.bfloat16),
        "dp",
        scatter_dimension=0,
        tiled=True,
    ).astype(jnp.float32)
    grad_proj_float, grad_q_gain, grad_k_gain = prepare_back(
        (grad_queries, key_grads[:, :head_dim], key_grads[:, head_dim:])
    )
    grad_projected = grad_proj_float.astype(jnp.bfloat16)
    grad_hidden = jnp.einsum(
        "tc,dc->td", grad_projected, input_back, preferred_element_type=jnp.float32
    )
    grad_hidden_share = lax.psum_scatter(
        grad_hidden.astype(jnp.bfloat16), "tensor", scatter_dimension=0, tiled=True
    ).astype(jnp.float32)
    _, first_norm_back = jax.vjp(norm_rows, tokens_share, norm_gain_float)
    grad_tokens_part, grad_norm_gain = first_norm_back(grad_hidden_share)
    tokens_grad = grad_middle + grad_tokens_part
    input_part = jnp.einsum("td,tc->dc", hidden, grad_projected, preferred_element_type=jnp.float32)
    output_part = jnp.einsum("td,tc->dc", grad_branch, attended, preferred_element_type=jnp.float32)
    weight_share = lax.psum_scatter(
        jnp.concatenate([input_part, output_part], axis=1).astype(jnp.bfloat16),
        "dp",
        scatter_dimension=0,
        tiled=True,
    ).astype(jnp.float32)
    query_width = local_heads * head_dim
    grad_q_weight = weight_share[:, :query_width]
    grad_k_weight = weight_share[:, query_width : query_width + head_dim]
    grad_v_weight = weight_share[:, query_width + head_dim : query_width + 2 * head_dim]
    grad_out_weight = weight_share[:, query_width + 2 * head_dim :]
    small_sums = lax.psum(
        (grad_router, grad_norm_gain, grad_moe_gain, grad_q_gain, grad_k_gain), ("dp", "tensor")
    )
    return (
        layer_out,
        tokens_grad,
        small_sums[1],
        grad_q_weight,
        grad_k_weight,
        grad_v_weight,
        small_sums[3],
        small_sums[4],
        grad_out_weight,
        small_sums[2],
        small_sums[0],
        grad_gate_w[None],
        grad_up_w[None],
        grad_down[None],
    )


MESH = pl.DeviceIdType.MESH
HBM = pl.ANY
GATHER_FLANK = 384
REDUCE_FLANK = 384
ATTEND_FLANK = 256
OUT_GRAD_FLANK = 384
ATTEND_HALVES = True
BACK_HALVES = True
TOKEN_HALVES = True
BACK_FLANK = 0


class Place:
    def __init__(self, depth):
        d = lax.axis_index("dp")
        t = lax.axis_index("tensor")
        self.depth = depth
        self.d, self.t = d, t
        self.z, self.x = d // 2, lax.rem(d, 2)
        self.y, self.c = t // 2, lax.rem(t, 2)
        self.next_to = {
            "x": (self.z * 2 + 1 - self.x, t),
            "y": (d, (1 - self.y) * 2 + self.c),
            "c": (d, self.y * 2 + 1 - self.c),
            "up": (d + 2, t),
            "down": (d - 2, t),
        }
        self.groups = depth * 2
        self.head = self.z * 2 + self.c
        self.hub = self.x == self.c

    def shard(self, d):
        return (d, self.y * 2 + self.x)

    def owner(self, head):
        return ((head // 2) * 2 + self.c, self.y * 2 + lax.rem(head, 2))

    def block(self, z, fx=0, fy=0, fc=0):
        x = 1 - self.x if fx else self.x
        y = 1 - self.y if fy else self.y
        c = 1 - self.c if fc else self.c
        return (z * 2 + x) * 4 + y * 2 + c

    def at(self, dist, step):
        if dist == 0:
            step(self.z)
            return

        @pl.when(self.z >= dist)
        def _():
            step(self.z - dist)

        @pl.when(self.z + dist < self.depth)
        def _():
            step(self.z + dist)

    def greet(self, sharing=None):
        barrier = pltpu.get_barrier_semaphore()

        def signal(to):
            pl.semaphore_signal(barrier, inc=1, device_id=to, device_id_type=MESH)

        for to in ("x", "y", "c"):
            signal(self.next_to[to])

        @pl.when(self.z > 0)
        def _():
            signal(self.next_to["down"])

        @pl.when(self.z < self.depth - 1)
        def _():
            signal(self.next_to["up"])

        above = (self.z < self.depth - 1).astype(jnp.int32)
        below = (self.z > 0).astype(jnp.int32)
        count = 3 + above + below
        if sharing is not None:
            senders = self.shard if sharing == "out" else self.owner
            here = self.d if sharing == "out" else self.head

            for k in range(self.groups):

                @pl.when(jnp.logical_not(self.hub & (here == k)))
                def _():
                    signal(senders(k))

            count = count + self.groups - self.hub.astype(jnp.int32)
        pl.semaphore_wait(barrier, count)

    def copy(self, src, dst, send, recv, to):
        return pltpu.make_async_remote_copy(
            src_ref=src,
            dst_ref=dst,
            send_sem=send,
            recv_sem=recv,
            device_id=self.next_to[to],
            device_id_type=MESH,
        )


class Gather:
    SEND, RECV = 11, 10

    def __init__(self, pos, own, out, send, recv, halves, cols=None):
        self.pos, self.own, self.out = pos, own, out
        self.send, self.recv = send, recv
        if cols is not None:
            self.own, self.out = own.at[:, cols], out.at[:, :, cols]
        rows = out.shape[1]
        self.h0 = pl.ds(0, rows // 2 if halves else rows)
        self.h1 = pl.ds(rows // 2, rows // 2) if halves else None
        self.rounds = pos.depth + 2
        self.seen = set()

    def link(self, src, dst, sends, recvs, zo, to):
        return self.pos.copy(src, dst, self.send.at[sends, zo], self.recv.at[recvs, zo], to)

    def col(self, zo):
        return self.out.at[self.pos.block(zo)]

    def src(self, zo, mine):
        return self.own if mine else self.col(zo)

    def up(self, zo, mine=False):
        return self.link(self.src(zo, mine), self.col(zo), 0, 0, zo, "up")

    def down(self, zo, mine=False):
        return self.link(self.src(zo, mine), self.col(zo), 1, 0, zo, "down")

    def to_x(self, zo, mine=False):
        return self.link(self.src(zo, mine), self.col(zo), 2, 1, zo, "x")

    def to_y(self, zo, mine=False):
        return self.link(self.src(zo, mine), self.col(zo), 3, 2, zo, "y")

    def to_c(self, zo, mine=False):
        return self.link(self.src(zo, mine), self.col(zo), 4, 5, zo, "c")

    def part(self, zo, fx, fy, rows):
        whole = self.out.at[self.pos.block(zo, fx, fy)]
        return whole if rows is None else whole.at[rows]

    def pass_on(self, zo, fx, fy, rows, sends, recvs, to):
        ref = self.part(zo, fx, fy, rows)
        return self.link(ref, ref, sends, recvs, zo, to)

    def x_to_y(self, zo):
        return self.pass_on(zo, 1, 0, self.h0, 5, 3, "y")

    def x_to_c(self, zo):
        return self.pass_on(zo, 1, 0, None, 6, 6, "c")

    def y_to_x(self, zo):
        return self.pass_on(zo, 0, 1, self.h1, 7, 4, "x")

    def y_to_c(self, zo):
        return self.pass_on(zo, 0, 1, None, 8, 7, "c")

    def far0_to_c(self, zo):
        return self.pass_on(zo, 1, 1, self.h0, 9, 8, "c")

    def far1_to_c(self, zo):
        return self.pass_on(zo, 1, 1, self.h1, 10, 9, "c")

    def along_z(self, zo, mine, what):
        z, depth = self.pos.z, self.pos.depth
        if mine:
            up, down = z < depth - 1, z > 0
        else:
            up, down = (zo < z) & (z < depth - 1), (zo > z) & (z > 0)

        @pl.when(up)
        def _():
            what(self.up(zo, mine))

        @pl.when(down)
        def _():
            what(self.down(zo, mine))

    def on_column(self, zo, mine=False):
        if not mine:
            self.up(zo).wait_recv()
        self.along_z(zo, mine, lambda c: c.start())
        self.to_x(zo, mine).start()
        self.to_y(zo, mine).start()
        self.to_c(zo, mine).start()

    def on_sides(self, zo):
        self.to_x(zo).wait_recv()
        self.x_to_y(zo).start()
        self.x_to_c(zo).start()
        self.to_y(zo).wait_recv()
        if self.h1 is not None:
            self.y_to_x(zo).start()
        self.y_to_c(zo).start()

    def on_far(self, zo):
        self.x_to_y(zo).wait_recv()
        self.far0_to_c(zo).start()
        if self.h1 is not None:
            self.y_to_x(zo).wait_recv()
            self.far1_to_c(zo).start()

    def start(self):
        self.on_column(self.pos.z, True)

    def round(self, r):
        if 1 <= r < self.pos.depth:
            self.pos.at(r, self.on_column)
        if 1 <= r <= self.pos.depth:
            self.pos.at(r - 1, self.on_sides)
        if 2 <= r <= self.pos.depth + 1:
            self.pos.at(r - 2, self.on_far)

    def from_core(self, zo, mine=False):
        copies = [self.to_c(zo, mine), self.x_to_c(zo), self.y_to_c(zo), self.far0_to_c(zo)]
        return copies if self.h1 is None else copies + [self.far1_to_c(zo)]

    def arrived(self, dist):
        self.seen.add(dist)
        self.pos.at(dist, lambda zo: [c.wait_recv() for c in self.from_core(zo)])

    def end_one(self, zo, mine=False, seen=False):
        arrivals = self.from_core(zo, mine)
        sends = [self.to_x(zo, mine), self.to_y(zo, mine), self.x_to_y(zo)] + arrivals
        if self.h1 is not None:
            sends.append(self.y_to_x(zo))
        if not seen:
            for c in arrivals:
                c.wait_recv()
        self.along_z(zo, mine, lambda c: c.wait_send())
        for c in sends:
            c.wait_send()

    def end(self):
        self.end_one(self.pos.z, True, 0 in self.seen)
        for r in range(1, self.pos.depth):
            self.pos.at(r, lambda zo: self.end_one(zo, False, r in self.seen))

    @staticmethod
    def sems(depth):
        return [pltpu.SemaphoreType.DMA((Gather.SEND, depth)), pltpu.SemaphoreType.DMA((Gather.RECV, depth))]


class SideGather:
    def __init__(self, pos, own, out, send, recv, side_send, side_recv, cols):
        self.pos, self.own, self.out = pos, own.at[:, cols], out.at[:, :, cols]
        self.send, self.recv = send, recv
        self.side_send, self.side_recv = side_send, side_recv
        rows = out.shape[1]
        self.half = (pl.ds(0, rows // 2), pl.ds(rows // 2, rows // 2))
        self.rounds = pos.depth + 2
        self.seen = set()

    @staticmethod
    def sems(depth):
        dma = pltpu.SemaphoreType.DMA
        return [dma((4, depth, 3)), dma((4, depth, 2)), dma((4,)), dma((4,))]

    def place(self, zo, k):
        return self.out.at[self.pos.block(zo, k // 2, k % 2)]

    def src(self, zo, k, mine):
        return self.own if mine and k == 0 else self.place(zo, k)

    def along(self, zo, k, way, mine=False):
        return self.pos.copy(
            self.src(zo, k, mine), self.place(zo, k), self.send.at[k, zo, way], self.recv.at[k, zo, 0], ("up", "down")[way]
        )

    def to_core(self, zo, k, mine=False):
        return self.pos.copy(self.src(zo, k, mine), self.place(zo, k), self.send.at[k, zo, 2], self.recv.at[k, zo, 1], "c")

    def across(self, k, to):
        z = self.pos.z
        if k < 2:
            src, dst = self.own, self.place(z, 0)
        else:
            src = dst = self.place(z, k - 1).at[self.half[k - 2]]
        return self.pos.copy(src, dst, self.side_send.at[k], self.side_recv.at[k], to)

    def on(self, zo, k, mine=False):
        self.along_z(zo, k, mine, lambda c: c.start())
        self.to_core(zo, k, mine).start()

    def along_z(self, zo, k, mine, what):
        z, depth = self.pos.z, self.pos.depth
        if mine:
            up, down = z < depth - 1, z > 0
        else:
            up, down = (zo < z) & (z < depth - 1), (zo > z) & (z > 0)

        @pl.when(up)
        def _():
            what(self.along(zo, k, 0, mine))

        @pl.when(down)
        def _():
            what(self.along(zo, k, 1, mine))

    def start(self):
        self.across(0, "x").start()
        self.across(1, "y").start()
        self.on(self.pos.z, 0, True)

    def on_far_height(self, zo):
        for k in range(4):
            self.along(zo, k, 0).wait_recv()
            self.on(zo, k)

    def round(self, r):
        z = self.pos.z
        if r == 1:
            self.across(0, "x").wait_recv()
            self.across(3, "y").start()
            self.on(z, 2, True)
            self.across(1, "y").wait_recv()
            self.across(2, "x").start()
            self.on(z, 1, True)
        if r == 2:
            self.across(2, "x").wait_recv()
            self.across(3, "y").wait_recv()
            self.on(z, 3, True)
        if 3 <= r <= self.pos.depth + 1:
            self.pos.at(r - 2, self.on_far_height)

    def arrived(self, dist):
        self.seen.add(dist)
        self.pos.at(dist, lambda zo: [self.to_core(zo, k).wait_recv() for k in range(4)])

    def end_one(self, zo, mine=False, seen=False):
        for k in range(4):
            if not seen:
                self.to_core(zo, k, mine).wait_recv()
            self.to_core(zo, k, mine).wait_send()
            self.along_z(zo, k, mine, lambda c: c.wait_send())

    def end(self):
        for k in range(4):
            self.across(k, "xyxy"[k]).wait_send()
        self.end_one(self.pos.z, True, 0 in self.seen)
        for r in range(1, self.pos.depth):
            self.pos.at(r, lambda zo: self.end_one(zo, False, r in self.seen))


class Reduce:
    SENDS = 16

    def __init__(self, pos, part, core, far, side, column, flank_z, flank_far, flank_side, send, recv, halves=True):
        self.pos, self.part = pos, part
        self.core, self.far, self.side, self.column = core, far, side, column
        self.flank_z, self.flank_far, self.flank_side = flank_z, flank_far, flank_side
        self.send, self.recv = send, recv
        rows, width = core.shape[2:]
        flank = flank_z.shape[-1] if len(flank_z.shape) == 5 else 0
        self.main, self.flank = pl.ds(0, width - flank), pl.ds(width - flank, flank)
        self.flanked = flank > 0
        self.half = (pl.ds(0, rows // 2), pl.ds(rows // 2, rows // 2)) if halves else (pl.ds(0, rows),)
        self.rounds = pos.depth + 2

    @staticmethod
    def scratch(depth, rows, width, halves=True, flank=0):
        b = jnp.bfloat16
        main = width - flank
        refs = [
            pltpu.VMEM((depth, 4, rows, width), b),
            pltpu.VMEM((depth, 2, rows // 2, main) if halves else (depth, 1, rows, main), b),
            pltpu.VMEM((depth, 2, rows, main), b),
            pltpu.VMEM((depth, 2, rows, main), b),
        ]
        refs += [
            pltpu.VMEM((depth, 2, 4, rows, flank) if flank else (8, 128), b),
            pltpu.VMEM((2, rows // 2, flank) if flank else (8, 128), b),
            pltpu.VMEM((2, rows, flank) if flank else (8, 128), b),
        ]
        dma = pltpu.SemaphoreType.DMA
        return refs + [dma((Reduce.SENDS, depth)), dma((Reduce.SENDS, depth))]

    SCRATCH = 9

    def link(self, src, dst, k, zo, to):
        return self.pos.copy(src, dst, self.send.at[k, zo], self.recv.at[k, zo], to)

    def to_core(self, zo, fx, fy):
        k = fx * 2 + fy
        return self.link(self.part.at[self.pos.block(zo, fx, fy, 1)], self.core.at[zo, k], k, zo, "c")

    def far_to(self, zo, k):
        src = self.core.at[zo, 3, self.half[k], self.main]
        return self.link(src, self.far.at[zo, k], 4 + k, zo, ("y", "x")[k])

    def side_to(self, zo, k):
        return self.link(self.core.at[zo, 2 - k, :, self.main], self.side.at[zo, k], 6 + k, zo, ("x", "y")[k])

    def down(self, zo):
        return self.link(self.core.at[zo, 0, :, self.main], self.column.at[zo, 0], 8, zo, "down")

    def up(self, zo):
        return self.link(self.core.at[zo, 0, :, self.main], self.column.at[zo, 1], 9, zo, "up")

    def flank_down(self, zo):
        return self.link(self.core.at[zo, :, :, self.flank], self.flank_z.at[zo, 0], 10, zo, "down")

    def flank_up(self, zo):
        return self.link(self.core.at[zo, :, :, self.flank], self.flank_z.at[zo, 1], 11, zo, "up")

    def flank_far_to(self, k):
        z = self.pos.z
        rows = self.core.shape[2] // 2
        src = self.core.at[z, 3, pl.ds(k * rows, rows), self.flank]
        return self.link(src, self.flank_far.at[k], 12 + k, z, ("y", "x")[k])

    def flank_side_to(self, k):
        z = self.pos.z
        return self.link(self.core.at[z, 2 - k, :, self.flank], self.flank_side.at[k], 14 + k, z, ("x", "y")[k])

    def start_one(self, zo):
        for fx, fy in ((1, 1), (1, 0), (0, 1), (0, 0)):
            self.to_core(zo, fx, fy).start()

    def start(self):
        for dist in reversed(range(self.pos.depth)):
            self.pos.at(dist, self.start_one)

    def total(self, *refs):
        f = refs[0][...].astype(jnp.float32)
        for r in refs[1:]:
            f = f + r[...].astype(jnp.float32)
        return f

    def add(self, here, *refs):
        here[...] = self.total(here, *refs).astype(here.dtype)

    def filled(self, zo):
        for h in range(len(self.half)):
            self.far_to(zo, h).start()

    def on_core(self, zo):
        if self.part is None:
            return
        for fx, fy in ((1, 1), (1, 0), (0, 1), (0, 0)):
            k = fx * 2 + fy
            self.to_core(zo, fx, fy).wait_recv()
            self.add(self.core.at[zo, k], self.part.at[self.pos.block(zo, fx, fy)])
            if k == 3:
                self.filled(zo)

    def from_farther(self, zo, down, up, take):
        z, depth = self.pos.z, self.pos.depth

        @pl.when((zo <= z) & (z < depth - 1))
        def _():
            down(zo).wait_recv()
            take(0)

        @pl.when((zo >= z) & (z > 0))
        def _():
            up(zo).wait_recv()
            take(1)

    def to_nearer(self, zo, down, up, what):
        @pl.when(zo < self.pos.z)
        def _():
            what(down(zo))

        @pl.when(zo > self.pos.z)
        def _():
            what(up(zo))

    def flank_along_z(self, zo):
        here = self.core.at[zo, :, :, self.flank]
        self.from_farther(zo, self.flank_down, self.flank_up, lambda k: self.add(here, self.flank_z.at[zo, k]))
        self.to_nearer(zo, self.flank_down, self.flank_up, lambda c: c.start())

    def flank_far_start(self):
        for k in range(2):
            self.flank_far_to(k).start()

    def flank_on_far(self):
        z, rows = self.pos.z, self.core.shape[2] // 2
        for k in range(2):
            self.flank_far_to(k).wait_recv()
            self.add(self.core.at[z, 2 - k, pl.ds(k * rows, rows), self.flank], self.flank_far.at[k])
            self.flank_side_to(k).start()

    def flank_on_sides(self):
        self.flank_side_to(0).wait_recv()
        self.flank_side_to(1).wait_recv()
        here = self.core.at[self.pos.z, 0, :, self.flank]
        self.out[:, self.flank] = self.total(here, self.flank_side.at[0], self.flank_side.at[1])

    def on_far(self, zo):
        for k in range(2):
            if k < len(self.half):
                self.far_to(zo, k).wait_recv()
                self.add(self.core.at[zo, 2 - k, self.half[k], self.main], self.far.at[zo, k])
            self.side_to(zo, k).start()

    def on_sides(self, zo, mine=False):
        self.side_to(zo, 0).wait_recv()
        self.side_to(zo, 1).wait_recv()
        here = self.core.at[zo, 0, :, self.main]
        summed = self.total(here, self.side.at[zo, 0], self.side.at[zo, 1])
        if mine:
            self.out[:, self.main] = summed

            def take(k):
                self.out[:, self.main] += self.column[zo, k].astype(jnp.float32)

            self.from_farther(zo, self.down, self.up, take)
            return
        here[...] = summed.astype(here.dtype)
        self.from_farther(zo, self.down, self.up, lambda k: self.add(here, self.column.at[zo, k]))
        self.to_nearer(zo, self.down, self.up, lambda c: c.start())

    def round(self, r):
        depth = self.pos.depth
        for s in range(3):
            dist = depth - 1 - (r - s)
            if not 0 <= dist < depth:
                continue
            if s == 0:
                self.pos.at(dist, self.on_core)
                if self.flanked:
                    self.pos.at(dist, self.flank_along_z)
            elif s == 1:
                self.pos.at(dist, self.on_far)
            elif dist:
                self.pos.at(dist, self.on_sides)
            else:
                self.on_sides(self.pos.z, True)
        if self.flanked and r == depth - 1:
            self.flank_far_start()
        if self.flanked and r == depth:
            self.flank_on_far()
        if self.flanked and r == depth + 1:
            self.flank_on_sides()

    def end_one(self, zo):
        if self.part is not None:
            for fx in range(2):
                for fy in range(2):
                    self.to_core(zo, fx, fy).wait_send()
        for k in range(len(self.half)):
            self.far_to(zo, k).wait_send()
        for k in range(2):
            self.side_to(zo, k).wait_send()
        self.to_nearer(zo, self.down, self.up, lambda c: c.wait_send())
        if self.flanked:
            self.to_nearer(zo, self.flank_down, self.flank_up, lambda c: c.wait_send())

    def end(self):
        for r in range(self.pos.depth):
            self.pos.at(r, self.end_one)
        if self.flanked:
            for k in range(2):
                self.flank_far_to(k).wait_send()
                self.flank_side_to(k).wait_send()


class WideGather:
    def __init__(self, pos, own, out, flank, refs):
        main = out.shape[2] - flank
        self.parts = (
            SideGather(pos, own, out, *refs[2:6], pl.ds(main, flank)),
            Gather(pos, own, out, *refs[0:2], True, pl.ds(0, main)),
        )
        self.rounds = self.parts[0].rounds

    REFS = 6

    @staticmethod
    def sems(depth):
        return Gather.sems(depth) + SideGather.sems(depth)

    def start(self):
        for p in self.parts:
            p.start()

    def round(self, r):
        for p in self.parts:
            p.round(r)

    def arrived(self, dist):
        for p in self.parts:
            p.arrived(dist)

    def end(self):
        for p in self.parts:
            p.end()


class HubGather:
    def __init__(self, pos, own, dst, send, recv):
        self.pos, self.own, self.dst = pos, own, dst
        self.send, self.recv = send, recv
        self.rounds = pos.depth

    @staticmethod
    def sems(depth):
        return [pltpu.SemaphoreType.DMA((3, 2, depth)), pltpu.SemaphoreType.DMA((3, 2, depth))]

    def place(self, zo, k):
        return self.dst(zo * 2 + (1 - self.pos.x if k else self.pos.x))

    def link(self, zo, k, mine, way):
        src = self.own if mine and k == 0 else self.place(zo, k)
        recv = self.recv.at[1 if way == 2 else 0, k, zo]
        return self.pos.copy(src, self.place(zo, k), self.send.at[way, k, zo], recv, ("up", "down", "c")[way])

    def across(self):
        z = self.pos.z
        return self.pos.copy(self.own, self.dst(self.pos.d), self.send.at[0, 0, z], self.recv.at[2, 0, 0], "x")

    def along_z(self, zo, k, mine, what):
        z, depth = self.pos.z, self.pos.depth
        if mine:
            up, down = z < depth - 1, z > 0
        else:
            up, down = (zo < z) & (z < depth - 1), (zo > z) & (z > 0)

        @pl.when(up)
        def _():
            what(self.link(zo, k, mine, 0))

        @pl.when(down)
        def _():
            what(self.link(zo, k, mine, 1))

    def pass_on(self, zo, k, mine=False):
        self.along_z(zo, k, mine, lambda c: c.start())
        self.link(zo, k, mine, 2).start()

    def start(self):
        @pl.when(self.pos.hub)
        def _():
            self.pass_on(self.pos.z, 0, True)

        @pl.when(jnp.logical_not(self.pos.hub))
        def _():
            self.across().start()

    def on_height(self, zo):
        for k in range(2):
            self.link(zo, k, False, 0).wait_recv()
            self.pass_on(zo, k)

    def round(self, r):
        @pl.when(self.pos.hub)
        def _():
            if r == 1:
                self.across().wait_recv()
                self.pass_on(self.pos.z, 1, True)
            if 1 <= r < self.pos.depth:
                self.pos.at(r, self.on_height)

    def end_one(self, zo, mine=False):
        for k in range(2):

            @pl.when(self.pos.hub)
            def _():
                self.along_z(zo, k, mine, lambda c: c.wait_send())
                self.link(zo, k, mine, 2).wait_send()

            @pl.when(jnp.logical_not(self.pos.hub))
            def _():
                self.link(zo, k, mine, 2).wait_recv()

    def end(self):
        @pl.when(jnp.logical_not(self.pos.hub))
        def _():
            self.across().wait_send()

        self.end_one(self.pos.z, True)
        for r in range(1, self.pos.depth):
            self.pos.at(r, self.end_one)


class HubReduce:
    def __init__(self, pos, part, out, other, column, send, recv):
        self.pos, self.part, self.out = pos, part, out
        self.other, self.column = other, column
        self.send, self.recv = send, recv
        self.rounds = pos.depth + 1

    @staticmethod
    def scratch(depth, rows, width):
        b = jnp.bfloat16
        return [
            pltpu.VMEM((depth, 2, rows, width), b),
            pltpu.VMEM((depth, 2, 2, rows, width), b),
            pltpu.SemaphoreType.DMA((4, depth, 2)),
            pltpu.SemaphoreType.DMA((4, depth, 2)),
        ]

    def piece(self, zo, k):
        return self.part(zo * 2 + (1 - self.pos.x if k else self.pos.x))

    def to_core(self, zo, k):
        return self.pos.copy(self.piece(zo, k), self.other.at[zo, k], self.send.at[0, zo, k], self.recv.at[0, zo, k], "c")

    def chain(self, zo, way):
        return self.pos.copy(
            self.other.at[zo], self.column.at[zo, way], self.send.at[1 + way, zo, 0], self.recv.at[1 + way, zo, 0],
            ("down", "up")[way],
        )

    def across(self):
        z = self.pos.z
        landing = self.column.at[z, 0, 0]
        return self.pos.copy(self.other.at[z, 1], landing, self.send.at[3, 0, 0], self.recv.at[3, 0, 0], "x")

    def start_one(self, zo):
        for k in range(2):
            self.to_core(zo, k).start()

    def start(self):
        @pl.when(jnp.logical_not(self.pos.hub))
        def _():
            for dist in reversed(range(self.pos.depth)):
                self.pos.at(dist, self.start_one)

    def add(self, here, ref):
        here[...] = (here[...].astype(jnp.float32) + ref[...].astype(jnp.float32)).astype(here.dtype)

    def on_height(self, zo):
        z, depth = self.pos.z, self.pos.depth
        for k in range(2):
            self.to_core(zo, k).wait_recv()
            self.add(self.other.at[zo, k], self.piece(zo, k))

        @pl.when((zo <= z) & (z < depth - 1))
        def _():
            self.chain(zo, 0).wait_recv()
            self.add(self.other.at[zo], self.column.at[zo, 0])

        @pl.when((zo >= z) & (z > 0))
        def _():
            self.chain(zo, 1).wait_recv()
            self.add(self.other.at[zo], self.column.at[zo, 1])

        @pl.when(zo < z)
        def _():
            self.chain(zo, 0).start()

        @pl.when(zo > z)
        def _():
            self.chain(zo, 1).start()

    def round(self, r):
        depth = self.pos.depth

        @pl.when(self.pos.hub)
        def _():
            if r < depth:
                self.pos.at(depth - 1 - r, self.on_height)
            if r == depth - 1:
                self.across().start()
                self.out[...] = self.other[self.pos.z, 0].astype(jnp.float32)

        if r == depth:

            @pl.when(jnp.logical_not(self.pos.hub))
            def _():
                self.across().wait_recv()
                self.out[...] = self.column[self.pos.z, 0, 0].astype(jnp.float32)

    def end_one(self, zo):
        @pl.when(jnp.logical_not(self.pos.hub))
        def _():
            for k in range(2):
                self.to_core(zo, k).wait_send()

        @pl.when(self.pos.hub & (zo < self.pos.z))
        def _():
            self.chain(zo, 0).wait_send()

        @pl.when(self.pos.hub & (zo > self.pos.z))
        def _():
            self.chain(zo, 1).wait_send()

    def end(self):
        for r in range(self.pos.depth):
            self.pos.at(r, self.end_one)

        @pl.when(self.pos.hub)
        def _():
            self.across().wait_send()


class Exchange:
    def __init__(self, pos, out, piece, place, send, recv, local):
        self.pos, self.piece, self.place = pos, piece, place
        self.send, self.recv, self.local = send, recv, local
        self.groups = pos.groups
        self.rounds = 0
        self.mine, self.here = (pos.d, pos.head) if out else (pos.head, pos.d)
        self.to = pos.owner if out else pos.shard

    @staticmethod
    def sems(depth):
        n = depth * 2
        return [pltpu.SemaphoreType.DMA((n,)), pltpu.SemaphoreType.DMA((n,)), pltpu.SemaphoreType.DMA]

    def copy(self, k):
        return pltpu.make_async_remote_copy(
            src_ref=self.piece(k),
            dst_ref=self.place(self.mine),
            send_sem=self.send.at[k],
            recv_sem=self.recv.at[self.mine],
            device_id=self.to(k),
            device_id_type=MESH,
        )

    def arrival(self, k):
        return pltpu.make_async_remote_copy(
            src_ref=self.piece(k),
            dst_ref=self.place(k),
            send_sem=self.send.at[k],
            recv_sem=self.recv.at[k],
            device_id=self.to(k),
            device_id_type=MESH,
        )

    def inside(self):
        return pltpu.make_async_copy(self.piece(self.here), self.place(self.mine), self.local)

    def each(self, number, what):
        for i in range(1, self.groups + 1):
            k = lax.rem(number + i, self.groups)
            if i < self.groups:
                what(k)
            else:

                @pl.when(jnp.logical_not(self.pos.hub))
                def _():
                    what(k)

    def start(self):
        @pl.when(self.pos.hub)
        def _():
            self.inside().start()

        self.each(self.here, lambda k: self.copy(k).start())

    def round(self, r):
        pass

    def end(self):
        @pl.when(self.pos.hub)
        def _():
            self.inside().wait()

        self.each(self.mine, lambda k: self.arrival(k).wait_recv())
        self.each(self.here, lambda k: self.copy(k).wait_send())


class CoreSwap:
    def __init__(self, pos, stage, got, send, recv):
        self.pos, self.stage, self.got = pos, stage, got
        self.send, self.recv = send, recv

    @staticmethod
    def scratch(depth, rows, width):
        dma = pltpu.SemaphoreType.DMA
        return [pltpu.VMEM((depth, 4, rows, width), jnp.bfloat16)] * 2 + [dma((depth,)), dma((depth,))]

    def copy(self, zo):
        return self.pos.copy(self.stage.at[zo], self.got.at[zo], self.send.at[zo], self.recv.at[zo], "c")

    def rows(self, zo, k, other=0):
        size = self.stage.shape[2]
        return pl.ds(pl.multiple_of(self.pos.block(zo, k // 2, k % 2, other) * size, size), size)

    def start(self, zo, values):
        for k in range(4):
            self.stage[zo, k] = values[self.rows(zo, k, 1), :].astype(self.stage.dtype)
        self.copy(zo).start()

    def both(self, zo, values):
        self.copy(zo).wait_recv()
        mine = [values[self.rows(zo, k), :].astype(self.got.dtype) for k in range(4)]
        theirs = self.got[zo].reshape(-1, self.got.shape[3])
        return jnp.concatenate([jnp.concatenate(mine, axis=0), theirs], axis=1)

    def end(self):
        for zo in range(self.pos.depth):
            self.copy(zo).wait_send()


def drive(*parts):
    for p in parts:
        p.start()
    for r in range(max(p.rounds for p in parts)):
        for p in parts:
            p.round(r)
    for p in parts:
        p.end()


def params(number, vmem=None):
    return pltpu.CompilerParams(collective_id=number, has_side_effects=True, vmem_limit_bytes=vmem)


def rows_of(ref, p, rows):
    return ref.at[pl.ds(p * rows, rows)]


def cols_of(ref, p, cols):
    return ref.at[:, pl.ds(pl.multiple_of(p * cols, cols), cols)]


def part_of(ref, p, rows, first, cols):
    return ref.at[pl.ds(p * rows, rows), pl.ds(first, cols)]


def dot(a, b):
    return jnp.dot(a, b, preferred_element_type=jnp.float32)


def dot_nt(a, b):
    return lax.dot_general(a, b, (((1,), (1,)), ((), ())), preferred_element_type=jnp.float32)


def dot_tn(a, b):
    return lax.dot_general(a, b, (((0,), (0,)), ((), ())), preferred_element_type=jnp.float32)


def loop(count, step):
    lax.fori_loop(0, count, lambda i, _: (step(i), 0)[1], 0)


def norm_back(values, gain, grad):
    r = lax.rsqrt(jnp.mean(values * values, axis=-1, keepdims=True) + EPS)
    unit = values * r
    scaled = grad * gain
    return r * (scaled - unit * jnp.mean(scaled * unit, axis=-1, keepdims=True)), grad * unit


def experts(depth, number, normed, all_grad, all_named, middle, moe_gain, router_t, w_gate, w_up, w_down):
    f32, bf = jnp.float32, jnp.bfloat16
    rows, width = normed.shape
    devices = depth * 8
    plane_rows = rows * 8
    picks = plane_rows // 2
    slots = depth * picks
    ff = w_gate.shape[1]
    lanes = all_named.shape[2]
    count = router_t.shape[0]
    wide = width + lanes

    def body(
        n_ref, g_ref, named_hbm, mid_ref, gain_ref, router_ref, wg_hbm, wu_hbm, wd_hbm,
        layer_out, grad_middle, grad_block, gain_grad, n_all, x_out, gret_out, inner_out, gboth_out,
        wg, wu, wd, nb, gb, ob, part, xin, gret, ret, inner, gboth, act_a, act_u, gates, out_sum, grad_sum,
        named, select_t, router_wide, gain_row,
        w_sem, own_sem, all_sem, keep_sem, *rest,
    ):
        pos = Place(depth)
        expert = pos.block(pos.z)
        loads = [
            pltpu.make_async_copy(src, dst, w_sem.at[i])
            for i, (src, dst) in enumerate(((wg_hbm, wg), (wu_hbm, wu), (wd_hbm, wd), (named_hbm, named)))
        ]
        own = [
            pltpu.make_async_copy(n_ref, nb.at[expert], own_sem.at[0]),
            pltpu.make_async_copy(g_ref, gb, own_sem.at[1]),
        ]
        for c in [loads[3]] + own[:1] + loads[:3] + own[1:]:
            c.start()
        pos.greet()
        g_normed = WideGather(pos, n_ref, nb, GATHER_FLANK, rest[0:6])
        r_out = Reduce(pos, ob, *rest[6:15])
        r_grad = Reduce(pos, part, *rest[15:24])
        r_out.out, r_grad.out = out_sum, grad_sum

        def plane(ref, z):
            return ref[pl.ds(z * 8, 8)].reshape(plane_rows, ref.shape[2])

        def picked(z):
            return pl.ds(pl.multiple_of(z * picks, picks), picks)

        here = lax.broadcasted_iota(jnp.int32, (plane_rows, lanes), 1) == expert

        def choose(z):
            names = plane(named, z)
            ones = names.astype(f32)
            above = lax.broadcasted_iota(jnp.int32, (plane_rows, plane_rows), 0)
            upto = lax.broadcasted_iota(jnp.int32, (plane_rows, plane_rows), 1) <= above
            counts = dot(upto.astype(f32).astype(bf), names)
            place = jnp.sum(jnp.where(here, counts * ones, 0.0), axis=1, keepdims=True) - 1.0
            pick = lax.broadcasted_iota(jnp.int32, (plane_rows, picks), 1).astype(f32)
            select_t[z] = jnp.where(place == pick, 1.0, 0.0).astype(bf)

        def take(z):
            tok = plane(nb, z)
            logits = dot_nt(tok, router_wide[...])
            chosen = plane(named, z).astype(f32) > 0
            top = jnp.max(jnp.where(chosen, logits, -1e30), axis=1, keepdims=True)
            raised = jnp.where(chosen, jnp.exp(jnp.minimum(logits - top, 0.0)), 0.0)
            gates[z] = raised / jnp.sum(raised, axis=1, keepdims=True)
            xin[picked(z), :] = dot_tn(select_t[z], tok).astype(bf)

        near = pos.z // 2
        apart = 1 - near

        def both(h, step):
            loop(2, lambda j: step(2 * h + j))

        def in_pair(h):
            return pl.ds(pl.multiple_of(h * 2 * picks, 2 * picks), 2 * picks)

        def forward(h):
            x = xin[in_pair(h), :]
            a = dot(x, wg[...])
            u = dot(x, wu[...])
            act_a[in_pair(h), :] = a
            act_u[in_pair(h), :] = u
            inner[in_pair(h), :] = (a / (1.0 + jnp.exp(-a)) * u).astype(bf)

        def produce(h):
            ret[in_pair(h), :] = dot(inner[in_pair(h), :], wd[...]).astype(bf)

        def spread(z):
            gate = gates[z]
            mine = jnp.sum(jnp.where(here, gate, 0.0), axis=1, keepdims=True)
            g = plane(gb, z).astype(f32)
            gret[picked(z), :] = dot_tn(select_t[z], (mine * g).astype(bf)).astype(bf)
            back = dot(select_t[z], ret[picked(z), :])
            ob[pl.ds(z * 8, 8)] = (mine * back).astype(bf).reshape(8, rows, width)
            summed = jnp.sum(g * back, axis=1, keepdims=True)
            logit = gate * (jnp.where(here, 1.0, 0.0) - mine) * summed
            part[pl.ds(z * 8, 8), :, pl.ds(width, lanes)] = logit.astype(bf).reshape(8, rows, lanes)

        def backward(h):
            gi = dot_nt(gret[in_pair(h), :], wd[...])
            a = act_a[in_pair(h), :]
            s = 1.0 / (1.0 + jnp.exp(-a))
            gboth[in_pair(h), pl.ds(0, ff)] = (gi * act_u[in_pair(h), :] * (s + a * s * (1.0 - s))).astype(bf)
            gboth[in_pair(h), pl.ds(ff, ff)] = (gi * (a * s)).astype(bf)

        def inputs_back(h):
            by_gate, by_up = gboth[in_pair(h), pl.ds(0, ff)], gboth[in_pair(h), pl.ds(ff, ff)]
            ret[in_pair(h), :] = (dot_nt(by_gate, wg[...]) + dot_nt(by_up, wu[...])).astype(bf)

        def scatter(z):
            back = dot(select_t[z], ret[picked(z), :]).astype(bf)
            part[pl.ds(z * 8, 8), :, pl.ds(0, width)] = back.reshape(8, rows, width)
            r_grad.start_one(z)

        g_normed.start()
        as_row(gain_ref, gain_row)
        router_wide[...] = jnp.zeros(router_wide.shape, bf)
        router_wide[pl.ds(0, count), :] = router_ref[...]
        for r in range(1, 4):
            g_normed.round(r)
            if r == 1:
                loads[3].wait()
            if r < 3:
                both(r - 1, choose)
        own[0].wait()
        g_normed.arrived(0)
        g_normed.arrived(1)
        both(near, take)
        g_normed.round(4)
        loads[0].wait()
        loads[1].wait()
        forward(near)
        g_normed.round(5)
        loads[2].wait()
        produce(near)
        own[1].wait()
        both(near, spread)
        for dist in range(2, depth):
            g_normed.arrived(dist)
        both(apart, take)
        g_normed.end()
        keep = pltpu.make_async_copy(nb, n_all, all_sem)
        keep.start()
        forward(apart)
        produce(apart)
        both(apart, spread)
        r_out.start()
        backward(apart)
        r_out.round(0)
        inputs_back(apart)
        for dist in reversed(range(2, depth)):
            pos.at(dist, scatter)
        r_grad.round(0)
        r_out.round(1)
        backward(near)
        r_grad.round(1)
        r_out.round(2)
        inputs_back(near)
        for dist in reversed(range(2)):
            pos.at(dist, scatter)
        kept = [
            pltpu.make_async_copy(src, dst, keep_sem.at[i])
            for i, (src, dst) in enumerate(((xin, x_out), (gret, gret_out), (inner, inner_out), (gboth, gboth_out)))
        ]
        for c in kept:
            c.start()
        for r in range(3, r_out.rounds):
            r_grad.round(r - 1)
            r_out.round(r)
        r_grad.round(r_out.rounds - 1)
        keep.wait()
        mid = mid_ref[...]
        layer_out[...] = (mid + out_sum[...]).astype(bf)
        logit = grad_sum[:, pl.ds(width, lanes)].astype(bf)
        change, by_gain = norm_back(mid, gain_row[...], grad_sum[:, pl.ds(0, width)] + dot(logit, router_wide[...]))
        gain_grad[...] = jnp.sum(by_gain, axis=0, keepdims=True)
        change = gb[expert].astype(f32) + change
        grad_middle[...] = change
        grad_block[:, pl.ds(0, width)] = change.astype(bf)
        grad_block[:, pl.ds(width, lanes)] = logit
        for c in kept:
            c.wait()
        r_out.end()
        r_grad.end()

    vmem, hbm = pl.BlockSpec(memory_space=pltpu.VMEM), pl.BlockSpec(memory_space=HBM)
    dma = pltpu.SemaphoreType.DMA
    shape = jax.ShapeDtypeStruct
    return pl.pallas_call(
        body,
        out_shape=[
            shape((rows, width), bf),
            shape((rows, width), f32),
            shape((rows, wide), bf),
            shape((1, width), f32),
            shape((devices, rows, width), bf),
            shape((slots, width), bf),
            shape((slots, width), bf),
            shape((slots, ff), bf),
            shape((slots, 2 * ff), bf),
        ],
        in_specs=[hbm] * 3 + [vmem] * 3 + [hbm] * 3,
        out_specs=[vmem] * 4 + [hbm] * 5,
        scratch_shapes=[
            pltpu.VMEM((width, ff), bf),
            pltpu.VMEM((width, ff), bf),
            pltpu.VMEM((ff, width), bf),
            pltpu.VMEM((devices, rows, width), bf),
            pltpu.VMEM((devices, rows, width), bf),
            pltpu.VMEM((devices, rows, width), bf),
            pltpu.VMEM((devices, rows, wide), bf),
            pltpu.VMEM((slots, width), bf),
            pltpu.VMEM((slots, width), bf),
            pltpu.VMEM((slots, width), bf),
            pltpu.VMEM((slots, ff), bf),
            pltpu.VMEM((slots, 2 * ff), bf),
            pltpu.VMEM((slots, ff), f32),
            pltpu.VMEM((slots, ff), f32),
            pltpu.VMEM((depth, plane_rows, lanes), f32),
            pltpu.VMEM((rows, width), f32),
            pltpu.VMEM((rows, wide), f32),
            pltpu.VMEM((devices, rows, lanes), bf),
            pltpu.VMEM((depth, plane_rows, picks), bf),
            pltpu.VMEM((lanes, width), bf),
            pltpu.VMEM((1, width), f32),
            dma((4,)),
            dma((2,)),
            dma,
            dma((5,)),
        ]
        + WideGather.sems(depth)
        + Reduce.scratch(depth, rows, width, flank=REDUCE_FLANK)
        + Reduce.scratch(depth, rows, wide, flank=REDUCE_FLANK),
        compiler_params=params(number, 60 * 2**20),
        name="experts",
    )(normed, all_grad, all_named, middle, moe_gain, router_t, w_gate, w_up, w_down)


def finish(pairs, grad_q, grad_o, as_they_are):
    f32 = jnp.float32
    xin, gret, inner, gboth = pairs
    slots, width = xin.shape
    ff = inner.shape[1]
    tiles, halves = 8, 2
    n = len(as_they_are)

    def body(x_h, g_h, i_h, b_h, q_h, o_h, *refs):
        given, (wg, wu, wd, wq, wo), same = refs[:n], refs[n : n + 5], refs[n + 5 : 2 * n + 5]
        x, g, i, b, q, o, gate, up, down, q32, o32 = refs[2 * n + 5 : 2 * n + 16]
        held, (load_sem, store_sem, same_sem) = refs[2 * n + 16 : 3 * n + 16], refs[3 * n + 16 :]
        loads = [
            pltpu.make_async_copy(src, dst, load_sem.at[k])
            for k, (src, dst) in enumerate(((b_h, b), (x_h, x), (i_h, i), (g_h, g), (q_h, q), (o_h, o)))
        ]
        for c in loads:
            c.start()
        whole = [pltpu.make_async_copy(src, dst, same_sem.at[k]) for k, (src, dst) in enumerate(zip(given, held))]
        for c in whole:
            c.start()
        stores = []

        def store(src, dst):
            stores.append(pltpu.make_async_copy(src, dst, store_sem.at[len(stores)]))
            stores[-1].start()

        loads[0].wait()
        loads[1].wait()
        for t in range(tiles):
            rows = pl.ds(t * (width // tiles), width // tiles)
            both = dot_tn(x[:, rows], b[...])
            gate[rows, :] = both[:, :ff]
            up[rows, :] = both[:, ff:]
            store(gate.at[rows], wg.at[rows])
            store(up.at[rows], wu.at[rows])
        loads[2].wait()
        loads[3].wait()
        for t in range(halves):
            rows = pl.ds(t * (ff // halves), ff // halves)
            down[rows, :] = dot_tn(i[:, rows], g[...])
            store(down.at[rows], wd.at[rows])
        for k, (half, full, out) in enumerate(((q, q32, wq), (o, o32, wo))):
            loads[4 + k].wait()
            full[...] = half[...].astype(f32)
            store(full, out)
        for c, src, dst in zip(whole, held, same):
            c.wait()
            store(src, dst)
        for c in stores:
            c.wait()

    shape = jax.ShapeDtypeStruct
    dma = pltpu.SemaphoreType.DMA
    hbm = pl.BlockSpec(memory_space=HBM)
    inputs = (*pairs, grad_q, grad_o)
    return pl.pallas_call(
        body,
        out_shape=[shape((width, ff), f32)] * 2
        + [shape((ff, width), f32)]
        + [shape(grad_q.shape, f32)] * 2
        + [shape(a.shape, a.dtype) for a in as_they_are],
        in_specs=[hbm] * (6 + n),
        out_specs=[hbm] * (5 + n),
        scratch_shapes=[pltpu.VMEM(a.shape, a.dtype) for a in inputs]
        + [pltpu.VMEM((width, ff), f32)] * 2
        + [pltpu.VMEM((ff, width), f32)]
        + [pltpu.VMEM(grad_q.shape, f32)] * 2
        + [pltpu.VMEM(a.shape, a.dtype) for a in as_they_are]
        + [dma((6,)), dma((2 * tiles + halves + 2 + n,)), dma((n,))],
        compiler_params=pltpu.CompilerParams(vmem_limit_bytes=62 * 2**20),
        name="finish",
    )(*inputs, *as_they_are)


def as_row(ref, row):
    for i in range(ref.shape[0]):
        row[:, pl.ds(i * 128, 128)] = ref[pl.ds(i, 1), :].astype(jnp.float32)


def turn(u, cosine, sine):
    return u * cosine + pltpu.roll(u, u.shape[1] // 2, 1) * sine


def attend(depth, number, tokens, routes_t, out_grad, q_weight, k_weight, v_weight, out_weight, gains, frequency, docs):
    f32, bf = jnp.float32, jnp.bfloat16
    norm_gain, q_gain, k_gain, moe_gain = gains
    devices = depth * 8
    rows, width = tokens.shape[0] // 4, tokens.shape[1]
    w_rows, head = k_weight.shape
    total = devices * rows
    plane_rows = total // depth
    scale = head ** (-0.5)

    def body(
        tok, route, grad, wq, wk, wv, wo, ng, qg, kg, mg, freq, drow,
        middle, normed, all_named, all_grad, all_tok, hidden_out, wi_out, wo_out, proj_out, q_out, k_out, v_out, head_out,
        total_out, cos_out, sin_out,
        projected, queries, keys, values, heads, totals, cosines, sines, tb, hb, w_in, w_o, both_o, branch, doc, home, norm_row, moe_row, route_wide, names, own_sem, keep_sem, *rest,
    ):
        pos = Place(depth)
        device = pos.block(pos.z)
        share = tok.at[pl.ds(pl.multiple_of(pos.t * rows, rows), rows)]
        route_wide[...] = jnp.full(route_wide.shape, -1, jnp.int32)
        route_wide[pl.ds(0, route.shape[0]), pl.ds(0, rows)] = route[...]
        one = lax.broadcasted_iota(jnp.int32, (128, 128), 0)
        hits = jnp.zeros((128, 128), f32)
        for k in range(route.shape[0]):
            hits += jnp.where(route_wide[pl.ds(k, 1), :] == one, 1.0, 0.0)
        names[...] = hits.T[:rows].astype(bf)
        own = [
            pltpu.make_async_copy(src, dst, own_sem.at[i])
            for i, (src, dst) in enumerate(
                (
                    (names, all_named.at[device]),
                    (share, tb.at[device]),
                    (share, home),
                    (grad, all_grad.at[device]),
                )
            )
        ]
        for c in own:
            c.start()
        own_kv = [
            pltpu.make_async_copy(src, part_of(w_in, pos.d, w_rows, first, head), own_sem.at[4 + i])
            for i, (src, first) in enumerate(((wk, head), (wv, 2 * head)))
        ]

        @pl.when(pos.hub)
        def _():
            for c in own_kv:
                c.start()

        pos.greet("out")
        g_k = HubGather(pos, wk, lambda p: part_of(w_in, p, w_rows, head, head), *rest[0:2])
        g_v = HubGather(pos, wv, lambda p: part_of(w_in, p, w_rows, 2 * head, head), *rest[2:4])
        g_tok = Gather(pos, share, tb, *rest[4:6], TOKEN_HALVES)
        g_names = Gather(pos, names, all_named, *rest[6:8], False)
        x_q = Exchange(pos, True, lambda p: cols_of(wq, p, head), lambda p: part_of(w_in, p, w_rows, 0, head), *rest[8:11])
        x_o = Exchange(pos, True, lambda p: cols_of(wo, p, head), lambda p: rows_of(w_o, p, w_rows), *rest[11:14])
        red = Reduce(pos, None, *rest[14:23], halves=ATTEND_HALVES)
        swap = CoreSwap(pos, *rest[29:33])
        own_o, other_o = both_o.at[pl.ds(0, head)], both_o.at[pl.ds(head, head)]
        swap_o = pos.copy(own_o, other_o, rest[33].at[0], rest[33].at[1], "c")
        red.out = branch
        g_grad = WideGather(pos, grad, all_grad, OUT_GRAD_FLANK, rest[23:29])

        def span(z):
            return pl.ds(pl.multiple_of(z * plane_rows, plane_rows), plane_rows)

        def angle(z):
            place = lax.broadcasted_iota(jnp.int32, (plane_rows, total), 0) + z * plane_rows
            other = lax.broadcasted_iota(jnp.int32, (plane_rows, total), 1)
            all_docs = drow[...].astype(f32)
            docs_here = jnp.sum(jnp.where(other == place, all_docs, 0.0), axis=1, keepdims=True)
            doc[span(z), :] = jnp.broadcast_to(docs_here, (plane_rows, head))
            before = jnp.where((other < place) & (all_docs == docs_here), 1.0, 0.0)
            turned = jnp.sum(before, axis=1, keepdims=True) * freq[...]
            cosines[span(z), :] = jnp.cos(turned)
            sign = jnp.where(lax.broadcasted_iota(jnp.int32, (plane_rows, head), 1) < head // 2, -1.0, 1.0)
            sines[span(z), :] = jnp.sin(turned) * sign

        def normalise(z):
            t = tb[pl.ds(z * 8, 8)].reshape(plane_rows, width).astype(f32)
            r = lax.rsqrt(jnp.mean(t * t, axis=1, keepdims=True) + EPS)
            hb[pl.ds(z * 8, 8)] = (t * r * norm_row[...]).astype(bf).reshape(8, rows, width)

        def project(z):
            p = dot(hb[pl.ds(z * 8, 8)].reshape(plane_rows, width), w_in[...])
            projected[span(z), :] = p
            for ref, first, gain in ((queries, 0, qg), (keys, head, kg)):
                u = p[:, first : first + head]
                u = u * lax.rsqrt(jnp.mean(u * u, axis=1, keepdims=True) + EPS) * gain[...].astype(f32)
                ref[span(z), :] = turn(u, cosines[span(z), :], sines[span(z), :]).astype(bf)
            values[span(z), :] = p[:, 2 * head :].astype(bf)

        def attention(z):
            place = lax.broadcasted_iota(jnp.int32, (plane_rows, total), 0) + z * plane_rows
            allowed = (lax.broadcasted_iota(jnp.int32, (plane_rows, total), 1) <= place) & (
                doc[span(z), pl.ds(0, 1)] == drow[...].astype(f32)
            )
            s = jnp.where(allowed, dot_nt(queries[span(z), :], keys[...]) * scale, -1e30)
            top = jnp.max(s, axis=1, keepdims=True)
            w = jnp.exp(s - top)
            mass = jnp.sum(w, axis=1, keepdims=True)
            out = dot(w.astype(bf), values[...]) / mass
            heads[span(z), :] = out
            totals[span(z), :] = jnp.broadcast_to(top + jnp.log(mass), (plane_rows, head))

        def attend_one(z):
            attention(z)
            swap.start(z, heads)

        def spread(z):
            both = swap.both(z, heads)
            red.core[z] = dot(both, both_o[...]).astype(bf).reshape(4, rows, width)
            red.filled(z)

        kept = []

        def keep(src, dst):
            kept.append(pltpu.make_async_copy(src, dst, keep_sem.at[len(kept)]))
            kept[-1].start()

        g_tok.start()
        g_k.start()
        g_v.start()
        as_row(ng, norm_row)
        as_row(mg, moe_row)
        loop(depth, angle)
        keep(cosines, cos_out)
        keep(sines, sin_out)
        for c in own[:3]:
            c.wait()
        for r in range(1, g_tok.rounds):
            g_tok.round(r)
            g_k.round(r)
            g_v.round(r)
            if r == 2:
                x_q.start()
            if r == 4:
                x_o.start()
            if r >= 3:
                g_tok.arrived(r - 3)
                pos.at(r - 3, normalise)
        g_names.start()
        g_grad.start()
        g_tok.arrived(depth - 1)
        pos.at(depth - 1, normalise)
        g_tok.end()
        keep(tb, all_tok)
        keep(hb, hidden_out)
        g_k.end()
        g_v.end()

        @pl.when(pos.hub)
        def _():
            for c in own_kv:
                c.wait()

        x_q.end()
        keep(w_in, wi_out)
        loop(depth, project)
        for src, dst in ((projected, proj_out), (queries, q_out), (keys, k_out), (values, v_out)):
            keep(src, dst)
        g_grad.round(1)
        x_o.end()
        keep(w_o, wo_out)
        own_o[...] = w_o[...].T
        swap_o.start()
        for dist in reversed(range(depth)):
            pos.at(dist, attend_one)
        swap_o.wait_recv()
        keep(heads, head_out)
        keep(totals, total_out)
        for r in range(red.rounds):
            if r < depth:
                pos.at(depth - 1 - r, spread)
            red.round(r)
            g_names.round(r)
            if r >= 2:
                g_grad.round(r)
        mid = home[...].astype(f32) + branch[...]
        middle[...] = mid
        normed[...] = (mid * lax.rsqrt(jnp.mean(mid * mid, axis=1, keepdims=True) + EPS) * moe_row[...]).astype(bf)
        g_names.end()
        g_grad.end()
        for c in own[3:] + kept:
            c.wait()
        red.end()
        swap.end()
        swap_o.wait_send()

    vmem, hbm = pl.BlockSpec(memory_space=pltpu.VMEM), pl.BlockSpec(memory_space=HBM)
    dma = pltpu.SemaphoreType.DMA
    shape = jax.ShapeDtypeStruct
    return pl.pallas_call(
        body,
        out_shape=[
            shape((rows, width), f32),
            shape((rows, width), bf),
            shape((devices, rows, 128), bf),
            shape((devices, rows, width), bf),
            shape((devices, rows, width), bf),
            shape((devices, rows, width), bf),
            shape((width, 3 * head), bf),
            shape((width, head), bf),
            shape((total, 3 * head), f32),
            shape((total, head), bf),
            shape((total, head), bf),
            shape((total, head), bf),
            shape((total, head), f32),
            shape((total, head), f32),
            shape((total, head), f32),
            shape((total, head), f32),
        ],
        in_specs=[hbm, vmem] + [hbm] * 5 + [vmem] * 6,
        out_specs=[vmem] * 2 + [hbm] * 14,
        scratch_shapes=[
            pltpu.VMEM((total, 3 * head), f32),
            pltpu.VMEM((total, head), bf),
            pltpu.VMEM((total, head), bf),
            pltpu.VMEM((total, head), bf),
            pltpu.VMEM((total, head), f32),
            pltpu.VMEM((total, head), f32),
            pltpu.VMEM((total, head), f32),
            pltpu.VMEM((total, head), f32),
            pltpu.VMEM((devices, rows, width), bf),
            pltpu.VMEM((devices, rows, width), bf),
            pltpu.VMEM((width, 3 * head), bf),
            pltpu.VMEM((width, head), bf),
            pltpu.VMEM((2 * head, width), bf),
            pltpu.VMEM((rows, width), f32),
            pltpu.VMEM((total, head), f32),
            pltpu.VMEM((rows, width), bf),
            pltpu.VMEM((1, width), f32),
            pltpu.VMEM((1, width), f32),
            pltpu.VMEM((8, 128), jnp.int32),
            pltpu.VMEM((rows, 128), bf),
            dma((6,)),
            dma((12,)),
        ]
        + HubGather.sems(depth) * 2
        + Gather.sems(depth) * 2
        + Exchange.sems(depth) * 2
        + Reduce.scratch(depth, rows, width, ATTEND_HALVES, ATTEND_FLANK)
        + WideGather.sems(depth)
        + CoreSwap.scratch(depth, rows, head)
        + [dma((2,))],
        compiler_params=params(number, 60 * 2**20),
        name="attend",
    )(tokens, routes_t, out_grad, q_weight, k_weight, v_weight, out_weight, norm_gain, q_gain, k_gain, moe_gain, frequency, docs)


def attend_back(depth, number, block, moe_gain_grad, grad_middle, all_normed, experts_in_all, kept, gains, docs):
    f32, bf = jnp.float32, jnp.bfloat16
    all_tok, hidden, w_in, w_o, projected, queries, keys, values, heads, totals, cosines, sines = kept
    norm_gain, q_gain, k_gain = gains
    devices, rows, width = all_tok.shape
    wide = block.shape[1]
    lanes = wide - width
    total, head = queries.shape
    groups = depth * 2
    w_rows = width // groups
    plane_rows = total // depth
    scale = head ** (-0.5)
    gain_rows = width // 128
    small_rows = 2 * gain_rows + 8

    def body(
        blk, moe, gm, n_h, tok_h, hid_h, wi_h, wo_h, proj_h, q_h, k_h, v_h, head_h, tot_h, cos_h, sin_h, ng, qg, kg, drow,
        tokens_grad, q_grad, k_grad, v_grad, o_grad, norm_sum, moe_sum, q_sum, k_sum, router_grad,
        gb, nb, tb, hb, w_in, both_in, w_o, proj, qs, ks, vs, hs, ts, cos, sin, gh, dq, dk, dv, gproj, wpart, opart,
        kv_sum, hidden_sum, small, small_all, by_norm, by_q, by_k, doc, turned, norm_row, load_sem, own_sem, *rest,
    ):
        pos = Place(depth)
        device = pos.block(pos.z)
        own_in, other_in = both_in.at[pl.ds(0, 3 * head)], both_in.at[pl.ds(3 * head, 3 * head)]
        loads = [
            pltpu.make_async_copy(src, dst, load_sem.at[i])
            for i, (src, dst) in enumerate(
                (
                    (wo_h, w_o), (head_h, hs), (q_h, qs), (k_h, ks), (v_h, vs), (tot_h, ts), (wi_h, w_in), (proj_h, proj),
                    (cos_h, cos), (sin_h, sin), (hid_h, hb), (n_h, nb), (tok_h.at[device], tb),
                )
            )
        ]
        own = pltpu.make_async_copy(blk, gb.at[device], own_sem)
        own.start()
        for c in loads:
            c.start()
        pos.greet("back")
        g_branch = WideGather(pos, blk, gb, GATHER_FLANK, rest[0:6])
        g_small = Gather(pos, small, small_all, *rest[6:8], False)
        x_q = Exchange(
            pos, False, lambda p: part_of(wpart, p, w_rows, 0, head), lambda p: cols_of(q_grad, p, head), *rest[8:11]
        )
        x_o = Exchange(pos, False, lambda p: rows_of(opart, p, w_rows), lambda p: cols_of(o_grad, p, head), *rest[11:14])
        red = Reduce(pos, None, *rest[14:23], halves=BACK_HALVES)
        swap = CoreSwap(pos, *rest[27:31])
        swap_in = pos.copy(own_in, other_in, rest[31].at[0], rest[31].at[1], "c")
        red.out = hidden_sum
        r_kv = HubReduce(pos, lambda p: part_of(wpart, p, w_rows, head, 2 * head), kv_sum, *rest[23:27])

        def span(z):
            return pl.ds(pl.multiple_of(z * plane_rows, plane_rows), plane_rows)

        def column(z):
            place = lax.broadcasted_iota(jnp.int32, (plane_rows, total), 0) + z * plane_rows
            other = lax.broadcasted_iota(jnp.int32, (plane_rows, total), 1)
            docs_here = jnp.sum(jnp.where(other == place, drow[...].astype(f32), 0.0), axis=1, keepdims=True)
            doc[span(z), :] = jnp.broadcast_to(docs_here, (plane_rows, head))

        def heads_back(z):
            g = gb[pl.ds(z * 8, 8), :, pl.ds(0, width)].reshape(plane_rows, width)
            gh[span(z), :] = dot(g, w_o[...]).astype(bf)

        def out_weight_back():
            g = gb[:, :, pl.ds(0, width)].reshape(total, width)
            opart[...] = dot(turned[pl.ds(0, head), :], g).T.astype(bf)

        def attention_back(z):
            place = lax.broadcasted_iota(jnp.int32, (plane_rows, total), 0) + z * plane_rows
            allowed = (lax.broadcasted_iota(jnp.int32, (plane_rows, total), 1) <= place) & (
                doc[span(z), pl.ds(0, 1)] == drow[...].astype(f32)
            )
            q = qs[span(z), :]
            g = gh[span(z), :]
            delta = jnp.sum(g.astype(f32) * hs[span(z), :], axis=1, keepdims=True)
            s = dot_nt(q, ks[...]) * scale
            p = jnp.where(allowed, jnp.exp(jnp.minimum(s - ts[span(z), pl.ds(0, 1)], 0.0)), 0.0)
            ds = (p * (dot_nt(g, vs[...]) - delta)).astype(bf)
            dq[span(z), :] = dot(ds, ks[...]) * scale
            dk[...] += dot_tn(ds, q) * scale
            dv[...] += dot_tn(p.astype(bf), g)

        def project_back(z):
            for first, grad, gain, total_ref in ((0, dq, qg, by_q), (head, dk, kg, by_k)):
                g = turn(grad[span(z), :], cos[span(z), :], -sin[span(z), :])
                change, by_gain = norm_back(proj[span(z), pl.ds(first, head)], gain[...].astype(f32), g)
                gproj[span(z), pl.ds(first, head)] = change.astype(bf)
                total_ref[...] += jnp.sum(by_gain, axis=0, keepdims=True)
            gproj[span(z), pl.ds(2 * head, head)] = dv[span(z), :].astype(bf)

        def spread(z):
            red.core[z] = dot(swap.both(z, gproj), both_in[...]).astype(bf).reshape(4, rows, width)
            red.filled(z)

        def router_back():
            router_grad[...] = dot(turned[pl.ds(0, experts_in_all), :], nb[...].reshape(total, width))

        def in_weight_back():
            grads = dot(turned[...], hb[...].reshape(total, width))
            wpart[...] = grads.T.astype(bf)
            by_norm[...] = jnp.sum(grads * own_in[...].astype(f32), axis=0, keepdims=True) / norm_row[...]

        g_branch.start()
        as_row(ng, norm_row)
        loop(depth, column)
        dk[...] = jnp.zeros(dk.shape, f32)
        dv[...] = jnp.zeros(dv.shape, f32)
        by_q[...] = jnp.zeros(by_q.shape, f32)
        by_k[...] = jnp.zeros(by_k.shape, f32)
        small[...] = jnp.zeros(small.shape, f32)

        def plane_back(z):
            heads_back(z)
            attention_back(z)

        for r in range(1, g_branch.rounds):
            g_branch.round(r)
            if r == 2:
                own.wait()
                for c in loads[:7]:
                    c.wait()
                own_in[...] = w_in[...].T
                swap_in.start()
            if r >= 3:
                g_branch.arrived(r - 3)
                pos.at(r - 3, plane_back)
        turned[pl.ds(0, head), :] = hs[...].T.astype(bf)
        g_branch.arrived(depth - 1)
        g_branch.end()
        out_weight_back()
        x_o.start()
        pos.at(depth - 1, plane_back)
        for c in loads[7:]:
            c.wait()
        loop(depth, project_back)
        for dist in reversed(range(depth)):
            pos.at(dist, lambda z: swap.start(z, gproj))
        turned[...] = gproj[...].T
        in_weight_back()
        x_q.start()
        r_kv.start()
        swap_in.wait_recv()
        for dist in (depth - 1, depth - 2):
            pos.at(dist, spread)
        for i in range(gain_rows):
            small[pl.ds(i, 1), :] = by_norm[:, pl.ds(i * 128, 128)]
            small[pl.ds(gain_rows + i, 1), :] = moe[:, pl.ds(i * 128, 128)]
        small[pl.ds(2 * gain_rows, 1), :] = by_q[...]
        small[pl.ds(2 * gain_rows + 1, 1), :] = by_k[...]
        small_all[device] = small[...]
        g_small.start()
        for r in range(red.rounds):
            if 1 <= r < depth - 1:
                pos.at(depth - 2 - r, spread)
            red.round(r)
            r_kv.round(r)
            g_small.round(r)
            if r == 2:
                turned[pl.ds(0, lanes), :] = gb[:, :, pl.ds(width, lanes)].reshape(total, lanes).T
                router_back()
        change, _ = norm_back(tb[...].astype(f32), norm_row[...], hidden_sum[...])
        tokens_grad[...] = gm[...] + change
        k_grad[...] = kv_sum[:, pl.ds(0, head)]
        v_grad[...] = kv_sum[:, pl.ds(head, head)]
        g_small.end()
        summed = jnp.sum(small_all[...], axis=0)
        norm_sum[...] = summed[:gain_rows]
        moe_sum[...] = summed[gain_rows : 2 * gain_rows]
        q_sum[...] = summed[2 * gain_rows : 2 * gain_rows + 1]
        k_sum[...] = summed[2 * gain_rows + 1 : 2 * gain_rows + 2]
        x_o.end()
        x_q.end()
        red.end()
        r_kv.end()
        swap.end()
        swap_in.wait_send()

    vmem, hbm = pl.BlockSpec(memory_space=pltpu.VMEM), pl.BlockSpec(memory_space=HBM)
    dma = pltpu.SemaphoreType.DMA
    shape = jax.ShapeDtypeStruct
    V = pltpu.VMEM
    return pl.pallas_call(
        body,
        out_shape=[
            shape((rows, width), f32),
            shape((w_rows, groups * head), bf),
            shape((w_rows, head), f32),
            shape((w_rows, head), f32),
            shape((w_rows, groups * head), bf),
            shape((gain_rows, 128), f32),
            shape((gain_rows, 128), f32),
            shape((1, 128), f32),
            shape((1, 128), f32),
            shape((experts_in_all, width), f32),
        ],
        in_specs=[hbm, vmem, vmem] + [hbm] * 13 + [vmem] * 4,
        out_specs=[vmem, hbm, vmem, vmem, hbm] + [vmem] * 5,
        scratch_shapes=[
            V((devices, rows, wide), bf),
            V((devices, rows, width), bf),
            V((rows, width), bf),
            V((devices, rows, width), bf),
            V((width, 3 * head), bf),
            V((6 * head, width), bf),
            V((width, head), bf),
            V((total, 3 * head), f32),
            V((total, head), bf),
            V((total, head), bf),
            V((total, head), bf),
            V((total, head), f32),
            V((total, head), f32),
            V((total, head), f32),
            V((total, head), f32),
            V((total, head), bf),
            V((total, head), f32),
            V((total, head), f32),
            V((total, head), f32),
            V((total, 3 * head), bf),
            V((width, 3 * head), bf),
            V((width, head), bf),
            V((w_rows, 2 * head), f32),
            V((rows, width), f32),
            V((small_rows, 128), f32),
            V((devices, small_rows, 128), f32),
            V((1, width), f32),
            V((1, head), f32),
            V((1, head), f32),
            V((total, head), f32),
            V((3 * head, total), bf),
            V((1, width), f32),
            dma((13,)),
            dma,
        ]
        + WideGather.sems(depth)
        + Gather.sems(depth)
        + Exchange.sems(depth) * 2
        + Reduce.scratch(depth, rows, width, BACK_HALVES, BACK_FLANK)
        + HubReduce.scratch(depth, w_rows, 2 * head)
        + CoreSwap.scratch(depth, rows, 3 * head)
        + [dma((2,))],
        compiler_params=params(number, 60 * 2**20),
        name="attend_back",
    )(block, moe_gain_grad, grad_middle, all_normed, *kept, norm_gain, q_gain, k_gain, docs)


def head_shards(
    tokens,
    segments,
    routes,
    out_grad,
    norm_gain,
    q_weight,
    k_weight,
    v_weight,
    q_gain,
    k_gain,
    out_weight,
    moe_gain,
    router_weight,
    gate_weight,
    up_weight,
    down_weight,
):
    f32, bf = jnp.float32, jnp.bfloat16
    f32, bf = jnp.float32, jnp.bfloat16
    head_dim = q_gain.shape[0]
    tok_rows, width = tokens.shape
    all_tokens = segments.shape[0]
    expert_count = router_weight.shape[1]
    depth = all_tokens // tok_rows // 2
    norm_gain, q_gain, k_gain, moe_gain = (g.reshape(-1, 128) for g in (norm_gain, q_gain, k_gain, moe_gain))
    docs = segments[None]
    frequency = (THETA ** (np.arange(head_dim // 2) * -2.0 / head_dim)).astype(np.float32)
    middle, normed, all_named, all_grad, *kept = attend(
        depth,
        0,
        tokens,
        routes.T,
        out_grad,
        q_weight,
        k_weight,
        v_weight,
        out_weight,
        (norm_gain, q_gain, k_gain, moe_gain),
        np.concatenate([frequency, frequency])[None],
        docs,
    )
    layer_out, grad_middle, grad_block, moe_gain_grad, all_normed, *pairs = experts(
        depth,
        1,
        normed,
        all_grad,
        all_named,
        middle,
        moe_gain,
        router_weight.T,
        gate_weight[0],
        up_weight[0],
        down_weight[0],
    )
    tokens_grad, grad_q, grad_k, grad_v, grad_o, norm_sum, moe_sum, q_sum, k_sum, grad_router = attend_back(
        depth,
        2,
        grad_block,
        moe_gain_grad,
        grad_middle,
        all_normed,
        expert_count,
        kept,
        (norm_gain, q_gain, k_gain),
        docs,
    )
    grad_gate_w, grad_up_w, grad_down, grad_q, grad_o, *rest = finish(
        pairs,
        grad_q,
        grad_o,
        (layer_out, tokens_grad, grad_k, grad_v, norm_sum, moe_sum, q_sum, k_sum, grad_router),
    )
    layer_out, tokens_grad, grad_k, grad_v, norm_sum, moe_sum, q_sum, k_sum, grad_router = rest
    return (
        layer_out,
        tokens_grad,
        norm_sum.reshape(-1),
        grad_q,
        grad_k,
        grad_v,
        q_sum.reshape(-1),
        k_sum.reshape(-1),
        grad_o,
        moe_sum.reshape(-1),
        grad_router.T,
        grad_gate_w[None],
        grad_up_w[None],
        grad_down[None],
    )


def solution(mesh):
    per_device = shards if mesh.shape["dp"] != 8 or mesh.shape["tensor"] != 4 else head_shards
    placed = (
        P("dp", None),
        P(),
        P(("dp", "tensor"), None),
        P(("dp", "tensor"), None),
        P(),
        P("dp", "tensor"),
        P("dp", "tensor"),
        P("dp", "tensor"),
        P(),
        P(),
        P("dp", "tensor"),
        P(),
        P(),
        P(("dp", "tensor"), None, None),
        P(("dp", "tensor"), None, None),
        P(("dp", "tensor"), None, None),
    )
    return jax.shard_map(
        per_device,
        mesh=mesh,
        in_specs=placed,
        out_specs=(
            P(("dp", "tensor"), None),
            P(("dp", "tensor"), None),
            P(),
            P("dp", "tensor"),
            P("dp", "tensor"),
            P("dp", "tensor"),
            P(),
            P(),
            P("dp", "tensor"),
            P(),
            P(),
            P(("dp", "tensor"), None, None),
            P(("dp", "tensor"), None, None),
            P(("dp", "tensor"), None, None),
        ),
        check_vma=False,
    )
```
